32 devices in a mesh: dp: 8 (over y, x, core), seq: 4 (over z).
Axes of the slice: x: 2, y: 2, z: 4, core: 2. Of those that a mesh axis runs over, the one named last changes fastest.
Arguments:
- inputs: bfloat16 [16, 2048, 1024], P('dp', 'seq'), may hold values from -6 to 6
- cotangent: bfloat16 [16, 2048, 1024], P('dp', 'seq'), may hold values from -6 to 6
- full_attention: int32 [16], P('dp'), may hold values from 0 to 1
- mix_gain: float32 [1024], replicated, may hold values from 0.5 to 1.5
- smooth_alpha: float32 [16, 1024], replicated, may hold values from 0.1 to 0.9
- smooth_damp: float32 [16, 1024], replicated, may hold values from 0.0001 to 0.3
- smooth_beta: float32 [16, 1024], replicated, may hold values from -0.75 to 0.75
- smooth_eta: float32 [16, 1024], replicated, may hold values from -1.5 to 1.5
- smooth_omega: float32 [1024], replicated, may hold values from -6 to 6
- value_proj: bfloat16 [1024, 2048], replicated, may hold values from -0.1875 to 0.1875
- mix_proj: bfloat16 [1024, 4224], replicated, may hold values from -0.1875 to 0.1875
- score_affine: float32 [4, 128], replicated, may hold values from -6 to 6
- relative_bias: float32 [4096], replicated, may hold values from -6 to 6
- out_proj: bfloat16 [2048, 1024], replicated, may hold values from -0.5 to 0.5
- feed_gain: float32 [1024], replicated, may hold values from 0.1 to 1.9
- feed_in: bfloat16 [1024, 4096], replicated, may hold values from -0.1875 to 0.1875
- feed_out: bfloat16 [4096, 1024], replicated, may hold values from -0.09375 to 0.09375
Outputs:
- block_out: bfloat16 [16, 2048, 1024], P('dp', 'seq')
- grad_input: float32 [16, 2048, 1024], P('dp', 'seq')
- mix_gain_grad: float32 [1024], replicated
- alpha_grad: float32 [16, 1024], replicated
- damp_grad: float32 [16, 1024], replicated
- beta_grad: float32 [16, 1024], replicated
- eta_grad: float32 [16, 1024], replicated
- omega_grad: float32 [1024], replicated
- value_grad: float32 [1024, 2048], P('dp', 'seq')
- mix_grad: float32 [1024, 4224], P('dp', 'seq')
- affine_grad: float32 [4, 128], replicated
- relative_grad: float32 [4096], replicated
- out_grad: float32 [2048, 1024], P('dp', 'seq')
- feed_gain_grad: float32 [1024], replicated
- feed_in_grad: float32 [1024, 4096], P('dp', 'seq')
- feed_out_grad: float32 [4096, 1024], P('dp', 'seq')
The draws below stay inside these ranges and needn't reach their ends.
Inputs may be any that keep to these rules, and one draw needn't show every extreme that they name: `full_attention`: 1 marks a sequence whose tokens attend to all earlier tokens of it, 0 one whose tokens attend only within their block of 128 positions.
All inputs are finite; a program needn't handle non-finite values.
Results may differ from the reference program's by a relative error of at most 0.035.
Values may be sent and summed in bfloat16 or wider, within the bound.
No kernel may reach another device: no remote copies, remote signals or barrier semaphores. Data moves between devices by JAX's collectives and lax.ppermute only.
A program may use at most 512 MiB of HBM per device.

```python
import math
import jax
import jax.numpy as jnp
from jax import lax

D = 1024
Z = 128
V = 2048
NDIM = 16
FF = 4096
SEQ_LEN = 2048
STRETCH = 128
BATCH = 16
MIXW = 4224


def draw_smooth_damp(key, part):
    key = jax.random.fold_in(key, 17)
    unit_draw = jax.random.uniform(key, (NDIM, D), jnp.float32)
    upper = 0.3
    return jnp.exp(jnp.log(0.0001) + unit_draw * (jnp.log(upper) - jnp.log(0.0001)))


def with_ends(entries, own_key, least, largest):
    longest = entries.shape.index(max(entries.shape))
    spots = []
    for shift in (0, 1):
        where = [jax.random.randint(jax.random.fold_in(own_key, axis), (), 0, length) for axis, length in enumerate(entries.shape)]
        where[longest] = (where[longest] + shift) % entries.shape[longest]
        spots.append(tuple(where))
    return entries.at[spots[0]].set(least).at[spots[1]].set(largest)


def level_of(stream_key, extent, cuts, low, top_value):
    loudness = 1.0
    for dim, blocks in cuts:
        steps = jax.random.uniform(jax.random.fold_in(jax.random.fold_in(stream_key, 6), dim), (blocks,), jnp.float32, low / len(cuts), top_value / len(cuts))
        loudness = loudness * jnp.repeat(jnp.exp(steps), extent[dim] // blocks).reshape((-1,) + (1,) * (len(extent) - 1 - dim))
    return loudness


def normal_values(own_key, shape, width, limit, pieces=(), dtype=jnp.bfloat16):
    array = jax.random.normal(own_key, shape, jnp.float32) * width
    if len(pieces) > 0:
        array = level_of(own_key, shape, pieces, -0.22, 0.18) * array
    return jnp.clip(array, min=-limit, max=limit).astype(dtype)


def setup_inputs(seed: int = 0) -> dict:
    keys = jax.random.split(jax.random.key(seed), 18)
    inputs = normal_values(keys[0], (BATCH, SEQ_LEN, D), 1.0, 6.0, ((0, 8), (1, 4)))
    cotangent = normal_values(keys[1], (BATCH, SEQ_LEN, D), 1.0, 6.0, ((0, 8), (1, 4)))
    full_attention = with_ends(jax.random.randint(keys[2], (BATCH,), 0, 2), jax.random.fold_in(keys[2], 1), 0, 1).astype(jnp.int32)
    mix_gain = jnp.clip(1.0 + 0.1 * jax.random.normal(keys[3], (D,), jnp.float32), 0.5, 1.5)
    smooth_alpha = jnp.clip(jnp.exp(jax.random.uniform(keys[4], (NDIM, D), jnp.float32, math.log(0.1), math.log(0.9))), 0.1, 0.9)
    smooth_damp = draw_smooth_damp(jax.random.fold_in(keys[17], 71), 0)
    smooth_beta = normal_values(keys[6], (NDIM, D), 0.05, 0.75, (), jnp.float32)
    smooth_eta = normal_values(keys[7], (NDIM, D), NDIM ** -0.5, 1.5, (), jnp.float32)
    smooth_omega = normal_values(keys[8], (D,), 1.0, 6.0, (), jnp.float32)
    value_proj = normal_values(keys[9], (D, V), D ** -0.5, 0.1875)
    mix_proj = normal_values(keys[10], (D, MIXW), D ** -0.5, 0.1875)
    score_affine = normal_values(keys[11], (4, Z), 1.0, 6.0, (), jnp.float32)
    relative_bias = normal_values(keys[12], (2 * SEQ_LEN,), 0.7, 6.0, (), jnp.float32)
    out_proj = normal_values(keys[13], (V, D), (V // 16) ** -0.5, 0.5)
    feed_gain = jnp.clip(1.0 + 0.18 * jax.random.normal(keys[14], (D,), jnp.float32), 0.1, 1.9)
    feed_in = normal_values(keys[15], (D, FF), D ** -0.5, 0.1875)
    feed_out = normal_values(keys[16], (FF, D), FF ** -0.5, 0.09375)
    return dict(inputs=inputs, cotangent=cotangent, full_attention=full_attention, mix_gain=mix_gain, smooth_alpha=smooth_alpha, smooth_damp=smooth_damp, smooth_beta=smooth_beta, smooth_eta=smooth_eta, smooth_omega=smooth_omega, value_proj=value_proj, mix_proj=mix_proj, score_affine=score_affine, relative_bias=relative_bias, out_proj=out_proj, feed_gain=feed_gain, feed_in=feed_in, feed_out=feed_out)


@jax.custom_vjp
def low(v):
    return lax.optimization_barrier(v.astype(jnp.bfloat16)).astype(jnp.float32)

@jax.custom_vjp
def low_back(v):
    return v

def low_keep(v):
    return (low(v), None)

def low_pass(kept, grad):
    return (grad,)

def back_keep(v):
    return (v, None)

def back_low(kept, grad):
    return (low(grad),)
low.defvjp(low_keep, low_pass)
low_back.defvjp(back_keep, back_low)

def matmul_hi(left, right):
    return jnp.dot(left, right, preferred_element_type=jnp.float32, precision=lax.Precision.HIGHEST)

def layer_norm(values, gain_vec):
    row_mean = lax.optimization_barrier(jnp.mean(values, axis=-1, keepdims=True))
    centred = values - row_mean
    variance = lax.optimization_barrier(jnp.mean(centred * centred, axis=-1, keepdims=True))
    return centred * lax.rsqrt(variance + 1e-05) * gain_vec

def block_forward(params, inputs, full_flag):
    mix_gain, smooth_alpha, smooth_damp, smooth_beta, smooth_eta, smooth_omega, value_proj, mix_proj, score_affine, relative_bias, out_proj, feed_gain, feed_in, feed_out = params
    length = inputs.shape[0]
    normed = layer_norm(inputs, mix_gain)
    decay_rate = 1.0 - smooth_alpha * smooth_damp
    rate_in = smooth_alpha * smooth_beta

    def smooth_step(carried_state, row_vec):
        carried_state = decay_rate * carried_state + rate_in * row_vec[None, :]
        return (carried_state, lax.optimization_barrier(jnp.sum(smooth_eta * carried_state, axis=0)))
    _, smoothed = lax.scan(jax.checkpoint(smooth_step), jnp.zeros(decay_rate.shape, jnp.float32), normed)
    mixed = low(jax.nn.silu(smoothed + smooth_omega * normed))
    mix_base = low_back(matmul_hi(mixed, mix_proj))
    shared_pre = mix_base[:, :Z]
    reset_pre = mix_base[:, Z:Z + V]
    update_pre = mix_base[:, Z + V:Z + V + D]
    cand_pre = mix_base[:, Z + V + D:]
    shared = jax.nn.silu(shared_pre)
    queries = low(shared * score_affine[0] + score_affine[1])
    key_rows = low(shared * score_affine[2] + score_affine[3])
    value_rows = low(jax.nn.silu(low_back(matmul_hi(low(normed), value_proj))))
    row_index = jnp.arange(length)[:, None]
    col_index = jnp.arange(length)[None, :]
    bias_tile = relative_bias[col_index - row_index + length]
    scores = low_back(matmul_hi(queries, key_rows.T) * Z ** (-0.5) + bias_tile)
    allowed = (col_index <= row_index) & ((full_flag == 1) | (col_index // STRETCH == row_index // STRETCH))
    scores = jnp.where(allowed, scores, -1e+30)
    row_max = lax.optimization_barrier(jnp.max(scores, axis=1, keepdims=True))
    exp_terms = jnp.exp(scores - row_max)
    soft_probs = low(exp_terms / lax.optimization_barrier(jnp.sum(exp_terms, axis=1, keepdims=True)))
    attended = low_back(matmul_hi(soft_probs, value_rows))
    gated = low(jax.nn.silu(reset_pre) * attended)
    candidate = jax.nn.silu(low_back(cand_pre + matmul_hi(gated, out_proj)))
    update = jax.nn.sigmoid(update_pre)
    first_sum = inputs + update * (candidate - inputs)
    hidden = low_back(matmul_hi(low(layer_norm(first_sum, feed_gain)), feed_in))
    return first_sum + low_back(matmul_hi(low(jax.nn.silu(hidden)), feed_out))

def reference(inputs, cotangent, full_attention, mix_gain, smooth_alpha, smooth_damp, smooth_beta, smooth_eta, smooth_omega, value_proj, mix_proj, score_affine, relative_bias, out_proj, feed_gain, feed_in, feed_out):
    params = tuple((p.astype(jnp.float32) for p in (mix_gain, smooth_alpha, smooth_damp, smooth_beta, smooth_eta, smooth_omega, value_proj, mix_proj, score_affine, relative_bias, out_proj, feed_gain, feed_in, feed_out)))

    def one_sequence(totals, seq_item):
        seq_inputs, cot_rows, full_flag = seq_item
        result, pull_back = jax.vjp(lambda p, v: block_forward(p, v, full_flag), params, seq_inputs.astype(jnp.float32))
        grad_parts, grad_in = pull_back(cot_rows.astype(jnp.float32))
        totals = jax.tree.map(lambda a, b: a + b, totals, grad_parts)
        return (totals, (result.astype(jnp.bfloat16), grad_in))
    zero_sums = jax.tree.map(jnp.zeros_like, params)
    totals, (block_out, grad_input) = lax.scan(one_sequence, zero_sums, (inputs, cotangent, full_attention))
    return (block_out, grad_input, totals[0], totals[1], totals[2], totals[3], totals[4], totals[5], totals[6], totals[7], totals[8], totals[9], totals[10], totals[11], totals[12], totals[13])
```

```python
import functools

import jax
import jax.numpy as jnp
from jax import lax
from jax.experimental import pallas as pl
from jax.experimental.pallas import tpu as pltpu
from jax.sharding import PartitionSpec as P

STRETCH = 128
EPSILON = 1e-05
TILE = 256
MASKED = -1e30
VMEM_LIMIT = 60 * 1024 * 1024
AXES = ("dp", "seq")

f32 = jnp.float32
bf16 = jnp.bfloat16


def unit_rows_of(values):
    centred = values - jnp.mean(values, axis=-1, keepdims=True)
    inv_std = lax.rsqrt(jnp.mean(centred * centred, axis=-1, keepdims=True) + EPSILON)
    return centred * inv_std, inv_std


def norm_back_rows(grad_out, gain_vec, unit_rows, inv_std):
    scaled = grad_out * gain_vec
    return inv_std * (
        scaled
        - jnp.mean(scaled, axis=-1, keepdims=True)
        - unit_rows * jnp.mean(scaled * unit_rows, axis=-1, keepdims=True)
    )


def silu_slope(pre_act):
    sigmoid_val = jax.nn.sigmoid(pre_act)
    return sigmoid_val * (1.0 + pre_act * (1.0 - sigmoid_val))


def params(semantics, limit=VMEM_LIMIT):
    return pltpu.CompilerParams(dimension_semantics=semantics, vmem_limit_bytes=limit)


def ignoring(body, first, count):
    def called(*refs):
        return body(*refs[:first], *refs[first + count :])

    return called


def to_slab(slab, rows):
    count, groups = rows.shape[0], rows.shape[1] // 128
    for c in range(groups):
        slab[pl.ds(c, count, stride=groups), :] = rows[:, c * 128 : (c + 1) * 128]


def from_slab(slab, count, groups):
    return jnp.concatenate(
        [slab[pl.ds(c, count, stride=groups), :] for c in range(groups)], axis=1
    )


def slab_row(slab, t, groups):
    return slab[pl.ds(pl.multiple_of(t * groups, groups), groups), :]


def front_ends_body(x_ref, gain_ref, decay_ref, low_ref, end_ref, slab):
    states, groups, _ = decay_ref.shape
    count = x_ref.shape[1]

    @pl.when(pl.program_id(1) == 0)
    def _():
        end_ref[...] = jnp.zeros_like(end_ref)

    unit, _ = unit_rows_of(x_ref[0].astype(f32))
    normed = unit * gain_ref[...]
    low_ref[0] = normed.astype(bf16)
    to_slab(slab, normed)
    decay = [decay_ref[n] for n in range(states)]

    def step(t, state):
        row = slab_row(slab, t, groups)
        return tuple(d * s + row for d, s in zip(decay, state))

    state = lax.fori_loop(
        0, count, step, tuple(end_ref[0, n] for n in range(states)), unroll=8
    )
    for n in range(states):
        end_ref[0, n] = state[n]


def front_ends(x, gain, decay, block=256, after=()):
    slots, length, width = x.shape
    states, groups, lanes = decay.shape
    block = min(block, length)
    return pl.pallas_call(
        ignoring(front_ends_body, 3, len(after)),
        grid=(slots, length // block),
        in_specs=[
            pl.BlockSpec((1, block, width), lambda k, b: (k, b, 0)),
            pl.BlockSpec((1, width), lambda k, b: (0, 0)),
            pl.BlockSpec((states, groups, lanes), lambda k, b: (0, 0, 0)),
        ]
        + [pl.BlockSpec(memory_space=pl.ANY)] * len(after),
        out_specs=[
            pl.BlockSpec((1, block, width), lambda k, b: (k, b, 0)),
            pl.BlockSpec((1, states, groups, lanes), lambda k, b: (k, 0, 0, 0)),
        ],
        out_shape=[
            jax.ShapeDtypeStruct((slots, length, width), bf16),
            jax.ShapeDtypeStruct((slots, states, groups, lanes), f32),
        ],
        scratch_shapes=[pltpu.VMEM((block * groups, lanes), f32)],
        compiler_params=params(("arbitrary", "arbitrary")),
        name="front_ends",
        cost_estimate=pl.CostEstimate(
            flops=slots * length * width * states * 4,
            bytes_accessed=4 * slots * length * width,
            transcendentals=0,
        ),
    )(x, gain, decay, *after)


def front_scan_body(
    table_ref,
    x_ref,
    gain_ref,
    decay_ref,
    coef_ref,
    span_ref,
    omega_ref,
    ends_ref,
    smooth_ref,
    mixed_ref,
    check_ref,
    slab,
    out_slab,
    carry,
):
    states, groups, _ = decay_ref.shape
    count = x_ref.shape[1]
    slot = pl.program_id(0)
    total = ends_ref.shape[0]

    @pl.when(pl.program_id(1) == 0)
    def _():
        carry[...] = jnp.zeros_like(carry)

        def link(i, _):
            carry[...] = span_ref[...] * carry[...] + ends_ref[table_ref[total + i]]
            return 0

        lax.fori_loop(0, table_ref[slot], link, 0)

    unit, _ = unit_rows_of(x_ref[0].astype(f32))
    normed = unit * gain_ref[...]
    to_slab(slab, normed)
    decay = [decay_ref[n] for n in range(states)]
    coef = [coef_ref[n] for n in range(states)]
    state = tuple(carry[n] for n in range(states))
    for n in range(states):
        check_ref[0, 0, n] = state[n]

    def step(t, state):
        row = slab_row(slab, t, groups)
        state = tuple(d * s + row for d, s in zip(decay, state))
        parts = [c * s for c, s in zip(coef, state)]
        while len(parts) > 1:
            parts = [a + b for a, b in zip(parts[::2], parts[1::2])]
        out_slab[pl.ds(pl.multiple_of(t * groups, groups), groups), :] = parts[0]
        return state

    state = lax.fori_loop(0, count, step, state, unroll=8)
    for n in range(states):
        carry[n] = state[n]
    smoothed = from_slab(out_slab, count, groups) + omega_ref[...] * normed
    smooth_ref[0] = smoothed
    mixed_ref[0] = (smoothed * jax.nn.sigmoid(smoothed)).astype(bf16)


def front_scan(table, x, gain, decay, coef, span, omega, ends, block):
    slots, length, width = x.shape
    states, groups, lanes = decay.shape
    whole3 = pl.BlockSpec((states, groups, lanes), lambda k, b, t: (0, 0, 0))
    row = pl.BlockSpec((1, width), lambda k, b, t: (0, 0))
    tokens = pl.BlockSpec((1, block, width), lambda k, b, t: (k, b, 0))
    return pl.pallas_call(
        front_scan_body,
        grid_spec=pltpu.PrefetchScalarGridSpec(
            num_scalar_prefetch=1,
            grid=(slots, length // block),
            in_specs=[
                tokens,
                row,
                whole3,
                whole3,
                whole3,
                row,
                pl.BlockSpec(ends.shape, lambda k, b, t: (0, 0, 0, 0)),
            ],
            out_specs=[
                tokens,
                tokens,
                pl.BlockSpec((1, 1, states, groups, lanes), lambda k, b, t: (k, b, 0, 0, 0)),
            ],
            scratch_shapes=[
                pltpu.VMEM((block * groups, lanes), f32),
                pltpu.VMEM((block * groups, lanes), f32),
                pltpu.VMEM((states, groups, lanes), f32),
            ],
        ),
        out_shape=[
            jax.ShapeDtypeStruct((slots, length, width), f32),
            jax.ShapeDtypeStruct((slots, length, width), bf16),
            jax.ShapeDtypeStruct((slots, length // block, states, groups, lanes), f32),
        ],
        compiler_params=params(("arbitrary", "arbitrary")),
        name="front_scan",
        cost_estimate=pl.CostEstimate(
            flops=slots * length * width * states * 8,
            bytes_accessed=8 * slots * length * width,
            transcendentals=slots * length * width,
        ),
    )(table, x, gain, decay, coef, span, omega, ends)


def back_ends_body(gs_ref, decay_ref, end_ref, slab):
    states, groups, _ = decay_ref.shape
    count = gs_ref.shape[1]

    @pl.when(pl.program_id(1) == 0)
    def _():
        end_ref[...] = jnp.zeros_like(end_ref)

    to_slab(slab, gs_ref[0])
    decay = [decay_ref[n] for n in range(states)]

    def step(t, state):
        row = slab_row(slab, count - 1 - t, groups)
        return tuple(d * s + row for d, s in zip(decay, state))

    state = lax.fori_loop(
        0, count, step, tuple(end_ref[0, n] for n in range(states)), unroll=8
    )
    for n in range(states):
        end_ref[0, n] = state[n]


def back_ends(gs, decay, block=256, after=()):
    slots, length, width = gs.shape
    states, groups, lanes = decay.shape
    block = min(block, length)
    blocks = length // block
    return pl.pallas_call(
        ignoring(back_ends_body, 2, len(after)),
        grid=(slots, blocks),
        in_specs=[
            pl.BlockSpec((1, block, width), lambda k, b: (k, blocks - 1 - b, 0)),
            pl.BlockSpec((states, groups, lanes), lambda k, b: (0, 0, 0)),
        ]
        + [pl.BlockSpec(memory_space=pl.ANY)] * len(after),
        out_specs=pl.BlockSpec((1, states, groups, lanes), lambda k, b: (k, 0, 0, 0)),
        out_shape=jax.ShapeDtypeStruct((slots, states, groups, lanes), f32),
        scratch_shapes=[pltpu.VMEM((block * groups, lanes), f32)],
        compiler_params=params(("arbitrary", "arbitrary")),
        name="back_ends",
        cost_estimate=pl.CostEstimate(
            flops=slots * length * width * states * 4,
            bytes_accessed=4 * slots * length * width,
            transcendentals=0,
        ),
    )(gs, decay, *after)


def back_scan_body(
    table_ref,
    x_ref,
    gs_ref,
    gv_ref,
    gi_ref,
    check_ref,
    gain_ref,
    decay_ref,
    coef_ref,
    span_ref,
    omega_ref,
    ends_ref,
    grad_ref,
    qx_ref,
    qs_ref,
    gain_grad_ref,
    omega_grad_ref,
    slab,
    gs_slab,
    out_slab,
    history,
    carry,
):
    states, groups, _ = decay_ref.shape
    count = x_ref.shape[1]
    slot = pl.program_id(0)
    total = ends_ref.shape[0]

    @pl.when((slot == 0) & (pl.program_id(1) == 0))
    def _():
        qx_ref[...] = jnp.zeros_like(qx_ref)
        qs_ref[...] = jnp.zeros_like(qs_ref)
        gain_grad_ref[...] = jnp.zeros_like(gain_grad_ref)
        omega_grad_ref[...] = jnp.zeros_like(omega_grad_ref)

    @pl.when(pl.program_id(1) == 0)
    def _():
        carry[...] = jnp.zeros_like(carry)

        def link(i, _):
            carry[...] = (
                span_ref[...] * carry[...] + ends_ref[table_ref[total + total - 1 - i]]
            )
            return 0

        lax.fori_loop(0, total - 1 - table_ref[slot], link, 0)

    unit, inv = unit_rows_of(x_ref[0].astype(f32))
    normed = unit * gain_ref[...]
    gs = gs_ref[0]
    to_slab(slab, normed)
    to_slab(gs_slab, gs)
    decay = [decay_ref[n] for n in range(states)]

    def recompute(t, state):
        for n in range(states):
            history[t, n] = state[n]
        row = slab_row(slab, t, groups)
        return tuple(d * s + row for d, s in zip(decay, state))

    lax.fori_loop(
        0, count, recompute, tuple(check_ref[0, 0, n] for n in range(states)), unroll=4
    )

    half = states // 2
    for part in range(2):
        chosen = range(part * half, (part + 1) * half)
        decay = [decay_ref[n] for n in chosen]
        coef = [coef_ref[n] for n in chosen]

        def step(i, held):
            q, qx, qs = held
            t = count - 1 - i
            row = slab_row(slab, t, groups)
            g = slab_row(gs_slab, t, groups)
            q = tuple(d * a + g for d, a in zip(decay, q))
            parts = [c * a for c, a in zip(coef, q)]
            while len(parts) > 1:
                parts = [a + b for a, b in zip(parts[::2], parts[1::2])]
            spot = pl.ds(pl.multiple_of(t * groups, groups), groups)
            if part == 0:
                out_slab[spot, :] = parts[0]
            else:
                out_slab[spot, :] = out_slab[spot, :] + parts[0]
            qx = tuple(a + b * row for a, b in zip(qx, q))
            qs = tuple(a + b * history[t, n] for a, b, n in zip(qs, q, chosen))
            return q, qx, qs

        q, qx, qs = lax.fori_loop(
            0,
            count,
            step,
            (
                tuple(carry[n] for n in chosen),
                tuple(qx_ref[n] for n in chosen),
                tuple(qs_ref[n] for n in chosen),
            ),
            unroll=4,
        )
        for i, n in enumerate(chosen):
            carry[n] = q[i]
            qx_ref[n] = qx[i]
            qs_ref[n] = qs[i]

    grad_normed = (
        gv_ref[0] + from_slab(out_slab, count, groups) + omega_ref[...] * gs
    )
    gain_grad_ref[...] += jnp.sum(grad_normed * unit, axis=0, keepdims=True)
    omega_grad_ref[...] += jnp.sum(gs * normed, axis=0, keepdims=True)
    grad_ref[0] = (
        gi_ref[0] + norm_back_rows(grad_normed, gain_ref[...], unit, inv)
    ).astype(bf16)


def back_scan(table, x, gs, gv, gi, check, gain, decay, coef, span, omega, ends, after=()):
    slots, length, width = x.shape
    states, groups, lanes = decay.shape
    blocks = check.shape[1]
    block = length // blocks
    whole3 = pl.BlockSpec((states, groups, lanes), lambda k, b, t: (0, 0, 0))
    row = pl.BlockSpec((1, width), lambda k, b, t: (0, 0))
    tokens = pl.BlockSpec((1, block, width), lambda k, b, t: (k, blocks - 1 - b, 0))
    return pl.pallas_call(
        ignoring(back_scan_body, 12, len(after)),
        grid_spec=pltpu.PrefetchScalarGridSpec(
            num_scalar_prefetch=1,
            grid=(slots, blocks),
            in_specs=[
                tokens,
                tokens,
                tokens,
                tokens,
                pl.BlockSpec(
                    (1, 1, states, groups, lanes),
                    lambda k, b, t: (k, blocks - 1 - b, 0, 0, 0),
                ),
                row,
                whole3,
                whole3,
                whole3,
                row,
                pl.BlockSpec(ends.shape, lambda k, b, t: (0, 0, 0, 0)),
            ]
            + [pl.BlockSpec(memory_space=pl.ANY)] * len(after),
            out_specs=[tokens, whole3, whole3, row, row],
            scratch_shapes=[
                pltpu.VMEM((block * groups, lanes), f32),
                pltpu.VMEM((block * groups, lanes), f32),
                pltpu.VMEM((block * groups, lanes), f32),
                pltpu.VMEM((block, states, groups, lanes), f32),
                pltpu.VMEM((states, groups, lanes), f32),
            ],
        ),
        out_shape=[
            jax.ShapeDtypeStruct((slots, length, width), bf16),
            jax.ShapeDtypeStruct((states, groups, lanes), f32),
            jax.ShapeDtypeStruct((states, groups, lanes), f32),
            jax.ShapeDtypeStruct((1, width), f32),
            jax.ShapeDtypeStruct((1, width), f32),
        ],
        compiler_params=params(("arbitrary", "arbitrary")),
        name="back_scan",
        cost_estimate=pl.CostEstimate(
            flops=slots * length * width * states * 20,
            bytes_accessed=16 * slots * length * width,
            transcendentals=0,
        ),
    )(table, x, gs, gv, gi, check, gain, decay, coef, span, omega, ends, *after)


def load_chunks(table_ref, sources, total, length, sem):
    copies = []
    for slot in range(total):
        place = pl.ds(pl.multiple_of(table_ref[slot] * length, length), length)
        for own, others, kept in sources:
            source = own.at[slot] if slot < 2 else others.at[slot - 2]
            copies.append(
                pltpu.make_async_copy(source, kept.at[place, :], sem.at[len(copies)])
            )
    for copy in copies:
        copy.start()
    for copy in copies:
        copy.wait()


def attend_body(
    table_ref,
    q_ref,
    bias_ref,
    reset_ref,
    k_own,
    k_oth,
    v_own,
    v_oth,
    out_ref,
    gated_ref,
    lse_ref,
    keys,
    values,
    scores,
    probs,
    sem,
    *,
    total,
):
    length, key_width = q_ref.shape[1:]
    value_width = values.shape[1]
    tiles = length // TILE
    scale = float(key_width) ** (-0.5)

    @pl.when(pl.program_id(0) == 0)
    def _():
        load_chunks(
            table_ref, ((k_own, k_oth, keys), (v_own, v_oth, values)), total, length, sem
        )

    chunk = table_ref[pl.program_id(0)]
    reach = jnp.where(table_ref[2 * total] == 1, chunk + 1, 1)
    base = (chunk + 1 - reach) * length
    queries = q_ref[0]

    def first(kt, peak):
        spot = pl.ds(pl.multiple_of(base + kt * TILE, TILE), TILE)
        tile = (
            lax.dot_general(
                queries, keys[spot, :], (((1,), (1,)), ((), ())), preferred_element_type=f32
            )
            * scale
        )
        for r in range(tiles):
            rows = slice(r * TILE, (r + 1) * TILE)
            gap = (reach - 1) * tiles + r - kt + tiles - 1
            scores[kt, rows, :] = tile[rows] + bias_ref[gap]
        return jnp.maximum(peak, jnp.max(scores[kt], axis=1, keepdims=True))

    peak = lax.fori_loop(
        0, reach * tiles, first, jnp.full((length, 1), 2 * MASKED, f32)
    )

    def second(kt, sums):
        terms = jnp.exp(scores[kt] - peak)
        probs[:, pl.ds(pl.multiple_of(kt * TILE, TILE), TILE)] = terms.astype(bf16)
        return sums + jnp.sum(terms, axis=1, keepdims=True)

    sums = lax.fori_loop(0, reach * tiles, second, jnp.zeros((length, 1), f32))
    lse_ref[0] = peak + jnp.log(sums)
    inverse = 1.0 / sums

    for count in range(1, total + 1):

        @pl.when(reach == count)
        def _(count=count):
            width = count * length
            span = pl.ds(pl.multiple_of(base, length), width)

            def column(ct, _):
                at = pl.ds(pl.multiple_of(ct * TILE, TILE), TILE)
                rows = (
                    jnp.dot(probs[:, :width], values[span, at], preferred_element_type=f32)
                    * inverse
                )
                out_ref[0, :, at] = rows.astype(bf16)
                gate = reset_ref[0, :, at].astype(f32)
                gated_ref[0, :, at] = (gate * jax.nn.sigmoid(gate) * rows).astype(bf16)
                return 0

            lax.fori_loop(0, value_width // TILE, column, 0)


def attend(table, q, bias, reset, k_own, k_oth, v_own, v_oth):
    slots, length, key_width = q.shape
    value_width = v_own.shape[2]
    total = slots + k_oth.shape[0]
    anywhere = pl.BlockSpec(memory_space=pl.ANY)
    tokens = pl.BlockSpec((1, length, value_width), lambda k, t: (k, 0, 0))
    return pl.pallas_call(
        functools.partial(attend_body, total=total),
        grid_spec=pltpu.PrefetchScalarGridSpec(
            num_scalar_prefetch=1,
            grid=(slots,),
            in_specs=[
                pl.BlockSpec((1, length, key_width), lambda k, t: (k, 0, 0)),
                pl.BlockSpec(bias.shape, lambda k, t: (0, 0, 0)),
                tokens,
                anywhere,
                anywhere,
                anywhere,
                anywhere,
            ],
            out_specs=[
                tokens,
                tokens,
                pl.BlockSpec((1, length, 1), lambda k, t: (k, 0, 0)),
            ],
            scratch_shapes=[
                pltpu.VMEM((total * length, key_width), bf16),
                pltpu.VMEM((total * length, value_width), bf16),
                pltpu.VMEM((total * length // TILE, length, TILE), f32),
                pltpu.VMEM((length, total * length), bf16),
                pltpu.SemaphoreType.DMA((2 * total,)),
            ],
        ),
        out_shape=[
            jax.ShapeDtypeStruct((slots, length, value_width), bf16),
            jax.ShapeDtypeStruct((slots, length, value_width), bf16),
            jax.ShapeDtypeStruct((slots, length, 1), f32),
        ],
        compiler_params=params(("arbitrary",)),
        name="attend",
        cost_estimate=pl.CostEstimate(
            flops=slots * length * total * length * (key_width + value_width),
            bytes_accessed=20 * slots * length * value_width,
            transcendentals=slots * length * total * length,
        ),
    )(table, q, bias, reset, k_own, k_oth, v_own, v_oth)


def attend_back_body(
    table_ref,
    q_ref,
    grad_ref,
    lse_ref,
    bias_ref,
    k_own,
    k_oth,
    v_own,
    v_oth,
    gq_ref,
    gk_own,
    gk_oth,
    gv_own,
    gv_oth,
    rel_out,
    keys,
    values,
    gk_sum,
    gv_sum,
    probs_kept,
    grads_kept,
    rel_ref,
    sem,
    *,
    total,
):
    length, key_width = q_ref.shape[1:]
    value_width = values.shape[1]
    tiles = length // TILE
    scale = float(key_width) ** (-0.5)
    step = pl.program_id(0)
    nt = (((1,), (1,)), ((), ()))
    tn = (((0,), (0,)), ((), ()))

    @pl.when(step == 0)
    def _():
        gk_sum[...] = jnp.zeros_like(gk_sum)
        gv_sum[...] = jnp.zeros_like(gv_sum)
        rel_ref[...] = jnp.zeros_like(rel_ref)
        load_chunks(
            table_ref, ((k_own, k_oth, keys), (v_own, v_oth, values)), total, length, sem
        )

    chunk = table_ref[step]
    reach = jnp.where(table_ref[2 * total] == 1, chunk + 1, 1)
    base = (chunk + 1 - reach) * length
    queries = q_ref[0]
    log_total = lse_ref[0]

    def gap_of(kc, a, r):
        return (reach - 1 - kc) * tiles + r - a + tiles - 1

    def first(kc, delta):
        spot = pl.ds(pl.multiple_of(base + kc * length, length), length)
        grads_kept[kc] = lax.dot_general(
            values[spot, :], grad_ref[0], nt, preferred_element_type=f32
        )
        tile = (
            lax.dot_general(keys[spot, :], queries, nt, preferred_element_type=f32) * scale
        )
        for a in range(tiles):
            for r in range(tiles):
                rows = slice(a * TILE, (a + 1) * TILE)
                cols = slice(r * TILE, (r + 1) * TILE)
                probs_kept[kc, rows, cols] = jnp.exp(
                    tile[rows, cols] + bias_ref[gap_of(kc, a, r)] - log_total[:, cols]
                )
        return delta + jnp.sum(probs_kept[kc] * grads_kept[kc], axis=0, keepdims=True)

    delta = lax.fori_loop(0, reach, first, jnp.zeros((1, length), f32))

    def second(kc, grad_query):
        spot = pl.ds(pl.multiple_of(base + kc * length, length), length)
        probs = probs_kept[kc]
        grad_scores = (probs * (grads_kept[kc] - delta)).astype(bf16)
        probs = probs.astype(bf16)
        for a in range(tiles):
            for r in range(tiles):
                rel_ref[gap_of(kc, a, r)] += grad_scores[
                    a * TILE : (a + 1) * TILE, r * TILE : (r + 1) * TILE
                ].astype(f32)
        gk_sum[spot, :] += jnp.dot(grad_scores, queries, preferred_element_type=f32)

        def column(ct, _):
            at = pl.ds(pl.multiple_of(ct * 512, 512), 512)
            gv_sum[spot, at] += jnp.dot(
                probs, grad_ref[0, :, at], preferred_element_type=f32
            )
            return 0

        lax.fori_loop(0, value_width // 512, column, 0)
        return grad_query + lax.dot_general(
            grad_scores, keys[spot, :], tn, preferred_element_type=f32
        )

    grad_query = lax.fori_loop(0, reach, second, jnp.zeros((length, key_width), f32))
    gq_ref[0] = grad_query * scale

    @pl.when(step == pl.num_programs(0) - 1)
    def _():
        for slot in range(total):
            place = pl.ds(pl.multiple_of(table_ref[slot] * length, length), length)
            key_out, value_out = (gk_own, gv_own) if slot < 2 else (gk_oth, gv_oth)
            at = slot if slot < 2 else slot - 2
            key_out[at] = (gk_sum[place, :] * scale).astype(bf16)
            value_out[at] = gv_sum[place, :].astype(bf16)
        down = lax.broadcasted_iota(jnp.int32, (TILE, TILE), 0)
        across = lax.broadcasted_iota(jnp.int32, (TILE, TILE), 1)
        mirror = jnp.where(down + across == TILE - 1, 1.0, 0.0)
        for d in range(rel_out.shape[0]):
            flipped = jnp.dot(
                rel_ref[d + tiles - 1],
                mirror,
                precision=lax.Precision.HIGHEST,
                preferred_element_type=f32,
            )
            wide = jnp.concatenate([flipped, jnp.zeros((TILE, TILE), f32)], axis=1)
            turned = pltpu.roll(wide, 0, 1, stride=1, stride_axis=0)
            rel_out[d] = jnp.sum(turned, axis=0, keepdims=True)


def attend_back(table, q, grads, lse, bias, k_own, k_oth, v_own, v_oth, after=()):
    slots, length, key_width = q.shape
    value_width = v_own.shape[2]
    total = slots + k_oth.shape[0]
    rel_shape = (total * length // TILE, 1, 2 * TILE)
    anywhere = pl.BlockSpec(memory_space=pl.ANY)

    def all_of(shape):
        return pl.BlockSpec(
            shape, lambda k, t: (0,) * len(shape), pipeline_mode=pl.Buffered(1)
        )

    return pl.pallas_call(
        ignoring(functools.partial(attend_back_body, total=total), 9, len(after)),
        grid_spec=pltpu.PrefetchScalarGridSpec(
            num_scalar_prefetch=1,
            grid=(slots,),
            in_specs=[
                pl.BlockSpec((1, length, key_width), lambda k, t: (k, 0, 0)),
                pl.BlockSpec((1, length, value_width), lambda k, t: (k, 0, 0)),
                pl.BlockSpec((1, 1, length), lambda k, t: (k, 0, 0)),
                all_of(bias.shape),
                anywhere,
                anywhere,
                anywhere,
                anywhere,
            ]
            + [anywhere] * len(after),
            out_specs=[
                pl.BlockSpec((1, length, key_width), lambda k, t: (k, 0, 0)),
                all_of(k_own.shape),
                all_of(k_oth.shape),
                all_of(v_own.shape),
                all_of(v_oth.shape),
                all_of(rel_shape),
            ],
            scratch_shapes=[
                pltpu.VMEM((total * length, key_width), bf16),
                pltpu.VMEM((total * length, value_width), bf16),
                pltpu.VMEM((total * length, key_width), f32),
                pltpu.VMEM((total * length, value_width), f32),
                pltpu.VMEM((total, length, length), f32),
                pltpu.VMEM((total, length, length), f32),
                pltpu.VMEM(bias.shape, f32),
                pltpu.SemaphoreType.DMA((2 * total,)),
            ],
        ),
        out_shape=[
            jax.ShapeDtypeStruct((slots, length, key_width), f32),
            jax.ShapeDtypeStruct(k_own.shape, bf16),
            jax.ShapeDtypeStruct(k_oth.shape, bf16),
            jax.ShapeDtypeStruct(v_own.shape, bf16),
            jax.ShapeDtypeStruct(v_oth.shape, bf16),
            jax.ShapeDtypeStruct(rel_shape, f32),
        ],
        compiler_params=params(("arbitrary",)),
        name="attend_back",
        cost_estimate=pl.CostEstimate(
            flops=2 * slots * length * total * length * (key_width + value_width),
            bytes_accessed=20 * slots * length * value_width,
            transcendentals=slots * length * total * length,
        ),
    )(table, q, grads, lse, bias, k_own, k_oth, v_own, v_oth, *after)


def bias_body(flag_ref, back_row, front_row, back_ref, front_ref, *, spare):
    tile = pl.program_id(0) - spare
    full = flag_ref[0] == 1

    @pl.when(tile < 0)
    def _():
        back_ref[...] = jnp.full_like(back_ref, MASKED)
        front_ref[...] = jnp.full_like(front_ref, MASKED)

    @pl.when(tile >= 0)
    def _():
        down = lax.broadcasted_iota(jnp.int32, (TILE, TILE), 0)
        across = lax.broadcasted_iota(jnp.int32, (TILE, TILE), 1)
        near = jnp.where(down // STRETCH == across // STRETCH, 1, 0)
        for row, out, ordered in (
            (back_row, back_ref, jnp.where(down <= across, 1, 0)),
            (front_row, front_ref, jnp.where(across <= down, 1, 0)),
        ):
            wide = jnp.broadcast_to(row[0], (TILE, 2 * TILE))
            turned = pltpu.roll(wide, 0, 1, stride=1, stride_axis=0)[:, :TILE]
            allowed = jnp.where(
                tile == 0, jnp.where(full, ordered, ordered * near), jnp.where(full, 1, 0)
            )
            out[0] = jnp.where(allowed == 1, turned, MASKED)


def bias_tiles(relative_bias, spare, full):
    length = relative_bias.shape[0] // 2
    count = length // TILE
    windows = jnp.stack(
        [
            lax.slice_in_dim(relative_bias, length - d * TILE - TILE, length - d * TILE + TILE)
            for d in range(count)
        ]
    )
    front = jnp.concatenate([windows[:, TILE:], windows[:, :TILE]], axis=1)
    back = jnp.concatenate([windows[:, TILE:TILE + 1], windows[:, ::-1][:, TILE:], windows[:, ::-1][:, : TILE - 1]], axis=1)
    row = pl.BlockSpec((1, 1, 2 * TILE), lambda d, t: (jnp.maximum(d - spare, 0), 0, 0))
    out = pl.BlockSpec((1, TILE, TILE), lambda d, t: (d, 0, 0))
    shape = jax.ShapeDtypeStruct((spare + count, TILE, TILE), f32)
    return pl.pallas_call(
        functools.partial(bias_body, spare=spare),
        grid_spec=pltpu.PrefetchScalarGridSpec(
            num_scalar_prefetch=1,
            grid=(spare + count,),
            in_specs=[row, row],
            out_specs=[out, out],
        ),
        out_shape=[shape, shape],
        compiler_params=params(("arbitrary",)),
        name="bias",
    )(full.astype(jnp.int32)[None], back[:, None], front[:, None])


def bias_grad(sums, length):
    count = sums.shape[0]
    shifted = jnp.concatenate([jnp.zeros((count, 1), f32), sums[:, :-1]], axis=1)
    none = jnp.zeros((1, TILE), f32)
    blocks = jnp.concatenate([none, shifted[:, :TILE]]) + jnp.concatenate(
        [shifted[:, TILE:], none]
    )
    return jnp.concatenate(
        [blocks[::-1].reshape(-1), jnp.zeros((2 * length - (count + 1) * TILE,), f32)]
    )


def gate_body(
    back_ref,
    cot_ref,
    x_ref,
    cand_ref,
    update_ref,
    reset_ref,
    attended_ref,
    gain_ref,
    proj_ref,
    input_ref,
    main_ref,
    grad_att_ref,
    gain_grad_ref,
):
    width = x_ref.shape[1]
    value_width = proj_ref.shape[0]

    @pl.when(pl.program_id(0) == 0)
    def _():
        gain_grad_ref[...] = jnp.zeros_like(gain_grad_ref)

    x = x_ref[...].astype(f32)
    cand_in = cand_ref[...]
    gate = jax.nn.sigmoid(cand_in)
    candidate = cand_in * gate
    update = jax.nn.sigmoid(update_ref[...].astype(f32))
    change = candidate - x
    unit, inv = unit_rows_of(x + update * change)
    grad_feed = back_ref[...]
    gain_grad_ref[...] += jnp.sum(grad_feed * unit, axis=0, keepdims=True)
    grad_first = cot_ref[...].astype(f32) + norm_back_rows(
        grad_feed, gain_ref[...], unit, inv
    )
    kept = grad_first * (1.0 - update)
    input_ref[...] = kept
    main_ref[:, value_width : value_width + width] = (kept * change * update).astype(bf16)
    grad_cand = (grad_first * update * (gate + candidate * (1.0 - gate))).astype(bf16)
    main_ref[:, value_width + width :] = grad_cand
    for c in range(value_width // 512):
        at = slice(c * 512, (c + 1) * 512)
        grad_gated = mm_nt(grad_cand, proj_ref[at, :])
        reset = reset_ref[:, at].astype(f32)
        open_gate = jax.nn.sigmoid(reset)
        passed = reset * open_gate
        grad_att_ref[:, at] = (grad_gated * passed).astype(bf16)
        main_ref[:, at] = (
            grad_gated
            * attended_ref[:, at].astype(f32)
            * (open_gate + passed * (1.0 - open_gate))
        ).astype(bf16)


def gate(back, cot, x, cand_in, base, attended, gain, proj, after=()):
    tokens, width = x.shape
    value_width = proj.shape[0]
    rows = min(128, tokens)
    wide = value_width // width

    def block(columns, at=0):
        return pl.BlockSpec((rows, columns), lambda i: (i, at))

    return pl.pallas_call(
        ignoring(gate_body, 9, len(after)),
        grid=(tokens // rows,),
        in_specs=[
            block(width),
            block(width),
            block(width),
            block(width),
            block(width, wide),
            block(value_width),
            block(value_width),
            pl.BlockSpec((1, width), lambda i: (0, 0)),
            pl.BlockSpec(proj.shape, lambda i: (0, 0), pipeline_mode=pl.Buffered(1)),
        ]
        + [pl.BlockSpec(memory_space=pl.ANY)] * len(after),
        out_specs=[
            block(width),
            block(value_width + 2 * width),
            block(value_width),
            pl.BlockSpec((1, width), lambda i: (0, 0)),
        ],
        out_shape=[
            jax.ShapeDtypeStruct((tokens, width), f32),
            jax.ShapeDtypeStruct((tokens, value_width + 2 * width), bf16),
            jax.ShapeDtypeStruct((tokens, value_width), bf16),
            jax.ShapeDtypeStruct((1, width), f32),
        ],
        compiler_params=params(("arbitrary",)),
        name="gate",
        cost_estimate=pl.CostEstimate(
            flops=2 * tokens * width * value_width,
            bytes_accessed=40 * tokens * width,
            transcendentals=4 * tokens * width,
        ),
    )(back, cot, x, cand_in, base, base, attended, gain, proj, *after)


def ordered_transpose(ids_ref, source, plain, ordered):
    plain[...] = source[...].T
    count = ids_ref.shape[0]
    rows = plain.shape[0] // count

    def place(p, _):
        ordered[pl.ds(pl.multiple_of(p * rows, rows), rows), :] = plain[
            pl.ds(pl.multiple_of(ids_ref[p] * rows, rows), rows), :
        ]
        return 0

    lax.fori_loop(0, count, place, 0)


def feed_body(
    ids_ref,
    places_ref,
    low_ref,
    cot_ref,
    first_ref,
    in_ref,
    out_ref,
    result_ref,
    back_ref,
    out_send,
    out_keep,
    in_send,
    in_keep,
    total,
    cot_turned,
    low_turned,
    plain,
):
    step = pl.program_id(0)
    half = pl.num_programs(0) // 2
    tokens = low_ref.shape[0]
    rows = min(256, tokens)
    nt = (((1,), (1,)), ((), ()))

    @pl.when(step == 0)
    def _():
        cot_turned[...] = cot_ref[...].T
        ordered_transpose(ids_ref, low_ref, plain, low_turned)
        total[...] = first_ref[...]
        back_ref[...] = jnp.zeros_like(back_ref)

    acts, grads = [], []
    for r in range(tokens // rows):
        at = slice(r * rows, (r + 1) * rows)
        hidden = jnp.dot(low_ref[at, :], in_ref[...], preferred_element_type=f32)
        grad_act = lax.dot_general(
            cot_ref[at, :], out_ref[...], nt, preferred_element_type=f32
        )
        gate = jax.nn.sigmoid(hidden)
        act = hidden * gate
        grad = (grad_act * (gate + act * (1.0 - gate))).astype(bf16)
        act = act.astype(bf16)
        total[at, :] += jnp.dot(act, out_ref[...], preferred_element_type=f32)
        back_ref[at, :] += lax.dot_general(
            grad, in_ref[...], nt, preferred_element_type=f32
        )
        acts.append(act)
        grads.append(grad)
    out_grad = jnp.dot(
        cot_turned[...], jnp.concatenate(acts), preferred_element_type=f32
    ).astype(bf16)
    in_grad = jnp.dot(
        low_turned[...], jnp.concatenate(grads), preferred_element_type=f32
    ).astype(bf16)
    middle = in_grad.shape[0] // 2
    in_send[...] = in_grad[:middle].reshape(in_send.shape)
    in_keep[...] = in_grad[middle:].reshape(in_keep.shape)

    @pl.when(step < half)
    def _():
        out_send[0] = out_grad

    @pl.when(step >= half)
    def _():
        out_keep[0] = out_grad

    @pl.when(step == pl.num_programs(0) - 1)
    def _():
        result_ref[...] = total[...].astype(bf16)


def feed(ids, places, low, cot, first_sum, feed_in, feed_out, seq, after=()):
    tokens, width = low.shape
    features = feed_in.shape[1]
    parts = ids.shape[0]
    half = parts // 2
    columns = features // parts
    rows = width // parts
    share = parts // seq
    anywhere = pl.BlockSpec(memory_space=pl.ANY)

    def all_of(shape):
        return pl.BlockSpec(
            shape, lambda i, t, u: (0,) * len(shape), pipeline_mode=pl.Buffered(1)
        )

    def at(i, t):
        return t[jnp.minimum(i, parts - 1)]

    split = pl.BlockSpec(
        (half, 1, rows, columns), lambda i, t, u: (0, u[at(i, t) // share], 0, at(i, t) % share)
    )
    return pl.pallas_call(
        ignoring(feed_body, 7, len(after)),
        grid_spec=pltpu.PrefetchScalarGridSpec(
            num_scalar_prefetch=2,
            grid=(parts,),
            in_specs=[
                all_of(low.shape),
                all_of(cot.shape),
                all_of(first_sum.shape),
                pl.BlockSpec((width, columns), lambda i, t, u: (0, at(i, t))),
                pl.BlockSpec((columns, width), lambda i, t, u: (at(i, t), 0)),
            ]
            + [anywhere] * len(after),
            out_specs=[
                all_of(low.shape),
                all_of(low.shape),
                pl.BlockSpec(
                    (1, width, columns), lambda i, t, u: (jnp.minimum(i, half - 1), 0, 0)
                ),
                pl.BlockSpec(
                    (1, width, columns), lambda i, t, u: (jnp.maximum(i - half, 0), 0, 0)
                ),
                split,
                split,
            ],
            scratch_shapes=[
                pltpu.VMEM((tokens, width), f32),
                pltpu.VMEM((width, tokens), bf16),
                pltpu.VMEM((width, tokens), bf16),
                pltpu.VMEM((width, tokens), bf16),
            ],
        ),
        out_shape=[
            jax.ShapeDtypeStruct((tokens, width), bf16),
            jax.ShapeDtypeStruct((tokens, width), f32),
            jax.ShapeDtypeStruct((half, width, columns), bf16),
            jax.ShapeDtypeStruct((half, width, columns), bf16),
            jax.ShapeDtypeStruct((half, seq, rows, features // seq), bf16),
            jax.ShapeDtypeStruct((half, seq, rows, features // seq), bf16),
        ],
        compiler_params=params(("arbitrary",)),
        name="feed",
        cost_estimate=pl.CostEstimate(
            flops=12 * tokens * width * features,
            bytes_accessed=8 * width * features + 16 * tokens * width,
            transcendentals=tokens * features,
        ),
    )(ids, places, low, cot, first_sum, feed_in, feed_out, *after)


def by_columns_body(ids_ref, left_ref, right_ref, send, keep, turned):
    step = pl.program_id(0)
    half = pl.num_programs(0) // 2

    @pl.when(step == 0)
    def _():
        turned[...] = left_ref[...].T

    grad = jnp.dot(turned[...], right_ref[...], preferred_element_type=f32).astype(bf16)

    @pl.when(step < half)
    def _():
        send[0] = grad

    @pl.when(step >= half)
    def _():
        keep[0] = grad


def by_columns(ids, left, right, after=(), rows=None, at=0):
    tokens = left.shape[0]
    rows = rows or left.shape[1]
    parts = ids.shape[0]
    half = parts // 2
    columns = right.shape[1] // parts
    shape = jax.ShapeDtypeStruct((half, rows, columns), bf16)
    if columns % 128:
        left = left[:, at * rows : (at + 1) * rows]
        grad = mm_tn(left, right).astype(bf16).reshape(rows, parts, columns)
        grad = jnp.take(grad, ids, axis=1).transpose(1, 0, 2)
        return grad[:half], grad[half:]
    return pl.pallas_call(
        ignoring(by_columns_body, 3, len(after)),
        grid_spec=pltpu.PrefetchScalarGridSpec(
            num_scalar_prefetch=1,
            grid=(parts,),
            in_specs=[
                pl.BlockSpec(
                    (tokens, rows), lambda i, t: (0, at), pipeline_mode=pl.Buffered(1)
                ),
                pl.BlockSpec((tokens, columns), lambda i, t: (0, t[jnp.minimum(i, parts - 1)])),
            ]
            + [pl.BlockSpec(memory_space=pl.ANY)] * len(after),
            out_specs=[
                pl.BlockSpec(
                    (1, rows, columns), lambda i, t: (jnp.minimum(i, half - 1), 0, 0)
                ),
                pl.BlockSpec(
                    (1, rows, columns), lambda i, t: (jnp.maximum(i - half, 0), 0, 0)
                ),
            ],
            scratch_shapes=[pltpu.VMEM((rows, tokens), bf16)],
        ),
        out_shape=[shape, shape],
        compiler_params=params(("arbitrary",)),
        name="by_columns",
        cost_estimate=pl.CostEstimate(
            flops=2 * tokens * rows * right.shape[1],
            bytes_accessed=2 * (tokens + rows) * right.shape[1],
            transcendentals=0,
        ),
    )(ids, left, right, *after)


def by_rows_body(ids_ref, places_ref, left_ref, right_ref, send, keep, plain, turned):
    @pl.when(pl.program_id(0) == 0)
    def _():
        ordered_transpose(ids_ref, left_ref, plain, turned)

    grad = jnp.dot(turned[...], right_ref[...], preferred_element_type=f32).astype(bf16)
    middle = grad.shape[0] // 2
    send[...] = grad[:middle].reshape(send.shape)
    keep[...] = grad[middle:].reshape(keep.shape)


def by_rows(ids, places, left, right, seq=1, after=()):
    tokens, rows = left.shape
    parts = ids.shape[0]
    half = parts // 2
    if places is None:
        seq, places = 1, jnp.zeros((1,), jnp.int32)
    columns = right.shape[1] // seq
    tile = min(512, columns)
    share = columns // tile
    shape = jax.ShapeDtypeStruct((half, seq, rows // parts, columns), bf16)
    split = pl.BlockSpec(
        (half, 1, rows // parts, tile), lambda i, t, u: (0, u[jnp.minimum(i // share, seq - 1)], 0, i % share)
    )
    return pl.pallas_call(
        ignoring(by_rows_body, 4, len(after)),
        grid_spec=pltpu.PrefetchScalarGridSpec(
            num_scalar_prefetch=2,
            grid=(seq * share,),
            in_specs=[
                pl.BlockSpec(
                    left.shape, lambda i, t, u: (0, 0), pipeline_mode=pl.Buffered(1)
                ),
                pl.BlockSpec((tokens, tile), lambda i, t, u: (0, i)),
            ]
            + [pl.BlockSpec(memory_space=pl.ANY)] * len(after),
            out_specs=[split, split],
            scratch_shapes=[
                pltpu.VMEM((rows, tokens), bf16),
                pltpu.VMEM((rows, tokens), bf16),
            ],
        ),
        out_shape=[shape, shape],
        compiler_params=params(("arbitrary",)),
        name="by_rows",
        cost_estimate=pl.CostEstimate(
            flops=2 * tokens * rows * right.shape[1],
            bytes_accessed=2 * (tokens + rows) * right.shape[1],
            transcendentals=0,
        ),
    )(ids, places, left, right, *after)


class Layout:
    def __init__(self, mesh):
        self.dp = mesh.shape["dp"]
        self.seq = mesh.shape["seq"]
        self.members = self.seq // 2
        self.chips = self.seq // 4

    def pairs(self, move):
        return [
            (d * self.seq + z, e * self.seq + w)
            for d in range(self.dp)
            for z in range(self.seq)
            for e, w in [move(d, z)]
        ]

    def send(self, value, move):
        return lax.ppermute(value, AXES, self.pairs(move))

    def place(self, sequence, member):
        return member % 2 ^ (1 - sequence % 2), sequence * self.chips + member // 2

    def member(self, core, z):
        sequence = z // self.chips
        return (z % self.chips) * 2 + (core ^ (1 - sequence % 2))

    def home_to_work(self, round_index):
        def move(d, z):
            part = (1 if z >= self.seq // 2 else 0) ^ round_index
            core, at = self.place(2 * (d % 2) + part, min(z, self.seq - 1 - z))
            return d - d % 2 + core, at

        return move

    def spread(self, value):
        late = lax.axis_index("seq") >= self.seq // 2
        out = []
        for round_index in range(2):
            sent = lax.dynamic_index_in_dim(
                value, jnp.where(late, 1 - round_index, round_index), 0, False
            )
            out.append(self.send(sent, self.home_to_work(round_index)))
        return out

    def collect(self, values):
        back = []
        for round_index in range(2):
            pairs = [(b, a) for a, b in self.pairs(self.home_to_work(round_index))]
            back.append(lax.ppermute(values[round_index], AXES, pairs))
        late = lax.axis_index("seq") >= self.seq // 2
        return jnp.stack([jnp.where(late, back[1], back[0]), jnp.where(late, back[0], back[1])])

    def rotate(self, value, by):
        def move(d, z):
            member = (self.member(d % 2, z) + by) % self.members
            core, at = self.place(z // self.chips, member)
            return d - d % 2 + core, at

        return self.send(value, move)

    def gather(self, value):
        return jnp.concatenate([self.rotate(value, by) for by in range(1, self.members)], axis=0)

    def scatter_sum(self, own, others):
        slots = own.shape[0]
        total = own.astype(f32)
        for by in range(1, self.members):
            total = total + self.rotate(
                others[(by - 1) * slots : by * slots], self.members - by
            ).astype(f32)
        return total

    def orders(self):
        dp, z = lax.axis_index("dp"), lax.axis_index("seq")
        bits = self.dp.bit_length() - 1
        ids = []
        for core in range(2):
            orders = [[0, *range(1, bits)], [0, *reversed(range(1, bits))]]
            flips = []
            for p in range(self.dp):
                order = orders[core if p >= self.dp // 2 else 1 - core]
                flips.append(
                    sum(
                        (0 if p >> (bits - 1 - i) & 1 else 1) << bit
                        for i, bit in enumerate(order)
                    )
                )
            ids.append(dp ^ jnp.array(flips, jnp.int32))
        ids = jnp.where(dp % 2 == 0, ids[0], ids[1])
        bits = self.seq.bit_length() - 1
        flips = [
            sum((0 if p >> (bits - 1 - i) & 1 else 1) << i for i in range(bits))
            for p in range(self.seq)
        ]
        blocks = z ^ jnp.array(flips, jnp.int32)
        return ids, jnp.argsort(blocks).astype(jnp.int32), blocks

    def partner(self, stage):
        bits = self.dp.bit_length() - 1
        if stage == 0:
            return lambda d, z: (d ^ 1, z)
        if stage < bits:
            return lambda d, z: (d ^ (1 << stage if d % 2 == 0 else 1 << (bits - stage)), z)
        return lambda d, z: (d, z ^ (1 << (stage - bits)))

    def halve(self, held, stage):
        sent, kept = held
        arrived = self.send(sent, self.partner(stage))
        middle = kept.shape[0] // 2
        if middle == 0:
            return None, kept[0] + arrived[0]
        return kept[:middle] + arrived[:middle], kept[middle:] + arrived[middle:]

    def reduce_all(self, flat):
        core = lax.axis_index("dp") % 2
        count = flat.shape[0]
        split = jnp.pad(flat, (0, -count % 2048)).reshape(2, -1, 128)
        held = lax.dynamic_index_in_dim(split, core, 0, False)
        sent = lax.dynamic_index_in_dim(split, 1 - core, 0, False)
        held = held + self.send(sent, lambda d, z: (d ^ 1, z))
        for bit in range(1, self.dp.bit_length() - 1):
            held = held + self.send(held, lambda d, z: (d ^ (1 << bit), z))
        for bit in range(self.seq.bit_length() - 1):
            held = held + self.send(held, lambda d, z: (d, z ^ (1 << bit)))
        other = self.send(held, lambda d, z: (d ^ 1, z))
        return jnp.where(
            core == 0, jnp.stack([held, other]), jnp.stack([other, held])
        ).reshape(-1)[:count]


def mm(a, b):
    return jnp.dot(a, b, preferred_element_type=f32)


def mm_nt(a, b):
    return lax.dot_general(a, b, (((1,), (1,)), ((), ())), preferred_element_type=f32)


def mm_tn(a, b):
    return lax.dot_general(a, b, (((0,), (0,)), ((), ())), preferred_element_type=f32)


def layer(
    layout,
    inputs,
    cotangent,
    full_attention,
    mix_gain,
    smooth_alpha,
    smooth_damp,
    smooth_beta,
    smooth_eta,
    smooth_omega,
    value_proj,
    mix_proj,
    score_affine,
    relative_bias,
    out_proj,
    feed_gain,
    feed_in,
    feed_out,
):
    slots, chunk_rows, width = inputs.shape
    key_width = score_affine.shape[1]
    value_width = value_proj.shape[1]
    tokens = slots * chunk_rows
    total = layout.seq
    seq_length = relative_bias.shape[0] // 2
    block = min(64, chunk_rows)
    core = lax.axis_index("dp") % 2
    z = lax.axis_index("seq")

    sequence = z // layout.chips
    member = layout.member(core, z)
    swap = sequence % 2
    chunks = []
    for by in range(layout.members):
        source = (member - by) % layout.members
        low, high = source, total - 1 - source
        chunks += [jnp.where(swap == 0, low, high), jnp.where(swap == 0, high, low)]
    chunks = jnp.stack(chunks).astype(jnp.int32)
    slot_of = jnp.sum(
        jnp.where(chunks[None, :] == jnp.arange(total)[:, None], jnp.arange(total)[None, :], 0),
        axis=1,
    ).astype(jnp.int32)
    flags = full_attention.astype(f32)
    flags_other = layout.send(flags, lambda d, z: (d ^ 1, z))
    flags = jnp.where(
        core == 0, jnp.concatenate([flags, flags_other]), jnp.concatenate([flags_other, flags])
    )
    full = lax.dynamic_index_in_dim(flags, sequence, 0, False) == 1.0
    table = jnp.concatenate([chunks, slot_of, full.astype(jnp.int32)[None]])
    ids, places, blocks = layout.orders()

    x = jnp.stack(layout.spread(inputs))
    cot = jnp.concatenate(layout.spread(cotangent))
    bias_back, bias_front = bias_tiles(relative_bias, chunk_rows // TILE - 1, full)

    states = smooth_alpha.shape[0]
    lanes = (states, width // 128, 128)
    decay = 1.0 - smooth_alpha * smooth_damp
    rate = smooth_alpha * smooth_beta
    span = (decay**chunk_rows).reshape(lanes)
    coef = (smooth_eta * rate).reshape(lanes)
    decay_slab = decay.reshape(lanes)
    gain_row = mix_gain[None]
    omega_row = smooth_omega[None]
    mix_shared, mix_main = mix_proj[:, :key_width], mix_proj[:, key_width:]

    normed_low, ends = front_ends(
        x, gain_row, decay_slab, after=(bias_back, bias_front, mix_main, mix_shared, span, coef)
    )
    ends_all = jnp.concatenate([ends, layout.gather(ends)])
    normed_low = normed_low.reshape(tokens, width)
    value_pre = mm(normed_low, value_proj)
    value_low = jax.nn.silu(value_pre).astype(bf16).reshape(slots, chunk_rows, value_width)
    value_slope = silu_slope(value_pre).astype(bf16)
    value_others = layout.gather(value_low)
    smoothed, mixed, check = front_scan(
        table, x, gain_row, decay_slab, coef, span, omega_row, ends_all, block
    )
    smoothed = smoothed.reshape(tokens, width)
    mixed = mixed.reshape(tokens, width)

    shared_pre = mm(mixed, mix_shared)
    shared = jax.nn.silu(shared_pre)
    query_low = (shared * score_affine[0] + score_affine[1]).astype(bf16)
    key_low = (shared * score_affine[2] + score_affine[3]).astype(bf16)
    query_low = query_low.reshape(slots, chunk_rows, key_width)
    key_low = key_low.reshape(slots, chunk_rows, key_width)
    key_others = layout.gather(key_low)
    base = mm(mixed, mix_main).astype(bf16)
    attended, gated, lse = attend(
        table,
        query_low,
        bias_front,
        base.reshape(slots, chunk_rows, -1),
        key_low,
        key_others,
        value_low,
        value_others,
    )
    attended = attended.reshape(tokens, value_width)
    gated = gated.reshape(tokens, value_width)

    flat_low = x.reshape(tokens, width)
    flat = flat_low.astype(f32)
    update_pre = base[:, value_width : value_width + width].astype(f32)
    cand_in = base[:, value_width + width :].astype(f32) + mm(gated, out_proj)
    first_sum = flat + jax.nn.sigmoid(update_pre) * (jax.nn.silu(cand_in) - flat)
    unit_two, _ = unit_rows_of(first_sum)
    feed_low = (unit_two * feed_gain).astype(bf16)

    result, grad_feed, out_send, out_keep, in_send, in_keep = feed(
        ids, places, feed_low, cot, first_sum, feed_in, feed_out, layout.seq
    )
    result = result.reshape(slots, chunk_rows, width)
    block_out = layout.collect([result[0], result[1]])
    feed_out_sum = layout.halve((out_send, out_keep), 0)
    feed_in_sum = layout.halve((in_send, in_keep), 0)

    grad_input, grad_main, grad_att, feed_gain_grad = gate(
        grad_feed, cot, flat_low, cand_in, base, attended, feed_gain[None], out_proj
    )
    proj_sum = layout.halve(
        by_columns(
            ids,
            grad_main,
            gated,
            rows=width,
            at=grad_main.shape[1] // width - 1,
            after=(*feed_out_sum, *feed_in_sum),
        ),
        0,
    )
    mix_sum = layout.halve(by_rows(ids, None, mixed, grad_main), 0)
    feed_out_sum = layout.halve(feed_out_sum, 1)
    grad_query, gk_own, gk_oth, gv_own, gv_oth, rel_sums = attend_back(
        table,
        query_low,
        grad_att.reshape(slots, chunk_rows, value_width),
        lse.reshape(slots, 1, chunk_rows),
        bias_back,
        key_low,
        key_others,
        value_low,
        value_others,
        after=(*proj_sum, *feed_out_sum),
    )
    feed_in_sum = layout.halve(feed_in_sum, 1)
    grad_key = layout.scatter_sum(gk_own, gk_oth).reshape(tokens, key_width)
    grad_query = grad_query.reshape(tokens, key_width)
    grad_shared = (
        (grad_query * score_affine[0] + grad_key * score_affine[2]) * silu_slope(shared_pre)
    ).astype(bf16)
    grad_smooth = (mm_nt(grad_main, mix_main) + mm_nt(grad_shared, mix_shared)) * silu_slope(
        smoothed
    )
    grad_smooth = grad_smooth.reshape(slots, chunk_rows, width)
    back = back_ends(grad_smooth, decay_slab, after=(*feed_in_sum, *mix_sum))
    back_all = jnp.concatenate([back, layout.gather(back)])
    grad_value = layout.scatter_sum(gv_own, gv_oth).reshape(tokens, value_width)
    grad_value_pre = (grad_value * value_slope.astype(f32)).astype(bf16)
    value_sum = layout.halve(
        by_rows(ids, places, normed_low, grad_value_pre, layout.seq), 0
    )
    shared_sum = layout.halve(
        by_rows(ids, None, mixed, grad_shared), 0
    )
    grad_normed = mm_nt(grad_value_pre, value_proj)

    feed_out_sum = layout.halve(feed_out_sum, 2)
    proj_sum = layout.halve(proj_sum, 1)
    mix_sum = layout.halve(mix_sum, 1)
    grad_in, qx, qs, mix_gain_grad, omega_grad = back_scan(
        table,
        x,
        grad_smooth,
        grad_normed.reshape(slots, chunk_rows, width),
        grad_input.reshape(slots, chunk_rows, width),
        check,
        gain_row,
        decay_slab,
        coef,
        span,
        omega_row,
        back_all,
        after=(*value_sum, *shared_sum, *[v for v in feed_out_sum if v is not None], *proj_sum),
    )
    grad_in = layout.collect([grad_in[0], grad_in[1]]).astype(f32)

    affine_grad = jnp.stack(
        [
            jnp.sum(grad_query * shared_pre * jax.nn.sigmoid(shared_pre), axis=0),
            jnp.sum(grad_query, axis=0),
            jnp.sum(grad_key * shared_pre * jax.nn.sigmoid(shared_pre), axis=0),
            jnp.sum(grad_key, axis=0),
        ]
    )
    relative_grad = bias_grad(rel_sums[:, 0], seq_length)
    small = [
        qx.reshape(-1),
        qs.reshape(-1),
        mix_gain_grad.reshape(-1),
        omega_grad.reshape(-1),
        feed_gain_grad.reshape(-1),
        affine_grad.reshape(-1),
        relative_grad,
    ]
    sums = layout.reduce_all(jnp.concatenate(small))
    parts, start = [], 0
    for item in small:
        parts.append(lax.slice_in_dim(sums, start, start + item.shape[0]))
        start += item.shape[0]
    input_sum = parts[0].reshape(states, width)
    decay_sum = parts[1].reshape(states, width)
    input_total = smooth_eta * input_sum
    decay_total = smooth_eta * rate * decay_sum
    eta_grad = rate * input_sum
    alpha_grad = smooth_beta * input_total - smooth_damp * decay_total
    damp_grad = -smooth_alpha * decay_total
    beta_grad = smooth_alpha * input_total

    stages = layout.dp.bit_length() - 1

    def rest(held, stage):
        while stage < stages:
            held = layout.halve(held, stage)
            stage += 1
        return held[1]

    def over_seq(held):
        middle = layout.seq // 2
        held = (held[:middle], held[middle:])
        for stage in range(stages, stages + layout.seq.bit_length() - 1):
            held = layout.halve(held, stage)
        return held[1].astype(f32)

    feed_out_grad = over_seq(
        rest(feed_out_sum, 3).reshape(layout.seq, width // layout.seq, -1)[blocks]
    ).T
    feed_in_grad = over_seq(rest(feed_in_sum, 2))
    out_grad = over_seq(rest(proj_sum, 2).reshape(layout.seq, width // layout.seq, -1)[blocks]).T
    value_grad = over_seq(rest(value_sum, 1))
    mix_rows = jnp.concatenate([rest(shared_sum, 1)[0], rest(mix_sum, 2)[0]], axis=1)
    mix_rows = mix_rows.reshape(mix_rows.shape[0], layout.seq, -1).transpose(1, 0, 2)
    mix_grad = over_seq(mix_rows[blocks])
    return (
        block_out,
        grad_in,
        parts[2],
        alpha_grad,
        damp_grad,
        beta_grad,
        eta_grad,
        parts[3],
        value_grad,
        mix_grad,
        parts[5].reshape(4, key_width),
        parts[6],
        out_grad,
        parts[4],
        feed_in_grad,
        feed_out_grad,
    )


def solution(mesh):
    tokens = P("dp", "seq", None)
    split = P("dp", "seq")
    return jax.shard_map(
        functools.partial(layer, Layout(mesh)),
        mesh=mesh,
        in_specs=(tokens, tokens, P("dp")) + (P(),) * 14,
        out_specs=(tokens, tokens)
        + (P(),) * 6
        + (split, split, P(), P(), split, P(), split, split),
        check_vma=False,
    )
```

```python
import functools

import jax
import jax.numpy as jnp
from jax import lax
from jax.experimental import pallas as pl
from jax.experimental.pallas import tpu as pltpu
from jax.sharding import PartitionSpec as P

STRETCH = 128
EPSILON = 1e-05
TILE = 256
MASKED = -1e30
VMEM_LIMIT = 60 * 1024 * 1024
AXES = ("dp", "seq")

f32 = jnp.float32
bf16 = jnp.bfloat16


def unit_rows_of(values):
    centred = values - jnp.mean(values, axis=-1, keepdims=True)
    inv_std = lax.rsqrt(jnp.mean(centred * centred, axis=-1, keepdims=True) + EPSILON)
    return centred * inv_std, inv_std


def norm_back_rows(grad_out, gain_vec, unit_rows, inv_std):
    scaled = grad_out * gain_vec
    return inv_std * (
        scaled
        - jnp.mean(scaled, axis=-1, keepdims=True)
        - unit_rows * jnp.mean(scaled * unit_rows, axis=-1, keepdims=True)
    )


def silu_slope(pre_act):
    sigmoid_val = jax.nn.sigmoid(pre_act)
    return sigmoid_val * (1.0 + pre_act * (1.0 - sigmoid_val))


def params(semantics, limit=VMEM_LIMIT):
    return pltpu.CompilerParams(dimension_semantics=semantics, vmem_limit_bytes=limit)


def ignoring(body, first, count):
    def called(*refs):
        return body(*refs[:first], *refs[first + count :])

    return called


def to_slab(slab, rows):
    count, groups = rows.shape[0], rows.shape[1] // 128
    for c in range(groups):
        slab[pl.ds(c, count, stride=groups), :] = rows[:, c * 128 : (c + 1) * 128]


def from_slab(slab, count, groups):
    return jnp.concatenate(
        [slab[pl.ds(c, count, stride=groups), :] for c in range(groups)], axis=1
    )


def slab_row(slab, t, groups):
    return slab[pl.ds(pl.multiple_of(t * groups, groups), groups), :]


def front_ends_body(x_ref, gain_ref, decay_ref, low_ref, end_ref, slab):
    states, groups, _ = decay_ref.shape
    count = x_ref.shape[1]

    @pl.when(pl.program_id(1) == 0)
    def _():
        end_ref[...] = jnp.zeros_like(end_ref)

    unit, _ = unit_rows_of(x_ref[0].astype(f32))
    normed = unit * gain_ref[...]
    low_ref[0] = normed.astype(bf16)
    to_slab(slab, normed)
    decay = [decay_ref[n] for n in range(states)]

    def step(t, state):
        row = slab_row(slab, t, groups)
        return tuple(d * s + row for d, s in zip(decay, state))

    state = lax.fori_loop(
        0, count, step, tuple(end_ref[0, n] for n in range(states)), unroll=8
    )
    for n in range(states):
        end_ref[0, n] = state[n]


def front_ends(x, gain, decay, block=256, after=()):
    slots, length, width = x.shape
    states, groups, lanes = decay.shape
    block = min(block, length)
    return pl.pallas_call(
        ignoring(front_ends_body, 3, len(after)),
        grid=(slots, length // block),
        in_specs=[
            pl.BlockSpec((1, block, width), lambda k, b: (k, b, 0)),
            pl.BlockSpec((1, width), lambda k, b: (0, 0)),
            pl.BlockSpec((states, groups, lanes), lambda k, b: (0, 0, 0)),
        ]
        + [pl.BlockSpec(memory_space=pl.ANY)] * len(after),
        out_specs=[
            pl.BlockSpec((1, block, width), lambda k, b: (k, b, 0)),
            pl.BlockSpec((1, states, groups, lanes), lambda k, b: (k, 0, 0, 0)),
        ],
        out_shape=[
            jax.ShapeDtypeStruct((slots, length, width), bf16),
            jax.ShapeDtypeStruct((slots, states, groups, lanes), f32),
        ],
        scratch_shapes=[pltpu.VMEM((block * groups, lanes), f32)],
        compiler_params=params(("arbitrary", "arbitrary")),
        name="front_ends",
        cost_estimate=pl.CostEstimate(
            flops=slots * length * width * states * 4,
            bytes_accessed=4 * slots * length * width,
            transcendentals=0,
        ),
    )(x, gain, decay, *after)


def front_scan_body(
    table_ref,
    x_ref,
    gain_ref,
    decay_ref,
    coef_ref,
    span_ref,
    omega_ref,
    ends_ref,
    smooth_ref,
    mixed_ref,
    check_ref,
    slab,
    out_slab,
    carry,
):
    states, groups, _ = decay_ref.shape
    count = x_ref.shape[1]
    slot = pl.program_id(0)
    total = ends_ref.shape[0]

    @pl.when(pl.program_id(1) == 0)
    def _():
        carry[...] = jnp.zeros_like(carry)

        def link(i, _):
            carry[...] = span_ref[...] * carry[...] + ends_ref[table_ref[total + i]]
            return 0

        lax.fori_loop(0, table_ref[slot], link, 0)

    unit, _ = unit_rows_of(x_ref[0].astype(f32))
    normed = unit * gain_ref[...]
    to_slab(slab, normed)
    decay = [decay_ref[n] for n in range(states)]
    coef = [coef_ref[n] for n in range(states)]
    state = tuple(carry[n] for n in range(states))
    for n in range(states):
        check_ref[0, 0, n] = state[n]

    def step(t, state):
        row = slab_row(slab, t, groups)
        state = tuple(d * s + row for d, s in zip(decay, state))
        parts = [c * s for c, s in zip(coef, state)]
        while len(parts) > 1:
            parts = [a + b for a, b in zip(parts[::2], parts[1::2])]
        out_slab[pl.ds(pl.multiple_of(t * groups, groups), groups), :] = parts[0]
        return state

    state = lax.fori_loop(0, count, step, state, unroll=8)
    for n in range(states):
        carry[n] = state[n]
    smoothed = from_slab(out_slab, count, groups) + omega_ref[...] * normed
    smooth_ref[0] = smoothed
    mixed_ref[0] = (smoothed * jax.nn.sigmoid(smoothed)).astype(bf16)


def front_scan(table, x, gain, decay, coef, span, omega, ends, block):
    slots, length, width = x.shape
    states, groups, lanes = decay.shape
    whole3 = pl.BlockSpec((states, groups, lanes), lambda k, b, t: (0, 0, 0))
    row = pl.BlockSpec((1, width), lambda k, b, t: (0, 0))
    tokens = pl.BlockSpec((1, block, width), lambda k, b, t: (k, b, 0))
    return pl.pallas_call(
        front_scan_body,
        grid_spec=pltpu.PrefetchScalarGridSpec(
            num_scalar_prefetch=1,
            grid=(slots, length // block),
            in_specs=[
                tokens,
                row,
                whole3,
                whole3,
                whole3,
                row,
                pl.BlockSpec(ends.shape, lambda k, b, t: (0, 0, 0, 0)),
            ],
            out_specs=[
                tokens,
                tokens,
                pl.BlockSpec((1, 1, states, groups, lanes), lambda k, b, t: (k, b, 0, 0, 0)),
            ],
            scratch_shapes=[
                pltpu.VMEM((block * groups, lanes), f32),
                pltpu.VMEM((block * groups, lanes), f32),
                pltpu.VMEM((states, groups, lanes), f32),
            ],
        ),
        out_shape=[
            jax.ShapeDtypeStruct((slots, length, width), f32),
            jax.ShapeDtypeStruct((slots, length, width), bf16),
            jax.ShapeDtypeStruct((slots, length // block, states, groups, lanes), f32),
        ],
        compiler_params=params(("arbitrary", "arbitrary")),
        name="front_scan",
        cost_estimate=pl.CostEstimate(
            flops=slots * length * width * states * 8,
            bytes_accessed=8 * slots * length * width,
            transcendentals=slots * length * width,
        ),
    )(table, x, gain, decay, coef, span, omega, ends)


def back_ends_body(gs_ref, decay_ref, end_ref, slab):
    states, groups, _ = decay_ref.shape
    count = gs_ref.shape[1]

    @pl.when(pl.program_id(1) == 0)
    def _():
        end_ref[...] = jnp.zeros_like(end_ref)

    to_slab(slab, gs_ref[0])
    decay = [decay_ref[n] for n in range(states)]

    def step(t, state):
        row = slab_row(slab, count - 1 - t, groups)
        return tuple(d * s + row for d, s in zip(decay, state))

    state = lax.fori_loop(
        0, count, step, tuple(end_ref[0, n] for n in range(states)), unroll=8
    )
    for n in range(states):
        end_ref[0, n] = state[n]


def back_ends(gs, decay, block=256, after=()):
    slots, length, width = gs.shape
    states, groups, lanes = decay.shape
    block = min(block, length)
    blocks = length // block
    return pl.pallas_call(
        ignoring(back_ends_body, 2, len(after)),
        grid=(slots, blocks),
        in_specs=[
            pl.BlockSpec((1, block, width), lambda k, b: (k, blocks - 1 - b, 0)),
            pl.BlockSpec((states, groups, lanes), lambda k, b: (0, 0, 0)),
        ]
        + [pl.BlockSpec(memory_space=pl.ANY)] * len(after),
        out_specs=pl.BlockSpec((1, states, groups, lanes), lambda k, b: (k, 0, 0, 0)),
        out_shape=jax.ShapeDtypeStruct((slots, states, groups, lanes), f32),
        scratch_shapes=[pltpu.VMEM((block * groups, lanes), f32)],
        compiler_params=params(("arbitrary", "arbitrary")),
        name="back_ends",
        cost_estimate=pl.CostEstimate(
            flops=slots * length * width * states * 4,
            bytes_accessed=4 * slots * length * width,
            transcendentals=0,
        ),
    )(gs, decay, *after)


def back_scan_body(
    table_ref,
    slot_ref,
    x_ref,
    gs_ref,
    gv_ref,
    gi_ref,
    check_ref,
    gain_ref,
    decay_ref,
    coef_ref,
    span_ref,
    omega_ref,
    ends_ref,
    grad_ref,
    qx_ref,
    qs_ref,
    gain_grad_ref,
    omega_grad_ref,
    slab,
    gs_slab,
    out_slab,
    history,
    carry,
):
    states, groups, _ = decay_ref.shape
    count = x_ref.shape[1]
    slot = slot_ref[0]
    total = ends_ref.shape[0]

    @pl.when(pl.program_id(0) == 0)
    def _():
        qx_ref[...] = jnp.zeros_like(qx_ref)
        qs_ref[...] = jnp.zeros_like(qs_ref)
        gain_grad_ref[...] = jnp.zeros_like(gain_grad_ref)
        omega_grad_ref[...] = jnp.zeros_like(omega_grad_ref)

    @pl.when(pl.program_id(0) == 0)
    def _():
        carry[...] = jnp.zeros_like(carry)

        def link(i, _):
            carry[...] = (
                span_ref[...] * carry[...] + ends_ref[table_ref[total + total - 1 - i]]
            )
            return 0

        lax.fori_loop(0, total - 1 - table_ref[slot], link, 0)

    unit, inv = unit_rows_of(x_ref[0].astype(f32))
    normed = unit * gain_ref[...]
    gs = gs_ref[0]
    to_slab(slab, normed)
    to_slab(gs_slab, gs)
    decay = [decay_ref[n] for n in range(states)]

    def recompute(t, state):
        for n in range(states):
            history[t, n] = state[n]
        row = slab_row(slab, t, groups)
        return tuple(d * s + row for d, s in zip(decay, state))

    lax.fori_loop(
        0, count, recompute, tuple(check_ref[0, 0, n] for n in range(states)), unroll=4
    )

    half = states // 2
    for part in range(2):
        chosen = range(part * half, (part + 1) * half)
        decay = [decay_ref[n] for n in chosen]
        coef = [coef_ref[n] for n in chosen]

        def step(i, held):
            q, qx, qs = held
            t = count - 1 - i
            row = slab_row(slab, t, groups)
            g = slab_row(gs_slab, t, groups)
            q = tuple(d * a + g for d, a in zip(decay, q))
            parts = [c * a for c, a in zip(coef, q)]
            while len(parts) > 1:
                parts = [a + b for a, b in zip(parts[::2], parts[1::2])]
            spot = pl.ds(pl.multiple_of(t * groups, groups), groups)
            if part == 0:
                out_slab[spot, :] = parts[0]
            else:
                out_slab[spot, :] = out_slab[spot, :] + parts[0]
            qx = tuple(a + b * row for a, b in zip(qx, q))
            qs = tuple(a + b * history[t, n] for a, b, n in zip(qs, q, chosen))
            return q, qx, qs

        q, qx, qs = lax.fori_loop(
            0,
            count,
            step,
            (
                tuple(carry[n] for n in chosen),
                tuple(qx_ref[n] for n in chosen),
                tuple(qs_ref[n] for n in chosen),
            ),
            unroll=4,
        )
        for i, n in enumerate(chosen):
            carry[n] = q[i]
            qx_ref[n] = qx[i]
            qs_ref[n] = qs[i]

    grad_normed = (
        gv_ref[0] + from_slab(out_slab, count, groups) + omega_ref[...] * gs
    )
    gain_grad_ref[...] += jnp.sum(grad_normed * unit, axis=0, keepdims=True)
    omega_grad_ref[...] += jnp.sum(gs * normed, axis=0, keepdims=True)
    grad_ref[...] = (
        gi_ref[0] + norm_back_rows(grad_normed, gain_ref[...], unit, inv)
    ).astype(bf16)


def back_scan(table, slot, x, gs, gv, gi, check, gain, decay, coef, span, omega, ends, after=()):
    _, length, width = x.shape
    states, groups, lanes = decay.shape
    blocks = check.shape[1]
    block = length // blocks
    whole3 = pl.BlockSpec((states, groups, lanes), lambda b, t, u: (0, 0, 0))
    row = pl.BlockSpec((1, width), lambda b, t, u: (0, 0))
    tokens = pl.BlockSpec((1, block, width), lambda b, t, u: (slot, blocks - 1 - b, 0))
    return pl.pallas_call(
        ignoring(back_scan_body, 13, len(after)),
        grid_spec=pltpu.PrefetchScalarGridSpec(
            num_scalar_prefetch=2,
            grid=(blocks,),
            in_specs=[
                tokens,
                tokens,
                tokens,
                tokens,
                pl.BlockSpec(
                    (1, 1, states, groups, lanes),
                    lambda b, t, u: (slot, blocks - 1 - b, 0, 0, 0),
                ),
                row,
                whole3,
                whole3,
                whole3,
                row,
                pl.BlockSpec(ends.shape, lambda b, t, u: (0, 0, 0, 0)),
            ]
            + [pl.BlockSpec(memory_space=pl.ANY)] * len(after),
            out_specs=[
                pl.BlockSpec((block, width), lambda b, t, u: (blocks - 1 - b, 0)),
                whole3,
                whole3,
                row,
                row,
            ],
            scratch_shapes=[
                pltpu.VMEM((block * groups, lanes), f32),
                pltpu.VMEM((block * groups, lanes), f32),
                pltpu.VMEM((block * groups, lanes), f32),
                pltpu.VMEM((block, states, groups, lanes), f32),
                pltpu.VMEM((states, groups, lanes), f32),
            ],
        ),
        out_shape=[
            jax.ShapeDtypeStruct((length, width), bf16),
            jax.ShapeDtypeStruct((states, groups, lanes), f32),
            jax.ShapeDtypeStruct((states, groups, lanes), f32),
            jax.ShapeDtypeStruct((1, width), f32),
            jax.ShapeDtypeStruct((1, width), f32),
        ],
        compiler_params=params(("arbitrary",)),
        name="back_scan",
        cost_estimate=pl.CostEstimate(
            flops=length * width * states * 20,
            bytes_accessed=16 * length * width,
            transcendentals=0,
        ),
    )(table, jnp.full((1,), slot, jnp.int32), x, gs, gv, gi, check, gain, decay, coef, span, omega, ends, *after)


def load_chunks(table_ref, sources, total, length, sem):
    copies = []
    for slot in range(total):
        place = pl.ds(pl.multiple_of(table_ref[slot] * length, length), length)
        for own, others, kept in sources:
            source = own.at[slot] if slot < 2 else others.at[slot - 2]
            copies.append(
                pltpu.make_async_copy(source, kept.at[place, :], sem.at[len(copies)])
            )
    for copy in copies:
        copy.start()
    for copy in copies:
        copy.wait()


def attend_body(
    table_ref,
    q_ref,
    bias_ref,
    reset_ref,
    k_own,
    k_oth,
    v_own,
    v_oth,
    out_ref,
    gated_ref,
    lse_ref,
    keys,
    values,
    scores,
    probs,
    sem,
    *,
    total,
):
    length, key_width = q_ref.shape[1:]
    value_width = values.shape[1]
    tiles = length // TILE
    scale = float(key_width) ** (-0.5)

    @pl.when(pl.program_id(0) == 0)
    def _():
        load_chunks(
            table_ref, ((k_own, k_oth, keys), (v_own, v_oth, values)), total, length, sem
        )

    chunk = table_ref[pl.program_id(0)]
    reach = jnp.where(table_ref[2 * total] == 1, chunk + 1, 1)
    base = (chunk + 1 - reach) * length
    queries = q_ref[0]

    def first(kt, peak):
        spot = pl.ds(pl.multiple_of(base + kt * TILE, TILE), TILE)
        tile = (
            lax.dot_general(
                queries, keys[spot, :], (((1,), (1,)), ((), ())), preferred_element_type=f32
            )
            * scale
        )
        for r in range(tiles):
            rows = slice(r * TILE, (r + 1) * TILE)
            gap = (reach - 1) * tiles + r - kt + tiles - 1
            scores[kt, rows, :] = tile[rows] + bias_ref[gap]
        return jnp.maximum(peak, jnp.max(scores[kt], axis=1, keepdims=True))

    peak = lax.fori_loop(
        0, reach * tiles, first, jnp.full((length, 1), 2 * MASKED, f32)
    )

    def second(kt, sums):
        terms = jnp.exp(scores[kt] - peak)
        probs[:, pl.ds(pl.multiple_of(kt * TILE, TILE), TILE)] = terms.astype(bf16)
        return sums + jnp.sum(terms, axis=1, keepdims=True)

    sums = lax.fori_loop(0, reach * tiles, second, jnp.zeros((length, 1), f32))
    lse_ref[0] = peak + jnp.log(sums)
    inverse = 1.0 / sums

    for count in range(1, total + 1):

        @pl.when(reach == count)
        def _(count=count):
            width = count * length
            span = pl.ds(pl.multiple_of(base, length), width)

            def column(ct, _):
                at = pl.ds(pl.multiple_of(ct * TILE, TILE), TILE)
                rows = (
                    jnp.dot(probs[:, :width], values[span, at], preferred_element_type=f32)
                    * inverse
                )
                out_ref[0, :, at] = rows.astype(bf16)
                gate = reset_ref[0, :, at].astype(f32)
                gated_ref[0, :, at] = (gate * jax.nn.sigmoid(gate) * rows).astype(bf16)
                return 0

            lax.fori_loop(0, value_width // TILE, column, 0)


def attend(table, q, bias, reset, k_own, k_oth, v_own, v_oth):
    slots, length, key_width = q.shape
    value_width = v_own.shape[2]
    total = slots + k_oth.shape[0]
    anywhere = pl.BlockSpec(memory_space=pl.ANY)
    tokens = pl.BlockSpec((1, length, value_width), lambda k, t: (k, 0, 0))
    return pl.pallas_call(
        functools.partial(attend_body, total=total),
        grid_spec=pltpu.PrefetchScalarGridSpec(
            num_scalar_prefetch=1,
            grid=(slots,),
            in_specs=[
                pl.BlockSpec((1, length, key_width), lambda k, t: (k, 0, 0)),
                pl.BlockSpec(bias.shape, lambda k, t: (0, 0, 0)),
                tokens,
                anywhere,
                anywhere,
                anywhere,
                anywhere,
            ],
            out_specs=[
                tokens,
                tokens,
                pl.BlockSpec((1, length, 1), lambda k, t: (k, 0, 0)),
            ],
            scratch_shapes=[
                pltpu.VMEM((total * length, key_width), bf16),
                pltpu.VMEM((total * length, value_width), bf16),
                pltpu.VMEM((total * length // TILE, length, TILE), f32),
                pltpu.VMEM((length, total * length), bf16),
                pltpu.SemaphoreType.DMA((2 * total,)),
            ],
        ),
        out_shape=[
            jax.ShapeDtypeStruct((slots, length, value_width), bf16),
            jax.ShapeDtypeStruct((slots, length, value_width), bf16),
            jax.ShapeDtypeStruct((slots, length, 1), f32),
        ],
        compiler_params=params(("arbitrary",)),
        name="attend",
        cost_estimate=pl.CostEstimate(
            flops=slots * length * total * length * (key_width + value_width),
            bytes_accessed=20 * slots * length * value_width,
            transcendentals=slots * length * total * length,
        ),
    )(table, q, bias, reset, k_own, k_oth, v_own, v_oth)


def attend_back_body(
    table_ref,
    q_ref,
    grad_ref,
    lse_ref,
    bias_ref,
    k_own,
    k_oth,
    v_own,
    v_oth,
    gq_ref,
    gk_own,
    gk_oth,
    gv_own,
    gv_oth,
    rel_out,
    keys,
    values,
    gk_sum,
    gv_sum,
    probs_kept,
    grads_kept,
    rel_ref,
    sem,
    *,
    total,
):
    length, key_width = q_ref.shape[1:]
    value_width = values.shape[1]
    tiles = length // TILE
    scale = float(key_width) ** (-0.5)
    step = pl.program_id(0)
    nt = (((1,), (1,)), ((), ()))
    tn = (((0,), (0,)), ((), ()))

    @pl.when(step == 0)
    def _():
        gk_sum[...] = jnp.zeros_like(gk_sum)
        gv_sum[...] = jnp.zeros_like(gv_sum)
        rel_ref[...] = jnp.zeros_like(rel_ref)
        load_chunks(
            table_ref, ((k_own, k_oth, keys), (v_own, v_oth, values)), total, length, sem
        )

    chunk = table_ref[step]
    reach = jnp.where(table_ref[2 * total] == 1, chunk + 1, 1)
    base = (chunk + 1 - reach) * length
    queries = q_ref[0]
    log_total = lse_ref[0]

    def gap_of(kc, a, r):
        return (reach - 1 - kc) * tiles + r - a + tiles - 1

    def first(kc, delta):
        spot = pl.ds(pl.multiple_of(base + kc * length, length), length)
        grads_kept[kc] = lax.dot_general(
            values[spot, :], grad_ref[0], nt, preferred_element_type=f32
        )
        tile = (
            lax.dot_general(keys[spot, :], queries, nt, preferred_element_type=f32) * scale
        )
        for a in range(tiles):
            for r in range(tiles):
                rows = slice(a * TILE, (a + 1) * TILE)
                cols = slice(r * TILE, (r + 1) * TILE)
                probs_kept[kc, rows, cols] = jnp.exp(
                    tile[rows, cols] + bias_ref[gap_of(kc, a, r)] - log_total[:, cols]
                )
        return delta + jnp.sum(probs_kept[kc] * grads_kept[kc], axis=0, keepdims=True)

    delta = lax.fori_loop(0, reach, first, jnp.zeros((1, length), f32))

    def second(kc, grad_query):
        spot = pl.ds(pl.multiple_of(base + kc * length, length), length)
        probs = probs_kept[kc]
        grad_scores = (probs * (grads_kept[kc] - delta)).astype(bf16)
        probs = probs.astype(bf16)
        for a in range(tiles):
            for r in range(tiles):
                rel_ref[gap_of(kc, a, r)] += grad_scores[
                    a * TILE : (a + 1) * TILE, r * TILE : (r + 1) * TILE
                ].astype(f32)
        gk_sum[spot, :] += jnp.dot(grad_scores, queries, preferred_element_type=f32)

        def column(ct, _):
            at = pl.ds(pl.multiple_of(ct * 512, 512), 512)
            gv_sum[spot, at] += jnp.dot(
                probs, grad_ref[0, :, at], preferred_element_type=f32
            )
            return 0

        lax.fori_loop(0, value_width // 512, column, 0)
        return grad_query + lax.dot_general(
            grad_scores, keys[spot, :], tn, preferred_element_type=f32
        )

    grad_query = lax.fori_loop(0, reach, second, jnp.zeros((length, key_width), f32))
    gq_ref[0] = grad_query * scale

    @pl.when(step == pl.num_programs(0) - 1)
    def _():
        for slot in range(total):
            place = pl.ds(pl.multiple_of(table_ref[slot] * length, length), length)
            key_out, value_out = (gk_own, gv_own) if slot < 2 else (gk_oth, gv_oth)
            at = slot if slot < 2 else slot - 2
            key_out[at] = (gk_sum[place, :] * scale).astype(bf16)
            value_out[at] = gv_sum[place, :].astype(bf16)
        down = lax.broadcasted_iota(jnp.int32, (TILE, TILE), 0)
        across = lax.broadcasted_iota(jnp.int32, (TILE, TILE), 1)
        mirror = jnp.where(down + across == TILE - 1, 1.0, 0.0)
        for d in range(rel_out.shape[0]):
            flipped = jnp.dot(
                rel_ref[d + tiles - 1],
                mirror,
                precision=lax.Precision.HIGHEST,
                preferred_element_type=f32,
            )
            wide = jnp.concatenate([flipped, jnp.zeros((TILE, TILE), f32)], axis=1)
            turned = pltpu.roll(wide, 0, 1, stride=1, stride_axis=0)
            rel_out[d] = jnp.sum(turned, axis=0, keepdims=True)


def attend_back(table, q, grads, lse, bias, k_own, k_oth, v_own, v_oth, after=()):
    slots, length, key_width = q.shape
    value_width = v_own.shape[2]
    total = slots + k_oth.shape[0]
    rel_shape = (total * length // TILE, 1, 2 * TILE)
    anywhere = pl.BlockSpec(memory_space=pl.ANY)

    def all_of(shape):
        return pl.BlockSpec(
            shape, lambda k, t: (0,) * len(shape), pipeline_mode=pl.Buffered(1)
        )

    return pl.pallas_call(
        ignoring(functools.partial(attend_back_body, total=total), 9, len(after)),
        grid_spec=pltpu.PrefetchScalarGridSpec(
            num_scalar_prefetch=1,
            grid=(slots,),
            in_specs=[
                pl.BlockSpec((1, length, key_width), lambda k, t: (k, 0, 0)),
                pl.BlockSpec((1, length, value_width), lambda k, t: (k, 0, 0)),
                pl.BlockSpec((1, 1, length), lambda k, t: (k, 0, 0)),
                all_of(bias.shape),
                anywhere,
                anywhere,
                anywhere,
                anywhere,
            ]
            + [anywhere] * len(after),
            out_specs=[
                pl.BlockSpec((1, length, key_width), lambda k, t: (k, 0, 0)),
                all_of(k_own.shape),
                all_of(k_oth.shape),
                all_of(v_own.shape),
                all_of(v_oth.shape),
                all_of(rel_shape),
            ],
            scratch_shapes=[
                pltpu.VMEM((total * length, key_width), bf16),
                pltpu.VMEM((total * length, value_width), bf16),
                pltpu.VMEM((total * length, key_width), f32),
                pltpu.VMEM((total * length, value_width), f32),
                pltpu.VMEM((total, length, length), f32),
                pltpu.VMEM((total, length, length), f32),
                pltpu.VMEM(bias.shape, f32),
                pltpu.SemaphoreType.DMA((2 * total,)),
            ],
        ),
        out_shape=[
            jax.ShapeDtypeStruct((slots, length, key_width), f32),
            jax.ShapeDtypeStruct(k_own.shape, bf16),
            jax.ShapeDtypeStruct(k_oth.shape, bf16),
            jax.ShapeDtypeStruct(v_own.shape, bf16),
            jax.ShapeDtypeStruct(v_oth.shape, bf16),
            jax.ShapeDtypeStruct(rel_shape, f32),
        ],
        compiler_params=params(("arbitrary",)),
        name="attend_back",
        cost_estimate=pl.CostEstimate(
            flops=2 * slots * length * total * length * (key_width + value_width),
            bytes_accessed=20 * slots * length * value_width,
            transcendentals=slots * length * total * length,
        ),
    )(table, q, grads, lse, bias, k_own, k_oth, v_own, v_oth, *after)


def bias_body(flag_ref, back_row, front_row, back_ref, front_ref, *, spare):
    tile = pl.program_id(0) - spare
    full = flag_ref[0] == 1

    @pl.when(tile < 0)
    def _():
        back_ref[...] = jnp.full_like(back_ref, MASKED)
        front_ref[...] = jnp.full_like(front_ref, MASKED)

    @pl.when(tile >= 0)
    def _():
        down = lax.broadcasted_iota(jnp.int32, (TILE, TILE), 0)
        across = lax.broadcasted_iota(jnp.int32, (TILE, TILE), 1)
        near = jnp.where(down // STRETCH == across // STRETCH, 1, 0)
        for row, out, ordered in (
            (back_row, back_ref, jnp.where(down <= across, 1, 0)),
            (front_row, front_ref, jnp.where(across <= down, 1, 0)),
        ):
            wide = jnp.broadcast_to(row[0], (TILE, 2 * TILE))
            turned = pltpu.roll(wide, 0, 1, stride=1, stride_axis=0)[:, :TILE]
            allowed = jnp.where(
                tile == 0, jnp.where(full, ordered, ordered * near), jnp.where(full, 1, 0)
            )
            out[0] = jnp.where(allowed == 1, turned, MASKED)


def bias_tiles(relative_bias, spare, full):
    length = relative_bias.shape[0] // 2
    count = length // TILE
    windows = jnp.stack(
        [
            lax.slice_in_dim(relative_bias, length - d * TILE - TILE, length - d * TILE + TILE)
            for d in range(count)
        ]
    )
    front = jnp.concatenate([windows[:, TILE:], windows[:, :TILE]], axis=1)
    back = jnp.concatenate([windows[:, TILE:TILE + 1], windows[:, ::-1][:, TILE:], windows[:, ::-1][:, : TILE - 1]], axis=1)
    row = pl.BlockSpec((1, 1, 2 * TILE), lambda d, t: (jnp.maximum(d - spare, 0), 0, 0))
    out = pl.BlockSpec((1, TILE, TILE), lambda d, t: (d, 0, 0))
    shape = jax.ShapeDtypeStruct((spare + count, TILE, TILE), f32)
    return pl.pallas_call(
        functools.partial(bias_body, spare=spare),
        grid_spec=pltpu.PrefetchScalarGridSpec(
            num_scalar_prefetch=1,
            grid=(spare + count,),
            in_specs=[row, row],
            out_specs=[out, out],
        ),
        out_shape=[shape, shape],
        compiler_params=params(("arbitrary",)),
        name="bias",
    )(full.astype(jnp.int32)[None], back[:, None], front[:, None])


def bias_grad(sums, length):
    count = sums.shape[0]
    shifted = jnp.concatenate([jnp.zeros((count, 1), f32), sums[:, :-1]], axis=1)
    none = jnp.zeros((1, TILE), f32)
    blocks = jnp.concatenate([none, shifted[:, :TILE]]) + jnp.concatenate(
        [shifted[:, TILE:], none]
    )
    return jnp.concatenate(
        [blocks[::-1].reshape(-1), jnp.zeros((2 * length - (count + 1) * TILE,), f32)]
    )


def gate_body(
    back_ref,
    cot_a,
    cot_b,
    x_ref,
    cand_ref,
    update_ref,
    reset_ref,
    attended_ref,
    gain_ref,
    proj_ref,
    input_ref,
    main_ref,
    grad_att_ref,
    gain_grad_ref,
):
    width = x_ref.shape[1]
    value_width = proj_ref.shape[0]

    @pl.when(pl.program_id(0) == 0)
    def _():
        gain_grad_ref[...] = jnp.zeros_like(gain_grad_ref)

    x = x_ref[...].astype(f32)
    cand_in = cand_ref[...]
    gate = jax.nn.sigmoid(cand_in)
    candidate = cand_in * gate
    update = jax.nn.sigmoid(update_ref[...].astype(f32))
    change = candidate - x
    unit, inv = unit_rows_of(x + update * change)
    grad_feed = back_ref[...]
    gain_grad_ref[...] += jnp.sum(grad_feed * unit, axis=0, keepdims=True)
    early = pl.program_id(0) < pl.num_programs(0) // 2
    cot = jnp.where(early, cot_a[...].astype(f32), cot_b[...].astype(f32))
    grad_first = cot + norm_back_rows(
        grad_feed, gain_ref[...], unit, inv
    )
    kept = grad_first * (1.0 - update)
    input_ref[...] = kept
    main_ref[:, value_width : value_width + width] = (kept * change * update).astype(bf16)
    grad_cand = (grad_first * update * (gate + candidate * (1.0 - gate))).astype(bf16)
    main_ref[:, value_width + width :] = grad_cand
    for c in range(value_width // 512):
        at = slice(c * 512, (c + 1) * 512)
        grad_gated = mm_nt(grad_cand, proj_ref[at, :])
        reset = reset_ref[:, at].astype(f32)
        open_gate = jax.nn.sigmoid(reset)
        passed = reset * open_gate
        grad_att_ref[:, at] = (grad_gated * passed).astype(bf16)
        main_ref[:, at] = (
            grad_gated
            * attended_ref[:, at].astype(f32)
            * (open_gate + passed * (1.0 - open_gate))
        ).astype(bf16)


def gate(back, cots, x, cand_in, base, attended, gain, proj, after=()):
    tokens, width = x.shape
    value_width = proj.shape[0]
    rows = min(128, tokens)
    half = tokens // rows // 2
    wide = value_width // width

    def block(columns, at=0):
        return pl.BlockSpec((rows, columns), lambda i: (i, at))

    return pl.pallas_call(
        ignoring(gate_body, 10, len(after)),
        grid=(tokens // rows,),
        in_specs=[
            block(width),
            pl.BlockSpec((rows, width), lambda i: (jnp.minimum(i, half - 1), 0)),
            pl.BlockSpec((rows, width), lambda i: (jnp.maximum(i - half, 0), 0)),
            block(width),
            block(width),
            block(width, wide),
            block(value_width),
            block(value_width),
            pl.BlockSpec((1, width), lambda i: (0, 0)),
            pl.BlockSpec(proj.shape, lambda i: (0, 0), pipeline_mode=pl.Buffered(1)),
        ]
        + [pl.BlockSpec(memory_space=pl.ANY)] * len(after),
        out_specs=[
            block(width),
            block(value_width + 2 * width),
            block(value_width),
            pl.BlockSpec((1, width), lambda i: (0, 0)),
        ],
        out_shape=[
            jax.ShapeDtypeStruct((tokens, width), f32),
            jax.ShapeDtypeStruct((tokens, value_width + 2 * width), bf16),
            jax.ShapeDtypeStruct((tokens, value_width), bf16),
            jax.ShapeDtypeStruct((1, width), f32),
        ],
        compiler_params=params(("arbitrary",)),
        name="gate",
        cost_estimate=pl.CostEstimate(
            flops=2 * tokens * width * value_width,
            bytes_accessed=40 * tokens * width,
            transcendentals=4 * tokens * width,
        ),
    )(back, *cots, x, cand_in, base, base, attended, gain, proj, *after)


def ordered_transpose(ids_ref, source, plain, ordered):
    plain[...] = source[...].T
    count = ids_ref.shape[0]
    rows = plain.shape[0] // count

    def place(p, _):
        ordered[pl.ds(pl.multiple_of(p * rows, rows), rows), :] = plain[
            pl.ds(pl.multiple_of(ids_ref[p] * rows, rows), rows), :
        ]
        return 0

    lax.fori_loop(0, count, place, 0)


def placed_transpose(places_ref, sources, plain, ordered):
    start = 0
    for source in sources:
        plain[:, start : start + source.shape[0]] = source[...].T
        start += source.shape[0]
    count = places_ref.shape[0]
    rows = plain.shape[0] // count

    def place(q, _):
        ordered[pl.ds(pl.multiple_of(places_ref[q] * rows, rows), rows), :] = plain[
            pl.ds(pl.multiple_of(q * rows, rows), rows), :
        ]
        return 0

    lax.fori_loop(0, count, place, 0)


def feed_body(
    ids_ref,
    places_ref,
    low_ref,
    cot_a,
    cot_b,
    first_ref,
    in_ref,
    out_ref,
    result_a,
    result_b,
    back_ref,
    out_send,
    out_keep,
    in_send,
    in_keep,
    total,
    cot_turned,
    low_turned,
    plain,
):
    step = pl.program_id(0)
    half = pl.num_programs(0) // 2
    tokens = low_ref.shape[0]
    middle = tokens // 2
    nt = (((1,), (1,)), ((), ()))

    @pl.when(step == 0)
    def _():
        placed_transpose(places_ref, (cot_a, cot_b), plain, cot_turned)
        ordered_transpose(ids_ref, low_ref, plain, low_turned)
        total[...] = first_ref[...]
        back_ref[...] = jnp.zeros_like(back_ref)

    acts, grads = [], []
    for r, cot_ref in enumerate((cot_a, cot_b)):
        at = slice(r * middle, (r + 1) * middle)
        hidden = jnp.dot(low_ref[at, :], in_ref[...], preferred_element_type=f32)
        grad_act = lax.dot_general(
            cot_ref[...], out_ref[...], nt, preferred_element_type=f32
        )
        gate = jax.nn.sigmoid(hidden)
        act = hidden * gate
        grad = (grad_act * (gate + act * (1.0 - gate))).astype(bf16)
        act = act.astype(bf16)
        total[at, :] += jnp.dot(act, out_ref[...], preferred_element_type=f32)
        back_ref[at, :] += lax.dot_general(
            grad, in_ref[...], nt, preferred_element_type=f32
        )
        acts.append(act)
        grads.append(grad)
    out_grad = jnp.dot(
        cot_turned[...], jnp.concatenate(acts), preferred_element_type=f32
    ).astype(bf16)
    in_grad = jnp.dot(
        low_turned[...], jnp.concatenate(grads), preferred_element_type=f32
    ).astype(bf16)
    split = in_grad.shape[0] // 2
    in_send[...] = in_grad[:split].reshape(in_send.shape)
    in_keep[...] = in_grad[split:].reshape(in_keep.shape)

    @pl.when(step < half)
    def _():
        out_send[0] = out_grad

    @pl.when(step >= half)
    def _():
        out_keep[0] = out_grad

    @pl.when(step == pl.num_programs(0) - 1)
    def _():
        result_a[...] = total[:middle, :].astype(bf16)
        result_b[...] = total[middle:, :].astype(bf16)


def feed(ids, places, low, cots, first_sum, feed_in, feed_out, seq, after=()):
    tokens, width = low.shape
    features = feed_in.shape[1]
    parts = ids.shape[0]
    half = parts // 2
    columns = features // parts
    rows = width // parts
    share = parts // seq
    anywhere = pl.BlockSpec(memory_space=pl.ANY)

    def all_of(shape):
        return pl.BlockSpec(
            shape, lambda i, t, u: (0,) * len(shape), pipeline_mode=pl.Buffered(1)
        )

    def at(i, t):
        return t[jnp.minimum(i, parts - 1)]

    split = pl.BlockSpec(
        (half, 1, rows, columns), lambda i, t, u: (0, u[at(i, t) // share], 0, at(i, t) % share)
    )
    return pl.pallas_call(
        ignoring(feed_body, 8, len(after)),
        grid_spec=pltpu.PrefetchScalarGridSpec(
            num_scalar_prefetch=2,
            grid=(parts,),
            in_specs=[
                all_of(low.shape),
                all_of(cots[0].shape),
                all_of(cots[1].shape),
                all_of(first_sum.shape),
                pl.BlockSpec((width, columns), lambda i, t, u: (0, at(i, t))),
                pl.BlockSpec((columns, width), lambda i, t, u: (at(i, t), 0)),
            ]
            + [anywhere] * len(after),
            out_specs=[
                all_of(cots[0].shape),
                all_of(cots[1].shape),
                all_of(low.shape),
                pl.BlockSpec(
                    (1, width, columns), lambda i, t, u: (jnp.minimum(i, half - 1), 0, 0)
                ),
                pl.BlockSpec(
                    (1, width, columns), lambda i, t, u: (jnp.maximum(i - half, 0), 0, 0)
                ),
                split,
                split,
            ],
            scratch_shapes=[
                pltpu.VMEM((tokens, width), f32),
                pltpu.VMEM((width, tokens), bf16),
                pltpu.VMEM((width, tokens), bf16),
                pltpu.VMEM((width, tokens), bf16),
            ],
        ),
        out_shape=[
            jax.ShapeDtypeStruct(cots[0].shape, bf16),
            jax.ShapeDtypeStruct(cots[1].shape, bf16),
            jax.ShapeDtypeStruct((tokens, width), f32),
            jax.ShapeDtypeStruct((half, width, columns), bf16),
            jax.ShapeDtypeStruct((half, width, columns), bf16),
            jax.ShapeDtypeStruct((half, seq, rows, features // seq), bf16),
            jax.ShapeDtypeStruct((half, seq, rows, features // seq), bf16),
        ],
        compiler_params=params(("arbitrary",)),
        name="feed",
        cost_estimate=pl.CostEstimate(
            flops=12 * tokens * width * features,
            bytes_accessed=8 * width * features + 16 * tokens * width,
            transcendentals=tokens * features,
        ),
    )(ids, places, low, *cots, first_sum, feed_in, feed_out, *after)


def by_columns_body(ids_ref, places_ref, left_ref, right_ref, send, keep, plain, turned):
    step = pl.program_id(0)
    half = pl.num_programs(0) // 2

    @pl.when(step == 0)
    def _():
        placed_transpose(places_ref, (left_ref,), plain, turned)

    grad = jnp.dot(turned[...], right_ref[...], preferred_element_type=f32).astype(bf16)

    @pl.when(step < half)
    def _():
        send[0] = grad

    @pl.when(step >= half)
    def _():
        keep[0] = grad


def by_columns(ids, places, left, right, after=(), rows=None, at=0):
    tokens = left.shape[0]
    rows = rows or left.shape[1]
    parts = ids.shape[0]
    half = parts // 2
    columns = right.shape[1] // parts
    shape = jax.ShapeDtypeStruct((half, rows, columns), bf16)
    if columns % 128:
        left = left[:, at * rows : (at + 1) * rows]
        grad = mm_tn(left, right).astype(bf16).reshape(rows, parts, columns)
        grad = jnp.take(grad, ids, axis=1).transpose(1, 0, 2)
        grad = grad.reshape(parts, places.shape[0], -1, columns)
        grad = jnp.take(grad, jnp.argsort(places), axis=1).reshape(parts, rows, columns)
        return grad[:half], grad[half:]
    return pl.pallas_call(
        ignoring(by_columns_body, 4, len(after)),
        grid_spec=pltpu.PrefetchScalarGridSpec(
            num_scalar_prefetch=2,
            grid=(parts,),
            in_specs=[
                pl.BlockSpec(
                    (tokens, rows), lambda i, t, u: (0, at), pipeline_mode=pl.Buffered(1)
                ),
                pl.BlockSpec((tokens, columns), lambda i, t, u: (0, t[jnp.minimum(i, parts - 1)])),
            ]
            + [pl.BlockSpec(memory_space=pl.ANY)] * len(after),
            out_specs=[
                pl.BlockSpec(
                    (1, rows, columns), lambda i, t, u: (jnp.minimum(i, half - 1), 0, 0)
                ),
                pl.BlockSpec(
                    (1, rows, columns), lambda i, t, u: (jnp.maximum(i - half, 0), 0, 0)
                ),
            ],
            scratch_shapes=[
                pltpu.VMEM((rows, tokens), bf16),
                pltpu.VMEM((rows, tokens), bf16),
            ],
        ),
        out_shape=[shape, shape],
        compiler_params=params(("arbitrary",)),
        name="by_columns",
        cost_estimate=pl.CostEstimate(
            flops=2 * tokens * rows * right.shape[1],
            bytes_accessed=2 * (tokens + rows) * right.shape[1],
            transcendentals=0,
        ),
    )(ids, places, left, right, *after)


def by_rows_body(ids_ref, places_ref, left_ref, right_ref, send, keep, plain, turned):
    @pl.when(pl.program_id(0) == 0)
    def _():
        ordered_transpose(ids_ref, left_ref, plain, turned)

    grad = jnp.dot(turned[...], right_ref[...], preferred_element_type=f32).astype(bf16)
    middle = grad.shape[0] // 2
    send[...] = grad[:middle].reshape(send.shape)
    keep[...] = grad[middle:].reshape(keep.shape)


def by_rows(ids, places, left, right, seq=1, after=()):
    tokens, rows = left.shape
    parts = ids.shape[0]
    half = parts // 2
    if places is None:
        seq, places = 1, jnp.zeros((1,), jnp.int32)
    columns = right.shape[1] // seq
    tile = min(512, columns)
    share = columns // tile
    shape = jax.ShapeDtypeStruct((half, seq, rows // parts, columns), bf16)
    split = pl.BlockSpec(
        (half, 1, rows // parts, tile), lambda i, t, u: (0, u[jnp.minimum(i // share, seq - 1)], 0, i % share)
    )
    return pl.pallas_call(
        ignoring(by_rows_body, 4, len(after)),
        grid_spec=pltpu.PrefetchScalarGridSpec(
            num_scalar_prefetch=2,
            grid=(seq * share,),
            in_specs=[
                pl.BlockSpec(
                    left.shape, lambda i, t, u: (0, 0), pipeline_mode=pl.Buffered(1)
                ),
                pl.BlockSpec((tokens, tile), lambda i, t, u: (0, i)),
            ]
            + [pl.BlockSpec(memory_space=pl.ANY)] * len(after),
            out_specs=[split, split],
            scratch_shapes=[
                pltpu.VMEM((rows, tokens), bf16),
                pltpu.VMEM((rows, tokens), bf16),
            ],
        ),
        out_shape=[shape, shape],
        compiler_params=params(("arbitrary",)),
        name="by_rows",
        cost_estimate=pl.CostEstimate(
            flops=2 * tokens * rows * right.shape[1],
            bytes_accessed=2 * (tokens + rows) * right.shape[1],
            transcendentals=0,
        ),
    )(ids, places, left, right, *after)


def value_back_body(
    ids_ref,
    places_ref,
    left_ref,
    own_ref,
    other_ref,
    slope_ref,
    proj_ref,
    total_ref,
    send,
    keep,
    plain,
    turned,
):
    @pl.when(pl.program_id(0) == 0)
    def _():
        total_ref[...] = jnp.zeros_like(total_ref)
        ordered_transpose(ids_ref, left_ref, plain, turned)

    grad = own_ref[...].astype(f32)
    for k in range(other_ref.shape[0]):
        grad = grad + other_ref[k].astype(f32)
    grad = (grad * slope_ref[...].astype(f32)).astype(bf16)
    total_ref[...] += mm_nt(grad, proj_ref[...])
    weights = jnp.dot(turned[...], grad, preferred_element_type=f32).astype(bf16)
    middle = weights.shape[0] // 2
    send[...] = weights[:middle].reshape(send.shape)
    keep[...] = weights[middle:].reshape(keep.shape)


def value_back(ids, places, left, own, others, slope, proj, seq, after=()):
    tokens, rows = left.shape
    parts = ids.shape[0]
    half = parts // 2
    columns = proj.shape[1] // seq
    tile = min(512, columns)
    share = columns // tile
    shape = jax.ShapeDtypeStruct((half, seq, rows // parts, columns), bf16)
    split = pl.BlockSpec(
        (half, 1, rows // parts, tile),
        lambda i, t, u: (0, u[jnp.minimum(i // share, seq - 1)], 0, i % share),
    )
    stripe = pl.BlockSpec((tokens, tile), lambda i, t, u: (0, i))
    fixed = pl.BlockSpec(
        (tokens, rows), lambda i, t, u: (0, 0), pipeline_mode=pl.Buffered(1)
    )
    return pl.pallas_call(
        ignoring(value_back_body, 7, len(after)),
        grid_spec=pltpu.PrefetchScalarGridSpec(
            num_scalar_prefetch=2,
            grid=(seq * share,),
            in_specs=[
                fixed,
                stripe,
                pl.BlockSpec((others.shape[0], tokens, tile), lambda i, t, u: (0, 0, i)),
                stripe,
                pl.BlockSpec((rows, tile), lambda i, t, u: (0, i)),
            ]
            + [pl.BlockSpec(memory_space=pl.ANY)] * len(after),
            out_specs=[fixed, split, split],
            scratch_shapes=[
                pltpu.VMEM((rows, tokens), bf16),
                pltpu.VMEM((rows, tokens), bf16),
            ],
        ),
        out_shape=[jax.ShapeDtypeStruct((tokens, rows), f32), shape, shape],
        compiler_params=params(("arbitrary",)),
        name="value_back",
        cost_estimate=pl.CostEstimate(
            flops=4 * tokens * rows * proj.shape[1],
            bytes_accessed=20 * tokens * rows,
            transcendentals=0,
        ),
    )(ids, places, left, own, others, slope, proj, *after)


def stage_body(*refs, shapes):
    count = len(shapes)
    ins, outs = refs[: 2 * count], list(refs[2 * count :])
    for k in range(count):
        kept, arrived = ins[2 * k], ins[2 * k + 1]
        for part in range(shapes[k][0]):
            out = outs.pop(0)
            out[...] = (kept[part].astype(f32) + arrived[part].astype(f32)).astype(out.dtype)


def stage_sums(pairs, after=(), steps=4, wide=()):
    shapes, ins, in_specs, out_specs, out_shapes, whole = [], [], [], [], [], []
    for kept, _ in pairs:
        rows = kept.size // kept.shape[-1] // min(2, kept.shape[0])
        while rows % (16 * steps):
            steps //= 2
    for number, (kept, arrived) in enumerate(pairs):
        halves = 1 if kept.shape[0] == 1 else 2
        columns = kept.shape[-1]
        rows = kept.size // columns // halves
        rows_each = rows // steps
        shapes.append((halves, rows, columns))
        for v in (kept, arrived):
            ins.append(v.reshape(halves, rows, columns))
            in_specs.append(pl.BlockSpec((halves, rows_each, columns), lambda i: (0, i, 0)))
        for _ in range(halves):
            out_specs.append(pl.BlockSpec((rows_each, columns), lambda i: (i, 0)))
            out_shapes.append(
                jax.ShapeDtypeStruct((rows, columns), f32 if number in wide else bf16)
            )
        whole.append((halves, (kept.shape[0] // halves, *kept.shape[1:])))
    sums = list(
        pl.pallas_call(
            ignoring(functools.partial(stage_body, shapes=shapes), len(ins), len(after)),
            grid=(steps,),
            in_specs=in_specs + [pl.BlockSpec(memory_space=pl.ANY)] * len(after),
            out_specs=out_specs,
            out_shape=out_shapes,
            compiler_params=params(("arbitrary",)),
            name="stage_sums",
            cost_estimate=pl.CostEstimate(
                flops=sum(v.size for v in ins),
                bytes_accessed=sum(3 * v.size for v in ins),
                transcendentals=0,
            ),
        )(*ins, *after)
    )
    out = []
    for halves, shape in whole:
        out.append(tuple(sums.pop(0).reshape(shape) for _ in range(halves)))
    return out


class Layout:
    def __init__(self, mesh):
        self.dp = mesh.shape["dp"]
        self.seq = mesh.shape["seq"]
        self.members = self.seq // 2
        self.chips = self.seq // 4

    def pairs(self, move):
        return [
            (d * self.seq + z, e * self.seq + w)
            for d in range(self.dp)
            for z in range(self.seq)
            for e, w in [move(d, z)]
        ]

    def send(self, value, move):
        return lax.ppermute(value, AXES, self.pairs(move))

    def place(self, sequence, member):
        return member % 2 ^ (1 - sequence % 2), sequence * self.chips + member // 2

    def member(self, core, z):
        sequence = z // self.chips
        return (z % self.chips) * 2 + (core ^ (1 - sequence % 2))

    def home_to_work(self, round_index):
        def move(d, z):
            part = (1 if z >= self.seq // 2 else 0) ^ round_index
            core, at = self.place(2 * (d % 2) + part, min(z, self.seq - 1 - z))
            return d - d % 2 + core, at

        return move

    def spread(self, value):
        late = lax.axis_index("seq") >= self.seq // 2
        out = []
        for round_index in range(2):
            sent = lax.dynamic_index_in_dim(
                value, jnp.where(late, 1 - round_index, round_index), 0, False
            )
            out.append(self.send(sent, self.home_to_work(round_index)))
        return out

    def collect(self, values):
        back = []
        for round_index in range(2):
            pairs = [(b, a) for a, b in self.pairs(self.home_to_work(round_index))]
            back.append(lax.ppermute(values[round_index], AXES, pairs))
        late = lax.axis_index("seq") >= self.seq // 2
        return jnp.stack([jnp.where(late, back[1], back[0]), jnp.where(late, back[0], back[1])])

    def rotate(self, value, by):
        def move(d, z):
            member = (self.member(d % 2, z) + by) % self.members
            core, at = self.place(z // self.chips, member)
            return d - d % 2 + core, at

        return self.send(value, move)

    def gather(self, value):
        return jnp.concatenate([self.rotate(value, by) for by in range(1, self.members)], axis=0)

    def returns(self, others):
        slots = others.shape[0] // (self.members - 1)
        return jnp.stack(
            [
                self.rotate(others[(by - 1) * slots : by * slots], self.members - by).reshape(
                    -1, others.shape[-1]
                )
                for by in range(1, self.members)
            ]
        )

    def scatter_sum(self, own, others):
        slots = own.shape[0]
        total = own.astype(f32)
        for by in range(1, self.members):
            total = total + self.rotate(
                others[(by - 1) * slots : by * slots], self.members - by
            ).astype(f32)
        return total

    def orders(self):
        dp, z = lax.axis_index("dp"), lax.axis_index("seq")
        bits = self.dp.bit_length() - 1
        ids = []
        for core in range(2):
            orders = [[0, *range(1, bits)], [0, *reversed(range(1, bits))]]
            flips = []
            for p in range(self.dp):
                order = orders[core if p >= self.dp // 2 else 1 - core]
                flips.append(
                    sum(
                        (0 if p >> (bits - 1 - i) & 1 else 1) << bit
                        for i, bit in enumerate(order)
                    )
                )
            ids.append(dp ^ jnp.array(flips, jnp.int32))
        ids = jnp.where(dp % 2 == 0, ids[0], ids[1])
        bits = self.seq.bit_length() - 1
        flips = [
            sum((0 if p >> (bits - 1 - i) & 1 else 1) << i for i in range(bits))
            for p in range(self.seq)
        ]
        blocks = z ^ jnp.array(flips, jnp.int32)
        return ids, jnp.argsort(blocks).astype(jnp.int32), blocks

    def partner(self, stage):
        bits = self.dp.bit_length() - 1
        if stage == 0:
            return lambda d, z: (d ^ 1, z)
        if stage < bits:
            return lambda d, z: (d ^ (1 << stage if d % 2 == 0 else 1 << (bits - stage)), z)
        return lambda d, z: (d, z ^ (1 << (stage - bits)))

    def turn(self, sums, after):
        sums = [s for s in sums if s.arrived is not None]
        if not sums:
            return after
        dp_stages = self.dp.bit_length() - 1
        last = dp_stages + self.seq.bit_length() - 1
        wide = [k for k, s in enumerate(sums) if s.stage + 1 == last]
        out = stage_sums([(s.kept, s.arrived) for s in sums], after, wide=wide)
        for s, held in zip(sums, out):
            s.stage += 1
            s.arrived = None
            if s.stage == last:
                s.total = held[0][0]
            elif s.stage == dp_stages:
                s.block = held[0]
                if s.over_seq:
                    s.begin_seq(held[0])
            else:
                s.send(*held)
        return [part for held in out for part in held]

    def reduce_all(self, flat):
        core = lax.axis_index("dp") % 2
        count = flat.shape[0]
        split = jnp.pad(flat, (0, -count % 2048)).reshape(2, -1, 128)
        held = lax.dynamic_index_in_dim(split, core, 0, False)
        sent = lax.dynamic_index_in_dim(split, 1 - core, 0, False)
        held = held + self.send(sent, lambda d, z: (d ^ 1, z))
        for bit in range(1, self.dp.bit_length() - 1):
            held = held + self.send(held, lambda d, z: (d ^ (1 << bit), z))
        for bit in range(self.seq.bit_length() - 1):
            held = held + self.send(held, lambda d, z: (d, z ^ (1 << bit)))
        other = self.send(held, lambda d, z: (d ^ 1, z))
        return jnp.where(
            core == 0, jnp.stack([held, other]), jnp.stack([other, held])
        ).reshape(-1)[:count]


class Sum:
    def __init__(self, layout, sent, kept, over_seq=True):
        self.layout, self.over_seq, self.stage = layout, over_seq, 0
        self.block = self.total = None
        self.send(sent, kept)

    def send(self, sent, kept):
        self.kept = kept
        self.arrived = self.layout.send(sent, self.layout.partner(self.stage))

    def begin_seq(self, block):
        block = block.reshape(self.layout.seq, -1, block.shape[-1])
        middle = self.layout.seq // 2
        self.send(block[:middle], block[middle:])


def mm(a, b):
    return jnp.dot(a, b, preferred_element_type=f32)


def mm_nt(a, b):
    return lax.dot_general(a, b, (((1,), (1,)), ((), ())), preferred_element_type=f32)


def mm_tn(a, b):
    return lax.dot_general(a, b, (((0,), (0,)), ((), ())), preferred_element_type=f32)


def layer(
    layout,
    inputs,
    cotangent,
    full_attention,
    mix_gain,
    smooth_alpha,
    smooth_damp,
    smooth_beta,
    smooth_eta,
    smooth_omega,
    value_proj,
    mix_proj,
    score_affine,
    relative_bias,
    out_proj,
    feed_gain,
    feed_in,
    feed_out,
):
    slots, chunk_rows, width = inputs.shape
    key_width = score_affine.shape[1]
    value_width = value_proj.shape[1]
    tokens = slots * chunk_rows
    total = layout.seq
    seq_length = relative_bias.shape[0] // 2
    block = min(64, chunk_rows)
    core = lax.axis_index("dp") % 2
    z = lax.axis_index("seq")

    sequence = z // layout.chips
    member = layout.member(core, z)
    swap = sequence % 2
    chunks = []
    for by in range(layout.members):
        source = (member - by) % layout.members
        low, high = source, total - 1 - source
        chunks += [jnp.where(swap == 0, low, high), jnp.where(swap == 0, high, low)]
    chunks = jnp.stack(chunks).astype(jnp.int32)
    slot_of = jnp.sum(
        jnp.where(chunks[None, :] == jnp.arange(total)[:, None], jnp.arange(total)[None, :], 0),
        axis=1,
    ).astype(jnp.int32)
    flags = full_attention.astype(f32)
    flags_other = layout.send(flags, lambda d, z: (d ^ 1, z))
    flags = jnp.where(
        core == 0, jnp.concatenate([flags, flags_other]), jnp.concatenate([flags_other, flags])
    )
    full = lax.dynamic_index_in_dim(flags, sequence, 0, False) == 1.0
    table = jnp.concatenate([chunks, slot_of, full.astype(jnp.int32)[None]])
    ids, places, blocks = layout.orders()

    x = jnp.stack(layout.spread(inputs))
    cots = layout.spread(cotangent)
    bias_back, bias_front = bias_tiles(relative_bias, chunk_rows // TILE - 1, full)

    states = smooth_alpha.shape[0]
    lanes = (states, width // 128, 128)
    decay = 1.0 - smooth_alpha * smooth_damp
    rate = smooth_alpha * smooth_beta
    span = (decay**chunk_rows).reshape(lanes)
    coef = (smooth_eta * rate).reshape(lanes)
    decay_slab = decay.reshape(lanes)
    gain_row = mix_gain[None]
    omega_row = smooth_omega[None]
    mix_shared, mix_main = mix_proj[:, :key_width], mix_proj[:, key_width:]

    normed_low, ends = front_ends(
        x, gain_row, decay_slab, after=(bias_back, bias_front, mix_main, mix_shared, span, coef)
    )
    ends_all = jnp.concatenate([ends, layout.gather(ends)])
    normed_low = normed_low.reshape(tokens, width)
    value_pre = mm(normed_low, value_proj)
    value_low = jax.nn.silu(value_pre).astype(bf16).reshape(slots, chunk_rows, value_width)
    value_slope = silu_slope(value_pre).astype(bf16)
    value_others = layout.gather(value_low)
    smoothed, mixed, check = front_scan(
        table, x, gain_row, decay_slab, coef, span, omega_row, ends_all, block
    )
    smoothed = smoothed.reshape(tokens, width)
    mixed = mixed.reshape(tokens, width)

    shared_pre = mm(mixed, mix_shared)
    shared = jax.nn.silu(shared_pre)
    query_low = (shared * score_affine[0] + score_affine[1]).astype(bf16)
    key_low = (shared * score_affine[2] + score_affine[3]).astype(bf16)
    query_low = query_low.reshape(slots, chunk_rows, key_width)
    key_low = key_low.reshape(slots, chunk_rows, key_width)
    key_others = layout.gather(key_low)
    base = mm(mixed, mix_main).astype(bf16)
    attended, gated, lse = attend(
        table,
        query_low,
        bias_front,
        base.reshape(slots, chunk_rows, -1),
        key_low,
        key_others,
        value_low,
        value_others,
    )
    attended = attended.reshape(tokens, value_width)
    gated = gated.reshape(tokens, value_width)

    flat_low = x.reshape(tokens, width)
    flat = flat_low.astype(f32)
    update_pre = base[:, value_width : value_width + width].astype(f32)
    cand_in = base[:, value_width + width :].astype(f32) + mm(gated, out_proj)
    first_sum = flat + jax.nn.sigmoid(update_pre) * (jax.nn.silu(cand_in) - flat)
    unit_two, _ = unit_rows_of(first_sum)
    feed_low = (unit_two * feed_gain).astype(bf16)

    result_a, result_b, grad_feed, out_send, out_keep, in_send, in_keep = feed(
        ids, places, feed_low, cots, first_sum, feed_in, feed_out, layout.seq
    )
    block_out = layout.collect([result_a, result_b])
    feed_out_sum = Sum(layout, out_send, out_keep)
    feed_in_sum = Sum(layout, in_send, in_keep)

    grad_input, grad_main, grad_att, feed_gain_grad = gate(
        grad_feed, cots, flat_low, cand_in, base, attended, feed_gain[None], out_proj
    )
    after = layout.turn((feed_out_sum, feed_in_sum), (grad_att,))
    proj_parts = by_columns(
        ids,
        places,
        grad_main,
        gated,
        rows=width,
        at=grad_main.shape[1] // width - 1,
        after=after,
    )
    proj_sum = Sum(layout, *proj_parts)
    mix_parts = by_rows(ids, None, mixed, grad_main, after=proj_parts)
    mix_sum = Sum(layout, *mix_parts, over_seq=False)
    after = layout.turn((proj_sum,), mix_parts)
    grad_query, gk_own, gk_oth, gv_own, gv_oth, rel_sums = attend_back(
        table,
        query_low,
        grad_att.reshape(slots, chunk_rows, value_width),
        lse.reshape(slots, 1, chunk_rows),
        bias_back,
        key_low,
        key_others,
        value_low,
        value_others,
        after=after,
    )
    after = layout.turn((feed_out_sum, feed_in_sum, mix_sum), (grad_query,))
    grad_key = layout.scatter_sum(gk_own, gk_oth).reshape(tokens, key_width)
    grad_query = grad_query.reshape(tokens, key_width)
    grad_shared = (
        (grad_query * score_affine[0] + grad_key * score_affine[2]) * silu_slope(shared_pre)
    ).astype(bf16)
    grad_smooth = (mm_nt(grad_main, mix_main) + mm_nt(grad_shared, mix_shared)) * silu_slope(
        smoothed
    )
    grad_smooth = grad_smooth.reshape(slots, chunk_rows, width)
    back = back_ends(grad_smooth, decay_slab, after=after)
    back_all = jnp.concatenate([back, layout.gather(back)])
    after = layout.turn((proj_sum, feed_out_sum, feed_in_sum), (back,))
    grad_normed, value_send, value_keep = value_back(
        ids,
        places,
        normed_low,
        gv_own.reshape(tokens, value_width),
        layout.returns(gv_oth),
        value_slope,
        value_proj,
        layout.seq,
        after=after,
    )
    value_sum = Sum(layout, value_send, value_keep)
    shared_parts = by_rows(ids, None, mixed, grad_shared, after=(grad_normed,))
    shared_sum = Sum(layout, *shared_parts, over_seq=False)
    after = layout.turn((mix_sum, value_sum, shared_sum), shared_parts)

    def scan_back(slot, after):
        return back_scan(
            table,
            slot,
            x,
            grad_smooth,
            grad_normed.reshape(slots, chunk_rows, width),
            grad_input.reshape(slots, chunk_rows, width),
            check,
            gain_row,
            decay_slab,
            coef,
            span,
            omega_row,
            back_all,
            after=after,
        )

    first = scan_back(0, after)
    after = layout.turn(
        (feed_out_sum, feed_in_sum, proj_sum, mix_sum, value_sum, shared_sum), (first[0],)
    )
    second = scan_back(1, after)
    grad_in = layout.collect([first[0], second[0]]).astype(f32)
    after = layout.turn((proj_sum, value_sum, shared_sum), (second[0],))
    while mix_sum.block is None or shared_sum.block is None:
        after = layout.turn((mix_sum, shared_sum), after)
    mix_rows = jnp.concatenate([shared_sum.block[0, 0], mix_sum.block[0, 0]], axis=1)
    mix_rows = mix_rows.reshape(mix_rows.shape[0], layout.seq, -1).transpose(1, 0, 2)
    mix_sum.begin_seq(mix_rows[blocks])
    sums = (feed_out_sum, feed_in_sum, proj_sum, value_sum, mix_sum)
    while any(v.total is None for v in sums):
        after = layout.turn(sums, after)
    feed_out_grad, feed_in_grad, out_grad, value_grad, mix_grad = (v.total for v in sums)
    feed_out_grad, out_grad = feed_out_grad.T, out_grad.T
    qx, qs, mix_gain_grad, omega_grad = (a + b for a, b in zip(first[1:], second[1:]))

    affine_grad = jnp.stack(
        [
            jnp.sum(grad_query * shared_pre * jax.nn.sigmoid(shared_pre), axis=0),
            jnp.sum(grad_query, axis=0),
            jnp.sum(grad_key * shared_pre * jax.nn.sigmoid(shared_pre), axis=0),
            jnp.sum(grad_key, axis=0),
        ]
    )
    relative_grad = bias_grad(rel_sums[:, 0], seq_length)
    small = [
        qx.reshape(-1),
        qs.reshape(-1),
        mix_gain_grad.reshape(-1),
        omega_grad.reshape(-1),
        feed_gain_grad.reshape(-1),
        affine_grad.reshape(-1),
        relative_grad,
    ]
    sums = layout.reduce_all(jnp.concatenate(small))
    parts, start = [], 0
    for item in small:
        parts.append(lax.slice_in_dim(sums, start, start + item.shape[0]))
        start += item.shape[0]
    input_sum = parts[0].reshape(states, width)
    decay_sum = parts[1].reshape(states, width)
    input_total = smooth_eta * input_sum
    decay_total = smooth_eta * rate * decay_sum
    eta_grad = rate * input_sum
    alpha_grad = smooth_beta * input_total - smooth_damp * decay_total
    damp_grad = -smooth_alpha * decay_total
    beta_grad = smooth_alpha * input_total

    return (
        block_out,
        grad_in,
        parts[2],
        alpha_grad,
        damp_grad,
        beta_grad,
        eta_grad,
        parts[3],
        value_grad,
        mix_grad,
        parts[5].reshape(4, key_width),
        parts[6],
        out_grad,
        parts[4],
        feed_in_grad,
        feed_out_grad,
    )


def solution(mesh):
    tokens = P("dp", "seq", None)
    split = P("dp", "seq")
    return jax.shard_map(
        functools.partial(layer, Layout(mesh)),
        mesh=mesh,
        in_specs=(tokens, tokens, P("dp")) + (P(),) * 14,
        out_specs=(tokens, tokens)
        + (P(),) * 6
        + (split, split, P(), P(), split, P(), split, split),
        check_vma=False,
    )
```

```python
import functools

import jax
import jax.numpy as jnp
from jax import lax
from jax.experimental import pallas as pl
from jax.experimental.pallas import tpu as pltpu
from jax.sharding import PartitionSpec as P

STRETCH = 128
EPSILON = 1e-05
TILE = 256
MASKED = -1e30
VMEM_LIMIT = 60 * 1024 * 1024
AXES = ("dp", "seq")
BRIEF = pl.CostEstimate(flops=1, bytes_accessed=1, transcendentals=0)
LONG = pl.CostEstimate(flops=10**11, bytes_accessed=1, transcendentals=0)

f32 = jnp.float32
bf16 = jnp.bfloat16


def unit_rows_of(values):
    centred = values - jnp.mean(values, axis=-1, keepdims=True)
    inv_std = lax.rsqrt(jnp.mean(centred * centred, axis=-1, keepdims=True) + EPSILON)
    return centred * inv_std, inv_std


def norm_back_rows(grad_out, gain_vec, unit_rows, inv_std):
    scaled = grad_out * gain_vec
    return inv_std * (
        scaled
        - jnp.mean(scaled, axis=-1, keepdims=True)
        - unit_rows * jnp.mean(scaled * unit_rows, axis=-1, keepdims=True)
    )


def silu_slope(pre_act):
    sigmoid_val = jax.nn.sigmoid(pre_act)
    return sigmoid_val * (1.0 + pre_act * (1.0 - sigmoid_val))


def params(semantics, limit=VMEM_LIMIT):
    return pltpu.CompilerParams(dimension_semantics=semantics, vmem_limit_bytes=limit)


def ignoring(body, first, count):
    def called(*refs):
        return body(*refs[:first], *refs[first + count :])

    return called


def to_slab(slab, rows):
    count, groups = rows.shape[0], rows.shape[1] // 128
    for c in range(groups):
        slab[pl.ds(c, count, stride=groups), :] = rows[:, c * 128 : (c + 1) * 128]


def from_slab(slab, count, groups):
    return jnp.concatenate(
        [slab[pl.ds(c, count, stride=groups), :] for c in range(groups)], axis=1
    )


def slab_row(slab, t, groups):
    return slab[pl.ds(pl.multiple_of(t * groups, groups), groups), :]


def front_ends_body(x_ref, gain_ref, decay_ref, low_ref, end_ref, slab):
    states, groups, _ = decay_ref.shape
    count = x_ref.shape[1]

    @pl.when(pl.program_id(1) == 0)
    def _():
        end_ref[...] = jnp.zeros_like(end_ref)

    unit, _ = unit_rows_of(x_ref[0].astype(f32))
    normed = unit * gain_ref[...]
    low_ref[0] = normed.astype(bf16)
    to_slab(slab, normed)
    decay = [decay_ref[n] for n in range(states)]

    def step(t, state):
        row = slab_row(slab, t, groups)
        return tuple(d * s + row for d, s in zip(decay, state))

    state = lax.fori_loop(
        0, count, step, tuple(end_ref[0, n] for n in range(states)), unroll=8
    )
    for n in range(states):
        end_ref[0, n] = state[n]


def front_ends(x, gain, decay, block=256, after=()):
    slots, length, width = x.shape
    states, groups, lanes = decay.shape
    block = min(block, length)
    return pl.pallas_call(
        ignoring(front_ends_body, 3, len(after)),
        grid=(slots, length // block),
        in_specs=[
            pl.BlockSpec((1, block, width), lambda k, b: (k, b, 0)),
            pl.BlockSpec((1, width), lambda k, b: (0, 0)),
            pl.BlockSpec((states, groups, lanes), lambda k, b: (0, 0, 0)),
        ]
        + [pl.BlockSpec(memory_space=pl.ANY)] * len(after),
        out_specs=[
            pl.BlockSpec((1, block, width), lambda k, b: (k, b, 0)),
            pl.BlockSpec((1, states, groups, lanes), lambda k, b: (k, 0, 0, 0)),
        ],
        out_shape=[
            jax.ShapeDtypeStruct((slots, length, width), bf16),
            jax.ShapeDtypeStruct((slots, states, groups, lanes), f32),
        ],
        scratch_shapes=[pltpu.VMEM((block * groups, lanes), f32)],
        compiler_params=params(("arbitrary", "arbitrary")),
        name="front_ends",
        cost_estimate=BRIEF,
    )(x, gain, decay, *after)


def front_scan_body(
    table_ref,
    x_ref,
    gain_ref,
    decay_ref,
    coef_ref,
    span_ref,
    omega_ref,
    ends_ref,
    smooth_ref,
    mixed_ref,
    check_ref,
    slab,
    out_slab,
    carry,
):
    states, groups, _ = decay_ref.shape
    count = x_ref.shape[1]
    slot = pl.program_id(0)
    total = ends_ref.shape[0]

    @pl.when(pl.program_id(1) == 0)
    def _():
        carry[...] = jnp.zeros_like(carry)

        def link(i, _):
            carry[...] = span_ref[...] * carry[...] + ends_ref[table_ref[total + i]]
            return 0

        lax.fori_loop(0, table_ref[slot], link, 0)

    unit, _ = unit_rows_of(x_ref[0].astype(f32))
    normed = unit * gain_ref[...]
    to_slab(slab, normed)
    decay = [decay_ref[n] for n in range(states)]
    coef = [coef_ref[n] for n in range(states)]
    state = tuple(carry[n] for n in range(states))
    for n in range(states):
        check_ref[0, 0, n] = state[n]

    def step(t, state):
        row = slab_row(slab, t, groups)
        state = tuple(d * s + row for d, s in zip(decay, state))
        parts = [c * s for c, s in zip(coef, state)]
        while len(parts) > 1:
            parts = [a + b for a, b in zip(parts[::2], parts[1::2])]
        out_slab[pl.ds(pl.multiple_of(t * groups, groups), groups), :] = parts[0]
        return state

    state = lax.fori_loop(0, count, step, state, unroll=8)
    for n in range(states):
        carry[n] = state[n]
    smoothed = from_slab(out_slab, count, groups) + omega_ref[...] * normed
    smooth_ref[0] = smoothed
    mixed_ref[0] = (smoothed * jax.nn.sigmoid(smoothed)).astype(bf16)


def front_scan(table, x, gain, decay, coef, span, omega, ends, block):
    slots, length, width = x.shape
    states, groups, lanes = decay.shape
    whole3 = pl.BlockSpec((states, groups, lanes), lambda k, b, t: (0, 0, 0))
    row = pl.BlockSpec((1, width), lambda k, b, t: (0, 0))
    tokens = pl.BlockSpec((1, block, width), lambda k, b, t: (k, b, 0))
    return pl.pallas_call(
        front_scan_body,
        grid_spec=pltpu.PrefetchScalarGridSpec(
            num_scalar_prefetch=1,
            grid=(slots, length // block),
            in_specs=[
                tokens,
                row,
                whole3,
                whole3,
                whole3,
                row,
                pl.BlockSpec(ends.shape, lambda k, b, t: (0, 0, 0, 0)),
            ],
            out_specs=[
                tokens,
                tokens,
                pl.BlockSpec((1, 1, states, groups, lanes), lambda k, b, t: (k, b, 0, 0, 0)),
            ],
            scratch_shapes=[
                pltpu.VMEM((block * groups, lanes), f32),
                pltpu.VMEM((block * groups, lanes), f32),
                pltpu.VMEM((states, groups, lanes), f32),
            ],
        ),
        out_shape=[
            jax.ShapeDtypeStruct((slots, length, width), f32),
            jax.ShapeDtypeStruct((slots, length, width), bf16),
            jax.ShapeDtypeStruct((slots, length // block, states, groups, lanes), f32),
        ],
        compiler_params=params(("arbitrary", "arbitrary")),
        name="front_scan",
        cost_estimate=LONG,
    )(table, x, gain, decay, coef, span, omega, ends)


def back_ends_body(gs_ref, decay_ref, end_ref, slab):
    states, groups, _ = decay_ref.shape
    count = gs_ref.shape[1]

    @pl.when(pl.program_id(1) == 0)
    def _():
        end_ref[...] = jnp.zeros_like(end_ref)

    to_slab(slab, gs_ref[0])
    decay = [decay_ref[n] for n in range(states)]

    def step(t, state):
        row = slab_row(slab, count - 1 - t, groups)
        return tuple(d * s + row for d, s in zip(decay, state))

    state = lax.fori_loop(
        0, count, step, tuple(end_ref[0, n] for n in range(states)), unroll=8
    )
    for n in range(states):
        end_ref[0, n] = state[n]


def back_ends(gs, decay, block=256, after=()):
    slots, length, width = gs.shape
    states, groups, lanes = decay.shape
    block = min(block, length)
    blocks = length // block
    return pl.pallas_call(
        ignoring(back_ends_body, 2, len(after)),
        grid=(slots, blocks),
        in_specs=[
            pl.BlockSpec((1, block, width), lambda k, b: (k, blocks - 1 - b, 0)),
            pl.BlockSpec((states, groups, lanes), lambda k, b: (0, 0, 0)),
        ]
        + [pl.BlockSpec(memory_space=pl.ANY)] * len(after),
        out_specs=pl.BlockSpec((1, states, groups, lanes), lambda k, b: (k, 0, 0, 0)),
        out_shape=jax.ShapeDtypeStruct((slots, states, groups, lanes), f32),
        scratch_shapes=[pltpu.VMEM((block * groups, lanes), f32)],
        compiler_params=params(("arbitrary", "arbitrary")),
        name="back_ends",
        cost_estimate=BRIEF,
    )(gs, decay, *after)


def back_scan_body(
    table_ref,
    slot_ref,
    x_ref,
    gs_ref,
    gv_ref,
    gi_ref,
    check_ref,
    gain_ref,
    decay_ref,
    coef_ref,
    span_ref,
    omega_ref,
    ends_ref,
    grad_ref,
    qx_ref,
    qs_ref,
    gain_grad_ref,
    omega_grad_ref,
    slab,
    gs_slab,
    out_slab,
    history,
    carry,
):
    states, groups, _ = decay_ref.shape
    count = x_ref.shape[1]
    slot = slot_ref[0]
    total = ends_ref.shape[0]

    @pl.when(pl.program_id(0) == 0)
    def _():
        qx_ref[...] = jnp.zeros_like(qx_ref)
        qs_ref[...] = jnp.zeros_like(qs_ref)
        gain_grad_ref[...] = jnp.zeros_like(gain_grad_ref)
        omega_grad_ref[...] = jnp.zeros_like(omega_grad_ref)

    @pl.when(pl.program_id(0) == 0)
    def _():
        carry[...] = jnp.zeros_like(carry)

        def link(i, _):
            carry[...] = (
                span_ref[...] * carry[...] + ends_ref[table_ref[total + total - 1 - i]]
            )
            return 0

        lax.fori_loop(0, total - 1 - table_ref[slot], link, 0)

    unit, inv = unit_rows_of(x_ref[0].astype(f32))
    normed = unit * gain_ref[...]
    gs = gs_ref[0]
    to_slab(slab, normed)
    to_slab(gs_slab, gs)
    decay = [decay_ref[n] for n in range(states)]

    def recompute(t, state):
        for n in range(states):
            history[t, n] = state[n]
        row = slab_row(slab, t, groups)
        return tuple(d * s + row for d, s in zip(decay, state))

    lax.fori_loop(
        0, count, recompute, tuple(check_ref[0, 0, n] for n in range(states)), unroll=4
    )

    half = states // 2
    for part in range(2):
        chosen = range(part * half, (part + 1) * half)
        decay = [decay_ref[n] for n in chosen]
        coef = [coef_ref[n] for n in chosen]

        def step(i, held):
            q, qx, qs = held
            t = count - 1 - i
            row = slab_row(slab, t, groups)
            g = slab_row(gs_slab, t, groups)
            q = tuple(d * a + g for d, a in zip(decay, q))
            parts = [c * a for c, a in zip(coef, q)]
            while len(parts) > 1:
                parts = [a + b for a, b in zip(parts[::2], parts[1::2])]
            spot = pl.ds(pl.multiple_of(t * groups, groups), groups)
            if part == 0:
                out_slab[spot, :] = parts[0]
            else:
                out_slab[spot, :] = out_slab[spot, :] + parts[0]
            qx = tuple(a + b * row for a, b in zip(qx, q))
            qs = tuple(a + b * history[t, n] for a, b, n in zip(qs, q, chosen))
            return q, qx, qs

        q, qx, qs = lax.fori_loop(
            0,
            count,
            step,
            (
                tuple(carry[n] for n in chosen),
                tuple(qx_ref[n] for n in chosen),
                tuple(qs_ref[n] for n in chosen),
            ),
            unroll=4,
        )
        for i, n in enumerate(chosen):
            carry[n] = q[i]
            qx_ref[n] = qx[i]
            qs_ref[n] = qs[i]

    grad_normed = (
        gv_ref[0] + from_slab(out_slab, count, groups) + omega_ref[...] * gs
    )
    gain_grad_ref[...] += jnp.sum(grad_normed * unit, axis=0, keepdims=True)
    omega_grad_ref[...] += jnp.sum(gs * normed, axis=0, keepdims=True)
    grad_ref[...] = (
        gi_ref[0] + norm_back_rows(grad_normed, gain_ref[...], unit, inv)
    ).astype(bf16)


def back_scan(table, slot, x, gs, gv, gi, check, gain, decay, coef, span, omega, ends, after=()):
    _, length, width = x.shape
    states, groups, lanes = decay.shape
    blocks = check.shape[1]
    block = length // blocks
    whole3 = pl.BlockSpec((states, groups, lanes), lambda b, t, u: (0, 0, 0))
    row = pl.BlockSpec((1, width), lambda b, t, u: (0, 0))
    tokens = pl.BlockSpec((1, block, width), lambda b, t, u: (slot, blocks - 1 - b, 0))
    return pl.pallas_call(
        ignoring(back_scan_body, 13, len(after)),
        grid_spec=pltpu.PrefetchScalarGridSpec(
            num_scalar_prefetch=2,
            grid=(blocks,),
            in_specs=[
                tokens,
                tokens,
                tokens,
                tokens,
                pl.BlockSpec(
                    (1, 1, states, groups, lanes),
                    lambda b, t, u: (slot, blocks - 1 - b, 0, 0, 0),
                ),
                row,
                whole3,
                whole3,
                whole3,
                row,
                pl.BlockSpec(ends.shape, lambda b, t, u: (0, 0, 0, 0)),
            ]
            + [pl.BlockSpec(memory_space=pl.ANY)] * len(after),
            out_specs=[
                pl.BlockSpec((block, width), lambda b, t, u: (blocks - 1 - b, 0)),
                whole3,
                whole3,
                row,
                row,
            ],
            scratch_shapes=[
                pltpu.VMEM((block * groups, lanes), f32),
                pltpu.VMEM((block * groups, lanes), f32),
                pltpu.VMEM((block * groups, lanes), f32),
                pltpu.VMEM((block, states, groups, lanes), f32),
                pltpu.VMEM((states, groups, lanes), f32),
            ],
        ),
        out_shape=[
            jax.ShapeDtypeStruct((length, width), bf16),
            jax.ShapeDtypeStruct((states, groups, lanes), f32),
            jax.ShapeDtypeStruct((states, groups, lanes), f32),
            jax.ShapeDtypeStruct((1, width), f32),
            jax.ShapeDtypeStruct((1, width), f32),
        ],
        compiler_params=params(("arbitrary",)),
        name="back_scan",
        cost_estimate=LONG,
    )(table, jnp.full((1,), slot, jnp.int32), x, gs, gv, gi, check, gain, decay, coef, span, omega, ends, *after)


def load_chunks(table_ref, sources, total, length, sem):
    copies = []
    for slot in range(total):
        place = pl.ds(pl.multiple_of(table_ref[slot] * length, length), length)
        for own, others, kept in sources:
            source = own.at[slot] if slot < 2 else others.at[slot - 2]
            copies.append(
                pltpu.make_async_copy(source, kept.at[place, :], sem.at[len(copies)])
            )
    for copy in copies:
        copy.start()
    for copy in copies:
        copy.wait()


def attend_body(
    table_ref,
    q_ref,
    bias_ref,
    reset_ref,
    k_own,
    k_oth,
    v_own,
    v_oth,
    out_ref,
    gated_ref,
    lse_ref,
    keys,
    values,
    scores,
    probs,
    sem,
    *,
    total,
):
    length, key_width = q_ref.shape[1:]
    value_width = values.shape[1]
    tiles = length // TILE
    scale = float(key_width) ** (-0.5)

    @pl.when(pl.program_id(0) == 0)
    def _():
        load_chunks(
            table_ref, ((k_own, k_oth, keys), (v_own, v_oth, values)), total, length, sem
        )

    chunk = table_ref[pl.program_id(0)]
    reach = jnp.where(table_ref[2 * total] == 1, chunk + 1, 1)
    base = (chunk + 1 - reach) * length
    queries = q_ref[0]

    def first(kt, peak):
        spot = pl.ds(pl.multiple_of(base + kt * TILE, TILE), TILE)
        tile = (
            lax.dot_general(
                queries, keys[spot, :], (((1,), (1,)), ((), ())), preferred_element_type=f32
            )
            * scale
        )
        for r in range(tiles):
            rows = slice(r * TILE, (r + 1) * TILE)
            gap = (reach - 1) * tiles + r - kt + tiles - 1
            scores[kt, rows, :] = tile[rows] + bias_ref[gap]
        return jnp.maximum(peak, jnp.max(scores[kt], axis=1, keepdims=True))

    peak = lax.fori_loop(
        0, reach * tiles, first, jnp.full((length, 1), 2 * MASKED, f32)
    )

    def second(kt, sums):
        terms = jnp.exp(scores[kt] - peak)
        probs[:, pl.ds(pl.multiple_of(kt * TILE, TILE), TILE)] = terms.astype(bf16)
        return sums + jnp.sum(terms, axis=1, keepdims=True)

    sums = lax.fori_loop(0, reach * tiles, second, jnp.zeros((length, 1), f32))
    lse_ref[0] = peak + jnp.log(sums)
    inverse = 1.0 / sums

    for count in range(1, total + 1):

        @pl.when(reach == count)
        def _(count=count):
            width = count * length
            span = pl.ds(pl.multiple_of(base, length), width)

            def column(ct, _):
                at = pl.ds(pl.multiple_of(ct * TILE, TILE), TILE)
                rows = (
                    jnp.dot(probs[:, :width], values[span, at], preferred_element_type=f32)
                    * inverse
                )
                out_ref[0, :, at] = rows.astype(bf16)
                gate = reset_ref[0, :, at].astype(f32)
                gated_ref[0, :, at] = (gate * jax.nn.sigmoid(gate) * rows).astype(bf16)
                return 0

            lax.fori_loop(0, value_width // TILE, column, 0)


def attend(table, q, bias, reset, k_own, k_oth, v_own, v_oth):
    slots, length, key_width = q.shape
    value_width = v_own.shape[2]
    total = slots + k_oth.shape[0]
    anywhere = pl.BlockSpec(memory_space=pl.ANY)
    tokens = pl.BlockSpec((1, length, value_width), lambda k, t: (k, 0, 0))
    return pl.pallas_call(
        functools.partial(attend_body, total=total),
        grid_spec=pltpu.PrefetchScalarGridSpec(
            num_scalar_prefetch=1,
            grid=(slots,),
            in_specs=[
                pl.BlockSpec((1, length, key_width), lambda k, t: (k, 0, 0)),
                pl.BlockSpec(bias.shape, lambda k, t: (0, 0, 0)),
                tokens,
                anywhere,
                anywhere,
                anywhere,
                anywhere,
            ],
            out_specs=[
                tokens,
                tokens,
                pl.BlockSpec((1, length, 1), lambda k, t: (k, 0, 0)),
            ],
            scratch_shapes=[
                pltpu.VMEM((total * length, key_width), bf16),
                pltpu.VMEM((total * length, value_width), bf16),
                pltpu.VMEM((total * length // TILE, length, TILE), f32),
                pltpu.VMEM((length, total * length), bf16),
                pltpu.SemaphoreType.DMA((2 * total,)),
            ],
        ),
        out_shape=[
            jax.ShapeDtypeStruct((slots, length, value_width), bf16),
            jax.ShapeDtypeStruct((slots, length, value_width), bf16),
            jax.ShapeDtypeStruct((slots, length, 1), f32),
        ],
        compiler_params=params(("arbitrary",)),
        name="attend",
        cost_estimate=BRIEF,
    )(table, q, bias, reset, k_own, k_oth, v_own, v_oth)


def attend_back_body(
    table_ref,
    q_ref,
    grad_ref,
    lse_ref,
    bias_ref,
    k_own,
    k_oth,
    v_own,
    v_oth,
    gq_ref,
    gk_own,
    gv_own,
    both_oth,
    rel_out,
    keys,
    values,
    gk_sum,
    gv_sum,
    probs_kept,
    grads_kept,
    rel_ref,
    sem,
    *,
    total,
):
    length, key_width = q_ref.shape[1:]
    value_width = values.shape[1]
    tiles = length // TILE
    scale = float(key_width) ** (-0.5)
    step = pl.program_id(0)
    nt = (((1,), (1,)), ((), ()))
    tn = (((0,), (0,)), ((), ()))

    @pl.when(step == 0)
    def _():
        gk_sum[...] = jnp.zeros_like(gk_sum)
        gv_sum[...] = jnp.zeros_like(gv_sum)
        rel_ref[...] = jnp.zeros_like(rel_ref)
        load_chunks(
            table_ref, ((k_own, k_oth, keys), (v_own, v_oth, values)), total, length, sem
        )

    chunk = table_ref[step]
    reach = jnp.where(table_ref[2 * total] == 1, chunk + 1, 1)
    base = (chunk + 1 - reach) * length
    queries = q_ref[0]
    log_total = lse_ref[0]

    def gap_of(kc, a, r):
        return (reach - 1 - kc) * tiles + r - a + tiles - 1

    def first(kc, delta):
        spot = pl.ds(pl.multiple_of(base + kc * length, length), length)
        grads_kept[kc] = lax.dot_general(
            values[spot, :], grad_ref[0], nt, preferred_element_type=f32
        )
        tile = (
            lax.dot_general(keys[spot, :], queries, nt, preferred_element_type=f32) * scale
        )
        for a in range(tiles):
            for r in range(tiles):
                rows = slice(a * TILE, (a + 1) * TILE)
                cols = slice(r * TILE, (r + 1) * TILE)
                probs_kept[kc, rows, cols] = jnp.exp(
                    tile[rows, cols] + bias_ref[gap_of(kc, a, r)] - log_total[:, cols]
                )
        return delta + jnp.sum(probs_kept[kc] * grads_kept[kc], axis=0, keepdims=True)

    delta = lax.fori_loop(0, reach, first, jnp.zeros((1, length), f32))

    def second(kc, grad_query):
        spot = pl.ds(pl.multiple_of(base + kc * length, length), length)
        probs = probs_kept[kc]
        grad_scores = (probs * (grads_kept[kc] - delta)).astype(bf16)
        probs = probs.astype(bf16)
        for a in range(tiles):
            for r in range(tiles):
                rel_ref[gap_of(kc, a, r)] += grad_scores[
                    a * TILE : (a + 1) * TILE, r * TILE : (r + 1) * TILE
                ].astype(f32)
        gk_sum[spot, :] += jnp.dot(grad_scores, queries, preferred_element_type=f32)

        def column(ct, _):
            at = pl.ds(pl.multiple_of(ct * 512, 512), 512)
            gv_sum[spot, at] += jnp.dot(
                probs, grad_ref[0, :, at], preferred_element_type=f32
            )
            return 0

        lax.fori_loop(0, value_width // 512, column, 0)
        return grad_query + lax.dot_general(
            grad_scores, keys[spot, :], tn, preferred_element_type=f32
        )

    grad_query = lax.fori_loop(0, reach, second, jnp.zeros((length, key_width), f32))
    gq_ref[0] = grad_query * scale

    @pl.when(step == pl.num_programs(0) - 1)
    def _():
        for slot in range(total):
            place = pl.ds(pl.multiple_of(table_ref[slot] * length, length), length)
            key_grad = (gk_sum[place, :] * scale).astype(bf16)
            value_grad = gv_sum[place, :].astype(bf16)
            if slot < 2:
                gk_own[slot] = key_grad
                gv_own[slot] = value_grad
            else:
                both_oth[slot - 2, :, :value_width] = value_grad
                both_oth[slot - 2, :, value_width:] = key_grad
        down = lax.broadcasted_iota(jnp.int32, (TILE, TILE), 0)
        across = lax.broadcasted_iota(jnp.int32, (TILE, TILE), 1)
        mirror = jnp.where(down + across == TILE - 1, 1.0, 0.0)
        for d in range(rel_out.shape[0]):
            flipped = jnp.dot(
                rel_ref[d + tiles - 1],
                mirror,
                precision=lax.Precision.HIGHEST,
                preferred_element_type=f32,
            )
            wide = jnp.concatenate([flipped, jnp.zeros((TILE, TILE), f32)], axis=1)
            turned = pltpu.roll(wide, 0, 1, stride=1, stride_axis=0)
            rel_out[d] = jnp.sum(turned, axis=0, keepdims=True)


def attend_back(table, q, grads, lse, bias, k_own, k_oth, v_own, v_oth, after=()):
    slots, length, key_width = q.shape
    value_width = v_own.shape[2]
    total = slots + k_oth.shape[0]
    rel_shape = (total * length // TILE, 1, 2 * TILE)
    both_shape = (k_oth.shape[0], length, key_width + value_width)
    anywhere = pl.BlockSpec(memory_space=pl.ANY)

    def all_of(shape):
        return pl.BlockSpec(
            shape, lambda k, t: (0,) * len(shape), pipeline_mode=pl.Buffered(1)
        )

    return pl.pallas_call(
        ignoring(functools.partial(attend_back_body, total=total), 9, len(after)),
        grid_spec=pltpu.PrefetchScalarGridSpec(
            num_scalar_prefetch=1,
            grid=(slots,),
            in_specs=[
                pl.BlockSpec((1, length, key_width), lambda k, t: (k, 0, 0)),
                pl.BlockSpec((1, length, value_width), lambda k, t: (k, 0, 0)),
                pl.BlockSpec((1, 1, length), lambda k, t: (k, 0, 0)),
                all_of(bias.shape),
                anywhere,
                anywhere,
                anywhere,
                anywhere,
            ]
            + [anywhere] * len(after),
            out_specs=[
                pl.BlockSpec((1, length, key_width), lambda k, t: (k, 0, 0)),
                all_of(k_own.shape),
                all_of(v_own.shape),
                all_of(both_shape),
                all_of(rel_shape),
            ],
            scratch_shapes=[
                pltpu.VMEM((total * length, key_width), bf16),
                pltpu.VMEM((total * length, value_width), bf16),
                pltpu.VMEM((total * length, key_width), f32),
                pltpu.VMEM((total * length, value_width), f32),
                pltpu.VMEM((total, length, length), f32),
                pltpu.VMEM((total, length, length), f32),
                pltpu.VMEM(bias.shape, f32),
                pltpu.SemaphoreType.DMA((2 * total,)),
            ],
        ),
        out_shape=[
            jax.ShapeDtypeStruct((slots, length, key_width), f32),
            jax.ShapeDtypeStruct(k_own.shape, bf16),
            jax.ShapeDtypeStruct(v_own.shape, bf16),
            jax.ShapeDtypeStruct(both_shape, bf16),
            jax.ShapeDtypeStruct(rel_shape, f32),
        ],
        compiler_params=params(("arbitrary",)),
        name="attend_back",
        cost_estimate=LONG,
    )(table, q, grads, lse, bias, k_own, k_oth, v_own, v_oth, *after)


def bias_body(flag_ref, back_row, front_row, back_ref, front_ref, *, spare):
    tile = pl.program_id(0) - spare
    full = flag_ref[0] == 1

    @pl.when(tile < 0)
    def _():
        back_ref[...] = jnp.full_like(back_ref, MASKED)
        front_ref[...] = jnp.full_like(front_ref, MASKED)

    @pl.when(tile >= 0)
    def _():
        down = lax.broadcasted_iota(jnp.int32, (TILE, TILE), 0)
        across = lax.broadcasted_iota(jnp.int32, (TILE, TILE), 1)
        near = jnp.where(down // STRETCH == across // STRETCH, 1, 0)
        for row, out, ordered in (
            (back_row, back_ref, jnp.where(down <= across, 1, 0)),
            (front_row, front_ref, jnp.where(across <= down, 1, 0)),
        ):
            wide = jnp.broadcast_to(row[0], (TILE, 2 * TILE))
            turned = pltpu.roll(wide, 0, 1, stride=1, stride_axis=0)[:, :TILE]
            allowed = jnp.where(
                tile == 0, jnp.where(full, ordered, ordered * near), jnp.where(full, 1, 0)
            )
            out[0] = jnp.where(allowed == 1, turned, MASKED)


def bias_tiles(relative_bias, spare, full):
    length = relative_bias.shape[0] // 2
    count = length // TILE
    windows = jnp.stack(
        [
            lax.slice_in_dim(relative_bias, length - d * TILE - TILE, length - d * TILE + TILE)
            for d in range(count)
        ]
    )
    front = jnp.concatenate([windows[:, TILE:], windows[:, :TILE]], axis=1)
    back = jnp.concatenate([windows[:, TILE:TILE + 1], windows[:, ::-1][:, TILE:], windows[:, ::-1][:, : TILE - 1]], axis=1)
    row = pl.BlockSpec((1, 1, 2 * TILE), lambda d, t: (jnp.maximum(d - spare, 0), 0, 0))
    out = pl.BlockSpec((1, TILE, TILE), lambda d, t: (d, 0, 0))
    shape = jax.ShapeDtypeStruct((spare + count, TILE, TILE), f32)
    return pl.pallas_call(
        functools.partial(bias_body, spare=spare),
        grid_spec=pltpu.PrefetchScalarGridSpec(
            num_scalar_prefetch=1,
            grid=(spare + count,),
            in_specs=[row, row],
            out_specs=[out, out],
        ),
        out_shape=[shape, shape],
        compiler_params=params(("arbitrary",)),
        name="bias",
    )(full.astype(jnp.int32)[None], back[:, None], front[:, None])


def bias_grad(sums, length):
    count = sums.shape[0]
    shifted = jnp.concatenate([jnp.zeros((count, 1), f32), sums[:, :-1]], axis=1)
    none = jnp.zeros((1, TILE), f32)
    blocks = jnp.concatenate([none, shifted[:, :TILE]]) + jnp.concatenate(
        [shifted[:, TILE:], none]
    )
    return jnp.concatenate(
        [blocks[::-1].reshape(-1), jnp.zeros((2 * length - (count + 1) * TILE,), f32)]
    )


def gate_body(
    back_ref,
    cot_a,
    cot_b,
    x_ref,
    cand_ref,
    update_ref,
    reset_ref,
    attended_ref,
    gain_ref,
    proj_ref,
    input_ref,
    main_ref,
    grad_att_ref,
    gain_grad_ref,
):
    width = x_ref.shape[1]
    value_width = proj_ref.shape[0]

    @pl.when(pl.program_id(0) == 0)
    def _():
        gain_grad_ref[...] = jnp.zeros_like(gain_grad_ref)

    x = x_ref[...].astype(f32)
    cand_in = cand_ref[...]
    gate = jax.nn.sigmoid(cand_in)
    candidate = cand_in * gate
    update = jax.nn.sigmoid(update_ref[...].astype(f32))
    change = candidate - x
    unit, inv = unit_rows_of(x + update * change)
    grad_feed = back_ref[...]
    gain_grad_ref[...] += jnp.sum(grad_feed * unit, axis=0, keepdims=True)
    early = pl.program_id(0) < pl.num_programs(0) // 2
    cot = jnp.where(early, cot_a[...].astype(f32), cot_b[...].astype(f32))
    grad_first = cot + norm_back_rows(
        grad_feed, gain_ref[...], unit, inv
    )
    kept = grad_first * (1.0 - update)
    input_ref[...] = kept
    main_ref[:, value_width : value_width + width] = (kept * change * update).astype(bf16)
    grad_cand = (grad_first * update * (gate + candidate * (1.0 - gate))).astype(bf16)
    main_ref[:, value_width + width :] = grad_cand
    for c in range(value_width // 512):
        at = slice(c * 512, (c + 1) * 512)
        grad_gated = mm_nt(grad_cand, proj_ref[at, :])
        reset = reset_ref[:, at].astype(f32)
        open_gate = jax.nn.sigmoid(reset)
        passed = reset * open_gate
        grad_att_ref[:, at] = (grad_gated * passed).astype(bf16)
        main_ref[:, at] = (
            grad_gated
            * attended_ref[:, at].astype(f32)
            * (open_gate + passed * (1.0 - open_gate))
        ).astype(bf16)


def gate(back, cots, x, cand_in, base, attended, gain, proj, after=()):
    tokens, width = x.shape
    value_width = proj.shape[0]
    rows = min(256, tokens // 2)
    half = tokens // rows // 2
    wide = value_width // width

    def block(columns, at=0):
        return pl.BlockSpec((rows, columns), lambda i: (i, at))

    return pl.pallas_call(
        ignoring(gate_body, 10, len(after)),
        grid=(tokens // rows,),
        in_specs=[
            block(width),
            pl.BlockSpec((rows, width), lambda i: (jnp.minimum(i, half - 1), 0)),
            pl.BlockSpec((rows, width), lambda i: (jnp.maximum(i - half, 0), 0)),
            block(width),
            block(width),
            block(width, wide),
            block(value_width),
            block(value_width),
            pl.BlockSpec((1, width), lambda i: (0, 0)),
            pl.BlockSpec(proj.shape, lambda i: (0, 0), pipeline_mode=pl.Buffered(1)),
        ]
        + [pl.BlockSpec(memory_space=pl.ANY)] * len(after),
        out_specs=[
            block(width),
            block(value_width + 2 * width),
            block(value_width),
            pl.BlockSpec((1, width), lambda i: (0, 0)),
        ],
        out_shape=[
            jax.ShapeDtypeStruct((tokens, width), f32),
            jax.ShapeDtypeStruct((tokens, value_width + 2 * width), bf16),
            jax.ShapeDtypeStruct((tokens, value_width), bf16),
            jax.ShapeDtypeStruct((1, width), f32),
        ],
        compiler_params=params(("arbitrary",)),
        name="gate",
        cost_estimate=LONG,
    )(back, *cots, x, cand_in, base, base, attended, gain, proj, *after)


def ordered_transpose(ids_ref, source, plain, ordered):
    plain[...] = source[...].T
    count = ids_ref.shape[0]
    rows = plain.shape[0] // count

    def place(p, _):
        ordered[pl.ds(pl.multiple_of(p * rows, rows), rows), :] = plain[
            pl.ds(pl.multiple_of(ids_ref[p] * rows, rows), rows), :
        ]
        return 0

    lax.fori_loop(0, count, place, 0)


def placed_transpose(places_ref, sources, plain, ordered):
    start = 0
    for source in sources:
        plain[:, start : start + source.shape[0]] = source[...].T
        start += source.shape[0]
    count = places_ref.shape[0]
    rows = plain.shape[0] // count

    def place(q, _):
        ordered[pl.ds(pl.multiple_of(places_ref[q] * rows, rows), rows), :] = plain[
            pl.ds(pl.multiple_of(q * rows, rows), rows), :
        ]
        return 0

    lax.fori_loop(0, count, place, 0)


def feed_body(
    ids_ref,
    places_ref,
    low_ref,
    cot_a,
    cot_b,
    first_ref,
    in_ref,
    out_ref,
    result_a,
    result_b,
    back_ref,
    out_send,
    out_keep,
    in_send,
    in_keep,
    total,
    cot_turned,
    low_turned,
    plain,
):
    step = pl.program_id(0)
    half = pl.num_programs(0) // 2
    tokens = low_ref.shape[0]
    middle = tokens // 2
    nt = (((1,), (1,)), ((), ()))

    @pl.when(step == 0)
    def _():
        placed_transpose(places_ref, (cot_a, cot_b), plain, cot_turned)
        ordered_transpose(ids_ref, low_ref, plain, low_turned)
        total[...] = first_ref[...]
        back_ref[...] = jnp.zeros_like(back_ref)

    acts, grads = [], []
    for r, cot_ref in enumerate((cot_a, cot_b)):
        at = slice(r * middle, (r + 1) * middle)
        hidden = jnp.dot(low_ref[at, :], in_ref[...], preferred_element_type=f32)
        grad_act = lax.dot_general(
            cot_ref[...], out_ref[...], nt, preferred_element_type=f32
        )
        gate = jax.nn.sigmoid(hidden)
        act = hidden * gate
        grad = (grad_act * (gate + act * (1.0 - gate))).astype(bf16)
        act = act.astype(bf16)
        total[at, :] += jnp.dot(act, out_ref[...], preferred_element_type=f32)
        back_ref[at, :] += lax.dot_general(
            grad, in_ref[...], nt, preferred_element_type=f32
        )
        acts.append(act)
        grads.append(grad)
    out_grad = jnp.dot(
        cot_turned[...], jnp.concatenate(acts), preferred_element_type=f32
    ).astype(bf16)
    in_grad = jnp.dot(
        low_turned[...], jnp.concatenate(grads), preferred_element_type=f32
    ).astype(bf16)
    split = in_grad.shape[0] // 2
    in_send[...] = in_grad[:split].reshape(in_send.shape)
    in_keep[...] = in_grad[split:].reshape(in_keep.shape)

    @pl.when(step < half)
    def _():
        out_send[0] = out_grad

    @pl.when(step >= half)
    def _():
        out_keep[0] = out_grad

    @pl.when(step == pl.num_programs(0) - 1)
    def _():
        result_a[...] = total[:middle, :].astype(bf16)
        result_b[...] = total[middle:, :].astype(bf16)


def feed(ids, places, low, cots, first_sum, feed_in, feed_out, seq, after=()):
    tokens, width = low.shape
    features = feed_in.shape[1]
    parts = ids.shape[0]
    half = parts // 2
    columns = features // parts
    rows = width // parts
    share = parts // seq
    anywhere = pl.BlockSpec(memory_space=pl.ANY)

    def all_of(shape):
        return pl.BlockSpec(
            shape, lambda i, t, u: (0,) * len(shape), pipeline_mode=pl.Buffered(1)
        )

    def at(i, t):
        return t[jnp.minimum(i, parts - 1)]

    split = pl.BlockSpec(
        (half, 1, 1, rows, columns),
        lambda i, t, u: (0, u[at(i, t) // share], at(i, t) % share, 0, 0),
    )
    return pl.pallas_call(
        ignoring(feed_body, 8, len(after)),
        grid_spec=pltpu.PrefetchScalarGridSpec(
            num_scalar_prefetch=2,
            grid=(parts,),
            in_specs=[
                all_of(low.shape),
                all_of(cots[0].shape),
                all_of(cots[1].shape),
                all_of(first_sum.shape),
                pl.BlockSpec((width, columns), lambda i, t, u: (0, at(i, t))),
                pl.BlockSpec((columns, width), lambda i, t, u: (at(i, t), 0)),
            ]
            + [anywhere] * len(after),
            out_specs=[
                all_of(cots[0].shape),
                all_of(cots[1].shape),
                all_of(low.shape),
                pl.BlockSpec(
                    (1, width, columns), lambda i, t, u: (jnp.minimum(i, half - 1), 0, 0)
                ),
                pl.BlockSpec(
                    (1, width, columns), lambda i, t, u: (jnp.maximum(i - half, 0), 0, 0)
                ),
                split,
                split,
            ],
            scratch_shapes=[
                pltpu.VMEM((tokens, width), f32),
                pltpu.VMEM((width, tokens), bf16),
                pltpu.VMEM((width, tokens), bf16),
                pltpu.VMEM((width, tokens), bf16),
            ],
        ),
        out_shape=[
            jax.ShapeDtypeStruct(cots[0].shape, bf16),
            jax.ShapeDtypeStruct(cots[1].shape, bf16),
            jax.ShapeDtypeStruct((tokens, width), f32),
            jax.ShapeDtypeStruct((half, width, columns), bf16),
            jax.ShapeDtypeStruct((half, width, columns), bf16),
            jax.ShapeDtypeStruct((half, seq, share, rows, columns), bf16),
            jax.ShapeDtypeStruct((half, seq, share, rows, columns), bf16),
        ],
        compiler_params=params(("arbitrary",)),
        name="feed",
        cost_estimate=BRIEF,
    )(ids, places, low, *cots, first_sum, feed_in, feed_out, *after)


def by_columns_body(ids_ref, places_ref, left_ref, right_ref, send, keep, plain, turned):
    step = pl.program_id(0)
    half = pl.num_programs(0) // 2

    @pl.when(step == 0)
    def _():
        placed_transpose(places_ref, (left_ref,), plain, turned)

    grad = jnp.dot(turned[...], right_ref[...], preferred_element_type=f32).astype(bf16)

    @pl.when(step < half)
    def _():
        send[0] = grad

    @pl.when(step >= half)
    def _():
        keep[0] = grad


def by_columns(ids, places, left, right, after=(), rows=None, at=0):
    tokens = left.shape[0]
    rows = rows or left.shape[1]
    parts = ids.shape[0]
    half = parts // 2
    columns = right.shape[1] // parts
    shape = jax.ShapeDtypeStruct((half, rows, columns), bf16)
    if columns % 128:
        left = left[:, at * rows : (at + 1) * rows]
        grad = mm_tn(left, right).astype(bf16).reshape(rows, parts, columns)
        grad = jnp.take(grad, ids, axis=1).transpose(1, 0, 2)
        grad = grad.reshape(parts, places.shape[0], -1, columns)
        grad = jnp.take(grad, jnp.argsort(places), axis=1).reshape(parts, rows, columns)
        return grad[:half], grad[half:]
    return pl.pallas_call(
        ignoring(by_columns_body, 4, len(after)),
        grid_spec=pltpu.PrefetchScalarGridSpec(
            num_scalar_prefetch=2,
            grid=(parts,),
            in_specs=[
                pl.BlockSpec(
                    (tokens, rows), lambda i, t, u: (0, at), pipeline_mode=pl.Buffered(1)
                ),
                pl.BlockSpec((tokens, columns), lambda i, t, u: (0, t[jnp.minimum(i, parts - 1)])),
            ]
            + [pl.BlockSpec(memory_space=pl.ANY)] * len(after),
            out_specs=[
                pl.BlockSpec(
                    (1, rows, columns), lambda i, t, u: (jnp.minimum(i, half - 1), 0, 0)
                ),
                pl.BlockSpec(
                    (1, rows, columns), lambda i, t, u: (jnp.maximum(i - half, 0), 0, 0)
                ),
            ],
            scratch_shapes=[
                pltpu.VMEM((rows, tokens), bf16),
                pltpu.VMEM((rows, tokens), bf16),
            ],
        ),
        out_shape=[shape, shape],
        compiler_params=params(("arbitrary",)),
        name="by_columns",
        cost_estimate=BRIEF,
    )(ids, places, left, right, *after)


def by_rows_body(ids_ref, places_ref, left_ref, right_ref, send, keep, plain, turned):
    @pl.when(pl.program_id(0) == 0)
    def _():
        ordered_transpose(ids_ref, left_ref, plain, turned)

    grad = jnp.dot(turned[...], right_ref[...], preferred_element_type=f32).astype(bf16)
    middle = grad.shape[0] // 2
    send[...] = grad[:middle].reshape(send.shape)
    keep[...] = grad[middle:].reshape(keep.shape)


def by_rows(ids, places, left, right, seq=1, after=(), cost=BRIEF):
    tokens, rows = left.shape
    parts = ids.shape[0]
    half = parts // 2
    if places is None:
        seq, places = 1, jnp.zeros((1,), jnp.int32)
    columns = right.shape[1] // seq
    tile = min(512, columns)
    share = columns // tile
    shape = jax.ShapeDtypeStruct((half, seq, rows // parts, columns), bf16)
    split = pl.BlockSpec(
        (half, 1, rows // parts, tile), lambda i, t, u: (0, u[jnp.minimum(i // share, seq - 1)], 0, i % share)
    )
    return pl.pallas_call(
        ignoring(by_rows_body, 4, len(after)),
        grid_spec=pltpu.PrefetchScalarGridSpec(
            num_scalar_prefetch=2,
            grid=(seq * share,),
            in_specs=[
                pl.BlockSpec(
                    left.shape, lambda i, t, u: (0, 0), pipeline_mode=pl.Buffered(1)
                ),
                pl.BlockSpec((tokens, tile), lambda i, t, u: (0, i)),
            ]
            + [pl.BlockSpec(memory_space=pl.ANY)] * len(after),
            out_specs=[split, split],
            scratch_shapes=[
                pltpu.VMEM((rows, tokens), bf16),
                pltpu.VMEM((rows, tokens), bf16),
            ],
        ),
        out_shape=[shape, shape],
        compiler_params=params(("arbitrary",)),
        name="by_rows",
        cost_estimate=cost,
    )(ids, places, left, right, *after)


def value_back_body(
    ids_ref,
    places_ref,
    left_ref,
    own_ref,
    other_ref,
    slope_ref,
    proj_ref,
    total_ref,
    send,
    keep,
    plain,
    turned,
):
    @pl.when(pl.program_id(0) == 0)
    def _():
        total_ref[...] = jnp.zeros_like(total_ref)
        ordered_transpose(ids_ref, left_ref, plain, turned)

    grad = own_ref[...].astype(f32)
    for k in range(other_ref.shape[0]):
        grad = grad + other_ref[k].astype(f32)
    grad = (grad * slope_ref[...].astype(f32)).astype(bf16)
    total_ref[...] += mm_nt(grad, proj_ref[...])
    weights = jnp.dot(turned[...], grad, preferred_element_type=f32).astype(bf16)
    middle = weights.shape[0] // 2
    send[...] = weights[:middle].reshape(send.shape)
    keep[...] = weights[middle:].reshape(keep.shape)


def value_back(ids, places, left, own, others, slope, proj, seq, after=()):
    tokens, rows = left.shape
    parts = ids.shape[0]
    half = parts // 2
    columns = proj.shape[1] // seq
    tile = min(512, columns)
    share = columns // tile
    shape = jax.ShapeDtypeStruct((half, seq, rows // parts, columns), bf16)
    split = pl.BlockSpec(
        (half, 1, rows // parts, tile),
        lambda i, t, u: (0, u[jnp.minimum(i // share, seq - 1)], 0, i % share),
    )
    stripe = pl.BlockSpec((tokens, tile), lambda i, t, u: (0, i))
    fixed = pl.BlockSpec(
        (tokens, rows), lambda i, t, u: (0, 0), pipeline_mode=pl.Buffered(1)
    )
    return pl.pallas_call(
        ignoring(value_back_body, 7, len(after)),
        grid_spec=pltpu.PrefetchScalarGridSpec(
            num_scalar_prefetch=2,
            grid=(seq * share,),
            in_specs=[
                fixed,
                stripe,
                pl.BlockSpec((others.shape[0], tokens, tile), lambda i, t, u: (0, 0, i)),
                stripe,
                pl.BlockSpec((rows, tile), lambda i, t, u: (0, i)),
            ]
            + [pl.BlockSpec(memory_space=pl.ANY)] * len(after),
            out_specs=[fixed, split, split],
            scratch_shapes=[
                pltpu.VMEM((rows, tokens), bf16),
                pltpu.VMEM((rows, tokens), bf16),
            ],
        ),
        out_shape=[jax.ShapeDtypeStruct((tokens, rows), f32), shape, shape],
        compiler_params=params(("arbitrary",)),
        name="value_back",
        cost_estimate=LONG,
    )(ids, places, left, own, others, slope, proj, *after)


def stage_body(*refs, shapes):
    count = sum(pairs for pairs, _ in shapes)
    ins, outs = list(refs[: 2 * count]), list(refs[2 * count :])
    for pairs, halves in shapes:
        into = [outs.pop(0) for _ in range(halves)]
        start = 0
        for _ in range(pairs):
            kept, arrived = ins.pop(0), ins.pop(0)
            stop = start + kept.shape[0]
            for part, out in enumerate(into):
                out[start:stop] = (
                    kept[:, part].astype(f32) + arrived[:, part].astype(f32)
                ).astype(out.dtype)
            start = stop


def stage_sums(groups, after=(), steps=4, cost=BRIEF):
    shapes, ins, in_specs, out_specs, out_shapes, whole = [], [], [], [], [], []
    for pairs, single, _ in groups:
        _, n, rows, _ = pairs[0][0].shape
        while (n * rows // (1 if single else 2)) % (16 * steps):
            steps //= 2
    for pairs, single, kind in groups:
        halves = 1 if single else 2
        g, n, rows, columns = pairs[0][0].shape
        each = n * rows // halves // steps
        shapes.append((len(pairs), halves))
        for pair in pairs:
            for v in pair:
                ins.append(v.reshape(g, halves, n * rows // halves, columns))
                in_specs.append(
                    pl.BlockSpec((g, halves, each, columns), lambda i: (0, 0, i, 0))
                )
        for _ in range(halves):
            out_specs.append(pl.BlockSpec((len(pairs) * g, each, columns), lambda i: (0, i, 0)))
            out_shapes.append(
                jax.ShapeDtypeStruct((len(pairs) * g, n * rows // halves, columns), kind)
            )
        whole.append((halves, (len(pairs) * g, n // halves, rows, columns)))
    sums = list(
        pl.pallas_call(
            ignoring(functools.partial(stage_body, shapes=shapes), len(ins), len(after)),
            grid=(steps,),
            in_specs=in_specs + [pl.BlockSpec(memory_space=pl.ANY)] * len(after),
            out_specs=out_specs,
            out_shape=out_shapes,
            compiler_params=params(("arbitrary",)),
            name="stage_sums",
            cost_estimate=cost,
        )(*ins, *after)
    )
    return [tuple(sums.pop(0).reshape(shape) for _ in range(halves)) for halves, shape in whole]


class Layout:
    def __init__(self, mesh):
        self.dp = mesh.shape["dp"]
        self.seq = mesh.shape["seq"]
        self.members = self.seq // 2
        self.chips = self.seq // 4

    def pairs(self, move):
        return [
            (d * self.seq + z, e * self.seq + w)
            for d in range(self.dp)
            for z in range(self.seq)
            for e, w in [move(d, z)]
        ]

    def send(self, value, move):
        return lax.ppermute(value, AXES, self.pairs(move))

    def place(self, sequence, member):
        return member % 2 ^ (1 - sequence % 2), sequence * self.chips + member // 2

    def member(self, core, z):
        sequence = z // self.chips
        return (z % self.chips) * 2 + (core ^ (1 - sequence % 2))

    def home_to_work(self, round_index):
        def move(d, z):
            part = (1 if z >= self.seq // 2 else 0) ^ round_index
            core, at = self.place(2 * (d % 2) + part, min(z, self.seq - 1 - z))
            return d - d % 2 + core, at

        return move

    def spread(self, value):
        late = lax.axis_index("seq") >= self.seq // 2
        out = []
        for round_index in range(2):
            sent = lax.dynamic_index_in_dim(
                value, jnp.where(late, 1 - round_index, round_index), 0, False
            )
            out.append(self.send(sent, self.home_to_work(round_index)))
        return out

    def homeward(self, value, round_index):
        pairs = [(b, a) for a, b in self.pairs(self.home_to_work(round_index))]
        return lax.ppermute(value, AXES, pairs)

    def gathered(self, back):
        late = lax.axis_index("seq") >= self.seq // 2
        return jnp.stack([jnp.where(late, back[1], back[0]), jnp.where(late, back[0], back[1])])

    def collect(self, values):
        return self.gathered([self.homeward(v, r) for r, v in enumerate(values)])

    def rotate(self, value, by):
        def move(d, z):
            member = (self.member(d % 2, z) + by) % self.members
            core, at = self.place(z // self.chips, member)
            return d - d % 2 + core, at

        return self.send(value, move)

    def gather(self, value):
        return jnp.concatenate([self.rotate(value, by) for by in range(1, self.members)], axis=0)

    def returns(self, others):
        slots = others.shape[0] // (self.members - 1)
        return jnp.stack(
            [
                self.rotate(others[(by - 1) * slots : by * slots], self.members - by).reshape(
                    -1, others.shape[-1]
                )
                for by in range(1, self.members)
            ]
        )

    def orders(self):
        dp, z = lax.axis_index("dp"), lax.axis_index("seq")
        bits = self.dp.bit_length() - 1
        ids = []
        for core in range(2):
            orders = [[0, *range(1, bits)], [0, *reversed(range(1, bits))]]
            flips = []
            for p in range(self.dp):
                order = orders[core if p >= self.dp // 2 else 1 - core]
                flips.append(
                    sum(
                        (0 if p >> (bits - 1 - i) & 1 else 1) << bit
                        for i, bit in enumerate(order)
                    )
                )
            ids.append(dp ^ jnp.array(flips, jnp.int32))
        ids = jnp.where(dp % 2 == 0, ids[0], ids[1])
        bits = self.seq.bit_length() - 1
        flips = [
            sum((0 if p >> (bits - 1 - i) & 1 else 1) << i for i in range(bits))
            for p in range(self.seq)
        ]
        blocks = z ^ jnp.array(flips, jnp.int32)
        return ids, jnp.argsort(blocks).astype(jnp.int32), blocks

    def partner(self, stage):
        bits = self.dp.bit_length() - 1
        if stage == 0:
            return lambda d, z: (d ^ 1, z)
        if stage < bits:
            return lambda d, z: (d ^ (1 << stage if d % 2 == 0 else 1 << (bits - stage)), z)
        return lambda d, z: (d, z ^ (1 << (stage - bits)))

    def turn(self, sums, after, cost=BRIEF):
        sums = [s for s in sums if s.arrived]
        if not sums:
            return after
        dp_stages = self.dp.bit_length() - 1
        last = dp_stages + self.seq.bit_length() - 1
        groups = []
        for s in sums:
            pairs = list(zip(s.kept, s.arrived))
            single = s.stage + 1 == last
            if s.stage + 1 == dp_stages:
                single = not s.over_seq
                if s.over_seq:
                    pairs = [
                        tuple(
                            v.reshape(v.shape[0], self.seq, -1, v.shape[-1]) for v in pair
                        )
                        for pair in pairs
                    ]
            groups.append((pairs, single, f32 if s.stage + 1 == last else bf16))
        out = stage_sums(groups, after, cost=cost)
        for s, held, (_, single, _) in zip(sums, out, groups):
            s.stage += 1
            s.arrived = ()
            if single:
                s.total = held[0]
            else:
                s.send([held[0]], [held[1]])
        return [part for held in out for part in held]

    def sum_seq(self, held):
        low = 1
        while low < self.seq:
            others = [low] if 2 * low >= self.seq else [low, 2 * low, 3 * low]
            mine = held
            for other in others:
                held = held + self.send(mine, lambda d, z: (d, z ^ other))
            low *= 4
        return held

    def reduce_all(self, sent, held):
        core = lax.axis_index("dp") % 2
        held = held + self.send(sent, lambda d, z: (d ^ 1, z))
        held = self.sum_seq(held)
        low = 2
        while low < self.dp:
            others = [low] if 2 * low >= self.dp else [low, 2 * low, 3 * low]
            mine = held
            for other in others:
                held = held + self.send(mine, lambda d, z: (d ^ other, z))
            low *= 4
        other = self.send(held, lambda d, z: (d ^ 1, z))
        return jnp.where(core == 0, jnp.stack([held, other]), jnp.stack([other, held]))


def pack_body(core_ref, qx_a, qx_b, qs_a, qs_b, rest_ref, sent, held):
    rows = jnp.concatenate(
        [qx_a[...] + qx_b[...], qs_a[...] + qs_b[...], rest_ref[...]], axis=0
    )
    middle = rows.shape[0] // 2
    first = core_ref[0] == 0
    sent[...] = jnp.where(first, rows[middle:], rows[:middle])
    held[...] = jnp.where(first, rows[:middle], rows[middle:])


def pack(core, first, second, rest, after=()):
    ins = [v.reshape(-1, 128) for v in (first[0], second[0], first[1], second[1])] + [rest]
    rows = 2 * ins[0].shape[0] + rest.shape[0]
    shape = jax.ShapeDtypeStruct((rows // 2, 128), f32)
    inside = pl.BlockSpec(memory_space=pltpu.VMEM)
    return pl.pallas_call(
        ignoring(pack_body, 6, len(after)),
        in_specs=[pl.BlockSpec(memory_space=pltpu.SMEM)]
        + [inside] * 5
        + [pl.BlockSpec(memory_space=pl.ANY)] * len(after),
        out_specs=[inside, inside],
        out_shape=[shape, shape],
        name="pack",
        cost_estimate=BRIEF,
    )(core[None].astype(jnp.int32), *ins, *after)


class Sum:
    def __init__(self, layout, *pairs, over_seq=True):
        self.layout, self.over_seq, self.stage = layout, over_seq, 0
        self.total = None
        pairs = [[v.reshape(1, v.shape[0], -1, v.shape[-1]) for v in pair] for pair in pairs]
        self.send([p[0] for p in pairs], [p[1] for p in pairs])

    def send(self, sent, kept):
        self.kept = kept
        self.arrived = [self.layout.send(v, self.layout.partner(self.stage)) for v in sent]

    def begin_seq(self, block):
        self.total = None
        middle = self.layout.seq // 2
        self.send([block[None, :middle]], [block[None, middle:]])


def mm(a, b):
    return jnp.dot(a, b, preferred_element_type=f32)


def mm_nt(a, b):
    return lax.dot_general(a, b, (((1,), (1,)), ((), ())), preferred_element_type=f32)


def mm_tn(a, b):
    return lax.dot_general(a, b, (((0,), (0,)), ((), ())), preferred_element_type=f32)


def layer(
    layout,
    inputs,
    cotangent,
    full_attention,
    mix_gain,
    smooth_alpha,
    smooth_damp,
    smooth_beta,
    smooth_eta,
    smooth_omega,
    value_proj,
    mix_proj,
    score_affine,
    relative_bias,
    out_proj,
    feed_gain,
    feed_in,
    feed_out,
):
    slots, chunk_rows, width = inputs.shape
    key_width = score_affine.shape[1]
    value_width = value_proj.shape[1]
    tokens = slots * chunk_rows
    total = layout.seq
    seq_length = relative_bias.shape[0] // 2
    block = min(64, chunk_rows)
    core = lax.axis_index("dp") % 2
    z = lax.axis_index("seq")

    sequence = z // layout.chips
    member = layout.member(core, z)
    swap = sequence % 2
    chunks = []
    for by in range(layout.members):
        source = (member - by) % layout.members
        low, high = source, total - 1 - source
        chunks += [jnp.where(swap == 0, low, high), jnp.where(swap == 0, high, low)]
    chunks = jnp.stack(chunks).astype(jnp.int32)
    slot_of = jnp.sum(
        jnp.where(chunks[None, :] == jnp.arange(total)[:, None], jnp.arange(total)[None, :], 0),
        axis=1,
    ).astype(jnp.int32)
    flags = full_attention.astype(f32)
    flags_other = layout.send(flags, lambda d, z: (d ^ 1, z))
    flags = jnp.where(
        core == 0, jnp.concatenate([flags, flags_other]), jnp.concatenate([flags_other, flags])
    )
    full = lax.dynamic_index_in_dim(flags, sequence, 0, False) == 1.0
    table = jnp.concatenate([chunks, slot_of, full.astype(jnp.int32)[None]])
    ids, places, blocks = layout.orders()

    x = jnp.stack(layout.spread(inputs))
    cots = layout.spread(cotangent)
    bias_back, bias_front = bias_tiles(relative_bias, chunk_rows // TILE - 1, full)

    states = smooth_alpha.shape[0]
    lanes = (states, width // 128, 128)
    decay = 1.0 - smooth_alpha * smooth_damp
    rate = smooth_alpha * smooth_beta
    span = (decay**chunk_rows).reshape(lanes)
    coef = (smooth_eta * rate).reshape(lanes)
    decay_slab = decay.reshape(lanes)
    gain_row = mix_gain[None]
    omega_row = smooth_omega[None]
    mix_shared, mix_main = mix_proj[:, :key_width], mix_proj[:, key_width:]

    normed_low, ends = front_ends(
        x, gain_row, decay_slab, after=(bias_back, bias_front, mix_main, mix_shared, span, coef)
    )
    ends_all = jnp.concatenate([ends, layout.gather(ends)])
    normed_low = normed_low.reshape(tokens, width)
    value_pre = mm(normed_low, value_proj)
    value_low = jax.nn.silu(value_pre).astype(bf16).reshape(slots, chunk_rows, value_width)
    value_slope = silu_slope(value_pre).astype(bf16)
    value_others = layout.gather(value_low)
    smoothed, mixed, check = front_scan(
        table, x, gain_row, decay_slab, coef, span, omega_row, ends_all, block
    )
    smoothed = smoothed.reshape(tokens, width)
    mixed = mixed.reshape(tokens, width)

    shared_pre = mm(mixed, mix_shared)
    shared = jax.nn.silu(shared_pre)
    query_low = (shared * score_affine[0] + score_affine[1]).astype(bf16)
    key_low = (shared * score_affine[2] + score_affine[3]).astype(bf16)
    query_low = query_low.reshape(slots, chunk_rows, key_width)
    key_low = key_low.reshape(slots, chunk_rows, key_width)
    key_others = layout.gather(key_low)
    base = mm(mixed, mix_main).astype(bf16)
    attended, gated, lse = attend(
        table,
        query_low,
        bias_front,
        base.reshape(slots, chunk_rows, -1),
        key_low,
        key_others,
        value_low,
        value_others,
    )
    attended = attended.reshape(tokens, value_width)
    gated = gated.reshape(tokens, value_width)

    flat_low = x.reshape(tokens, width)
    flat = flat_low.astype(f32)
    update_pre = base[:, value_width : value_width + width].astype(f32)
    cand_in = base[:, value_width + width :].astype(f32) + mm(gated, out_proj)
    first_sum = flat + jax.nn.sigmoid(update_pre) * (jax.nn.silu(cand_in) - flat)
    unit_two, _ = unit_rows_of(first_sum)
    feed_low = (unit_two * feed_gain).astype(bf16)

    result_a, result_b, grad_feed, out_send, out_keep, in_send, in_keep = feed(
        ids, places, feed_low, cots, first_sum, feed_in, feed_out, layout.seq
    )
    home = [layout.homeward(result_a, 0), layout.homeward(result_b, 1)]
    block_out = layout.gathered(home)
    out_sum = Sum(layout, (out_send, out_keep))
    in_sum = Sum(layout, (in_send, in_keep))

    grad_input, grad_main, grad_att, feed_gain_grad = gate(
        grad_feed, cots, flat_low, cand_in, base, attended, feed_gain[None], out_proj
    )
    after = layout.turn((out_sum, in_sum), (grad_att,))
    mix_parts = by_rows(ids, None, mixed, grad_main, after=after, cost=LONG)
    proj_parts = by_columns(
        ids,
        places,
        grad_main,
        gated,
        rows=width,
        at=grad_main.shape[1] // width - 1,
        after=mix_parts,
    )
    after = layout.turn((out_sum,), (*proj_parts, *home))
    mix_sum = Sum(layout, mix_parts, over_seq=False)
    proj_sum = Sum(layout, proj_parts)
    grad_query, gk_own, gv_own, both_oth, rel_sums = attend_back(
        table,
        query_low,
        grad_att.reshape(slots, chunk_rows, value_width),
        lse.reshape(slots, 1, chunk_rows),
        bias_back,
        key_low,
        key_others,
        value_low,
        value_others,
        after=after,
    )
    both_back = layout.returns(both_oth)
    after = layout.turn((in_sum, out_sum, proj_sum), (grad_query,), cost=LONG)
    grad_normed, value_send, value_keep = value_back(
        ids,
        places,
        normed_low,
        gv_own.reshape(tokens, value_width),
        both_back,
        value_slope,
        value_proj,
        layout.seq,
        after=after,
    )
    grad_key = jnp.sum(both_back[:, :, value_width:].astype(f32), axis=0) + gk_own.reshape(
        tokens, key_width
    ).astype(f32)
    grad_query = grad_query.reshape(tokens, key_width)
    grad_shared = (
        (grad_query * score_affine[0] + grad_key * score_affine[2]) * silu_slope(shared_pre)
    ).astype(bf16)
    shared_grad = mm_tn(mixed, grad_shared).astype(bf16)
    shared_grad = lax.psum_scatter(shared_grad, "dp", scatter_dimension=0, tiled=True)
    after = layout.turn((in_sum, out_sum, proj_sum, mix_sum), (grad_normed,))
    value_sum = Sum(layout, (value_send, value_keep))
    grad_smooth = (mm_nt(grad_main, mix_main) + mm_nt(grad_shared, mix_shared)) * silu_slope(
        smoothed
    )
    grad_smooth = grad_smooth.reshape(slots, chunk_rows, width)
    back = back_ends(grad_smooth, decay_slab, after=after)
    back_all = jnp.concatenate([back, layout.gather(back)])
    after = layout.turn((out_sum, in_sum, mix_sum, value_sum), (back,))

    def scan_back(slot, after):
        return back_scan(
            table,
            slot,
            x,
            grad_smooth,
            grad_normed.reshape(slots, chunk_rows, width),
            grad_input.reshape(slots, chunk_rows, width),
            check,
            gain_row,
            decay_slab,
            coef,
            span,
            omega_row,
            back_all,
            after=after,
        )

    first = scan_back(0, after)
    after = layout.turn(
        (in_sum, mix_sum, value_sum, proj_sum, out_sum), (first[0], shared_grad)
    )
    home_first = layout.homeward(first[0], 0)
    while mix_sum.total is None:
        after = layout.turn((mix_sum,), after)
    rows = jnp.concatenate([shared_grad, mix_sum.total[0, 0]], axis=1)
    rows = rows.reshape(rows.shape[0], layout.seq, -1).transpose(1, 0, 2)
    mix_sum.begin_seq(rows[blocks])
    second = scan_back(1, (*after, *mix_sum.kept))
    home_second = layout.homeward(second[0], 1)
    after = (second[0], home_first)
    sums = (mix_sum, proj_sum, value_sum, out_sum, in_sum)
    turned = layout.turn(sums, after)
    after = (*turned, home_second)
    while any(v.total is None for v in sums):
        after = layout.turn(sums, after)
    grad_in = layout.gathered([home_first, home_second]).astype(f32)
    feed_out_grad, feed_in_grad = out_sum.total[0, 0].T, in_sum.total[0, 0]
    rows = width // layout.dp
    feed_in_grad = feed_in_grad.reshape(-1, rows, feed_in_grad.shape[-1])
    feed_in_grad = feed_in_grad.transpose(1, 0, 2).reshape(rows, -1)
    out_grad, value_grad = proj_sum.total[0, 0].T, value_sum.total[0, 0]
    mix_grad = mix_sum.total[0, 0]
    affine_grad = jnp.stack(
        [
            jnp.sum(grad_query * shared_pre * jax.nn.sigmoid(shared_pre), axis=0),
            jnp.sum(grad_query, axis=0),
            jnp.sum(grad_key * shared_pre * jax.nn.sigmoid(shared_pre), axis=0),
            jnp.sum(grad_key, axis=0),
        ]
    )
    relative_grad = bias_grad(rel_sums[:, 0], seq_length)
    small = [
        first[3] + second[3],
        first[4] + second[4],
        feed_gain_grad,
        affine_grad,
        relative_grad,
    ]
    small = [v.reshape(-1, 128) for v in small]
    rest = jnp.concatenate(small)
    rest = jnp.pad(rest, ((0, -rest.shape[0] % 16), (0, 0)))
    totals = layout.reduce_all(*pack(core, first[1:3], second[1:3], rest, after=turned))
    totals = totals.reshape(-1, 128)
    count = states * width // 128
    input_sum = totals[:count].reshape(states, width)
    decay_sum = totals[count : 2 * count].reshape(states, width)
    parts, start = [], 2 * count
    for item in small:
        parts.append(totals[start : start + item.shape[0]].reshape(-1))
        start += item.shape[0]
    input_total = smooth_eta * input_sum
    decay_total = smooth_eta * rate * decay_sum
    eta_grad = rate * input_sum
    alpha_grad = smooth_beta * input_total - smooth_damp * decay_total
    damp_grad = -smooth_alpha * decay_total
    beta_grad = smooth_alpha * input_total

    return (
        block_out,
        grad_in,
        parts[0],
        alpha_grad,
        damp_grad,
        beta_grad,
        eta_grad,
        parts[1],
        value_grad,
        mix_grad,
        parts[3].reshape(4, key_width),
        parts[4],
        out_grad,
        parts[2],
        feed_in_grad,
        feed_out_grad,
    )


def solution(mesh):
    tokens = P("dp", "seq", None)
    split = P("dp", "seq")
    return jax.shard_map(
        functools.partial(layer, Layout(mesh)),
        mesh=mesh,
        in_specs=(tokens, tokens, P("dp")) + (P(),) * 14,
        out_specs=(tokens, tokens)
        + (P(),) * 6
        + (split, split, P(), P(), split, P(), split, split),
        check_vma=False,
    )
```

```python
import functools

import jax
import jax.numpy as jnp
from jax import lax
from jax.experimental import pallas as pl
from jax.experimental.pallas import tpu as pltpu
from jax.sharding import PartitionSpec as P

STRETCH = 128
EPSILON = 1e-05
TILE = 256
MASKED = -1e30
VMEM_LIMIT = 60 * 1024 * 1024
AXES = ("dp", "seq")
BRIEF = pl.CostEstimate(flops=1, bytes_accessed=1, transcendentals=0)
LONG = pl.CostEstimate(flops=10**11, bytes_accessed=1, transcendentals=0)

f32 = jnp.float32
bf16 = jnp.bfloat16


def unit_rows_of(values):
    centred = values - jnp.mean(values, axis=-1, keepdims=True)
    inv_std = lax.rsqrt(jnp.mean(centred * centred, axis=-1, keepdims=True) + EPSILON)
    return centred * inv_std, inv_std


def norm_back_rows(grad_out, gain_vec, unit_rows, inv_std):
    scaled = grad_out * gain_vec
    return inv_std * (
        scaled
        - jnp.mean(scaled, axis=-1, keepdims=True)
        - unit_rows * jnp.mean(scaled * unit_rows, axis=-1, keepdims=True)
    )


def silu_slope(pre_act):
    sigmoid_val = jax.nn.sigmoid(pre_act)
    return sigmoid_val * (1.0 + pre_act * (1.0 - sigmoid_val))


def params(semantics, limit=VMEM_LIMIT):
    return pltpu.CompilerParams(dimension_semantics=semantics, vmem_limit_bytes=limit)


def ignoring(body, first, count):
    def called(*refs):
        return body(*refs[:first], *refs[first + count :])

    return called


def to_slab(slab, rows):
    count, groups = rows.shape[0], rows.shape[1] // 128
    for c in range(groups):
        slab[pl.ds(c, count, stride=groups), :] = rows[:, c * 128 : (c + 1) * 128]


def from_slab(slab, count, groups):
    return jnp.concatenate(
        [slab[pl.ds(c, count, stride=groups), :] for c in range(groups)], axis=1
    )


def slab_row(slab, t, groups):
    return slab[pl.ds(pl.multiple_of(t * groups, groups), groups), :]


def front_ends_body(x_ref, gain_ref, decay_ref, low_ref, end_ref, slab):
    states, groups, _ = decay_ref.shape
    count = x_ref.shape[1]

    @pl.when(pl.program_id(1) == 0)
    def _():
        end_ref[...] = jnp.zeros_like(end_ref)

    unit, _ = unit_rows_of(x_ref[0].astype(f32))
    normed = unit * gain_ref[...]
    low_ref[0] = normed.astype(bf16)
    to_slab(slab, normed)
    decay = [decay_ref[n] for n in range(states)]

    def step(t, state):
        row = slab_row(slab, t, groups)
        return tuple(d * s + row for d, s in zip(decay, state))

    state = lax.fori_loop(
        0, count, step, tuple(end_ref[0, n] for n in range(states)), unroll=8
    )
    for n in range(states):
        end_ref[0, n] = state[n]


def front_ends(x, gain, decay, block=256, after=()):
    slots, length, width = x.shape
    states, groups, lanes = decay.shape
    block = min(block, length)
    return pl.pallas_call(
        ignoring(front_ends_body, 3, len(after)),
        grid=(slots, length // block),
        in_specs=[
            pl.BlockSpec((1, block, width), lambda k, b: (k, b, 0)),
            pl.BlockSpec((1, width), lambda k, b: (0, 0)),
            pl.BlockSpec((states, groups, lanes), lambda k, b: (0, 0, 0)),
        ]
        + [pl.BlockSpec(memory_space=pl.ANY)] * len(after),
        out_specs=[
            pl.BlockSpec((1, block, width), lambda k, b: (k, b, 0)),
            pl.BlockSpec((1, states, groups, lanes), lambda k, b: (k, 0, 0, 0)),
        ],
        out_shape=[
            jax.ShapeDtypeStruct((slots, length, width), bf16),
            jax.ShapeDtypeStruct((slots, states, groups, lanes), f32),
        ],
        scratch_shapes=[pltpu.VMEM((block * groups, lanes), f32)],
        compiler_params=params(("arbitrary", "arbitrary")),
        name="front_ends",
        cost_estimate=BRIEF,
    )(x, gain, decay, *after)


def front_scan_body(
    table_ref,
    x_ref,
    gain_ref,
    decay_ref,
    coef_ref,
    span_ref,
    omega_ref,
    ends_ref,
    smooth_ref,
    mixed_ref,
    check_ref,
    slab,
    out_slab,
    carry,
):
    states, groups, _ = decay_ref.shape
    count = x_ref.shape[1]
    slot = pl.program_id(0)
    total = ends_ref.shape[0]

    @pl.when(pl.program_id(1) == 0)
    def _():
        carry[...] = jnp.zeros_like(carry)

        def link(i, _):
            carry[...] = span_ref[...] * carry[...] + ends_ref[table_ref[total + i]]
            return 0

        lax.fori_loop(0, table_ref[slot], link, 0)

    unit, _ = unit_rows_of(x_ref[0].astype(f32))
    normed = unit * gain_ref[...]
    to_slab(slab, normed)
    decay = [decay_ref[n] for n in range(states)]
    coef = [coef_ref[n] for n in range(states)]
    state = tuple(carry[n] for n in range(states))
    for n in range(states):
        check_ref[0, 0, n] = state[n]

    def step(t, state):
        row = slab_row(slab, t, groups)
        state = tuple(d * s + row for d, s in zip(decay, state))
        parts = [c * s for c, s in zip(coef, state)]
        while len(parts) > 1:
            parts = [a + b for a, b in zip(parts[::2], parts[1::2])]
        out_slab[pl.ds(pl.multiple_of(t * groups, groups), groups), :] = parts[0]
        return state

    state = lax.fori_loop(0, count, step, state, unroll=8)
    for n in range(states):
        carry[n] = state[n]
    smoothed = from_slab(out_slab, count, groups) + omega_ref[...] * normed
    smooth_ref[0] = smoothed
    mixed_ref[0] = (smoothed * jax.nn.sigmoid(smoothed)).astype(bf16)


def front_scan(table, x, gain, decay, coef, span, omega, ends, block):
    slots, length, width = x.shape
    states, groups, lanes = decay.shape
    whole3 = pl.BlockSpec((states, groups, lanes), lambda k, b, t: (0, 0, 0))
    row = pl.BlockSpec((1, width), lambda k, b, t: (0, 0))
    tokens = pl.BlockSpec((1, block, width), lambda k, b, t: (k, b, 0))
    return pl.pallas_call(
        front_scan_body,
        grid_spec=pltpu.PrefetchScalarGridSpec(
            num_scalar_prefetch=1,
            grid=(slots, length // block),
            in_specs=[
                tokens,
                row,
                whole3,
                whole3,
                whole3,
                row,
                pl.BlockSpec(ends.shape, lambda k, b, t: (0, 0, 0, 0)),
            ],
            out_specs=[
                tokens,
                tokens,
                pl.BlockSpec((1, 1, states, groups, lanes), lambda k, b, t: (k, b, 0, 0, 0)),
            ],
            scratch_shapes=[
                pltpu.VMEM((block * groups, lanes), f32),
                pltpu.VMEM((block * groups, lanes), f32),
                pltpu.VMEM((states, groups, lanes), f32),
            ],
        ),
        out_shape=[
            jax.ShapeDtypeStruct((slots, length, width), f32),
            jax.ShapeDtypeStruct((slots, length, width), bf16),
            jax.ShapeDtypeStruct((slots, length // block, states, groups, lanes), f32),
        ],
        compiler_params=params(("arbitrary", "arbitrary")),
        name="front_scan",
        cost_estimate=LONG,
    )(table, x, gain, decay, coef, span, omega, ends)


def back_ends_body(gs_ref, decay_ref, end_ref, slab):
    states, groups, _ = decay_ref.shape
    count = gs_ref.shape[1]

    @pl.when(pl.program_id(1) == 0)
    def _():
        end_ref[...] = jnp.zeros_like(end_ref)

    to_slab(slab, gs_ref[0])
    decay = [decay_ref[n] for n in range(states)]

    def step(t, state):
        row = slab_row(slab, count - 1 - t, groups)
        return tuple(d * s + row for d, s in zip(decay, state))

    state = lax.fori_loop(
        0, count, step, tuple(end_ref[0, n] for n in range(states)), unroll=8
    )
    for n in range(states):
        end_ref[0, n] = state[n]


def back_ends(gs, decay, block=256, after=()):
    slots, length, width = gs.shape
    states, groups, lanes = decay.shape
    block = min(block, length)
    blocks = length // block
    return pl.pallas_call(
        ignoring(back_ends_body, 2, len(after)),
        grid=(slots, blocks),
        in_specs=[
            pl.BlockSpec((1, block, width), lambda k, b: (k, blocks - 1 - b, 0)),
            pl.BlockSpec((states, groups, lanes), lambda k, b: (0, 0, 0)),
        ]
        + [pl.BlockSpec(memory_space=pl.ANY)] * len(after),
        out_specs=pl.BlockSpec((1, states, groups, lanes), lambda k, b: (k, 0, 0, 0)),
        out_shape=jax.ShapeDtypeStruct((slots, states, groups, lanes), f32),
        scratch_shapes=[pltpu.VMEM((block * groups, lanes), f32)],
        compiler_params=params(("arbitrary", "arbitrary")),
        name="back_ends",
        cost_estimate=BRIEF,
    )(gs, decay, *after)


def back_scan_body(
    table_ref,
    slot_ref,
    x_ref,
    gs_ref,
    gv_ref,
    gi_ref,
    check_ref,
    gain_ref,
    decay_ref,
    coef_ref,
    span_ref,
    omega_ref,
    ends_ref,
    grad_ref,
    qx_ref,
    qs_ref,
    gain_grad_ref,
    omega_grad_ref,
    slab,
    gs_slab,
    out_slab,
    history,
    carry,
):
    states, groups, _ = decay_ref.shape
    count = x_ref.shape[1]
    slot = slot_ref[0]
    total = ends_ref.shape[0]

    @pl.when(pl.program_id(0) == 0)
    def _():
        qx_ref[...] = jnp.zeros_like(qx_ref)
        qs_ref[...] = jnp.zeros_like(qs_ref)
        gain_grad_ref[...] = jnp.zeros_like(gain_grad_ref)
        omega_grad_ref[...] = jnp.zeros_like(omega_grad_ref)

    @pl.when(pl.program_id(0) == 0)
    def _():
        carry[...] = jnp.zeros_like(carry)

        def link(i, _):
            carry[...] = (
                span_ref[...] * carry[...] + ends_ref[table_ref[total + total - 1 - i]]
            )
            return 0

        lax.fori_loop(0, total - 1 - table_ref[slot], link, 0)

    unit, inv = unit_rows_of(x_ref[0].astype(f32))
    normed = unit * gain_ref[...]
    gs = gs_ref[0]
    to_slab(slab, normed)
    to_slab(gs_slab, gs)
    decay = [decay_ref[n] for n in range(states)]

    def recompute(t, state):
        for n in range(states):
            history[t, n] = state[n]
        row = slab_row(slab, t, groups)
        return tuple(d * s + row for d, s in zip(decay, state))

    lax.fori_loop(
        0, count, recompute, tuple(check_ref[0, 0, n] for n in range(states)), unroll=4
    )

    half = states // 2
    for part in range(2):
        chosen = range(part * half, (part + 1) * half)
        decay = [decay_ref[n] for n in chosen]
        coef = [coef_ref[n] for n in chosen]

        def step(i, held):
            q, qx, qs = held
            t = count - 1 - i
            row = slab_row(slab, t, groups)
            g = slab_row(gs_slab, t, groups)
            q = tuple(d * a + g for d, a in zip(decay, q))
            parts = [c * a for c, a in zip(coef, q)]
            while len(parts) > 1:
                parts = [a + b for a, b in zip(parts[::2], parts[1::2])]
            spot = pl.ds(pl.multiple_of(t * groups, groups), groups)
            if part == 0:
                out_slab[spot, :] = parts[0]
            else:
                out_slab[spot, :] = out_slab[spot, :] + parts[0]
            qx = tuple(a + b * row for a, b in zip(qx, q))
            qs = tuple(a + b * history[t, n] for a, b, n in zip(qs, q, chosen))
            return q, qx, qs

        q, qx, qs = lax.fori_loop(
            0,
            count,
            step,
            (
                tuple(carry[n] for n in chosen),
                tuple(qx_ref[n] for n in chosen),
                tuple(qs_ref[n] for n in chosen),
            ),
            unroll=4,
        )
        for i, n in enumerate(chosen):
            carry[n] = q[i]
            qx_ref[n] = qx[i]
            qs_ref[n] = qs[i]

    grad_normed = (
        gv_ref[0] + from_slab(out_slab, count, groups) + omega_ref[...] * gs
    )
    gain_grad_ref[...] += jnp.sum(grad_normed * unit, axis=0, keepdims=True)
    omega_grad_ref[...] += jnp.sum(gs * normed, axis=0, keepdims=True)
    grad_ref[...] = (
        gi_ref[0] + norm_back_rows(grad_normed, gain_ref[...], unit, inv)
    ).astype(bf16)


def back_scan(table, slot, x, gs, gv, gi, check, gain, decay, coef, span, omega, ends, after=()):
    _, length, width = x.shape
    states, groups, lanes = decay.shape
    blocks = check.shape[1]
    block = length // blocks
    whole3 = pl.BlockSpec((states, groups, lanes), lambda b, t, u: (0, 0, 0))
    row = pl.BlockSpec((1, width), lambda b, t, u: (0, 0))
    tokens = pl.BlockSpec((1, block, width), lambda b, t, u: (slot, blocks - 1 - b, 0))
    return pl.pallas_call(
        ignoring(back_scan_body, 13, len(after)),
        grid_spec=pltpu.PrefetchScalarGridSpec(
            num_scalar_prefetch=2,
            grid=(blocks,),
            in_specs=[
                tokens,
                tokens,
                tokens,
                tokens,
                pl.BlockSpec(
                    (1, 1, states, groups, lanes),
                    lambda b, t, u: (slot, blocks - 1 - b, 0, 0, 0),
                ),
                row,
                whole3,
                whole3,
                whole3,
                row,
                pl.BlockSpec(ends.shape, lambda b, t, u: (0, 0, 0, 0)),
            ]
            + [pl.BlockSpec(memory_space=pl.ANY)] * len(after),
            out_specs=[
                pl.BlockSpec((block, width), lambda b, t, u: (blocks - 1 - b, 0)),
                whole3,
                whole3,
                row,
                row,
            ],
            scratch_shapes=[
                pltpu.VMEM((block * groups, lanes), f32),
                pltpu.VMEM((block * groups, lanes), f32),
                pltpu.VMEM((block * groups, lanes), f32),
                pltpu.VMEM((block, states, groups, lanes), f32),
                pltpu.VMEM((states, groups, lanes), f32),
            ],
        ),
        out_shape=[
            jax.ShapeDtypeStruct((length, width), bf16),
            jax.ShapeDtypeStruct((states, groups, lanes), f32),
            jax.ShapeDtypeStruct((states, groups, lanes), f32),
            jax.ShapeDtypeStruct((1, width), f32),
            jax.ShapeDtypeStruct((1, width), f32),
        ],
        compiler_params=params(("arbitrary",)),
        name="back_scan",
        cost_estimate=LONG,
    )(table, jnp.full((1,), slot, jnp.int32), x, gs, gv, gi, check, gain, decay, coef, span, omega, ends, *after)


def load_chunks(table_ref, sources, total, length, sem):
    copies = []
    for slot in range(total):
        place = pl.ds(pl.multiple_of(table_ref[slot] * length, length), length)
        for own, others, kept in sources:
            source = own.at[slot] if slot < 2 else others.at[slot - 2]
            copies.append(
                pltpu.make_async_copy(source, kept.at[place, :], sem.at[len(copies)])
            )
    for copy in copies:
        copy.start()
    for copy in copies:
        copy.wait()


def attend_body(
    table_ref,
    q_ref,
    bias_ref,
    reset_ref,
    k_own,
    k_oth,
    v_own,
    v_oth,
    out_ref,
    gated_ref,
    lse_ref,
    keys,
    values,
    scores,
    probs,
    sem,
    *,
    total,
):
    length, key_width = q_ref.shape[1:]
    value_width = values.shape[1]
    tiles = length // TILE
    scale = float(key_width) ** (-0.5)

    @pl.when(pl.program_id(0) == 0)
    def _():
        load_chunks(
            table_ref, ((k_own, k_oth, keys), (v_own, v_oth, values)), total, length, sem
        )

    chunk = table_ref[pl.program_id(0)]
    reach = jnp.where(table_ref[2 * total] == 1, chunk + 1, 1)
    base = (chunk + 1 - reach) * length
    queries = q_ref[0]

    def first(kt, peak):
        spot = pl.ds(pl.multiple_of(base + kt * TILE, TILE), TILE)
        tile = (
            lax.dot_general(
                queries, keys[spot, :], (((1,), (1,)), ((), ())), preferred_element_type=f32
            )
            * scale
        )
        for r in range(tiles):
            rows = slice(r * TILE, (r + 1) * TILE)
            gap = (reach - 1) * tiles + r - kt + tiles - 1
            scores[kt, rows, :] = tile[rows] + bias_ref[gap]
        return jnp.maximum(peak, jnp.max(scores[kt], axis=1, keepdims=True))

    peak = lax.fori_loop(
        0, reach * tiles, first, jnp.full((length, 1), 2 * MASKED, f32)
    )

    def second(kt, sums):
        terms = jnp.exp(scores[kt] - peak)
        probs[:, pl.ds(pl.multiple_of(kt * TILE, TILE), TILE)] = terms.astype(bf16)
        return sums + jnp.sum(terms, axis=1, keepdims=True)

    sums = lax.fori_loop(0, reach * tiles, second, jnp.zeros((length, 1), f32))
    lse_ref[0] = peak + jnp.log(sums)
    inverse = 1.0 / sums

    for count in range(1, total + 1):

        @pl.when(reach == count)
        def _(count=count):
            width = count * length
            span = pl.ds(pl.multiple_of(base, length), width)

            def column(ct, _):
                at = pl.ds(pl.multiple_of(ct * TILE, TILE), TILE)
                rows = (
                    jnp.dot(probs[:, :width], values[span, at], preferred_element_type=f32)
                    * inverse
                )
                out_ref[0, :, at] = rows.astype(bf16)
                gate = reset_ref[0, :, at].astype(f32)
                gated_ref[0, :, at] = (gate * jax.nn.sigmoid(gate) * rows).astype(bf16)
                return 0

            lax.fori_loop(0, value_width // TILE, column, 0)


def attend(table, q, bias, reset, k_own, k_oth, v_own, v_oth):
    slots, length, key_width = q.shape
    value_width = v_own.shape[2]
    total = slots + k_oth.shape[0]
    anywhere = pl.BlockSpec(memory_space=pl.ANY)
    tokens = pl.BlockSpec((1, length, value_width), lambda k, t: (k, 0, 0))
    return pl.pallas_call(
        functools.partial(attend_body, total=total),
        grid_spec=pltpu.PrefetchScalarGridSpec(
            num_scalar_prefetch=1,
            grid=(slots,),
            in_specs=[
                pl.BlockSpec((1, length, key_width), lambda k, t: (k, 0, 0)),
                pl.BlockSpec(bias.shape, lambda k, t: (0, 0, 0)),
                tokens,
                anywhere,
                anywhere,
                anywhere,
                anywhere,
            ],
            out_specs=[
                tokens,
                tokens,
                pl.BlockSpec((1, length, 1), lambda k, t: (k, 0, 0)),
            ],
            scratch_shapes=[
                pltpu.VMEM((total * length, key_width), bf16),
                pltpu.VMEM((total * length, value_width), bf16),
                pltpu.VMEM((total * length // TILE, length, TILE), f32),
                pltpu.VMEM((length, total * length), bf16),
                pltpu.SemaphoreType.DMA((2 * total,)),
            ],
        ),
        out_shape=[
            jax.ShapeDtypeStruct((slots, length, value_width), bf16),
            jax.ShapeDtypeStruct((slots, length, value_width), bf16),
            jax.ShapeDtypeStruct((slots, length, 1), f32),
        ],
        compiler_params=params(("arbitrary",)),
        name="attend",
        cost_estimate=BRIEF,
    )(table, q, bias, reset, k_own, k_oth, v_own, v_oth)


def attend_back_body(
    table_ref,
    q_ref,
    grad_ref,
    lse_ref,
    bias_ref,
    k_own,
    k_oth,
    v_own,
    v_oth,
    gq_ref,
    gk_own,
    gv_own,
    both_oth,
    rel_out,
    keys,
    values,
    gk_sum,
    gv_sum,
    probs_kept,
    grads_kept,
    rel_ref,
    sem,
    *,
    total,
):
    length, key_width = q_ref.shape[1:]
    value_width = values.shape[1]
    tiles = length // TILE
    scale = float(key_width) ** (-0.5)
    step = pl.program_id(0)
    nt = (((1,), (1,)), ((), ()))
    tn = (((0,), (0,)), ((), ()))

    @pl.when(step == 0)
    def _():
        gk_sum[...] = jnp.zeros_like(gk_sum)
        gv_sum[...] = jnp.zeros_like(gv_sum)
        rel_ref[...] = jnp.zeros_like(rel_ref)
        load_chunks(
            table_ref, ((k_own, k_oth, keys), (v_own, v_oth, values)), total, length, sem
        )

    chunk = table_ref[step]
    reach = jnp.where(table_ref[2 * total] == 1, chunk + 1, 1)
    base = (chunk + 1 - reach) * length
    queries = q_ref[0]
    log_total = lse_ref[0]

    def gap_of(kc, a, r):
        return (reach - 1 - kc) * tiles + r - a + tiles - 1

    def first(kc, delta):
        spot = pl.ds(pl.multiple_of(base + kc * length, length), length)
        grads_kept[kc] = lax.dot_general(
            values[spot, :], grad_ref[0], nt, preferred_element_type=f32
        )
        tile = (
            lax.dot_general(keys[spot, :], queries, nt, preferred_element_type=f32) * scale
        )
        for a in range(tiles):
            for r in range(tiles):
                rows = slice(a * TILE, (a + 1) * TILE)
                cols = slice(r * TILE, (r + 1) * TILE)
                probs_kept[kc, rows, cols] = jnp.exp(
                    tile[rows, cols] + bias_ref[gap_of(kc, a, r)] - log_total[:, cols]
                )
        return delta + jnp.sum(probs_kept[kc] * grads_kept[kc], axis=0, keepdims=True)

    delta = lax.fori_loop(0, reach, first, jnp.zeros((1, length), f32))

    def second(kc, grad_query):
        spot = pl.ds(pl.multiple_of(base + kc * length, length), length)
        probs = probs_kept[kc]
        grad_scores = (probs * (grads_kept[kc] - delta)).astype(bf16)
        probs = probs.astype(bf16)
        for a in range(tiles):
            for r in range(tiles):
                rel_ref[gap_of(kc, a, r)] += grad_scores[
                    a * TILE : (a + 1) * TILE, r * TILE : (r + 1) * TILE
                ].astype(f32)
        gk_sum[spot, :] += jnp.dot(grad_scores, queries, preferred_element_type=f32)

        def column(ct, _):
            at = pl.ds(pl.multiple_of(ct * 512, 512), 512)
            gv_sum[spot, at] += jnp.dot(
                probs, grad_ref[0, :, at], preferred_element_type=f32
            )
            return 0

        lax.fori_loop(0, value_width // 512, column, 0)
        return grad_query + lax.dot_general(
            grad_scores, keys[spot, :], tn, preferred_element_type=f32
        )

    grad_query = lax.fori_loop(0, reach, second, jnp.zeros((length, key_width), f32))
    gq_ref[0] = grad_query * scale

    @pl.when(step == pl.num_programs(0) - 1)
    def _():
        for slot in range(total):
            place = pl.ds(pl.multiple_of(table_ref[slot] * length, length), length)
            key_grad = (gk_sum[place, :] * scale).astype(bf16)
            value_grad = gv_sum[place, :].astype(bf16)
            if slot < 2:
                gk_own[slot] = key_grad
                gv_own[slot] = value_grad
            else:
                both_oth[slot - 2, :, :value_width] = value_grad
                both_oth[slot - 2, :, value_width:] = key_grad
        down = lax.broadcasted_iota(jnp.int32, (TILE, TILE), 0)
        across = lax.broadcasted_iota(jnp.int32, (TILE, TILE), 1)
        mirror = jnp.where(down + across == TILE - 1, 1.0, 0.0)
        for d in range(rel_out.shape[0]):
            flipped = jnp.dot(
                rel_ref[d + tiles - 1],
                mirror,
                precision=lax.Precision.HIGHEST,
                preferred_element_type=f32,
            )
            wide = jnp.concatenate([flipped, jnp.zeros((TILE, TILE), f32)], axis=1)
            turned = pltpu.roll(wide, 0, 1, stride=1, stride_axis=0)
            rel_out[d] = jnp.sum(turned, axis=0, keepdims=True)


def attend_back(table, q, grads, lse, bias, k_own, k_oth, v_own, v_oth, after=()):
    slots, length, key_width = q.shape
    value_width = v_own.shape[2]
    total = slots + k_oth.shape[0]
    rel_shape = (total * length // TILE, 1, 2 * TILE)
    both_shape = (k_oth.shape[0], length, key_width + value_width)
    anywhere = pl.BlockSpec(memory_space=pl.ANY)

    def all_of(shape):
        return pl.BlockSpec(
            shape, lambda k, t: (0,) * len(shape), pipeline_mode=pl.Buffered(1)
        )

    return pl.pallas_call(
        ignoring(functools.partial(attend_back_body, total=total), 9, len(after)),
        grid_spec=pltpu.PrefetchScalarGridSpec(
            num_scalar_prefetch=1,
            grid=(slots,),
            in_specs=[
                pl.BlockSpec((1, length, key_width), lambda k, t: (k, 0, 0)),
                pl.BlockSpec((1, length, value_width), lambda k, t: (k, 0, 0)),
                pl.BlockSpec((1, 1, length), lambda k, t: (k, 0, 0)),
                all_of(bias.shape),
                anywhere,
                anywhere,
                anywhere,
                anywhere,
            ]
            + [anywhere] * len(after),
            out_specs=[
                pl.BlockSpec((1, length, key_width), lambda k, t: (k, 0, 0)),
                all_of(k_own.shape),
                all_of(v_own.shape),
                all_of(both_shape),
                all_of(rel_shape),
            ],
            scratch_shapes=[
                pltpu.VMEM((total * length, key_width), bf16),
                pltpu.VMEM((total * length, value_width), bf16),
                pltpu.VMEM((total * length, key_width), f32),
                pltpu.VMEM((total * length, value_width), f32),
                pltpu.VMEM((total, length, length), f32),
                pltpu.VMEM((total, length, length), f32),
                pltpu.VMEM(bias.shape, f32),
                pltpu.SemaphoreType.DMA((2 * total,)),
            ],
        ),
        out_shape=[
            jax.ShapeDtypeStruct((slots, length, key_width), f32),
            jax.ShapeDtypeStruct(k_own.shape, bf16),
            jax.ShapeDtypeStruct(v_own.shape, bf16),
            jax.ShapeDtypeStruct(both_shape, bf16),
            jax.ShapeDtypeStruct(rel_shape, f32),
        ],
        compiler_params=params(("arbitrary",)),
        name="attend_back",
        cost_estimate=LONG,
    )(table, q, grads, lse, bias, k_own, k_oth, v_own, v_oth, *after)


def bias_body(flag_ref, back_row, front_row, back_ref, front_ref, *, spare):
    tile = pl.program_id(0) - spare
    full = flag_ref[0] == 1

    @pl.when(tile < 0)
    def _():
        back_ref[...] = jnp.full_like(back_ref, MASKED)
        front_ref[...] = jnp.full_like(front_ref, MASKED)

    @pl.when(tile >= 0)
    def _():
        down = lax.broadcasted_iota(jnp.int32, (TILE, TILE), 0)
        across = lax.broadcasted_iota(jnp.int32, (TILE, TILE), 1)
        near = jnp.where(down // STRETCH == across // STRETCH, 1, 0)
        for row, out, ordered in (
            (back_row, back_ref, jnp.where(down <= across, 1, 0)),
            (front_row, front_ref, jnp.where(across <= down, 1, 0)),
        ):
            wide = jnp.broadcast_to(row[0], (TILE, 2 * TILE))
            turned = pltpu.roll(wide, 0, 1, stride=1, stride_axis=0)[:, :TILE]
            allowed = jnp.where(
                tile == 0, jnp.where(full, ordered, ordered * near), jnp.where(full, 1, 0)
            )
            out[0] = jnp.where(allowed == 1, turned, MASKED)


def bias_tiles(relative_bias, spare, full):
    length = relative_bias.shape[0] // 2
    count = length // TILE
    windows = jnp.stack(
        [
            lax.slice_in_dim(relative_bias, length - d * TILE - TILE, length - d * TILE + TILE)
            for d in range(count)
        ]
    )
    front = jnp.concatenate([windows[:, TILE:], windows[:, :TILE]], axis=1)
    back = jnp.concatenate([windows[:, TILE:TILE + 1], windows[:, ::-1][:, TILE:], windows[:, ::-1][:, : TILE - 1]], axis=1)
    row = pl.BlockSpec((1, 1, 2 * TILE), lambda d, t: (jnp.maximum(d - spare, 0), 0, 0))
    out = pl.BlockSpec((1, TILE, TILE), lambda d, t: (d, 0, 0))
    shape = jax.ShapeDtypeStruct((spare + count, TILE, TILE), f32)
    return pl.pallas_call(
        functools.partial(bias_body, spare=spare),
        grid_spec=pltpu.PrefetchScalarGridSpec(
            num_scalar_prefetch=1,
            grid=(spare + count,),
            in_specs=[row, row],
            out_specs=[out, out],
        ),
        out_shape=[shape, shape],
        compiler_params=params(("arbitrary",)),
        name="bias",
    )(full.astype(jnp.int32)[None], back[:, None], front[:, None])


def bias_grad(sums, length):
    count = sums.shape[0]
    shifted = jnp.concatenate([jnp.zeros((count, 1), f32), sums[:, :-1]], axis=1)
    none = jnp.zeros((1, TILE), f32)
    blocks = jnp.concatenate([none, shifted[:, :TILE]]) + jnp.concatenate(
        [shifted[:, TILE:], none]
    )
    return jnp.concatenate(
        [blocks[::-1].reshape(-1), jnp.zeros((2 * length - (count + 1) * TILE,), f32)]
    )


def gate_body(
    back_ref,
    cot_a,
    cot_b,
    x_ref,
    cand_ref,
    update_ref,
    reset_ref,
    attended_ref,
    gain_ref,
    proj_ref,
    input_ref,
    main_ref,
    grad_att_ref,
    gain_grad_ref,
):
    width = x_ref.shape[1]
    value_width = proj_ref.shape[0]

    @pl.when(pl.program_id(0) == 0)
    def _():
        gain_grad_ref[...] = jnp.zeros_like(gain_grad_ref)

    x = x_ref[...].astype(f32)
    cand_in = cand_ref[...]
    gate = jax.nn.sigmoid(cand_in)
    candidate = cand_in * gate
    update = jax.nn.sigmoid(update_ref[...].astype(f32))
    change = candidate - x
    unit, inv = unit_rows_of(x + update * change)
    grad_feed = back_ref[...]
    gain_grad_ref[...] += jnp.sum(grad_feed * unit, axis=0, keepdims=True)
    early = pl.program_id(0) < pl.num_programs(0) // 2
    cot = jnp.where(early, cot_a[...].astype(f32), cot_b[...].astype(f32))
    grad_first = cot + norm_back_rows(
        grad_feed, gain_ref[...], unit, inv
    )
    kept = grad_first * (1.0 - update)
    input_ref[...] = kept
    main_ref[:, value_width : value_width + width] = (kept * change * update).astype(bf16)
    grad_cand = (grad_first * update * (gate + candidate * (1.0 - gate))).astype(bf16)
    main_ref[:, value_width + width :] = grad_cand
    for c in range(value_width // 512):
        at = slice(c * 512, (c + 1) * 512)
        grad_gated = mm_nt(grad_cand, proj_ref[at, :])
        reset = reset_ref[:, at].astype(f32)
        open_gate = jax.nn.sigmoid(reset)
        passed = reset * open_gate
        grad_att_ref[:, at] = (grad_gated * passed).astype(bf16)
        main_ref[:, at] = (
            grad_gated
            * attended_ref[:, at].astype(f32)
            * (open_gate + passed * (1.0 - open_gate))
        ).astype(bf16)


def gate(back, cots, x, cand_in, base, attended, gain, proj, after=()):
    tokens, width = x.shape
    value_width = proj.shape[0]
    rows = min(256, tokens // 2)
    half = tokens // rows // 2
    wide = value_width // width

    def block(columns, at=0):
        return pl.BlockSpec((rows, columns), lambda i: (i, at))

    return pl.pallas_call(
        ignoring(gate_body, 10, len(after)),
        grid=(tokens // rows,),
        in_specs=[
            block(width),
            pl.BlockSpec((rows, width), lambda i: (jnp.minimum(i, half - 1), 0)),
            pl.BlockSpec((rows, width), lambda i: (jnp.maximum(i - half, 0), 0)),
            block(width),
            block(width),
            block(width, wide),
            block(value_width),
            block(value_width),
            pl.BlockSpec((1, width), lambda i: (0, 0)),
            pl.BlockSpec(proj.shape, lambda i: (0, 0), pipeline_mode=pl.Buffered(1)),
        ]
        + [pl.BlockSpec(memory_space=pl.ANY)] * len(after),
        out_specs=[
            block(width),
            block(value_width + 2 * width),
            block(value_width),
            pl.BlockSpec((1, width), lambda i: (0, 0)),
        ],
        out_shape=[
            jax.ShapeDtypeStruct((tokens, width), f32),
            jax.ShapeDtypeStruct((tokens, value_width + 2 * width), bf16),
            jax.ShapeDtypeStruct((tokens, value_width), bf16),
            jax.ShapeDtypeStruct((1, width), f32),
        ],
        compiler_params=params(("arbitrary",)),
        name="gate",
        cost_estimate=LONG,
    )(back, *cots, x, cand_in, base, base, attended, gain, proj, *after)


def ordered_transpose(ids_ref, source, plain, ordered):
    plain[...] = source[...].T
    count = ids_ref.shape[0]
    rows = plain.shape[0] // count

    def place(p, _):
        ordered[pl.ds(pl.multiple_of(p * rows, rows), rows), :] = plain[
            pl.ds(pl.multiple_of(ids_ref[p] * rows, rows), rows), :
        ]
        return 0

    lax.fori_loop(0, count, place, 0)


def placed_transpose(places_ref, sources, plain, ordered):
    start = 0
    for source in sources:
        plain[:, start : start + source.shape[0]] = source[...].T
        start += source.shape[0]
    count = places_ref.shape[0]
    rows = plain.shape[0] // count

    def place(q, _):
        ordered[pl.ds(pl.multiple_of(places_ref[q] * rows, rows), rows), :] = plain[
            pl.ds(pl.multiple_of(q * rows, rows), rows), :
        ]
        return 0

    lax.fori_loop(0, count, place, 0)


def feed_body(
    ids_ref,
    places_ref,
    low_ref,
    cot_a,
    cot_b,
    first_ref,
    in_ref,
    out_ref,
    result_a,
    result_b,
    back_ref,
    out_send,
    out_keep,
    in_send,
    in_keep,
    total,
    cot_turned,
    low_turned,
    plain,
):
    step = pl.program_id(0)
    half = pl.num_programs(0) // 2
    tokens = low_ref.shape[0]
    middle = tokens // 2
    nt = (((1,), (1,)), ((), ()))

    @pl.when(step == 0)
    def _():
        placed_transpose(places_ref, (cot_a, cot_b), plain, cot_turned)
        ordered_transpose(ids_ref, low_ref, plain, low_turned)
        total[...] = first_ref[...]
        back_ref[...] = jnp.zeros_like(back_ref)

    acts, grads = [], []
    for r, cot_ref in enumerate((cot_a, cot_b)):
        at = slice(r * middle, (r + 1) * middle)
        hidden = jnp.dot(low_ref[at, :], in_ref[...], preferred_element_type=f32)
        grad_act = lax.dot_general(
            cot_ref[...], out_ref[...], nt, preferred_element_type=f32
        )
        gate = jax.nn.sigmoid(hidden)
        act = hidden * gate
        grad = (grad_act * (gate + act * (1.0 - gate))).astype(bf16)
        act = act.astype(bf16)
        total[at, :] += jnp.dot(act, out_ref[...], preferred_element_type=f32)
        back_ref[at, :] += lax.dot_general(
            grad, in_ref[...], nt, preferred_element_type=f32
        )
        acts.append(act)
        grads.append(grad)
    out_grad = jnp.dot(
        cot_turned[...], jnp.concatenate(acts), preferred_element_type=f32
    ).astype(bf16)
    in_grad = jnp.dot(
        low_turned[...], jnp.concatenate(grads), preferred_element_type=f32
    ).astype(bf16)
    split = in_grad.shape[0] // 2
    in_send[...] = in_grad[:split].reshape(in_send.shape)
    in_keep[...] = in_grad[split:].reshape(in_keep.shape)

    @pl.when(step < half)
    def _():
        out_send[0] = out_grad

    @pl.when(step >= half)
    def _():
        out_keep[0] = out_grad

    @pl.when(step == pl.num_programs(0) - 1)
    def _():
        result_a[...] = total[:middle, :].astype(bf16)
        result_b[...] = total[middle:, :].astype(bf16)


def feed(ids, places, low, cots, first_sum, feed_in, feed_out, seq, after=()):
    tokens, width = low.shape
    features = feed_in.shape[1]
    parts = ids.shape[0]
    half = parts // 2
    columns = features // parts
    rows = width // parts
    share = parts // seq
    anywhere = pl.BlockSpec(memory_space=pl.ANY)

    def all_of(shape):
        return pl.BlockSpec(
            shape, lambda i, t, u: (0,) * len(shape), pipeline_mode=pl.Buffered(1)
        )

    def at(i, t):
        return t[jnp.minimum(i, parts - 1)]

    split = pl.BlockSpec(
        (half, 1, 1, rows, columns),
        lambda i, t, u: (0, u[at(i, t) // share], at(i, t) % share, 0, 0),
    )
    return pl.pallas_call(
        ignoring(feed_body, 8, len(after)),
        grid_spec=pltpu.PrefetchScalarGridSpec(
            num_scalar_prefetch=2,
            grid=(parts,),
            in_specs=[
                all_of(low.shape),
                all_of(cots[0].shape),
                all_of(cots[1].shape),
                all_of(first_sum.shape),
                pl.BlockSpec((width, columns), lambda i, t, u: (0, at(i, t))),
                pl.BlockSpec((columns, width), lambda i, t, u: (at(i, t), 0)),
            ]
            + [anywhere] * len(after),
            out_specs=[
                all_of(cots[0].shape),
                all_of(cots[1].shape),
                all_of(low.shape),
                pl.BlockSpec(
                    (1, width, columns), lambda i, t, u: (jnp.minimum(i, half - 1), 0, 0)
                ),
                pl.BlockSpec(
                    (1, width, columns), lambda i, t, u: (jnp.maximum(i - half, 0), 0, 0)
                ),
                split,
                split,
            ],
            scratch_shapes=[
                pltpu.VMEM((tokens, width), f32),
                pltpu.VMEM((width, tokens), bf16),
                pltpu.VMEM((width, tokens), bf16),
                pltpu.VMEM((width, tokens), bf16),
            ],
        ),
        out_shape=[
            jax.ShapeDtypeStruct(cots[0].shape, bf16),
            jax.ShapeDtypeStruct(cots[1].shape, bf16),
            jax.ShapeDtypeStruct((tokens, width), f32),
            jax.ShapeDtypeStruct((half, width, columns), bf16),
            jax.ShapeDtypeStruct((half, width, columns), bf16),
            jax.ShapeDtypeStruct((half, seq, share, rows, columns), bf16),
            jax.ShapeDtypeStruct((half, seq, share, rows, columns), bf16),
        ],
        compiler_params=params(("arbitrary",)),
        name="feed",
        cost_estimate=BRIEF,
    )(ids, places, low, *cots, first_sum, feed_in, feed_out, *after)


def by_columns_body(ids_ref, places_ref, left_ref, right_ref, send, keep, plain, turned):
    step = pl.program_id(0)
    half = pl.num_programs(0) // 2

    @pl.when(step == 0)
    def _():
        placed_transpose(places_ref, (left_ref,), plain, turned)

    grad = jnp.dot(turned[...], right_ref[...], preferred_element_type=f32).astype(bf16)

    @pl.when(step < half)
    def _():
        send[0] = grad

    @pl.when(step >= half)
    def _():
        keep[0] = grad


def by_columns(ids, places, left, right, after=(), rows=None, at=0):
    tokens = left.shape[0]
    rows = rows or left.shape[1]
    parts = ids.shape[0]
    half = parts // 2
    columns = right.shape[1] // parts
    shape = jax.ShapeDtypeStruct((half, rows, columns), bf16)
    if columns % 128:
        left = left[:, at * rows : (at + 1) * rows]
        grad = mm_tn(left, right).astype(bf16).reshape(rows, parts, columns)
        grad = jnp.take(grad, ids, axis=1).transpose(1, 0, 2)
        grad = grad.reshape(parts, places.shape[0], -1, columns)
        grad = jnp.take(grad, jnp.argsort(places), axis=1).reshape(parts, rows, columns)
        return grad[:half], grad[half:]
    return pl.pallas_call(
        ignoring(by_columns_body, 4, len(after)),
        grid_spec=pltpu.PrefetchScalarGridSpec(
            num_scalar_prefetch=2,
            grid=(parts,),
            in_specs=[
                pl.BlockSpec(
                    (tokens, rows), lambda i, t, u: (0, at), pipeline_mode=pl.Buffered(1)
                ),
                pl.BlockSpec((tokens, columns), lambda i, t, u: (0, t[jnp.minimum(i, parts - 1)])),
            ]
            + [pl.BlockSpec(memory_space=pl.ANY)] * len(after),
            out_specs=[
                pl.BlockSpec(
                    (1, rows, columns), lambda i, t, u: (jnp.minimum(i, half - 1), 0, 0)
                ),
                pl.BlockSpec(
                    (1, rows, columns), lambda i, t, u: (jnp.maximum(i - half, 0), 0, 0)
                ),
            ],
            scratch_shapes=[
                pltpu.VMEM((rows, tokens), bf16),
                pltpu.VMEM((rows, tokens), bf16),
            ],
        ),
        out_shape=[shape, shape],
        compiler_params=params(("arbitrary",)),
        name="by_columns",
        cost_estimate=BRIEF,
    )(ids, places, left, right, *after)


def by_rows_body(ids_ref, places_ref, left_ref, right_ref, send, keep, plain, turned):
    @pl.when(pl.program_id(0) == 0)
    def _():
        ordered_transpose(ids_ref, left_ref, plain, turned)

    grad = jnp.dot(turned[...], right_ref[...], preferred_element_type=f32).astype(bf16)
    middle = grad.shape[0] // 2
    send[...] = grad[:middle].reshape(send.shape)
    keep[...] = grad[middle:].reshape(keep.shape)


def by_rows(ids, places, left, right, seq=1, after=(), cost=BRIEF):
    tokens, rows = left.shape
    parts = ids.shape[0]
    half = parts // 2
    if places is None:
        seq, places = 1, jnp.zeros((1,), jnp.int32)
    columns = right.shape[1] // seq
    tile = min(512, columns)
    share = columns // tile
    shape = jax.ShapeDtypeStruct((half, seq, rows // parts, columns), bf16)
    split = pl.BlockSpec(
        (half, 1, rows // parts, tile), lambda i, t, u: (0, u[jnp.minimum(i // share, seq - 1)], 0, i % share)
    )
    return pl.pallas_call(
        ignoring(by_rows_body, 4, len(after)),
        grid_spec=pltpu.PrefetchScalarGridSpec(
            num_scalar_prefetch=2,
            grid=(seq * share,),
            in_specs=[
                pl.BlockSpec(
                    left.shape, lambda i, t, u: (0, 0), pipeline_mode=pl.Buffered(1)
                ),
                pl.BlockSpec((tokens, tile), lambda i, t, u: (0, i)),
            ]
            + [pl.BlockSpec(memory_space=pl.ANY)] * len(after),
            out_specs=[split, split],
            scratch_shapes=[
                pltpu.VMEM((rows, tokens), bf16),
                pltpu.VMEM((rows, tokens), bf16),
            ],
        ),
        out_shape=[shape, shape],
        compiler_params=params(("arbitrary",)),
        name="by_rows",
        cost_estimate=cost,
    )(ids, places, left, right, *after)


def value_back_body(
    ids_ref,
    places_ref,
    left_ref,
    own_ref,
    other_ref,
    slope_ref,
    proj_ref,
    total_ref,
    send,
    keep,
    plain,
    turned,
):
    @pl.when(pl.program_id(0) == 0)
    def _():
        total_ref[...] = jnp.zeros_like(total_ref)
        ordered_transpose(ids_ref, left_ref, plain, turned)

    grad = own_ref[...].astype(f32)
    for k in range(other_ref.shape[0]):
        grad = grad + other_ref[k].astype(f32)
    grad = (grad * slope_ref[...].astype(f32)).astype(bf16)
    total_ref[...] += mm_nt(grad, proj_ref[...])
    weights = jnp.dot(turned[...], grad, preferred_element_type=f32).astype(bf16)
    middle = weights.shape[0] // 2
    send[...] = weights[:middle].reshape(send.shape)
    keep[...] = weights[middle:].reshape(keep.shape)


def value_back(ids, places, left, own, others, slope, proj, seq, after=()):
    tokens, rows = left.shape
    parts = ids.shape[0]
    half = parts // 2
    columns = proj.shape[1] // seq
    tile = min(512, columns)
    share = columns // tile
    shape = jax.ShapeDtypeStruct((half, seq, rows // parts, columns), bf16)
    split = pl.BlockSpec(
        (half, 1, rows // parts, tile),
        lambda i, t, u: (0, u[jnp.minimum(i // share, seq - 1)], 0, i % share),
    )
    stripe = pl.BlockSpec((tokens, tile), lambda i, t, u: (0, i))
    fixed = pl.BlockSpec(
        (tokens, rows), lambda i, t, u: (0, 0), pipeline_mode=pl.Buffered(1)
    )
    return pl.pallas_call(
        ignoring(value_back_body, 7, len(after)),
        grid_spec=pltpu.PrefetchScalarGridSpec(
            num_scalar_prefetch=2,
            grid=(seq * share,),
            in_specs=[
                fixed,
                stripe,
                pl.BlockSpec((others.shape[0], tokens, tile), lambda i, t, u: (0, 0, i)),
                stripe,
                pl.BlockSpec((rows, tile), lambda i, t, u: (0, i)),
            ]
            + [pl.BlockSpec(memory_space=pl.ANY)] * len(after),
            out_specs=[fixed, split, split],
            scratch_shapes=[
                pltpu.VMEM((rows, tokens), bf16),
                pltpu.VMEM((rows, tokens), bf16),
            ],
        ),
        out_shape=[jax.ShapeDtypeStruct((tokens, rows), f32), shape, shape],
        compiler_params=params(("arbitrary",)),
        name="value_back",
        cost_estimate=LONG,
    )(ids, places, left, own, others, slope, proj, *after)


def stage_body(*refs, shapes):
    count = sum(pairs for pairs, _ in shapes)
    ins, outs = list(refs[: 2 * count]), list(refs[2 * count :])
    for pairs, halves in shapes:
        into = [outs.pop(0) for _ in range(halves)]
        start = 0
        for _ in range(pairs):
            kept, arrived = ins.pop(0), ins.pop(0)
            stop = start + kept.shape[0]
            for part, out in enumerate(into):
                out[start:stop] = (
                    kept[:, part].astype(f32) + arrived[:, part].astype(f32)
                ).astype(out.dtype)
            start = stop


def stage_sums(groups, after=(), steps=4, cost=BRIEF):
    shapes, ins, in_specs, out_specs, out_shapes, whole = [], [], [], [], [], []
    for pairs, single, _ in groups:
        _, n, rows, _ = pairs[0][0].shape
        while (n * rows // (1 if single else 2)) % (16 * steps):
            steps //= 2
    for pairs, single, kind in groups:
        halves = 1 if single else 2
        g, n, rows, columns = pairs[0][0].shape
        each = n * rows // halves // steps
        shapes.append((len(pairs), halves))
        for pair in pairs:
            for v in pair:
                ins.append(v.reshape(g, halves, n * rows // halves, columns))
                in_specs.append(
                    pl.BlockSpec((g, halves, each, columns), lambda i: (0, 0, i, 0))
                )
        for _ in range(halves):
            out_specs.append(pl.BlockSpec((len(pairs) * g, each, columns), lambda i: (0, i, 0)))
            out_shapes.append(
                jax.ShapeDtypeStruct((len(pairs) * g, n * rows // halves, columns), kind)
            )
        whole.append((halves, (len(pairs) * g, n // halves, rows, columns)))
    sums = list(
        pl.pallas_call(
            ignoring(functools.partial(stage_body, shapes=shapes), len(ins), len(after)),
            grid=(steps,),
            in_specs=in_specs + [pl.BlockSpec(memory_space=pl.ANY)] * len(after),
            out_specs=out_specs,
            out_shape=out_shapes,
            compiler_params=params(("arbitrary",)),
            name="stage_sums",
            cost_estimate=cost,
        )(*ins, *after)
    )
    return [tuple(sums.pop(0).reshape(shape) for _ in range(halves)) for halves, shape in whole]


class Layout:
    def __init__(self, mesh):
        self.dp = mesh.shape["dp"]
        self.seq = mesh.shape["seq"]
        self.members = self.seq // 2
        self.chips = self.seq // 4

    def pairs(self, move):
        return [
            (d * self.seq + z, e * self.seq + w)
            for d in range(self.dp)
            for z in range(self.seq)
            for e, w in [move(d, z)]
        ]

    def send(self, value, move):
        return lax.ppermute(value, AXES, self.pairs(move))

    def place(self, sequence, member):
        return member % 2 ^ (1 - sequence % 2), sequence * self.chips + member // 2

    def member(self, core, z):
        sequence = z // self.chips
        return (z % self.chips) * 2 + (core ^ (1 - sequence % 2))

    def home_to_work(self, round_index):
        def move(d, z):
            part = (1 if z >= self.seq // 2 else 0) ^ round_index
            core, at = self.place(2 * (d % 2) + part, min(z, self.seq - 1 - z))
            return d - d % 2 + core, at

        return move

    def spread(self, value):
        late = lax.axis_index("seq") >= self.seq // 2
        out = []
        for round_index in range(2):
            sent = lax.dynamic_index_in_dim(
                value, jnp.where(late, 1 - round_index, round_index), 0, False
            )
            out.append(self.send(sent, self.home_to_work(round_index)))
        return out

    def homeward(self, value, round_index):
        pairs = [(b, a) for a, b in self.pairs(self.home_to_work(round_index))]
        return lax.ppermute(value, AXES, pairs)

    def gathered(self, back):
        late = lax.axis_index("seq") >= self.seq // 2
        return jnp.stack([jnp.where(late, back[1], back[0]), jnp.where(late, back[0], back[1])])

    def collect(self, values):
        return self.gathered([self.homeward(v, r) for r, v in enumerate(values)])

    def rotate(self, value, by):
        def move(d, z):
            member = (self.member(d % 2, z) + by) % self.members
            core, at = self.place(z // self.chips, member)
            return d - d % 2 + core, at

        return self.send(value, move)

    def gather(self, value):
        return jnp.concatenate([self.rotate(value, by) for by in range(1, self.members)], axis=0)

    def returns(self, others):
        slots = others.shape[0] // (self.members - 1)
        return jnp.stack(
            [
                self.rotate(others[(by - 1) * slots : by * slots], self.members - by).reshape(
                    -1, others.shape[-1]
                )
                for by in range(1, self.members)
            ]
        )

    def orders(self):
        dp, z = lax.axis_index("dp"), lax.axis_index("seq")
        bits = self.dp.bit_length() - 1
        ids = []
        for core in range(2):
            orders = [[0, *range(1, bits)], [0, *reversed(range(1, bits))]]
            flips = []
            for p in range(self.dp):
                order = orders[core if p >= self.dp // 2 else 1 - core]
                flips.append(
                    sum(
                        (0 if p >> (bits - 1 - i) & 1 else 1) << bit
                        for i, bit in enumerate(order)
                    )
                )
            ids.append(dp ^ jnp.array(flips, jnp.int32))
        ids = jnp.where(dp % 2 == 0, ids[0], ids[1])
        bits = self.seq.bit_length() - 1
        flips = [
            sum((0 if p >> (bits - 1 - i) & 1 else 1) << i for i in range(bits))
            for p in range(self.seq)
        ]
        blocks = z ^ jnp.array(flips, jnp.int32)
        return ids, jnp.argsort(blocks).astype(jnp.int32), blocks

    def partner(self, stage):
        bits = self.dp.bit_length() - 1
        if stage == 0:
            return lambda d, z: (d ^ 1, z)
        if stage < bits:
            return lambda d, z: (d ^ (1 << stage if d % 2 == 0 else 1 << (bits - stage)), z)
        return lambda d, z: (d, z ^ (1 << (stage - bits)))

    def turn(self, sums, after, cost=BRIEF):
        sums = [s for s in sums if s.arrived]
        if not sums:
            return after
        dp_stages = self.dp.bit_length() - 1
        last = dp_stages + self.seq.bit_length() - 1
        groups = []
        for s in sums:
            pairs = list(zip(s.kept, s.arrived))
            single = s.stage + 1 == last
            if s.stage + 1 == dp_stages:
                single = not s.over_seq
                if s.over_seq:
                    pairs = [
                        tuple(
                            v.reshape(v.shape[0], self.seq, -1, v.shape[-1]) for v in pair
                        )
                        for pair in pairs
                    ]
            groups.append((pairs, single, f32 if s.stage + 1 == last else bf16))
        out = stage_sums(groups, after, cost=cost)
        for s, held, (_, single, _) in zip(sums, out, groups):
            s.stage += 1
            s.arrived = ()
            if single:
                s.total = held[0]
            else:
                s.send([held[0]], [held[1]])
        return [part for held in out for part in held]

    def reduce_all(self, sent, held, after):
        core = lax.axis_index("dp") % 2
        held = held + self.send(sent, lambda d, z: (d ^ 1, z))
        for bit in range(1, self.dp.bit_length() - 1):
            held = held + self.send(held, lambda d, z: (d ^ (1 << bit), z))
        held = later(held, after)
        low = 1
        while low < self.seq:
            mine = held
            for other in [low] if 2 * low >= self.seq else [low, 2 * low, 3 * low]:
                held = held + self.send(mine, lambda d, z: (d, z ^ other))
            low *= 4
        other = self.send(held, lambda d, z: (d ^ 1, z))
        return jnp.where(core == 0, jnp.stack([held, other]), jnp.stack([other, held]))


def later_body(value, out):
    out[...] = value[...]


def later(value, after):
    inside = pl.BlockSpec(memory_space=pltpu.VMEM)
    return pl.pallas_call(
        ignoring(later_body, 1, len(after)),
        in_specs=[inside] + [pl.BlockSpec(memory_space=pl.ANY)] * len(after),
        out_specs=inside,
        out_shape=jax.ShapeDtypeStruct(value.shape, value.dtype),
        name="later",
        cost_estimate=BRIEF,
    )(value, *after)


def pack_body(core_ref, qx_a, qx_b, qs_a, qs_b, rest_ref, sent, held):
    rows = jnp.concatenate(
        [qx_a[...] + qx_b[...], qs_a[...] + qs_b[...], rest_ref[...]], axis=0
    )
    middle = rows.shape[0] // 2
    first = core_ref[0] == 0
    sent[...] = jnp.where(first, rows[middle:], rows[:middle])
    held[...] = jnp.where(first, rows[:middle], rows[middle:])


def pack(core, first, second, rest, after=()):
    ins = [v.reshape(-1, 128) for v in (first[0], second[0], first[1], second[1])] + [rest]
    rows = 2 * ins[0].shape[0] + rest.shape[0]
    shape = jax.ShapeDtypeStruct((rows // 2, 128), f32)
    inside = pl.BlockSpec(memory_space=pltpu.VMEM)
    return pl.pallas_call(
        ignoring(pack_body, 6, len(after)),
        in_specs=[pl.BlockSpec(memory_space=pltpu.SMEM)]
        + [inside] * 5
        + [pl.BlockSpec(memory_space=pl.ANY)] * len(after),
        out_specs=[inside, inside],
        out_shape=[shape, shape],
        name="pack",
        cost_estimate=BRIEF,
    )(core[None].astype(jnp.int32), *ins, *after)


class Sum:
    def __init__(self, layout, *pairs, over_seq=True):
        self.layout, self.over_seq, self.stage = layout, over_seq, 0
        self.total = None
        pairs = [[v.reshape(1, v.shape[0], -1, v.shape[-1]) for v in pair] for pair in pairs]
        self.send([p[0] for p in pairs], [p[1] for p in pairs])

    def send(self, sent, kept):
        self.kept = kept
        self.arrived = [self.layout.send(v, self.layout.partner(self.stage)) for v in sent]

    def begin_seq(self, block):
        self.total = None
        middle = self.layout.seq // 2
        self.send([block[None, :middle]], [block[None, middle:]])


def mm(a, b):
    return jnp.dot(a, b, preferred_element_type=f32)


def mm_nt(a, b):
    return lax.dot_general(a, b, (((1,), (1,)), ((), ())), preferred_element_type=f32)


def mm_tn(a, b):
    return lax.dot_general(a, b, (((0,), (0,)), ((), ())), preferred_element_type=f32)


def layer(
    layout,
    inputs,
    cotangent,
    full_attention,
    mix_gain,
    smooth_alpha,
    smooth_damp,
    smooth_beta,
    smooth_eta,
    smooth_omega,
    value_proj,
    mix_proj,
    score_affine,
    relative_bias,
    out_proj,
    feed_gain,
    feed_in,
    feed_out,
):
    slots, chunk_rows, width = inputs.shape
    key_width = score_affine.shape[1]
    value_width = value_proj.shape[1]
    tokens = slots * chunk_rows
    total = layout.seq
    seq_length = relative_bias.shape[0] // 2
    block = min(128, chunk_rows)
    core = lax.axis_index("dp") % 2
    z = lax.axis_index("seq")

    sequence = z // layout.chips
    member = layout.member(core, z)
    swap = sequence % 2
    chunks = []
    for by in range(layout.members):
        source = (member - by) % layout.members
        low, high = source, total - 1 - source
        chunks += [jnp.where(swap == 0, low, high), jnp.where(swap == 0, high, low)]
    chunks = jnp.stack(chunks).astype(jnp.int32)
    slot_of = jnp.sum(
        jnp.where(chunks[None, :] == jnp.arange(total)[:, None], jnp.arange(total)[None, :], 0),
        axis=1,
    ).astype(jnp.int32)
    flags = full_attention.astype(f32)
    flags_other = layout.send(flags, lambda d, z: (d ^ 1, z))
    flags = jnp.where(
        core == 0, jnp.concatenate([flags, flags_other]), jnp.concatenate([flags_other, flags])
    )
    full = lax.dynamic_index_in_dim(flags, sequence, 0, False) == 1.0
    table = jnp.concatenate([chunks, slot_of, full.astype(jnp.int32)[None]])
    ids, places, blocks = layout.orders()

    x = jnp.stack(layout.spread(inputs))
    cots = layout.spread(cotangent)
    bias_back, bias_front = bias_tiles(relative_bias, chunk_rows // TILE - 1, full)

    states = smooth_alpha.shape[0]
    lanes = (states, width // 128, 128)
    decay = 1.0 - smooth_alpha * smooth_damp
    rate = smooth_alpha * smooth_beta
    span = (decay**chunk_rows).reshape(lanes)
    coef = (smooth_eta * rate).reshape(lanes)
    decay_slab = decay.reshape(lanes)
    gain_row = mix_gain[None]
    omega_row = smooth_omega[None]
    mix_shared, mix_main = mix_proj[:, :key_width], mix_proj[:, key_width:]

    normed_low, ends = front_ends(
        x, gain_row, decay_slab, after=(bias_back, bias_front, mix_main, mix_shared, span, coef)
    )
    ends_all = jnp.concatenate([ends, layout.gather(ends)])
    normed_low = normed_low.reshape(tokens, width)
    value_pre = mm(normed_low, value_proj)
    value_low = jax.nn.silu(value_pre).astype(bf16).reshape(slots, chunk_rows, value_width)
    value_slope = silu_slope(value_pre).astype(bf16)
    value_others = layout.gather(value_low)
    smoothed, mixed, check = front_scan(
        table, x, gain_row, decay_slab, coef, span, omega_row, ends_all, block
    )
    smoothed = smoothed.reshape(tokens, width)
    mixed = mixed.reshape(tokens, width)

    shared_pre = mm(mixed, mix_shared)
    shared = jax.nn.silu(shared_pre)
    query_low = (shared * score_affine[0] + score_affine[1]).astype(bf16)
    key_low = (shared * score_affine[2] + score_affine[3]).astype(bf16)
    query_low = query_low.reshape(slots, chunk_rows, key_width)
    key_low = key_low.reshape(slots, chunk_rows, key_width)
    key_others = layout.gather(key_low)
    base = mm(mixed, mix_main).astype(bf16)
    attended, gated, lse = attend(
        table,
        query_low,
        bias_front,
        base.reshape(slots, chunk_rows, -1),
        key_low,
        key_others,
        value_low,
        value_others,
    )
    attended = attended.reshape(tokens, value_width)
    gated = gated.reshape(tokens, value_width)

    flat_low = x.reshape(tokens, width)
    flat = flat_low.astype(f32)
    update_pre = base[:, value_width : value_width + width].astype(f32)
    cand_in = base[:, value_width + width :].astype(f32) + mm(gated, out_proj)
    first_sum = flat + jax.nn.sigmoid(update_pre) * (jax.nn.silu(cand_in) - flat)
    unit_two, _ = unit_rows_of(first_sum)
    feed_low = (unit_two * feed_gain).astype(bf16)

    result_a, result_b, grad_feed, out_send, out_keep, in_send, in_keep = feed(
        ids, places, feed_low, cots, first_sum, feed_in, feed_out, layout.seq
    )
    home = [layout.homeward(result_a, 0), layout.homeward(result_b, 1)]
    block_out = layout.gathered(home)
    out_sum = Sum(layout, (out_send, out_keep))
    in_sum = Sum(layout, (in_send, in_keep))

    grad_input, grad_main, grad_att, feed_gain_grad = gate(
        grad_feed, cots, flat_low, cand_in, base, attended, feed_gain[None], out_proj
    )
    after = layout.turn((out_sum, in_sum), (grad_att,))
    mix_parts = by_rows(ids, None, mixed, grad_main, after=after, cost=LONG)
    proj_parts = by_columns(
        ids,
        places,
        grad_main,
        gated,
        rows=width,
        at=grad_main.shape[1] // width - 1,
        after=mix_parts,
    )
    after = layout.turn((out_sum,), (*proj_parts, *home))
    mix_sum = Sum(layout, mix_parts, over_seq=False)
    proj_sum = Sum(layout, proj_parts)
    grad_query, gk_own, gv_own, both_oth, rel_sums = attend_back(
        table,
        query_low,
        grad_att.reshape(slots, chunk_rows, value_width),
        lse.reshape(slots, 1, chunk_rows),
        bias_back,
        key_low,
        key_others,
        value_low,
        value_others,
        after=after,
    )
    both_back = layout.returns(both_oth)
    after = layout.turn((in_sum, out_sum, proj_sum), (grad_query,), cost=LONG)
    grad_normed, value_send, value_keep = value_back(
        ids,
        places,
        normed_low,
        gv_own.reshape(tokens, value_width),
        both_back,
        value_slope,
        value_proj,
        layout.seq,
        after=after,
    )
    grad_key = jnp.sum(both_back[:, :, value_width:].astype(f32), axis=0) + gk_own.reshape(
        tokens, key_width
    ).astype(f32)
    grad_query = grad_query.reshape(tokens, key_width)
    grad_shared = (
        (grad_query * score_affine[0] + grad_key * score_affine[2]) * silu_slope(shared_pre)
    ).astype(bf16)
    shared_grad = mm_tn(mixed, grad_shared).astype(bf16)
    shared_grad = lax.psum_scatter(shared_grad, "dp", scatter_dimension=0, tiled=True)
    after = layout.turn((in_sum, out_sum, mix_sum), (grad_normed,))
    value_sum = Sum(layout, (value_send, value_keep))
    grad_smooth = (mm_nt(grad_main, mix_main) + mm_nt(grad_shared, mix_shared)) * silu_slope(
        smoothed
    )
    grad_smooth = grad_smooth.reshape(slots, chunk_rows, width)
    after = layout.turn((value_sum, proj_sum), (grad_smooth,))
    back = back_ends(grad_smooth, decay_slab, after=after)
    back_all = jnp.concatenate([back, layout.gather(back)])
    after = layout.turn((out_sum, in_sum, mix_sum, value_sum), (back,))

    def scan_back(slot, after):
        return back_scan(
            table,
            slot,
            x,
            grad_smooth,
            grad_normed.reshape(slots, chunk_rows, width),
            grad_input.reshape(slots, chunk_rows, width),
            check,
            gain_row,
            decay_slab,
            coef,
            span,
            omega_row,
            back_all,
            after=after,
        )

    first = scan_back(0, after)
    after = layout.turn(
        (in_sum, mix_sum, value_sum, proj_sum, out_sum), (first[0], shared_grad)
    )
    home_first = layout.homeward(first[0], 0)
    while mix_sum.total is None:
        after = layout.turn((mix_sum,), after)
    rows = jnp.concatenate([shared_grad, mix_sum.total[0, 0]], axis=1)
    rows = rows.reshape(rows.shape[0], layout.seq, -1).transpose(1, 0, 2)
    mix_sum.begin_seq(rows[blocks])
    second = scan_back(1, (*after, *mix_sum.kept))
    home_second = layout.homeward(second[0], 1)
    after = (second[0], home_first)
    sums = (mix_sum, proj_sum, value_sum, out_sum, in_sum)
    turned = layout.turn(sums, after, cost=LONG)
    after = layout.turn(sums, (*turned, home_second))
    while any(v.total is None for v in sums):
        after = layout.turn(sums, after)
    grad_in = layout.gathered([home_first, home_second]).astype(f32)
    feed_out_grad, feed_in_grad = out_sum.total[0, 0].T, in_sum.total[0, 0]
    rows = width // layout.dp
    feed_in_grad = feed_in_grad.reshape(-1, rows, feed_in_grad.shape[-1])
    feed_in_grad = feed_in_grad.transpose(1, 0, 2).reshape(rows, -1)
    out_grad, value_grad = proj_sum.total[0, 0].T, value_sum.total[0, 0]
    mix_grad = mix_sum.total[0, 0]
    affine_grad = jnp.stack(
        [
            jnp.sum(grad_query * shared_pre * jax.nn.sigmoid(shared_pre), axis=0),
            jnp.sum(grad_query, axis=0),
            jnp.sum(grad_key * shared_pre * jax.nn.sigmoid(shared_pre), axis=0),
            jnp.sum(grad_key, axis=0),
        ]
    )
    relative_grad = bias_grad(rel_sums[:, 0], seq_length)
    small = [
        first[3] + second[3],
        first[4] + second[4],
        feed_gain_grad,
        affine_grad,
        relative_grad,
    ]
    small = [v.reshape(-1, 128) for v in small]
    rest = jnp.concatenate(small)
    rest = jnp.pad(rest, ((0, -rest.shape[0] % 16), (0, 0)))
    totals = layout.reduce_all(
        *pack(core, first[1:3], second[1:3], rest, after=turned), after=after
    )
    totals = totals.reshape(-1, 128)
    count = states * width // 128
    input_sum = totals[:count].reshape(states, width)
    decay_sum = totals[count : 2 * count].reshape(states, width)
    parts, start = [], 2 * count
    for item in small:
        parts.append(totals[start : start + item.shape[0]].reshape(-1))
        start += item.shape[0]
    input_total = smooth_eta * input_sum
    decay_total = smooth_eta * rate * decay_sum
    eta_grad = rate * input_sum
    alpha_grad = smooth_beta * input_total - smooth_damp * decay_total
    damp_grad = -smooth_alpha * decay_total
    beta_grad = smooth_alpha * input_total

    return (
        block_out,
        grad_in,
        parts[0],
        alpha_grad,
        damp_grad,
        beta_grad,
        eta_grad,
        parts[1],
        value_grad,
        mix_grad,
        parts[3].reshape(4, key_width),
        parts[4],
        out_grad,
        parts[2],
        feed_in_grad,
        feed_out_grad,
    )


def solution(mesh):
    tokens = P("dp", "seq", None)
    split = P("dp", "seq")
    return jax.shard_map(
        functools.partial(layer, Layout(mesh)),
        mesh=mesh,
        in_specs=(tokens, tokens, P("dp")) + (P(),) * 14,
        out_specs=(tokens, tokens)
        + (P(),) * 6
        + (split, split, P(), P(), split, P(), split, split),
        check_vma=False,
    )
```

```python
import functools

import jax
import jax.numpy as jnp
from jax import lax
from jax.experimental import pallas as pl
from jax.experimental.pallas import tpu as pltpu
from jax.sharding import PartitionSpec as P

STRETCH = 128
EPSILON = 1e-05
TILE = 256
MASKED = -1e30
VMEM_LIMIT = 60 * 1024 * 1024
AXES = ("dp", "seq")
BRIEF = pl.CostEstimate(flops=1, bytes_accessed=1, transcendentals=0)
LONG = pl.CostEstimate(flops=10**11, bytes_accessed=1, transcendentals=0)

f32 = jnp.float32
bf16 = jnp.bfloat16


def unit_rows_of(values):
    centred = values - jnp.mean(values, axis=-1, keepdims=True)
    inv_std = lax.rsqrt(jnp.mean(centred * centred, axis=-1, keepdims=True) + EPSILON)
    return centred * inv_std, inv_std


def norm_back_rows(grad_out, gain_vec, unit_rows, inv_std):
    scaled = grad_out * gain_vec
    return inv_std * (
        scaled
        - jnp.mean(scaled, axis=-1, keepdims=True)
        - unit_rows * jnp.mean(scaled * unit_rows, axis=-1, keepdims=True)
    )


def silu_slope(pre_act):
    sigmoid_val = jax.nn.sigmoid(pre_act)
    return sigmoid_val * (1.0 + pre_act * (1.0 - sigmoid_val))


def params(semantics, limit=VMEM_LIMIT):
    return pltpu.CompilerParams(dimension_semantics=semantics, vmem_limit_bytes=limit)


def ignoring(body, first, count):
    def called(*refs):
        return body(*refs[:first], *refs[first + count :])

    return called


def to_slab(slab, rows):
    count, groups = rows.shape[0], rows.shape[1] // 128
    for c in range(groups):
        slab[pl.ds(c, count, stride=groups), :] = rows[:, c * 128 : (c + 1) * 128]


def from_slab(slab, count, groups):
    return jnp.concatenate(
        [slab[pl.ds(c, count, stride=groups), :] for c in range(groups)], axis=1
    )


def slab_row(slab, t, groups):
    return slab[pl.ds(pl.multiple_of(t * groups, groups), groups), :]


def front_body(
    x_ref, gain_ref, decay_ref, proj_ref, low_ref, copy_ref, value_ref, slope_ref, end_ref, slab
):
    states, groups, _ = decay_ref.shape
    count = x_ref.shape[0]

    @pl.when(pl.program_id(0) == 0)
    def _():
        end_ref[...] = jnp.zeros_like(end_ref)

    copy_ref[0] = x_ref[...]
    unit, _ = unit_rows_of(x_ref[...].astype(f32))
    normed = unit * gain_ref[...]
    low_ref[0] = normed.astype(bf16)
    to_slab(slab, normed)
    decay = [decay_ref[n] for n in range(states)]

    def step(t, state):
        row = slab_row(slab, t, groups)
        return tuple(d * s + row for d, s in zip(decay, state))

    state = lax.fori_loop(
        0, count, step, tuple(end_ref[0, n] for n in range(states)), unroll=8
    )
    for n in range(states):
        end_ref[0, n] = state[n]
    for c in range(proj_ref.shape[1] // 512):
        at = slice(c * 512, (c + 1) * 512)
        pre = jnp.dot(low_ref[0], proj_ref[:, at], preferred_element_type=f32)
        gate = jax.nn.sigmoid(pre)
        value = pre * gate
        value_ref[0, :, at] = value.astype(bf16)
        slope_ref[0, :, at] = (gate + value * (1.0 - gate)).astype(bf16)


def front(x, slot, slots, earlier, gain, decay, proj, after=()):
    length, width = x.shape
    value_width = proj.shape[1]
    states, groups, lanes = decay.shape
    block = min(256, length)
    anywhere = pl.BlockSpec(memory_space=pl.ANY)

    def tokens(columns):
        return pl.BlockSpec((1, block, columns), lambda b: (slot, b, 0))

    return pl.pallas_call(
        ignoring(front_body, 4, len(earlier) + len(after)),
        grid=(length // block,),
        in_specs=[
            pl.BlockSpec((block, width), lambda b: (b, 0)),
            pl.BlockSpec((1, width), lambda b: (0, 0)),
            pl.BlockSpec((states, groups, lanes), lambda b: (0, 0, 0)),
            pl.BlockSpec(proj.shape, lambda b: (0, 0), pipeline_mode=pl.Buffered(1)),
        ]
        + [anywhere] * (len(earlier) + len(after)),
        out_specs=[
            tokens(width),
            tokens(width),
            tokens(value_width),
            tokens(value_width),
            pl.BlockSpec((1, states, groups, lanes), lambda b: (slot, 0, 0, 0)),
        ],
        out_shape=[
            jax.ShapeDtypeStruct((slots, length, width), bf16),
            jax.ShapeDtypeStruct((slots, length, width), bf16),
            jax.ShapeDtypeStruct((slots, length, value_width), bf16),
            jax.ShapeDtypeStruct((slots, length, value_width), bf16),
            jax.ShapeDtypeStruct((slots, states, groups, lanes), f32),
        ],
        scratch_shapes=[pltpu.VMEM((block * groups, lanes), f32)],
        input_output_aliases={4 + k: k for k in range(len(earlier))},
        compiler_params=params(("arbitrary",)),
        name="front",
        cost_estimate=BRIEF,
    )(x, gain, decay, proj, *earlier, *after)


def front_scan_body(
    table_ref,
    x_ref,
    gain_ref,
    decay_ref,
    coef_ref,
    span_ref,
    omega_ref,
    ends_ref,
    proj_ref,
    affine_ref,
    smooth_ref,
    mixed_ref,
    check_ref,
    shared_ref,
    query_ref,
    key_ref,
    slab,
    out_slab,
    carry,
):
    states, groups, _ = decay_ref.shape
    count = x_ref.shape[1]
    slot = pl.program_id(0)
    total = ends_ref.shape[0]

    @pl.when(pl.program_id(1) == 0)
    def _():
        carry[...] = jnp.zeros_like(carry)

        def link(i, _):
            carry[...] = span_ref[...] * carry[...] + ends_ref[table_ref[total + i]]
            return 0

        lax.fori_loop(0, table_ref[slot], link, 0)

    unit, _ = unit_rows_of(x_ref[0].astype(f32))
    normed = unit * gain_ref[...]
    to_slab(slab, normed)
    decay = [decay_ref[n] for n in range(states)]
    coef = [coef_ref[n] for n in range(states)]
    state = tuple(carry[n] for n in range(states))
    for n in range(states):
        check_ref[0, 0, n] = state[n]

    def step(t, state):
        row = slab_row(slab, t, groups)
        state = tuple(d * s + row for d, s in zip(decay, state))
        parts = [c * s for c, s in zip(coef, state)]
        while len(parts) > 1:
            parts = [a + b for a, b in zip(parts[::2], parts[1::2])]
        out_slab[pl.ds(pl.multiple_of(t * groups, groups), groups), :] = parts[0]
        return state

    state = lax.fori_loop(0, count, step, state, unroll=8)
    for n in range(states):
        carry[n] = state[n]
    smoothed = from_slab(out_slab, count, groups) + omega_ref[...] * normed
    smooth_ref[0] = smoothed
    mixed = (smoothed * jax.nn.sigmoid(smoothed)).astype(bf16)
    mixed_ref[0] = mixed
    shared_pre = jnp.dot(mixed, proj_ref[...], preferred_element_type=f32)
    shared = shared_pre * jax.nn.sigmoid(shared_pre)
    shared_ref[0] = shared_pre
    query_ref[0] = (shared * affine_ref[0:1] + affine_ref[1:2]).astype(bf16)
    key_ref[0] = (shared * affine_ref[2:3] + affine_ref[3:4]).astype(bf16)


def front_scan(table, x, gain, decay, coef, span, omega, ends, proj, affine, block):
    slots, length, width = x.shape
    states, groups, lanes = decay.shape
    whole3 = pl.BlockSpec((states, groups, lanes), lambda k, b, t: (0, 0, 0))
    row = pl.BlockSpec((1, width), lambda k, b, t: (0, 0))
    tokens = pl.BlockSpec((1, block, width), lambda k, b, t: (k, b, 0))
    narrow = pl.BlockSpec((1, block, proj.shape[1]), lambda k, b, t: (k, b, 0))
    return pl.pallas_call(
        front_scan_body,
        grid_spec=pltpu.PrefetchScalarGridSpec(
            num_scalar_prefetch=1,
            grid=(slots, length // block),
            in_specs=[
                tokens,
                row,
                whole3,
                whole3,
                whole3,
                row,
                pl.BlockSpec(ends.shape, lambda k, b, t: (0, 0, 0, 0)),
                pl.BlockSpec(proj.shape, lambda k, b, t: (0, 0)),
                pl.BlockSpec(affine.shape, lambda k, b, t: (0, 0)),
            ],
            out_specs=[
                tokens,
                tokens,
                pl.BlockSpec((1, 1, states, groups, lanes), lambda k, b, t: (k, b, 0, 0, 0)),
                narrow,
                narrow,
                narrow,
            ],
            scratch_shapes=[
                pltpu.VMEM((block * groups, lanes), f32),
                pltpu.VMEM((block * groups, lanes), f32),
                pltpu.VMEM((states, groups, lanes), f32),
            ],
        ),
        out_shape=[
            jax.ShapeDtypeStruct((slots, length, width), f32),
            jax.ShapeDtypeStruct((slots, length, width), bf16),
            jax.ShapeDtypeStruct((slots, length // block, states, groups, lanes), f32),
            jax.ShapeDtypeStruct((slots, length, proj.shape[1]), f32),
            jax.ShapeDtypeStruct((slots, length, proj.shape[1]), bf16),
            jax.ShapeDtypeStruct((slots, length, proj.shape[1]), bf16),
        ],
        compiler_params=params(("arbitrary", "arbitrary")),
        name="front_scan",
        cost_estimate=LONG,
    )(table, x, gain, decay, coef, span, omega, ends, proj, affine)


def back_ends_body(gs_ref, decay_ref, end_ref, slab):
    states, groups, _ = decay_ref.shape
    count = gs_ref.shape[1]

    @pl.when(pl.program_id(1) == 0)
    def _():
        end_ref[...] = jnp.zeros_like(end_ref)

    to_slab(slab, gs_ref[0])
    decay = [decay_ref[n] for n in range(states)]

    def step(t, state):
        row = slab_row(slab, count - 1 - t, groups)
        return tuple(d * s + row for d, s in zip(decay, state))

    state = lax.fori_loop(
        0, count, step, tuple(end_ref[0, n] for n in range(states)), unroll=8
    )
    for n in range(states):
        end_ref[0, n] = state[n]


def back_ends(gs, decay, block=256, after=()):
    slots, length, width = gs.shape
    states, groups, lanes = decay.shape
    block = min(block, length)
    blocks = length // block
    return pl.pallas_call(
        ignoring(back_ends_body, 2, len(after)),
        grid=(slots, blocks),
        in_specs=[
            pl.BlockSpec((1, block, width), lambda k, b: (k, blocks - 1 - b, 0)),
            pl.BlockSpec((states, groups, lanes), lambda k, b: (0, 0, 0)),
        ]
        + [pl.BlockSpec(memory_space=pl.ANY)] * len(after),
        out_specs=pl.BlockSpec((1, states, groups, lanes), lambda k, b: (k, 0, 0, 0)),
        out_shape=jax.ShapeDtypeStruct((slots, states, groups, lanes), f32),
        scratch_shapes=[pltpu.VMEM((block * groups, lanes), f32)],
        compiler_params=params(("arbitrary", "arbitrary")),
        name="back_ends",
        cost_estimate=BRIEF,
    )(gs, decay, *after)


def back_scan_body(
    table_ref,
    slot_ref,
    x_ref,
    gs_ref,
    gv_ref,
    gi_ref,
    check_ref,
    gain_ref,
    decay_ref,
    coef_ref,
    span_ref,
    omega_ref,
    ends_ref,
    grad_ref,
    qx_ref,
    qs_ref,
    gain_grad_ref,
    omega_grad_ref,
    slab,
    gs_slab,
    out_slab,
    history,
    carry,
):
    states, groups, _ = decay_ref.shape
    count = x_ref.shape[1]
    slot = slot_ref[0]
    total = ends_ref.shape[0]

    @pl.when(pl.program_id(0) == 0)
    def _():
        qx_ref[...] = jnp.zeros_like(qx_ref)
        qs_ref[...] = jnp.zeros_like(qs_ref)
        gain_grad_ref[...] = jnp.zeros_like(gain_grad_ref)
        omega_grad_ref[...] = jnp.zeros_like(omega_grad_ref)

    @pl.when(pl.program_id(0) == 0)
    def _():
        carry[...] = jnp.zeros_like(carry)

        def link(i, _):
            carry[...] = (
                span_ref[...] * carry[...] + ends_ref[table_ref[total + total - 1 - i]]
            )
            return 0

        lax.fori_loop(0, total - 1 - table_ref[slot], link, 0)

    unit, inv = unit_rows_of(x_ref[0].astype(f32))
    normed = unit * gain_ref[...]
    gs = gs_ref[0]
    to_slab(slab, normed)
    to_slab(gs_slab, gs)
    decay = [decay_ref[n] for n in range(states)]

    def recompute(t, state):
        for n in range(states):
            history[t, n] = state[n]
        row = slab_row(slab, t, groups)
        return tuple(d * s + row for d, s in zip(decay, state))

    lax.fori_loop(
        0, count, recompute, tuple(check_ref[0, 0, n] for n in range(states)), unroll=4
    )

    half = states // 2
    for part in range(2):
        chosen = range(part * half, (part + 1) * half)
        decay = [decay_ref[n] for n in chosen]
        coef = [coef_ref[n] for n in chosen]

        def step(i, held):
            q, qx, qs = held
            t = count - 1 - i
            row = slab_row(slab, t, groups)
            g = slab_row(gs_slab, t, groups)
            q = tuple(d * a + g for d, a in zip(decay, q))
            parts = [c * a for c, a in zip(coef, q)]
            while len(parts) > 1:
                parts = [a + b for a, b in zip(parts[::2], parts[1::2])]
            spot = pl.ds(pl.multiple_of(t * groups, groups), groups)
            if part == 0:
                out_slab[spot, :] = parts[0]
            else:
                out_slab[spot, :] = out_slab[spot, :] + parts[0]
            qx = tuple(a + b * row for a, b in zip(qx, q))
            qs = tuple(a + b * history[t, n] for a, b, n in zip(qs, q, chosen))
            return q, qx, qs

        q, qx, qs = lax.fori_loop(
            0,
            count,
            step,
            (
                tuple(carry[n] for n in chosen),
                tuple(qx_ref[n] for n in chosen),
                tuple(qs_ref[n] for n in chosen),
            ),
            unroll=4,
        )
        for i, n in enumerate(chosen):
            carry[n] = q[i]
            qx_ref[n] = qx[i]
            qs_ref[n] = qs[i]

    grad_normed = (
        gv_ref[0] + from_slab(out_slab, count, groups) + omega_ref[...] * gs
    )
    gain_grad_ref[...] += jnp.sum(grad_normed * unit, axis=0, keepdims=True)
    omega_grad_ref[...] += jnp.sum(gs * normed, axis=0, keepdims=True)
    grad_ref[...] = (
        gi_ref[0] + norm_back_rows(grad_normed, gain_ref[...], unit, inv)
    ).astype(bf16)


def back_scan(table, slot, x, gs, gv, gi, check, gain, decay, coef, span, omega, ends, after=()):
    _, length, width = x.shape
    states, groups, lanes = decay.shape
    blocks = check.shape[1]
    block = length // blocks
    whole3 = pl.BlockSpec((states, groups, lanes), lambda b, t, u: (0, 0, 0))
    row = pl.BlockSpec((1, width), lambda b, t, u: (0, 0))
    tokens = pl.BlockSpec((1, block, width), lambda b, t, u: (slot, blocks - 1 - b, 0))
    return pl.pallas_call(
        ignoring(back_scan_body, 13, len(after)),
        grid_spec=pltpu.PrefetchScalarGridSpec(
            num_scalar_prefetch=2,
            grid=(blocks,),
            in_specs=[
                tokens,
                tokens,
                tokens,
                tokens,
                pl.BlockSpec(
                    (1, 1, states, groups, lanes),
                    lambda b, t, u: (slot, blocks - 1 - b, 0, 0, 0),
                ),
                row,
                whole3,
                whole3,
                whole3,
                row,
                pl.BlockSpec(ends.shape, lambda b, t, u: (0, 0, 0, 0)),
            ]
            + [pl.BlockSpec(memory_space=pl.ANY)] * len(after),
            out_specs=[
                pl.BlockSpec((block, width), lambda b, t, u: (blocks - 1 - b, 0)),
                whole3,
                whole3,
                row,
                row,
            ],
            scratch_shapes=[
                pltpu.VMEM((block * groups, lanes), f32),
                pltpu.VMEM((block * groups, lanes), f32),
                pltpu.VMEM((block * groups, lanes), f32),
                pltpu.VMEM((block, states, groups, lanes), f32),
                pltpu.VMEM((states, groups, lanes), f32),
            ],
        ),
        out_shape=[
            jax.ShapeDtypeStruct((length, width), bf16),
            jax.ShapeDtypeStruct((states, groups, lanes), f32),
            jax.ShapeDtypeStruct((states, groups, lanes), f32),
            jax.ShapeDtypeStruct((1, width), f32),
            jax.ShapeDtypeStruct((1, width), f32),
        ],
        compiler_params=params(("arbitrary",)),
        name="back_scan",
        cost_estimate=LONG,
    )(table, jnp.full((1,), slot, jnp.int32), x, gs, gv, gi, check, gain, decay, coef, span, omega, ends, *after)


def chunk_copies(table_ref, own, others, kept, total, length, sem):
    copies = []
    for slot in range(total):
        place = pl.ds(pl.multiple_of(table_ref[slot] * length, length), length)
        source = own.at[slot] if slot < 2 else others.at[slot - 2]
        copies.append(pltpu.make_async_copy(source, kept.at[place, :], sem.at[slot]))
    return copies


def attend_body(
    table_ref,
    q_ref,
    bias_ref,
    reset_ref,
    k_own,
    k_oth,
    v_own,
    v_oth,
    out_ref,
    gated_ref,
    lse_ref,
    keys,
    values,
    scores,
    probs,
    key_sem,
    value_sem,
    *,
    total,
):
    length, key_width = q_ref.shape[1:]
    value_width = values.shape[1]
    tiles = length // TILE
    scale = float(key_width) ** (-0.5)

    key_copies = chunk_copies(table_ref, k_own, k_oth, keys, total, length, key_sem)
    value_copies = chunk_copies(table_ref, v_own, v_oth, values, total, length, value_sem)

    @pl.when(pl.program_id(0) == 0)
    def _():
        for copy in key_copies + value_copies:
            copy.start()
        for copy in key_copies:
            copy.wait()

    chunk = table_ref[pl.program_id(0)]
    reach = jnp.where(table_ref[2 * total] == 1, chunk + 1, 1)
    base = (chunk + 1 - reach) * length
    queries = q_ref[0]

    def first(kt, peak):
        spot = pl.ds(pl.multiple_of(base + kt * TILE, TILE), TILE)
        tile = (
            lax.dot_general(
                queries, keys[spot, :], (((1,), (1,)), ((), ())), preferred_element_type=f32
            )
            * scale
        )
        for r in range(tiles):
            rows = slice(r * TILE, (r + 1) * TILE)
            gap = (reach - 1) * tiles + r - kt + tiles - 1
            scores[kt, rows, :] = tile[rows] + bias_ref[gap]
        return jnp.maximum(peak, jnp.max(scores[kt], axis=1, keepdims=True))

    peak = lax.fori_loop(
        0, reach * tiles, first, jnp.full((length, 1), 2 * MASKED, f32)
    )

    def second(kt, sums):
        terms = jnp.exp(scores[kt] - peak)
        probs[:, pl.ds(pl.multiple_of(kt * TILE, TILE), TILE)] = terms.astype(bf16)
        return sums + jnp.sum(terms, axis=1, keepdims=True)

    sums = lax.fori_loop(0, reach * tiles, second, jnp.zeros((length, 1), f32))
    lse_ref[0] = peak + jnp.log(sums)
    inverse = 1.0 / sums

    @pl.when(pl.program_id(0) == 0)
    def _():
        for copy in value_copies:
            copy.wait()

    for count in range(1, total + 1):

        @pl.when(reach == count)
        def _(count=count):
            width = count * length
            span = pl.ds(pl.multiple_of(base, length), width)

            def column(ct, _):
                at = pl.ds(pl.multiple_of(ct * 512, 512), 512)
                rows = (
                    jnp.dot(probs[:, :width], values[span, at], preferred_element_type=f32)
                    * inverse
                )
                out_ref[0, :, at] = rows.astype(bf16)
                gate = reset_ref[0, :, at].astype(f32)
                gated_ref[0, :, at] = (gate * jax.nn.sigmoid(gate) * rows).astype(bf16)
                return 0

            lax.fori_loop(0, value_width // 512, column, 0)


def attend(table, q, bias, reset, k_own, k_oth, v_own, v_oth):
    slots, length, key_width = q.shape
    value_width = v_own.shape[2]
    total = slots + k_oth.shape[0]
    anywhere = pl.BlockSpec(memory_space=pl.ANY)
    tokens = pl.BlockSpec((1, length, value_width), lambda k, t: (k, 0, 0))
    return pl.pallas_call(
        functools.partial(attend_body, total=total),
        grid_spec=pltpu.PrefetchScalarGridSpec(
            num_scalar_prefetch=1,
            grid=(slots,),
            in_specs=[
                pl.BlockSpec((1, length, key_width), lambda k, t: (k, 0, 0)),
                pl.BlockSpec(bias.shape, lambda k, t: (0, 0, 0)),
                tokens,
                anywhere,
                anywhere,
                anywhere,
                anywhere,
            ],
            out_specs=[
                tokens,
                tokens,
                pl.BlockSpec((1, length, 1), lambda k, t: (k, 0, 0)),
            ],
            scratch_shapes=[
                pltpu.VMEM((total * length, key_width), bf16),
                pltpu.VMEM((total * length, value_width), bf16),
                pltpu.VMEM((total * length // TILE, length, TILE), f32),
                pltpu.VMEM((length, total * length), bf16),
                pltpu.SemaphoreType.DMA((total,)),
                pltpu.SemaphoreType.DMA((total,)),
            ],
        ),
        out_shape=[
            jax.ShapeDtypeStruct((slots, length, value_width), bf16),
            jax.ShapeDtypeStruct((slots, length, value_width), bf16),
            jax.ShapeDtypeStruct((slots, length, 1), f32),
        ],
        compiler_params=params(("arbitrary",)),
        name="attend",
        cost_estimate=BRIEF,
    )(table, q, bias, reset, k_own, k_oth, v_own, v_oth)


def attend_back_body(
    table_ref,
    q_ref,
    grad_ref,
    lse_ref,
    bias_ref,
    k_own,
    k_oth,
    v_own,
    v_oth,
    gq_ref,
    gk_own,
    gv_own,
    both_oth,
    rel_out,
    keys,
    values,
    gk_sum,
    gv_sum,
    probs_kept,
    grads_kept,
    rel_ref,
    key_sem,
    value_sem,
    *,
    total,
):
    length, key_width = q_ref.shape[1:]
    value_width = values.shape[1]
    tiles = length // TILE
    scale = float(key_width) ** (-0.5)
    step = pl.program_id(0)
    nt = (((1,), (1,)), ((), ()))
    tn = (((0,), (0,)), ((), ()))

    copies = chunk_copies(
        table_ref, k_own, k_oth, keys, total, length, key_sem
    ) + chunk_copies(table_ref, v_own, v_oth, values, total, length, value_sem)

    @pl.when(step == 0)
    def _():
        for copy in copies:
            copy.start()
        gk_sum[...] = jnp.zeros_like(gk_sum)
        gv_sum[...] = jnp.zeros_like(gv_sum)
        rel_ref[...] = jnp.zeros_like(rel_ref)
        for copy in copies:
            copy.wait()

    chunk = table_ref[step]
    reach = jnp.where(table_ref[2 * total] == 1, chunk + 1, 1)
    base = (chunk + 1 - reach) * length
    queries = q_ref[0]
    log_total = lse_ref[0]

    def gap_of(kc, a, r):
        return (reach - 1 - kc) * tiles + r - a + tiles - 1

    def first(kc, delta):
        spot = pl.ds(pl.multiple_of(base + kc * length, length), length)
        grads_kept[kc] = lax.dot_general(
            values[spot, :], grad_ref[0], nt, preferred_element_type=f32
        )
        tile = (
            lax.dot_general(keys[spot, :], queries, nt, preferred_element_type=f32) * scale
        )
        for a in range(tiles):
            for r in range(tiles):
                rows = slice(a * TILE, (a + 1) * TILE)
                cols = slice(r * TILE, (r + 1) * TILE)
                probs_kept[kc, rows, cols] = jnp.exp(
                    tile[rows, cols] + bias_ref[gap_of(kc, a, r)] - log_total[:, cols]
                )
        return delta + jnp.sum(probs_kept[kc] * grads_kept[kc], axis=0, keepdims=True)

    delta = lax.fori_loop(0, reach, first, jnp.zeros((1, length), f32))

    def second(kc, grad_query):
        spot = pl.ds(pl.multiple_of(base + kc * length, length), length)
        probs = probs_kept[kc]
        grad_scores = (probs * (grads_kept[kc] - delta)).astype(bf16)
        probs = probs.astype(bf16)
        for a in range(tiles):
            for r in range(tiles):
                rel_ref[gap_of(kc, a, r)] += grad_scores[
                    a * TILE : (a + 1) * TILE, r * TILE : (r + 1) * TILE
                ].astype(f32)
        gk_sum[spot, :] += jnp.dot(grad_scores, queries, preferred_element_type=f32)

        def column(ct, _):
            at = pl.ds(pl.multiple_of(ct * 512, 512), 512)
            gv_sum[spot, at] += jnp.dot(
                probs, grad_ref[0, :, at], preferred_element_type=f32
            )
            return 0

        lax.fori_loop(0, value_width // 512, column, 0)
        return grad_query + lax.dot_general(
            grad_scores, keys[spot, :], tn, preferred_element_type=f32
        )

    grad_query = lax.fori_loop(0, reach, second, jnp.zeros((length, key_width), f32))
    gq_ref[0] = grad_query * scale

    @pl.when(step == pl.num_programs(0) - 1)
    def _():
        for slot in range(total):
            place = pl.ds(pl.multiple_of(table_ref[slot] * length, length), length)
            key_grad = (gk_sum[place, :] * scale).astype(bf16)
            value_grad = gv_sum[place, :].astype(bf16)
            if slot < 2:
                gk_own[slot] = key_grad
                gv_own[slot] = value_grad
            else:
                both_oth[slot - 2, :, :value_width] = value_grad
                both_oth[slot - 2, :, value_width:] = key_grad
        down = lax.broadcasted_iota(jnp.int32, (TILE, TILE), 0)
        across = lax.broadcasted_iota(jnp.int32, (TILE, TILE), 1)
        mirror = jnp.where(down + across == TILE - 1, 1.0, 0.0)
        for d in range(rel_out.shape[0]):
            flipped = jnp.dot(
                rel_ref[d + tiles - 1],
                mirror,
                precision=lax.Precision.HIGHEST,
                preferred_element_type=f32,
            )
            wide = jnp.concatenate([flipped, jnp.zeros((TILE, TILE), f32)], axis=1)
            turned = pltpu.roll(wide, 0, 1, stride=1, stride_axis=0)
            rel_out[d] = jnp.sum(turned, axis=0, keepdims=True)


def attend_back(table, q, grads, lse, bias, k_own, k_oth, v_own, v_oth, after=()):
    slots, length, key_width = q.shape
    value_width = v_own.shape[2]
    total = slots + k_oth.shape[0]
    rel_shape = (total * length // TILE, 1, 2 * TILE)
    both_shape = (k_oth.shape[0], length, key_width + value_width)
    anywhere = pl.BlockSpec(memory_space=pl.ANY)

    def all_of(shape):
        return pl.BlockSpec(
            shape, lambda k, t: (0,) * len(shape), pipeline_mode=pl.Buffered(1)
        )

    return pl.pallas_call(
        ignoring(functools.partial(attend_back_body, total=total), 9, len(after)),
        grid_spec=pltpu.PrefetchScalarGridSpec(
            num_scalar_prefetch=1,
            grid=(slots,),
            in_specs=[
                pl.BlockSpec((1, length, key_width), lambda k, t: (k, 0, 0)),
                pl.BlockSpec((1, length, value_width), lambda k, t: (k, 0, 0)),
                pl.BlockSpec((1, 1, length), lambda k, t: (k, 0, 0)),
                all_of(bias.shape),
                anywhere,
                anywhere,
                anywhere,
                anywhere,
            ]
            + [anywhere] * len(after),
            out_specs=[
                pl.BlockSpec((1, length, key_width), lambda k, t: (k, 0, 0)),
                all_of(k_own.shape),
                all_of(v_own.shape),
                all_of(both_shape),
                all_of(rel_shape),
            ],
            scratch_shapes=[
                pltpu.VMEM((total * length, key_width), bf16),
                pltpu.VMEM((total * length, value_width), bf16),
                pltpu.VMEM((total * length, key_width), f32),
                pltpu.VMEM((total * length, value_width), f32),
                pltpu.VMEM((total, length, length), f32),
                pltpu.VMEM((total, length, length), f32),
                pltpu.VMEM(bias.shape, f32),
                pltpu.SemaphoreType.DMA((total,)),
                pltpu.SemaphoreType.DMA((total,)),
            ],
        ),
        out_shape=[
            jax.ShapeDtypeStruct((slots, length, key_width), f32),
            jax.ShapeDtypeStruct(k_own.shape, bf16),
            jax.ShapeDtypeStruct(v_own.shape, bf16),
            jax.ShapeDtypeStruct(both_shape, bf16),
            jax.ShapeDtypeStruct(rel_shape, f32),
        ],
        compiler_params=params(("arbitrary",)),
        name="attend_back",
        cost_estimate=LONG,
    )(table, q, grads, lse, bias, k_own, k_oth, v_own, v_oth, *after)


def bias_body(flag_ref, back_row, front_row, back_ref, front_ref, *, spare):
    tile = pl.program_id(0) - spare
    full = flag_ref[0] == 1

    @pl.when(tile < 0)
    def _():
        back_ref[...] = jnp.full_like(back_ref, MASKED)
        front_ref[...] = jnp.full_like(front_ref, MASKED)

    @pl.when(tile >= 0)
    def _():
        down = lax.broadcasted_iota(jnp.int32, (TILE, TILE), 0)
        across = lax.broadcasted_iota(jnp.int32, (TILE, TILE), 1)
        near = jnp.where(down // STRETCH == across // STRETCH, 1, 0)
        for row, out, ordered in (
            (back_row, back_ref, jnp.where(down <= across, 1, 0)),
            (front_row, front_ref, jnp.where(across <= down, 1, 0)),
        ):
            wide = jnp.broadcast_to(row[0], (TILE, 2 * TILE))
            turned = pltpu.roll(wide, 0, 1, stride=1, stride_axis=0)[:, :TILE]
            allowed = jnp.where(
                tile == 0, jnp.where(full, ordered, ordered * near), jnp.where(full, 1, 0)
            )
            out[0] = jnp.where(allowed == 1, turned, MASKED)


def bias_tiles(relative_bias, spare, full):
    length = relative_bias.shape[0] // 2
    count = length // TILE
    windows = jnp.stack(
        [
            lax.slice_in_dim(relative_bias, length - d * TILE - TILE, length - d * TILE + TILE)
            for d in range(count)
        ]
    )
    front = jnp.concatenate([windows[:, TILE:], windows[:, :TILE]], axis=1)
    back = jnp.concatenate([windows[:, TILE:TILE + 1], windows[:, ::-1][:, TILE:], windows[:, ::-1][:, : TILE - 1]], axis=1)
    row = pl.BlockSpec((1, 1, 2 * TILE), lambda d, t: (jnp.maximum(d - spare, 0), 0, 0))
    out = pl.BlockSpec((1, TILE, TILE), lambda d, t: (d, 0, 0))
    shape = jax.ShapeDtypeStruct((spare + count, TILE, TILE), f32)
    return pl.pallas_call(
        functools.partial(bias_body, spare=spare),
        grid_spec=pltpu.PrefetchScalarGridSpec(
            num_scalar_prefetch=1,
            grid=(spare + count,),
            in_specs=[row, row],
            out_specs=[out, out],
        ),
        out_shape=[shape, shape],
        compiler_params=params(("arbitrary",)),
        name="bias",
    )(full.astype(jnp.int32)[None], back[:, None], front[:, None])


def bias_grad(sums, length):
    count = sums.shape[0]
    shifted = jnp.concatenate([jnp.zeros((count, 1), f32), sums[:, :-1]], axis=1)
    none = jnp.zeros((1, TILE), f32)
    blocks = jnp.concatenate([none, shifted[:, :TILE]]) + jnp.concatenate(
        [shifted[:, TILE:], none]
    )
    return jnp.concatenate(
        [blocks[::-1].reshape(-1), jnp.zeros((2 * length - (count + 1) * TILE,), f32)]
    )


def gate_body(
    back_ref,
    cot_a,
    cot_b,
    x_ref,
    cand_ref,
    update_ref,
    reset_ref,
    attended_ref,
    gain_ref,
    proj_ref,
    input_ref,
    main_ref,
    grad_att_ref,
    gain_grad_ref,
):
    width = x_ref.shape[1]
    value_width = proj_ref.shape[0]

    @pl.when(pl.program_id(0) == 0)
    def _():
        gain_grad_ref[...] = jnp.zeros_like(gain_grad_ref)

    x = x_ref[...].astype(f32)
    cand_in = cand_ref[...]
    gate = jax.nn.sigmoid(cand_in)
    candidate = cand_in * gate
    update = jax.nn.sigmoid(update_ref[...].astype(f32))
    change = candidate - x
    unit, inv = unit_rows_of(x + update * change)
    grad_feed = back_ref[...]
    gain_grad_ref[...] += jnp.sum(grad_feed * unit, axis=0, keepdims=True)
    early = pl.program_id(0) < pl.num_programs(0) // 2
    cot = jnp.where(early, cot_a[...].astype(f32), cot_b[...].astype(f32))
    grad_first = cot + norm_back_rows(
        grad_feed, gain_ref[...], unit, inv
    )
    kept = grad_first * (1.0 - update)
    input_ref[...] = kept
    main_ref[:, value_width : value_width + width] = (kept * change * update).astype(bf16)
    grad_cand = (grad_first * update * (gate + candidate * (1.0 - gate))).astype(bf16)
    main_ref[:, value_width + width :] = grad_cand
    for c in range(value_width // 512):
        at = slice(c * 512, (c + 1) * 512)
        grad_gated = mm_nt(grad_cand, proj_ref[at, :])
        reset = reset_ref[:, at].astype(f32)
        open_gate = jax.nn.sigmoid(reset)
        passed = reset * open_gate
        grad_att_ref[:, at] = (grad_gated * passed).astype(bf16)
        main_ref[:, at] = (
            grad_gated
            * attended_ref[:, at].astype(f32)
            * (open_gate + passed * (1.0 - open_gate))
        ).astype(bf16)


def gate(back, cots, x, cand_in, base, attended, gain, proj, after=()):
    tokens, width = x.shape
    value_width = proj.shape[0]
    rows = min(256, tokens // 2)
    half = tokens // rows // 2
    wide = value_width // width

    def block(columns, at=0):
        return pl.BlockSpec((rows, columns), lambda i: (i, at))

    return pl.pallas_call(
        ignoring(gate_body, 10, len(after)),
        grid=(tokens // rows,),
        in_specs=[
            block(width),
            pl.BlockSpec((rows, width), lambda i: (jnp.minimum(i, half - 1), 0)),
            pl.BlockSpec((rows, width), lambda i: (jnp.maximum(i - half, 0), 0)),
            block(width),
            block(width),
            block(width, wide),
            block(value_width),
            block(value_width),
            pl.BlockSpec((1, width), lambda i: (0, 0)),
            pl.BlockSpec(proj.shape, lambda i: (0, 0), pipeline_mode=pl.Buffered(1)),
        ]
        + [pl.BlockSpec(memory_space=pl.ANY)] * len(after),
        out_specs=[
            block(width),
            block(value_width + 2 * width),
            block(value_width),
            pl.BlockSpec((1, width), lambda i: (0, 0)),
        ],
        out_shape=[
            jax.ShapeDtypeStruct((tokens, width), f32),
            jax.ShapeDtypeStruct((tokens, value_width + 2 * width), bf16),
            jax.ShapeDtypeStruct((tokens, value_width), bf16),
            jax.ShapeDtypeStruct((1, width), f32),
        ],
        compiler_params=params(("arbitrary",)),
        name="gate",
        cost_estimate=LONG,
    )(back, *cots, x, cand_in, base, base, attended, gain, proj, *after)


def ordered_transpose(ids_ref, source, plain, ordered):
    plain[...] = source[...].T
    count = ids_ref.shape[0]
    rows = plain.shape[0] // count

    def place(p, _):
        ordered[pl.ds(pl.multiple_of(p * rows, rows), rows), :] = plain[
            pl.ds(pl.multiple_of(ids_ref[p] * rows, rows), rows), :
        ]
        return 0

    lax.fori_loop(0, count, place, 0)


def placed_transpose(places_ref, sources, plain, ordered):
    start = 0
    for source in sources:
        plain[:, start : start + source.shape[0]] = source[...].T
        start += source.shape[0]
    count = places_ref.shape[0]
    rows = plain.shape[0] // count

    def place(q, _):
        ordered[pl.ds(pl.multiple_of(places_ref[q] * rows, rows), rows), :] = plain[
            pl.ds(pl.multiple_of(q * rows, rows), rows), :
        ]
        return 0

    lax.fori_loop(0, count, place, 0)


def feed_body(
    ids_ref,
    places_ref,
    low_ref,
    cot_a,
    cot_b,
    first_ref,
    in_ref,
    out_ref,
    result_a,
    result_b,
    back_ref,
    out_send,
    out_keep,
    in_send,
    in_keep,
    total,
    cot_turned,
    low_turned,
    plain,
):
    step = pl.program_id(0)
    half = pl.num_programs(0) // 2
    tokens = low_ref.shape[0]
    middle = tokens // 2
    nt = (((1,), (1,)), ((), ()))

    @pl.when(step == 0)
    def _():
        placed_transpose(places_ref, (cot_a, cot_b), plain, cot_turned)
        ordered_transpose(ids_ref, low_ref, plain, low_turned)
        total[...] = first_ref[...]
        back_ref[...] = jnp.zeros_like(back_ref)

    acts, grads = [], []
    for r, cot_ref in enumerate((cot_a, cot_b)):
        at = slice(r * middle, (r + 1) * middle)
        hidden = jnp.dot(low_ref[at, :], in_ref[...], preferred_element_type=f32)
        grad_act = lax.dot_general(
            cot_ref[...], out_ref[...], nt, preferred_element_type=f32
        )
        gate = jax.nn.sigmoid(hidden)
        act = hidden * gate
        grad = (grad_act * (gate + act * (1.0 - gate))).astype(bf16)
        act = act.astype(bf16)
        total[at, :] += jnp.dot(act, out_ref[...], preferred_element_type=f32)
        back_ref[at, :] += lax.dot_general(
            grad, in_ref[...], nt, preferred_element_type=f32
        )
        acts.append(act)
        grads.append(grad)
    out_grad = jnp.dot(
        cot_turned[...], jnp.concatenate(acts), preferred_element_type=f32
    ).astype(bf16)
    in_grad = jnp.dot(
        low_turned[...], jnp.concatenate(grads), preferred_element_type=f32
    ).astype(bf16)
    split = in_grad.shape[0] // 2
    in_send[...] = in_grad[:split].reshape(in_send.shape)
    in_keep[...] = in_grad[split:].reshape(in_keep.shape)

    @pl.when(step < half)
    def _():
        out_send[0] = out_grad

    @pl.when(step >= half)
    def _():
        out_keep[0] = out_grad

    @pl.when(step == pl.num_programs(0) - 1)
    def _():
        result_a[...] = total[:middle, :].astype(bf16)
        result_b[...] = total[middle:, :].astype(bf16)


def feed(ids, places, low, cots, first_sum, feed_in, feed_out, seq, after=()):
    tokens, width = low.shape
    features = feed_in.shape[1]
    parts = ids.shape[0]
    half = parts // 2
    columns = features // parts
    rows = width // parts
    share = parts // seq
    anywhere = pl.BlockSpec(memory_space=pl.ANY)

    def all_of(shape):
        return pl.BlockSpec(
            shape, lambda i, t, u: (0,) * len(shape), pipeline_mode=pl.Buffered(1)
        )

    def at(i, t):
        return t[jnp.minimum(i, parts - 1)]

    split = pl.BlockSpec(
        (half, 1, 1, rows, columns),
        lambda i, t, u: (0, u[at(i, t) // share], at(i, t) % share, 0, 0),
    )
    return pl.pallas_call(
        ignoring(feed_body, 8, len(after)),
        grid_spec=pltpu.PrefetchScalarGridSpec(
            num_scalar_prefetch=2,
            grid=(parts,),
            in_specs=[
                all_of(low.shape),
                all_of(cots[0].shape),
                all_of(cots[1].shape),
                all_of(first_sum.shape),
                pl.BlockSpec((width, columns), lambda i, t, u: (0, at(i, t))),
                pl.BlockSpec((columns, width), lambda i, t, u: (at(i, t), 0)),
            ]
            + [anywhere] * len(after),
            out_specs=[
                all_of(cots[0].shape),
                all_of(cots[1].shape),
                all_of(low.shape),
                pl.BlockSpec(
                    (1, width, columns), lambda i, t, u: (jnp.minimum(i, half - 1), 0, 0)
                ),
                pl.BlockSpec(
                    (1, width, columns), lambda i, t, u: (jnp.maximum(i - half, 0), 0, 0)
                ),
                split,
                split,
            ],
            scratch_shapes=[
                pltpu.VMEM((tokens, width), f32),
                pltpu.VMEM((width, tokens), bf16),
                pltpu.VMEM((width, tokens), bf16),
                pltpu.VMEM((width, tokens), bf16),
            ],
        ),
        out_shape=[
            jax.ShapeDtypeStruct(cots[0].shape, bf16),
            jax.ShapeDtypeStruct(cots[1].shape, bf16),
            jax.ShapeDtypeStruct((tokens, width), f32),
            jax.ShapeDtypeStruct((half, width, columns), bf16),
            jax.ShapeDtypeStruct((half, width, columns), bf16),
            jax.ShapeDtypeStruct((half, seq, share, rows, columns), bf16),
            jax.ShapeDtypeStruct((half, seq, share, rows, columns), bf16),
        ],
        compiler_params=params(("arbitrary",)),
        name="feed",
        cost_estimate=BRIEF,
    )(ids, places, low, *cots, first_sum, feed_in, feed_out, *after)


def product_body(left_ref, right_ref, out_ref):
    out_ref[...] = jnp.dot(
        left_ref[...], right_ref[...], preferred_element_type=f32
    ).astype(out_ref.dtype)


def product(left, right, tile=1024):
    tokens, depth = left.shape
    columns = right.shape[1]
    return pl.pallas_call(
        product_body,
        grid=(columns // tile,),
        in_specs=[
            pl.BlockSpec(left.shape, lambda i: (0, 0), pipeline_mode=pl.Buffered(1)),
            pl.BlockSpec((depth, tile), lambda i: (0, i)),
        ],
        out_specs=pl.BlockSpec((tokens, tile), lambda i: (0, i)),
        out_shape=jax.ShapeDtypeStruct((tokens, columns), bf16),
        compiler_params=params(("arbitrary",)),
        name="product",
        cost_estimate=BRIEF,
    )(left, right)


def by_columns_body(ids_ref, places_ref, left_ref, right_ref, send, keep, plain, turned):
    step = pl.program_id(0)
    half = pl.num_programs(0) // 2

    @pl.when(step == 0)
    def _():
        placed_transpose(places_ref, (left_ref,), plain, turned)

    grad = jnp.dot(turned[...], right_ref[...], preferred_element_type=f32).astype(bf16)

    @pl.when(step < half)
    def _():
        send[0] = grad

    @pl.when(step >= half)
    def _():
        keep[0] = grad


def by_columns(ids, places, left, right, after=(), rows=None, at=0):
    tokens = left.shape[0]
    rows = rows or left.shape[1]
    parts = ids.shape[0]
    half = parts // 2
    columns = right.shape[1] // parts
    shape = jax.ShapeDtypeStruct((half, rows, columns), bf16)
    if columns % 128:
        left = left[:, at * rows : (at + 1) * rows]
        grad = mm_tn(left, right).astype(bf16).reshape(rows, parts, columns)
        grad = jnp.take(grad, ids, axis=1).transpose(1, 0, 2)
        grad = grad.reshape(parts, places.shape[0], -1, columns)
        grad = jnp.take(grad, jnp.argsort(places), axis=1).reshape(parts, rows, columns)
        return grad[:half], grad[half:]
    return pl.pallas_call(
        ignoring(by_columns_body, 4, len(after)),
        grid_spec=pltpu.PrefetchScalarGridSpec(
            num_scalar_prefetch=2,
            grid=(parts,),
            in_specs=[
                pl.BlockSpec(
                    (tokens, rows), lambda i, t, u: (0, at), pipeline_mode=pl.Buffered(1)
                ),
                pl.BlockSpec((tokens, columns), lambda i, t, u: (0, t[jnp.minimum(i, parts - 1)])),
            ]
            + [pl.BlockSpec(memory_space=pl.ANY)] * len(after),
            out_specs=[
                pl.BlockSpec(
                    (1, rows, columns), lambda i, t, u: (jnp.minimum(i, half - 1), 0, 0)
                ),
                pl.BlockSpec(
                    (1, rows, columns), lambda i, t, u: (jnp.maximum(i - half, 0), 0, 0)
                ),
            ],
            scratch_shapes=[
                pltpu.VMEM((rows, tokens), bf16),
                pltpu.VMEM((rows, tokens), bf16),
            ],
        ),
        out_shape=[shape, shape],
        compiler_params=params(("arbitrary",)),
        name="by_columns",
        cost_estimate=BRIEF,
    )(ids, places, left, right, *after)


def by_rows_body(ids_ref, places_ref, left_ref, right_ref, send, keep, plain, turned):
    @pl.when(pl.program_id(0) == 0)
    def _():
        ordered_transpose(ids_ref, left_ref, plain, turned)

    grad = jnp.dot(turned[...], right_ref[...], preferred_element_type=f32).astype(bf16)
    middle = grad.shape[0] // 2
    send[...] = grad[:middle].reshape(send.shape)
    keep[...] = grad[middle:].reshape(keep.shape)


def by_rows(ids, places, left, right, seq=1, after=(), cost=BRIEF):
    tokens, rows = left.shape
    parts = ids.shape[0]
    half = parts // 2
    if places is None:
        seq, places = 1, jnp.zeros((1,), jnp.int32)
    columns = right.shape[1] // seq
    tile = min(512, columns)
    share = columns // tile
    shape = jax.ShapeDtypeStruct((half, seq, rows // parts, columns), bf16)
    split = pl.BlockSpec(
        (half, 1, rows // parts, tile), lambda i, t, u: (0, u[jnp.minimum(i // share, seq - 1)], 0, i % share)
    )
    return pl.pallas_call(
        ignoring(by_rows_body, 4, len(after)),
        grid_spec=pltpu.PrefetchScalarGridSpec(
            num_scalar_prefetch=2,
            grid=(seq * share,),
            in_specs=[
                pl.BlockSpec(
                    left.shape, lambda i, t, u: (0, 0), pipeline_mode=pl.Buffered(1)
                ),
                pl.BlockSpec((tokens, tile), lambda i, t, u: (0, i)),
            ]
            + [pl.BlockSpec(memory_space=pl.ANY)] * len(after),
            out_specs=[split, split],
            scratch_shapes=[
                pltpu.VMEM((rows, tokens), bf16),
                pltpu.VMEM((rows, tokens), bf16),
            ],
        ),
        out_shape=[shape, shape],
        compiler_params=params(("arbitrary",)),
        name="by_rows",
        cost_estimate=cost,
    )(ids, places, left, right, *after)


def value_back_body(
    ids_ref,
    places_ref,
    left_ref,
    own_ref,
    other_ref,
    slope_ref,
    proj_ref,
    total_ref,
    send,
    keep,
    plain,
    turned,
):
    @pl.when(pl.program_id(0) == 0)
    def _():
        total_ref[...] = jnp.zeros_like(total_ref)
        ordered_transpose(ids_ref, left_ref, plain, turned)

    grad = own_ref[...].astype(f32)
    for k in range(other_ref.shape[0]):
        grad = grad + other_ref[k].astype(f32)
    grad = (grad * slope_ref[...].astype(f32)).astype(bf16)
    total_ref[...] += mm_nt(grad, proj_ref[...])
    weights = jnp.dot(turned[...], grad, preferred_element_type=f32).astype(bf16)
    middle = weights.shape[0] // 2
    send[...] = weights[:middle].reshape(send.shape)
    keep[...] = weights[middle:].reshape(keep.shape)


def value_back(ids, places, left, own, others, slope, proj, seq, after=()):
    tokens, rows = left.shape
    parts = ids.shape[0]
    half = parts // 2
    columns = proj.shape[1] // seq
    tile = min(512, columns)
    share = columns // tile
    shape = jax.ShapeDtypeStruct((half, seq, rows // parts, columns), bf16)
    split = pl.BlockSpec(
        (half, 1, rows // parts, tile),
        lambda i, t, u: (0, u[jnp.minimum(i // share, seq - 1)], 0, i % share),
    )
    stripe = pl.BlockSpec((tokens, tile), lambda i, t, u: (0, i))
    fixed = pl.BlockSpec(
        (tokens, rows), lambda i, t, u: (0, 0), pipeline_mode=pl.Buffered(1)
    )
    return pl.pallas_call(
        ignoring(value_back_body, 7, len(after)),
        grid_spec=pltpu.PrefetchScalarGridSpec(
            num_scalar_prefetch=2,
            grid=(seq * share,),
            in_specs=[
                fixed,
                stripe,
                pl.BlockSpec((others.shape[0], tokens, tile), lambda i, t, u: (0, 0, i)),
                stripe,
                pl.BlockSpec((rows, tile), lambda i, t, u: (0, i)),
            ]
            + [pl.BlockSpec(memory_space=pl.ANY)] * len(after),
            out_specs=[fixed, split, split],
            scratch_shapes=[
                pltpu.VMEM((rows, tokens), bf16),
                pltpu.VMEM((rows, tokens), bf16),
            ],
        ),
        out_shape=[jax.ShapeDtypeStruct((tokens, rows), f32), shape, shape],
        compiler_params=params(("arbitrary",)),
        name="value_back",
        cost_estimate=LONG,
    )(ids, places, left, own, others, slope, proj, *after)


def stage_body(*refs, shapes):
    count = sum(pairs for pairs, _, _ in shapes)
    ins, outs = list(refs[: 2 * count]), list(refs[2 * count :])
    for pairs, halves, turned in shapes:
        into = [outs.pop(0) for _ in range(halves)]
        start = 0
        for _ in range(pairs):
            kept, arrived = ins.pop(0), ins.pop(0)
            stop = start + kept.shape[0]
            for part, out in enumerate(into):
                total = kept[:, part].astype(f32) + arrived[:, part].astype(f32)
                if turned:
                    out[0] = total[0].T
                else:
                    out[start:stop] = total.astype(out.dtype)
            start = stop


def stage_sums(groups, after=(), steps=4, cost=BRIEF):
    shapes, ins, in_specs, out_specs, out_shapes, whole = [], [], [], [], [], []
    for pairs, single, kind in groups:
        _, n, rows, _ = pairs[0][0].shape
        lanes = 128 if kind == "turned" else 16
        while (n * rows // (1 if single else 2)) % (lanes * steps) and steps > 1:
            steps //= 2
    for pairs, single, kind in groups:
        halves = 1 if single else 2
        g, n, rows, columns = pairs[0][0].shape
        each = n * rows // halves // steps
        shapes.append((len(pairs), halves, kind == "turned"))
        for pair in pairs:
            for v in pair:
                ins.append(v.reshape(g, halves, n * rows // halves, columns))
                in_specs.append(
                    pl.BlockSpec((g, halves, each, columns), lambda i: (0, 0, i, 0))
                )
        if kind == "turned":
            out_specs.append(pl.BlockSpec((1, columns, each), lambda i: (0, 0, i)))
            out_shapes.append(jax.ShapeDtypeStruct((1, columns, rows), f32))
            whole.append((1, (1, 1, columns, rows)))
            continue
        for _ in range(halves):
            out_specs.append(pl.BlockSpec((len(pairs) * g, each, columns), lambda i: (0, i, 0)))
            out_shapes.append(
                jax.ShapeDtypeStruct((len(pairs) * g, n * rows // halves, columns), kind)
            )
        whole.append((halves, (len(pairs) * g, n // halves, rows, columns)))
    sums = list(
        pl.pallas_call(
            ignoring(functools.partial(stage_body, shapes=shapes), len(ins), len(after)),
            grid=(steps,),
            in_specs=in_specs + [pl.BlockSpec(memory_space=pl.ANY)] * len(after),
            out_specs=out_specs,
            out_shape=out_shapes,
            compiler_params=params(("arbitrary",)),
            name="stage_sums",
            cost_estimate=cost,
        )(*ins, *after)
    )
    return [tuple(sums.pop(0).reshape(shape) for _ in range(halves)) for halves, shape in whole]


class Layout:
    def __init__(self, mesh):
        self.dp = mesh.shape["dp"]
        self.seq = mesh.shape["seq"]
        self.members = self.seq // 2
        self.chips = self.seq // 4

    def pairs(self, move):
        return [
            (d * self.seq + z, e * self.seq + w)
            for d in range(self.dp)
            for z in range(self.seq)
            for e, w in [move(d, z)]
        ]

    def send(self, value, move):
        return lax.ppermute(value, AXES, self.pairs(move))

    def place(self, sequence, member):
        return member % 2 ^ (1 - sequence % 2), sequence * self.chips + member // 2

    def member(self, core, z):
        sequence = z // self.chips
        return (z % self.chips) * 2 + (core ^ (1 - sequence % 2))

    def home_to_work(self, round_index):
        def move(d, z):
            part = (1 if z >= self.seq // 2 else 0) ^ round_index
            core, at = self.place(2 * (d % 2) + part, min(z, self.seq - 1 - z))
            return d - d % 2 + core, at

        return move

    def spread(self, value):
        late = lax.axis_index("seq") >= self.seq // 2
        out = []
        for round_index in range(2):
            sent = lax.dynamic_index_in_dim(
                value, jnp.where(late, 1 - round_index, round_index), 0, False
            )
            out.append(self.send(sent, self.home_to_work(round_index)))
        return out

    def homeward(self, value, round_index):
        pairs = [(b, a) for a, b in self.pairs(self.home_to_work(round_index))]
        return lax.ppermute(value, AXES, pairs)

    def gathered(self, back):
        late = lax.axis_index("seq") >= self.seq // 2
        return jnp.stack([jnp.where(late, back[1], back[0]), jnp.where(late, back[0], back[1])])

    def collect(self, values):
        return self.gathered([self.homeward(v, r) for r, v in enumerate(values)])

    def rotate(self, value, by):
        def move(d, z):
            member = (self.member(d % 2, z) + by) % self.members
            core, at = self.place(z // self.chips, member)
            return d - d % 2 + core, at

        return self.send(value, move)

    def gather(self, value):
        return jnp.concatenate([self.rotate(value, by) for by in range(1, self.members)], axis=0)

    def returns(self, others):
        slots = others.shape[0] // (self.members - 1)
        return jnp.stack(
            [
                self.rotate(others[(by - 1) * slots : by * slots], self.members - by).reshape(
                    -1, others.shape[-1]
                )
                for by in range(1, self.members)
            ]
        )

    def orders(self):
        dp, z = lax.axis_index("dp"), lax.axis_index("seq")
        bits = self.dp.bit_length() - 1
        ids = []
        for core in range(2):
            orders = [[0, *range(1, bits)], [0, *reversed(range(1, bits))]]
            flips = []
            for p in range(self.dp):
                order = orders[core if p >= self.dp // 2 else 1 - core]
                flips.append(
                    sum(
                        (0 if p >> (bits - 1 - i) & 1 else 1) << bit
                        for i, bit in enumerate(order)
                    )
                )
            ids.append(dp ^ jnp.array(flips, jnp.int32))
        ids = jnp.where(dp % 2 == 0, ids[0], ids[1])
        bits = self.seq.bit_length() - 1
        flips = [
            sum((0 if p >> (bits - 1 - i) & 1 else 1) << i for i in range(bits))
            for p in range(self.seq)
        ]
        blocks = z ^ jnp.array(flips, jnp.int32)
        return ids, jnp.argsort(blocks).astype(jnp.int32), blocks

    def partner(self, stage):
        bits = self.dp.bit_length() - 1
        if stage == 0:
            return lambda d, z: (d ^ 1, z)
        if stage < bits:
            return lambda d, z: (d ^ (1 << stage if d % 2 == 0 else 1 << (bits - stage)), z)
        return lambda d, z: (d, z ^ (1 << (stage - bits)))

    def turn(self, sums, after, cost=BRIEF):
        sums = [s for s in sums if s.arrived]
        if not sums:
            return after
        dp_stages = self.dp.bit_length() - 1
        last = dp_stages + self.seq.bit_length() - 1
        groups = []
        for s in sums:
            pairs = list(zip(s.kept, s.arrived))
            single = s.stage + 1 == last
            if s.stage + 1 == dp_stages:
                single = not s.over_seq
                if s.over_seq:
                    pairs = [
                        tuple(
                            v.reshape(v.shape[0], self.seq, -1, v.shape[-1]) for v in pair
                        )
                        for pair in pairs
                    ]
            kind = bf16
            if s.stage + 1 == last:
                kind = "turned" if s.turned else f32
            groups.append((pairs, single, kind))
        out = stage_sums(groups, after, cost=cost)
        for s, held, (_, single, _) in zip(sums, out, groups):
            s.stage += 1
            s.arrived = ()
            if single:
                s.total = held[0]
            else:
                s.send([held[0]], [held[1]])
        return [part for held in out for part in held]

    def over_seq(self, held):
        core = lax.axis_index("dp") % 2
        split = held.reshape(2, -1, held.shape[-1])
        held = lax.dynamic_index_in_dim(split, core, 0, False)
        for bit in range(self.seq.bit_length() - 1):
            held = held + self.send(held, lambda d, z: (d, z ^ (1 << bit)))
        return held, self.send(held, lambda d, z: (d ^ 1, z))


    def over_dp(self, held):
        bits = self.dp.bit_length() - 1
        for bit in range(bits - 1):
            held = held + self.send(held, lambda d, z: (d ^ (1 << bit), z))
        return held, self.send(held, lambda d, z: (d ^ (1 << (bits - 1)), z))


def later_body(left, right, out):
    out[...] = left[...] + right[...]


def later_sum(left, right, after):
    inside = pl.BlockSpec(memory_space=pltpu.VMEM)
    return pl.pallas_call(
        ignoring(later_body, 2, len(after)),
        in_specs=[inside] * 2 + [pl.BlockSpec(memory_space=pl.ANY)] * len(after),
        out_specs=inside,
        out_shape=jax.ShapeDtypeStruct(left.shape, left.dtype),
        name="later_sum",
        cost_estimate=BRIEF,
    )(left, right, *after)


def pack_body(qx_a, qx_b, qs_a, qs_b, rest_ref, out):
    rows = qx_a.shape[0]
    out[:rows] = qx_a[...] + qx_b[...]
    out[rows : 2 * rows] = qs_a[...] + qs_b[...]
    out[2 * rows :] = rest_ref[...]


def pack(first, second, rest, after=()):
    ins = [v.reshape(-1, 128) for v in (first[0], second[0], first[1], second[1])] + [rest]
    rows = 2 * ins[0].shape[0] + rest.shape[0]
    inside = pl.BlockSpec(memory_space=pltpu.VMEM)
    return pl.pallas_call(
        ignoring(pack_body, 5, len(after)),
        in_specs=[inside] * 5 + [pl.BlockSpec(memory_space=pl.ANY)] * len(after),
        out_specs=inside,
        out_shape=jax.ShapeDtypeStruct((rows, 128), f32),
        name="pack",
        cost_estimate=BRIEF,
    )(*ins, *after)


def finish_body(
    core_ref, mine, other, alpha, damp, beta, eta, alpha_out, damp_out, beta_out, eta_out, rest, rows
):
    half = mine.shape[0]
    first = core_ref[0] == 0
    rows[:half] = jnp.where(first, mine[...], other[...])
    rows[half:] = jnp.where(first, other[...], mine[...])
    states = alpha.shape[0]
    groups = alpha.shape[1] // 128
    for c in range(groups):
        at = slice(c * 128, (c + 1) * 128)
        x_sum = rows[pl.ds(c, states, stride=groups), :]
        s_sum = rows[pl.ds(states * groups + c, states, stride=groups), :]
        rate = alpha[:, at] * beta[:, at]
        input_total = eta[:, at] * x_sum
        decay_total = eta[:, at] * rate * s_sum
        alpha_out[:, at] = beta[:, at] * input_total - damp[:, at] * decay_total
        damp_out[:, at] = -alpha[:, at] * decay_total
        beta_out[:, at] = alpha[:, at] * input_total
        eta_out[:, at] = rate * x_sum
    rest[...] = rows[2 * states * groups :]


def finish(core, mine, other, alpha, damp, beta, eta):
    inside = pl.BlockSpec(memory_space=pltpu.VMEM)
    rows = 2 * mine.shape[0]
    shape = jax.ShapeDtypeStruct(alpha.shape, f32)
    left = rows - 2 * alpha.size // 128
    return pl.pallas_call(
        finish_body,
        in_specs=[pl.BlockSpec(memory_space=pltpu.SMEM)] + [inside] * 6,
        out_specs=[inside] * 5,
        out_shape=[shape] * 4 + [jax.ShapeDtypeStruct((left, 128), f32)],
        scratch_shapes=[pltpu.VMEM((rows, 128), f32)],
        name="finish",
        cost_estimate=BRIEF,
    )(core[None].astype(jnp.int32), mine, other, alpha, damp, beta, eta)


class Sum:
    def __init__(self, layout, *pairs, over_seq=True, turned=False):
        self.layout, self.over_seq, self.stage = layout, over_seq, 0
        self.turned = turned
        self.total = None
        pairs = [[v.reshape(1, v.shape[0], -1, v.shape[-1]) for v in pair] for pair in pairs]
        self.send([p[0] for p in pairs], [p[1] for p in pairs])

    def send(self, sent, kept):
        self.kept = kept
        self.arrived = [self.layout.send(v, self.layout.partner(self.stage)) for v in sent]

    def begin_seq(self, block):
        self.total = None
        middle = self.layout.seq // 2
        self.send([block[None, :middle]], [block[None, middle:]])


def mm(a, b):
    return jnp.dot(a, b, preferred_element_type=f32)


def mm_nt(a, b):
    return lax.dot_general(a, b, (((1,), (1,)), ((), ())), preferred_element_type=f32)


def mm_tn(a, b):
    return lax.dot_general(a, b, (((0,), (0,)), ((), ())), preferred_element_type=f32)


def layer(
    layout,
    inputs,
    cotangent,
    full_attention,
    mix_gain,
    smooth_alpha,
    smooth_damp,
    smooth_beta,
    smooth_eta,
    smooth_omega,
    value_proj,
    mix_proj,
    score_affine,
    relative_bias,
    out_proj,
    feed_gain,
    feed_in,
    feed_out,
):
    slots, chunk_rows, width = inputs.shape
    key_width = score_affine.shape[1]
    value_width = value_proj.shape[1]
    tokens = slots * chunk_rows
    total = layout.seq
    seq_length = relative_bias.shape[0] // 2
    block = min(128, chunk_rows)
    core = lax.axis_index("dp") % 2
    z = lax.axis_index("seq")

    sequence = z // layout.chips
    member = layout.member(core, z)
    swap = sequence % 2
    chunks = []
    for by in range(layout.members):
        source = (member - by) % layout.members
        low, high = source, total - 1 - source
        chunks += [jnp.where(swap == 0, low, high), jnp.where(swap == 0, high, low)]
    chunks = jnp.stack(chunks).astype(jnp.int32)
    slot_of = jnp.sum(
        jnp.where(chunks[None, :] == jnp.arange(total)[:, None], jnp.arange(total)[None, :], 0),
        axis=1,
    ).astype(jnp.int32)
    flags = full_attention.astype(f32)
    flags_other = layout.send(flags, lambda d, z: (d ^ 1, z))
    flags = jnp.where(
        core == 0, jnp.concatenate([flags, flags_other]), jnp.concatenate([flags_other, flags])
    )
    full = lax.dynamic_index_in_dim(flags, sequence, 0, False) == 1.0
    table = jnp.concatenate([chunks, slot_of, full.astype(jnp.int32)[None]])
    ids, places, blocks = layout.orders()

    arriving = layout.spread(inputs)
    bias_back, bias_front = bias_tiles(relative_bias, chunk_rows // TILE - 1, full)

    states = smooth_alpha.shape[0]
    lanes = (states, width // 128, 128)
    decay = 1.0 - smooth_alpha * smooth_damp
    rate = smooth_alpha * smooth_beta
    span = (decay**chunk_rows).reshape(lanes)
    coef = (smooth_eta * rate).reshape(lanes)
    decay_slab = decay.reshape(lanes)
    gain_row = mix_gain[None]
    omega_row = smooth_omega[None]
    mix_shared, mix_main = mix_proj[:, :key_width], mix_proj[:, key_width:]

    held, after = (), (bias_back, bias_front, mix_main, mix_shared, span, coef)
    for slot in range(slots):
        held = front(
            arriving[slot], slot, slots, held, gain_row, decay_slab, value_proj, after=after
        )
        after = ()
    normed_low, x, value_low, value_slope, ends = held
    ends_all = jnp.concatenate([ends, layout.gather(ends)])
    cotangent, ends_all = lax.optimization_barrier((cotangent, ends_all))
    cots = layout.spread(cotangent)
    normed_low = normed_low.reshape(tokens, width)
    value_slope = value_slope.reshape(tokens, value_width)
    value_others = layout.gather(value_low)
    smoothed, mixed, check, shared_pre, query_low, key_low = front_scan(
        table,
        x,
        gain_row,
        decay_slab,
        coef,
        span,
        omega_row,
        ends_all,
        mix_shared,
        score_affine,
        block,
    )
    smoothed = smoothed.reshape(tokens, width)
    mixed = mixed.reshape(tokens, width)
    shared_pre = shared_pre.reshape(tokens, key_width)
    key_others = layout.gather(key_low)
    base = product(mixed, mix_main)
    attended, gated, lse = attend(
        table,
        query_low,
        bias_front,
        base.reshape(slots, chunk_rows, -1),
        key_low,
        key_others,
        value_low,
        value_others,
    )
    attended = attended.reshape(tokens, value_width)
    gated = gated.reshape(tokens, value_width)

    flat_low = x.reshape(tokens, width)
    flat = flat_low.astype(f32)
    update_pre = base[:, value_width : value_width + width].astype(f32)
    cand_in = base[:, value_width + width :].astype(f32) + mm(gated, out_proj)
    first_sum = flat + jax.nn.sigmoid(update_pre) * (jax.nn.silu(cand_in) - flat)
    unit_two, _ = unit_rows_of(first_sum)
    feed_low = (unit_two * feed_gain).astype(bf16)

    result_a, result_b, grad_feed, out_send, out_keep, in_send, in_keep = feed(
        ids, places, feed_low, cots, first_sum, feed_in, feed_out, layout.seq
    )
    home = [layout.homeward(result_a, 0), layout.homeward(result_b, 1)]
    block_out = layout.gathered(home)
    out_sum = Sum(layout, (out_send, out_keep), turned=True)
    in_sum = Sum(layout, (in_send, in_keep))

    grad_input, grad_main, grad_att, feed_gain_grad = gate(
        grad_feed, cots, flat_low, cand_in, base, attended, feed_gain[None], out_proj
    )
    after = layout.turn((out_sum,), (grad_att,))
    after = layout.turn((in_sum,), after)
    mix_parts = by_rows(ids, None, mixed, grad_main, after=after, cost=LONG)
    proj_parts = by_columns(
        ids,
        places,
        grad_main,
        gated,
        rows=width,
        at=grad_main.shape[1] // width - 1,
        after=mix_parts,
    )
    after = layout.turn((out_sum,), (*proj_parts, *home))
    mix_sum = Sum(layout, mix_parts, over_seq=False)
    proj_sum = Sum(layout, proj_parts, turned=True)
    grad_query, gk_own, gv_own, both_oth, rel_sums = attend_back(
        table,
        query_low,
        grad_att.reshape(slots, chunk_rows, value_width),
        lse.reshape(slots, 1, chunk_rows),
        bias_back,
        key_low,
        key_others,
        value_low,
        value_others,
        after=after,
    )
    both_back = layout.returns(both_oth)
    after = layout.turn((in_sum, out_sum, proj_sum), (grad_query,), cost=LONG)
    grad_normed, value_send, value_keep = value_back(
        ids,
        places,
        normed_low,
        gv_own.reshape(tokens, value_width),
        both_back,
        value_slope,
        value_proj,
        layout.seq,
        after=after,
    )
    grad_key = jnp.sum(both_back[:, :, value_width:].astype(f32), axis=0) + gk_own.reshape(
        tokens, key_width
    ).astype(f32)
    grad_query = grad_query.reshape(tokens, key_width)
    grad_shared = (
        (grad_query * score_affine[0] + grad_key * score_affine[2]) * silu_slope(shared_pre)
    ).astype(bf16)
    shared_parts = by_rows(ids, None, mixed, grad_shared, after=(grad_normed,))
    after = layout.turn((out_sum, mix_sum), shared_parts)
    shared_sum = Sum(layout, shared_parts, over_seq=False)
    value_sum = Sum(layout, (value_send, value_keep))
    grad_smooth = (mm_nt(grad_main, mix_main) + mm_nt(grad_shared, mix_shared)) * silu_slope(
        smoothed
    )
    grad_smooth = grad_smooth.reshape(slots, chunk_rows, width)
    after = layout.turn((in_sum, value_sum, proj_sum, shared_sum), (grad_smooth,))
    back = back_ends(grad_smooth, decay_slab, after=after)
    back_all = jnp.concatenate([back, layout.gather(back)])
    after = layout.turn((out_sum, in_sum, mix_sum, value_sum, shared_sum), (back,))

    def scan_back(slot, after):
        return back_scan(
            table,
            slot,
            x,
            grad_smooth,
            grad_normed.reshape(slots, chunk_rows, width),
            grad_input.reshape(slots, chunk_rows, width),
            check,
            gain_row,
            decay_slab,
            coef,
            span,
            omega_row,
            back_all,
            after=after,
        )

    first = scan_back(0, after)
    after = layout.turn(
        (in_sum, mix_sum, value_sum, proj_sum, out_sum, shared_sum), (first[0],)
    )
    home_first = layout.homeward(first[0], 0)
    while mix_sum.total is None or shared_sum.total is None:
        after = layout.turn((mix_sum, shared_sum), after)
    rows = jnp.concatenate([shared_sum.total[0, 0], mix_sum.total[0, 0]], axis=1)
    rows = rows.reshape(rows.shape[0], layout.seq, -1).transpose(1, 0, 2)
    mix_sum.begin_seq(rows[blocks])
    second = scan_back(1, (*after, *mix_sum.kept))
    affine_grad = jnp.stack(
        [
            jnp.sum(grad_query * shared_pre * jax.nn.sigmoid(shared_pre), axis=0),
            jnp.sum(grad_query, axis=0),
            jnp.sum(grad_key * shared_pre * jax.nn.sigmoid(shared_pre), axis=0),
            jnp.sum(grad_key, axis=0),
        ]
    )
    relative_grad = bias_grad(rel_sums[:, 0], seq_length)
    small = [
        first[3] + second[3],
        first[4] + second[4],
        feed_gain_grad,
        affine_grad,
        relative_grad,
    ]
    small = [v.reshape(-1, 128) for v in small]
    rest = jnp.concatenate(small)
    rest = jnp.pad(rest, ((0, -rest.shape[0] % 16), (0, 0)))
    home_second = layout.homeward(second[0], 1)
    sums = (mix_sum, proj_sum, value_sum, out_sum, in_sum)
    turned = layout.turn(sums, (second[0], home_first), cost=LONG)
    totals = layout.over_dp(pack(first[1:3], second[1:3], rest, after=turned))
    after = layout.turn(sums, (*turned, home_second))
    totals = layout.over_seq(later_sum(*totals, after=after))
    while any(v.total is None for v in sums):
        after = layout.turn(sums, after)
    grad_in = layout.gathered([home_first, home_second]).astype(f32)
    feed_out_grad, feed_in_grad = out_sum.total[0, 0], in_sum.total[0, 0]
    rows = width // layout.dp
    feed_in_grad = feed_in_grad.reshape(-1, rows, feed_in_grad.shape[-1])
    feed_in_grad = feed_in_grad.transpose(1, 0, 2).reshape(rows, -1)
    out_grad, value_grad = proj_sum.total[0, 0], value_sum.total[0, 0]
    mix_grad = mix_sum.total[0, 0]
    alpha_grad, damp_grad, beta_grad, eta_grad, totals = finish(
        core, *totals, smooth_alpha, smooth_damp, smooth_beta, smooth_eta
    )
    parts, start = [], 0
    for item in small:
        parts.append(totals[start : start + item.shape[0]].reshape(-1))
        start += item.shape[0]
    return (
        block_out,
        grad_in,
        parts[0],
        alpha_grad,
        damp_grad,
        beta_grad,
        eta_grad,
        parts[1],
        value_grad,
        mix_grad,
        parts[3].reshape(4, key_width),
        parts[4],
        out_grad,
        parts[2],
        feed_in_grad,
        feed_out_grad,
    )


def solution(mesh):
    tokens = P("dp", "seq", None)
    split = P("dp", "seq")
    return jax.shard_map(
        functools.partial(layer, Layout(mesh)),
        mesh=mesh,
        in_specs=(tokens, tokens, P("dp")) + (P(),) * 14,
        out_specs=(tokens, tokens)
        + (P(),) * 6
        + (split, split, P(), P(), split, P(), split, split),
        check_vma=False,
    )
```

```python
import functools

import jax
import jax.numpy as jnp
from jax import lax
from jax.experimental import pallas as pl
from jax.experimental.pallas import tpu as pltpu
from jax.sharding import PartitionSpec as P

STRETCH = 128
EPSILON = 1e-05
TILE = 256
MASKED = -1e30
VMEM_LIMIT = 60 * 1024 * 1024
AXES = ("dp", "seq")
BRIEF = pl.CostEstimate(flops=1, bytes_accessed=1, transcendentals=0)
LONG = pl.CostEstimate(flops=10**11, bytes_accessed=1, transcendentals=0)

f32 = jnp.float32
bf16 = jnp.bfloat16


def unit_rows_of(values):
    centred = values - jnp.mean(values, axis=-1, keepdims=True)
    inv_std = lax.rsqrt(jnp.mean(centred * centred, axis=-1, keepdims=True) + EPSILON)
    return centred * inv_std, inv_std


def norm_back_rows(grad_out, gain_vec, unit_rows, inv_std):
    scaled = grad_out * gain_vec
    return inv_std * (
        scaled
        - jnp.mean(scaled, axis=-1, keepdims=True)
        - unit_rows * jnp.mean(scaled * unit_rows, axis=-1, keepdims=True)
    )


def silu_slope(pre_act):
    sigmoid_val = jax.nn.sigmoid(pre_act)
    return sigmoid_val * (1.0 + pre_act * (1.0 - sigmoid_val))


def params(semantics, limit=VMEM_LIMIT):
    return pltpu.CompilerParams(dimension_semantics=semantics, vmem_limit_bytes=limit)


def ignoring(body, first, count):
    def called(*refs):
        return body(*refs[:first], *refs[first + count :])

    return called


def to_slab(slab, rows):
    count, groups = rows.shape[0], rows.shape[1] // 128
    for c in range(groups):
        slab[pl.ds(c, count, stride=groups), :] = rows[:, c * 128 : (c + 1) * 128]


def from_slab(slab, count, groups):
    return jnp.concatenate(
        [slab[pl.ds(c, count, stride=groups), :] for c in range(groups)], axis=1
    )


def slab_row(slab, t, groups):
    return slab[pl.ds(pl.multiple_of(t * groups, groups), groups), :]


def front_body(
    x_ref, gain_ref, decay_ref, proj_ref, low_ref, copy_ref, value_ref, slope_ref, end_ref, slab
):
    states, groups, _ = decay_ref.shape
    count = x_ref.shape[0]

    @pl.when(pl.program_id(0) == 0)
    def _():
        end_ref[...] = jnp.zeros_like(end_ref)

    copy_ref[0] = x_ref[...]
    unit, _ = unit_rows_of(x_ref[...].astype(f32))
    normed = unit * gain_ref[...]
    low_ref[0] = normed.astype(bf16)
    to_slab(slab, normed)
    decay = [decay_ref[n] for n in range(states)]

    def step(t, state):
        row = slab_row(slab, t, groups)
        return tuple(d * s + row for d, s in zip(decay, state))

    state = lax.fori_loop(
        0, count, step, tuple(end_ref[0, n] for n in range(states)), unroll=8
    )
    for n in range(states):
        end_ref[0, n] = state[n]
    for c in range(proj_ref.shape[1] // 512):
        at = slice(c * 512, (c + 1) * 512)
        pre = jnp.dot(low_ref[0], proj_ref[:, at], preferred_element_type=f32)
        gate = jax.nn.sigmoid(pre)
        value = pre * gate
        value_ref[0, :, at] = value.astype(bf16)
        slope_ref[0, :, at] = (gate + value * (1.0 - gate)).astype(bf16)


def front(x, slot, slots, earlier, gain, decay, proj, after=()):
    length, width = x.shape
    value_width = proj.shape[1]
    states, groups, lanes = decay.shape
    block = min(256, length)
    anywhere = pl.BlockSpec(memory_space=pl.ANY)

    def tokens(columns):
        return pl.BlockSpec((1, block, columns), lambda b: (slot, b, 0))

    return pl.pallas_call(
        ignoring(front_body, 4, len(earlier) + len(after)),
        grid=(length // block,),
        in_specs=[
            pl.BlockSpec((block, width), lambda b: (b, 0)),
            pl.BlockSpec((1, width), lambda b: (0, 0)),
            pl.BlockSpec((states, groups, lanes), lambda b: (0, 0, 0)),
            pl.BlockSpec(proj.shape, lambda b: (0, 0), pipeline_mode=pl.Buffered(1)),
        ]
        + [anywhere] * (len(earlier) + len(after)),
        out_specs=[
            tokens(width),
            tokens(width),
            tokens(value_width),
            tokens(value_width),
            pl.BlockSpec((1, states, groups, lanes), lambda b: (slot, 0, 0, 0)),
        ],
        out_shape=[
            jax.ShapeDtypeStruct((slots, length, width), bf16),
            jax.ShapeDtypeStruct((slots, length, width), bf16),
            jax.ShapeDtypeStruct((slots, length, value_width), bf16),
            jax.ShapeDtypeStruct((slots, length, value_width), bf16),
            jax.ShapeDtypeStruct((slots, states, groups, lanes), f32),
        ],
        scratch_shapes=[pltpu.VMEM((block * groups, lanes), f32)],
        input_output_aliases={4 + k: k for k in range(len(earlier))},
        compiler_params=params(("arbitrary",)),
        name="front",
        cost_estimate=BRIEF,
    )(x, gain, decay, proj, *earlier, *after)


def front_scan_body(
    table_ref,
    x_ref,
    gain_ref,
    decay_ref,
    coef_ref,
    span_ref,
    omega_ref,
    ends_ref,
    proj_ref,
    affine_ref,
    smooth_ref,
    mixed_ref,
    check_ref,
    shared_ref,
    query_ref,
    key_ref,
    slab,
    out_slab,
    carry,
):
    states, groups, _ = decay_ref.shape
    count = x_ref.shape[1]
    slot = pl.program_id(0)
    total = ends_ref.shape[0]

    @pl.when(pl.program_id(1) == 0)
    def _():
        carry[...] = jnp.zeros_like(carry)

        def link(i, _):
            carry[...] = span_ref[...] * carry[...] + ends_ref[table_ref[total + i]]
            return 0

        lax.fori_loop(0, table_ref[slot], link, 0)

    unit, _ = unit_rows_of(x_ref[0].astype(f32))
    normed = unit * gain_ref[...]
    to_slab(slab, normed)
    decay = [decay_ref[n] for n in range(states)]
    coef = [coef_ref[n] for n in range(states)]
    state = tuple(carry[n] for n in range(states))
    for n in range(states):
        check_ref[0, 0, n] = state[n]

    def step(t, state):
        row = slab_row(slab, t, groups)
        state = tuple(d * s + row for d, s in zip(decay, state))
        parts = [c * s for c, s in zip(coef, state)]
        while len(parts) > 1:
            parts = [a + b for a, b in zip(parts[::2], parts[1::2])]
        out_slab[pl.ds(pl.multiple_of(t * groups, groups), groups), :] = parts[0]
        return state

    state = lax.fori_loop(0, count, step, state, unroll=8)
    for n in range(states):
        carry[n] = state[n]
    smoothed = from_slab(out_slab, count, groups) + omega_ref[...] * normed
    smooth_ref[0] = smoothed
    mixed = (smoothed * jax.nn.sigmoid(smoothed)).astype(bf16)
    mixed_ref[0] = mixed
    shared_pre = jnp.dot(mixed, proj_ref[...], preferred_element_type=f32)
    shared = shared_pre * jax.nn.sigmoid(shared_pre)
    shared_ref[0] = shared_pre
    query_ref[0] = (shared * affine_ref[0:1] + affine_ref[1:2]).astype(bf16)
    key_ref[0] = (shared * affine_ref[2:3] + affine_ref[3:4]).astype(bf16)


def front_scan(table, x, gain, decay, coef, span, omega, ends, proj, affine, block):
    slots, length, width = x.shape
    states, groups, lanes = decay.shape
    whole3 = pl.BlockSpec((states, groups, lanes), lambda k, b, t: (0, 0, 0))
    row = pl.BlockSpec((1, width), lambda k, b, t: (0, 0))
    tokens = pl.BlockSpec((1, block, width), lambda k, b, t: (k, b, 0))
    narrow = pl.BlockSpec((1, block, proj.shape[1]), lambda k, b, t: (k, b, 0))
    return pl.pallas_call(
        front_scan_body,
        grid_spec=pltpu.PrefetchScalarGridSpec(
            num_scalar_prefetch=1,
            grid=(slots, length // block),
            in_specs=[
                tokens,
                row,
                whole3,
                whole3,
                whole3,
                row,
                pl.BlockSpec(ends.shape, lambda k, b, t: (0, 0, 0, 0)),
                pl.BlockSpec(proj.shape, lambda k, b, t: (0, 0)),
                pl.BlockSpec(affine.shape, lambda k, b, t: (0, 0)),
            ],
            out_specs=[
                tokens,
                tokens,
                pl.BlockSpec((1, 1, states, groups, lanes), lambda k, b, t: (k, b, 0, 0, 0)),
                narrow,
                narrow,
                narrow,
            ],
            scratch_shapes=[
                pltpu.VMEM((block * groups, lanes), f32),
                pltpu.VMEM((block * groups, lanes), f32),
                pltpu.VMEM((states, groups, lanes), f32),
            ],
        ),
        out_shape=[
            jax.ShapeDtypeStruct((slots, length, width), f32),
            jax.ShapeDtypeStruct((slots, length, width), bf16),
            jax.ShapeDtypeStruct((slots, length // block, states, groups, lanes), f32),
            jax.ShapeDtypeStruct((slots, length, proj.shape[1]), f32),
            jax.ShapeDtypeStruct((slots, length, proj.shape[1]), bf16),
            jax.ShapeDtypeStruct((slots, length, proj.shape[1]), bf16),
        ],
        compiler_params=params(("arbitrary", "arbitrary")),
        name="front_scan",
        cost_estimate=LONG,
    )(table, x, gain, decay, coef, span, omega, ends, proj, affine)


def back_ends_body(gs_ref, decay_ref, end_ref, slab):
    states, groups, _ = decay_ref.shape
    slots, count, _ = gs_ref.shape

    @pl.when(pl.program_id(0) == 0)
    def _():
        end_ref[...] = jnp.zeros_like(end_ref)

    for k in range(slots):
        to_slab(slab.at[k], gs_ref[k])
    decay = [decay_ref[n] for n in range(states)]

    def step(t, state):
        rows = [slab_row(slab.at[k], count - 1 - t, groups) for k in range(slots)]
        return [tuple(d * s + row for d, s in zip(decay, held)) for row, held in zip(rows, state)]

    state = lax.fori_loop(
        0,
        count,
        step,
        [tuple(end_ref[k, n] for n in range(states)) for k in range(slots)],
        unroll=8,
    )
    for k in range(slots):
        for n in range(states):
            end_ref[k, n] = state[k][n]


def back_ends(gs, decay, block=128, after=()):
    slots, length, width = gs.shape
    states, groups, lanes = decay.shape
    block = min(block, length)
    blocks = length // block
    return pl.pallas_call(
        ignoring(back_ends_body, 2, len(after)),
        grid=(blocks,),
        in_specs=[
            pl.BlockSpec((slots, block, width), lambda b: (0, blocks - 1 - b, 0)),
            pl.BlockSpec((states, groups, lanes), lambda b: (0, 0, 0)),
        ]
        + [pl.BlockSpec(memory_space=pl.ANY)] * len(after),
        out_specs=pl.BlockSpec((slots, states, groups, lanes), lambda b: (0, 0, 0, 0)),
        out_shape=jax.ShapeDtypeStruct((slots, states, groups, lanes), f32),
        scratch_shapes=[pltpu.VMEM((slots, block * groups, lanes), f32)],
        compiler_params=params(("arbitrary",)),
        name="back_ends",
        cost_estimate=BRIEF,
    )(gs, decay, *after)


def back_scan_body(
    table_ref,
    slot_ref,
    x_ref,
    gs_ref,
    gv_ref,
    gi_ref,
    check_ref,
    gain_ref,
    decay_ref,
    coef_ref,
    span_ref,
    omega_ref,
    ends_ref,
    grad_ref,
    qx_ref,
    qs_ref,
    gain_grad_ref,
    omega_grad_ref,
    slab,
    gs_slab,
    out_slab,
    history,
    carry,
):
    states, groups, _ = decay_ref.shape
    count = x_ref.shape[1]
    slot = slot_ref[0]
    total = ends_ref.shape[0]

    @pl.when(pl.program_id(0) == 0)
    def _():
        qx_ref[...] = jnp.zeros_like(qx_ref)
        qs_ref[...] = jnp.zeros_like(qs_ref)
        gain_grad_ref[...] = jnp.zeros_like(gain_grad_ref)
        omega_grad_ref[...] = jnp.zeros_like(omega_grad_ref)

    @pl.when(pl.program_id(0) == 0)
    def _():
        carry[...] = jnp.zeros_like(carry)

        def link(i, _):
            carry[...] = (
                span_ref[...] * carry[...] + ends_ref[table_ref[total + total - 1 - i]]
            )
            return 0

        lax.fori_loop(0, total - 1 - table_ref[slot], link, 0)

    unit, inv = unit_rows_of(x_ref[0].astype(f32))
    normed = unit * gain_ref[...]
    gs = gs_ref[0]
    to_slab(slab, normed)
    to_slab(gs_slab, gs)
    decay = [decay_ref[n] for n in range(states)]

    def recompute(t, state):
        for n in range(states):
            history[t, n] = state[n]
        row = slab_row(slab, t, groups)
        return tuple(d * s + row for d, s in zip(decay, state))

    lax.fori_loop(
        0, count, recompute, tuple(check_ref[0, 0, n] for n in range(states)), unroll=4
    )

    half = states // 2
    for part in range(2):
        chosen = range(part * half, (part + 1) * half)
        decay = [decay_ref[n] for n in chosen]
        coef = [coef_ref[n] for n in chosen]

        def step(i, held):
            q, qx, qs = held
            t = count - 1 - i
            row = slab_row(slab, t, groups)
            g = slab_row(gs_slab, t, groups)
            q = tuple(d * a + g for d, a in zip(decay, q))
            parts = [c * a for c, a in zip(coef, q)]
            while len(parts) > 1:
                parts = [a + b for a, b in zip(parts[::2], parts[1::2])]
            spot = pl.ds(pl.multiple_of(t * groups, groups), groups)
            if part == 0:
                out_slab[spot, :] = parts[0]
            else:
                out_slab[spot, :] = out_slab[spot, :] + parts[0]
            qx = tuple(a + b * row for a, b in zip(qx, q))
            qs = tuple(a + b * history[t, n] for a, b, n in zip(qs, q, chosen))
            return q, qx, qs

        q, qx, qs = lax.fori_loop(
            0,
            count,
            step,
            (
                tuple(carry[n] for n in chosen),
                tuple(qx_ref[n] for n in chosen),
                tuple(qs_ref[n] for n in chosen),
            ),
            unroll=4,
        )
        for i, n in enumerate(chosen):
            carry[n] = q[i]
            qx_ref[n] = qx[i]
            qs_ref[n] = qs[i]

    grad_normed = (
        gv_ref[0] + from_slab(out_slab, count, groups) + omega_ref[...] * gs
    )
    gain_grad_ref[...] += jnp.sum(grad_normed * unit, axis=0, keepdims=True)
    omega_grad_ref[...] += jnp.sum(gs * normed, axis=0, keepdims=True)
    grad_ref[...] = (
        gi_ref[0] + norm_back_rows(grad_normed, gain_ref[...], unit, inv)
    ).astype(bf16)


def back_scan(table, slot, x, gs, gv, gi, check, gain, decay, coef, span, omega, ends, after=()):
    _, length, width = x.shape
    states, groups, lanes = decay.shape
    blocks = check.shape[1]
    block = length // blocks
    whole3 = pl.BlockSpec((states, groups, lanes), lambda b, t, u: (0, 0, 0))
    row = pl.BlockSpec((1, width), lambda b, t, u: (0, 0))
    tokens = pl.BlockSpec((1, block, width), lambda b, t, u: (slot, blocks - 1 - b, 0))
    return pl.pallas_call(
        ignoring(back_scan_body, 13, len(after)),
        grid_spec=pltpu.PrefetchScalarGridSpec(
            num_scalar_prefetch=2,
            grid=(blocks,),
            in_specs=[
                tokens,
                tokens,
                tokens,
                tokens,
                pl.BlockSpec(
                    (1, 1, states, groups, lanes),
                    lambda b, t, u: (slot, blocks - 1 - b, 0, 0, 0),
                ),
                row,
                whole3,
                whole3,
                whole3,
                row,
                pl.BlockSpec(ends.shape, lambda b, t, u: (0, 0, 0, 0)),
            ]
            + [pl.BlockSpec(memory_space=pl.ANY)] * len(after),
            out_specs=[
                pl.BlockSpec((block, width), lambda b, t, u: (blocks - 1 - b, 0)),
                whole3,
                whole3,
                row,
                row,
            ],
            scratch_shapes=[
                pltpu.VMEM((block * groups, lanes), f32),
                pltpu.VMEM((block * groups, lanes), f32),
                pltpu.VMEM((block * groups, lanes), f32),
                pltpu.VMEM((block, states, groups, lanes), f32),
                pltpu.VMEM((states, groups, lanes), f32),
            ],
        ),
        out_shape=[
            jax.ShapeDtypeStruct((length, width), bf16),
            jax.ShapeDtypeStruct((states, groups, lanes), f32),
            jax.ShapeDtypeStruct((states, groups, lanes), f32),
            jax.ShapeDtypeStruct((1, width), f32),
            jax.ShapeDtypeStruct((1, width), f32),
        ],
        compiler_params=params(("arbitrary",)),
        name="back_scan",
        cost_estimate=LONG,
    )(table, jnp.full((1,), slot, jnp.int32), x, gs, gv, gi, check, gain, decay, coef, span, omega, ends, *after)


def chunk_copies(table_ref, own, others, kept, total, length, sem):
    copies = []
    for slot in range(total):
        place = pl.ds(pl.multiple_of(table_ref[slot] * length, length), length)
        source = own.at[slot] if slot < 2 else others.at[slot - 2]
        copies.append(pltpu.make_async_copy(source, kept.at[place, :], sem.at[slot]))
    return copies


def attend_body(
    table_ref,
    q_ref,
    bias_ref,
    reset_ref,
    k_own,
    k_oth,
    v_own,
    v_oth,
    out_ref,
    gated_ref,
    lse_ref,
    keys,
    values,
    scores,
    probs,
    key_sem,
    value_sem,
    *,
    total,
):
    length, key_width = q_ref.shape[1:]
    value_width = values.shape[1]
    tiles = length // TILE
    scale = float(key_width) ** (-0.5)

    key_copies = chunk_copies(table_ref, k_own, k_oth, keys, total, length, key_sem)
    value_copies = chunk_copies(table_ref, v_own, v_oth, values, total, length, value_sem)

    @pl.when(pl.program_id(0) == 0)
    def _():
        for copy in key_copies + value_copies:
            copy.start()
        for copy in key_copies:
            copy.wait()

    chunk = table_ref[pl.program_id(0)]
    reach = jnp.where(table_ref[2 * total] == 1, chunk + 1, 1)
    base = (chunk + 1 - reach) * length
    queries = q_ref[0]

    def first(kt, peak):
        spot = pl.ds(pl.multiple_of(base + kt * TILE, TILE), TILE)
        tile = (
            lax.dot_general(
                queries, keys[spot, :], (((1,), (1,)), ((), ())), preferred_element_type=f32
            )
            * scale
        )
        for r in range(tiles):
            rows = slice(r * TILE, (r + 1) * TILE)
            gap = (reach - 1) * tiles + r - kt + tiles - 1
            scores[kt, rows, :] = tile[rows] + bias_ref[gap]
        return jnp.maximum(peak, jnp.max(scores[kt], axis=1, keepdims=True))

    peak = lax.fori_loop(
        0, reach * tiles, first, jnp.full((length, 1), 2 * MASKED, f32)
    )

    def second(kt, sums):
        terms = jnp.exp(scores[kt] - peak)
        probs[:, pl.ds(pl.multiple_of(kt * TILE, TILE), TILE)] = terms.astype(bf16)
        return sums + jnp.sum(terms, axis=1, keepdims=True)

    sums = lax.fori_loop(0, reach * tiles, second, jnp.zeros((length, 1), f32))
    lse_ref[0] = peak + jnp.log(sums)
    inverse = 1.0 / sums

    @pl.when(pl.program_id(0) == 0)
    def _():
        for copy in value_copies:
            copy.wait()

    for count in range(1, total + 1):

        @pl.when(reach == count)
        def _(count=count):
            width = count * length
            span = pl.ds(pl.multiple_of(base, length), width)

            def column(ct, _):
                at = pl.ds(pl.multiple_of(ct * 1024, 1024), 1024)
                rows = (
                    jnp.dot(probs[:, :width], values[span, at], preferred_element_type=f32)
                    * inverse
                )
                out_ref[0, :, at] = rows.astype(bf16)
                gate = reset_ref[0, :, at].astype(f32)
                gated_ref[0, :, at] = (gate * jax.nn.sigmoid(gate) * rows).astype(bf16)
                return 0

            lax.fori_loop(0, value_width // 1024, column, 0)


def attend(table, q, bias, reset, k_own, k_oth, v_own, v_oth):
    slots, length, key_width = q.shape
    value_width = v_own.shape[2]
    total = slots + k_oth.shape[0]
    anywhere = pl.BlockSpec(memory_space=pl.ANY)
    tokens = pl.BlockSpec((1, length, value_width), lambda k, t: (k, 0, 0))
    return pl.pallas_call(
        functools.partial(attend_body, total=total),
        grid_spec=pltpu.PrefetchScalarGridSpec(
            num_scalar_prefetch=1,
            grid=(slots,),
            in_specs=[
                pl.BlockSpec((1, length, key_width), lambda k, t: (k, 0, 0)),
                pl.BlockSpec(bias.shape, lambda k, t: (0, 0, 0)),
                tokens,
                anywhere,
                anywhere,
                anywhere,
                anywhere,
            ],
            out_specs=[
                tokens,
                tokens,
                pl.BlockSpec((1, length, 1), lambda k, t: (k, 0, 0)),
            ],
            scratch_shapes=[
                pltpu.VMEM((total * length, key_width), bf16),
                pltpu.VMEM((total * length, value_width), bf16),
                pltpu.VMEM((total * length // TILE, length, TILE), f32),
                pltpu.VMEM((length, total * length), bf16),
                pltpu.SemaphoreType.DMA((total,)),
                pltpu.SemaphoreType.DMA((total,)),
            ],
        ),
        out_shape=[
            jax.ShapeDtypeStruct((slots, length, value_width), bf16),
            jax.ShapeDtypeStruct((slots, length, value_width), bf16),
            jax.ShapeDtypeStruct((slots, length, 1), f32),
        ],
        compiler_params=params(("arbitrary",)),
        name="attend",
        cost_estimate=BRIEF,
    )(table, q, bias, reset, k_own, k_oth, v_own, v_oth)


def attend_back_body(
    table_ref,
    q_ref,
    grad_ref,
    lse_ref,
    bias_ref,
    k_own,
    k_oth,
    v_own,
    v_oth,
    gq_ref,
    gk_own,
    gv_own,
    both_oth,
    rel_out,
    keys,
    values,
    gk_sum,
    gv_sum,
    probs_kept,
    grads_kept,
    rel_ref,
    key_sem,
    value_sem,
    *,
    total,
):
    length, key_width = q_ref.shape[1:]
    value_width = values.shape[1]
    tiles = length // TILE
    scale = float(key_width) ** (-0.5)
    step = pl.program_id(0)
    nt = (((1,), (1,)), ((), ()))
    tn = (((0,), (0,)), ((), ()))

    copies = chunk_copies(
        table_ref, k_own, k_oth, keys, total, length, key_sem
    ) + chunk_copies(table_ref, v_own, v_oth, values, total, length, value_sem)

    @pl.when(step == 0)
    def _():
        for copy in copies:
            copy.start()
        gk_sum[...] = jnp.zeros_like(gk_sum)
        gv_sum[...] = jnp.zeros_like(gv_sum)
        rel_ref[...] = jnp.zeros_like(rel_ref)
        for copy in copies:
            copy.wait()

    chunk = table_ref[step]
    reach = jnp.where(table_ref[2 * total] == 1, chunk + 1, 1)
    base = (chunk + 1 - reach) * length
    queries = q_ref[0]
    log_total = lse_ref[0]

    def gap_of(kc, a, r):
        return (reach - 1 - kc) * tiles + r - a + tiles - 1

    def first(kc, delta):
        spot = pl.ds(pl.multiple_of(base + kc * length, length), length)
        grads_kept[kc] = lax.dot_general(
            values[spot, :], grad_ref[0], nt, preferred_element_type=f32
        )
        tile = (
            lax.dot_general(keys[spot, :], queries, nt, preferred_element_type=f32) * scale
        )
        for a in range(tiles):
            for r in range(tiles):
                rows = slice(a * TILE, (a + 1) * TILE)
                cols = slice(r * TILE, (r + 1) * TILE)
                probs_kept[kc, rows, cols] = jnp.exp(
                    tile[rows, cols] + bias_ref[gap_of(kc, a, r)] - log_total[:, cols]
                )
        return delta + jnp.sum(probs_kept[kc] * grads_kept[kc], axis=0, keepdims=True)

    delta = lax.fori_loop(0, reach, first, jnp.zeros((1, length), f32))

    def second(kc, grad_query):
        spot = pl.ds(pl.multiple_of(base + kc * length, length), length)
        probs = probs_kept[kc]
        grad_scores = (probs * (grads_kept[kc] - delta)).astype(bf16)
        probs = probs.astype(bf16)
        for a in range(tiles):
            for r in range(tiles):
                rel_ref[gap_of(kc, a, r)] += grad_scores[
                    a * TILE : (a + 1) * TILE, r * TILE : (r + 1) * TILE
                ].astype(f32)
        gk_sum[spot, :] += jnp.dot(grad_scores, queries, preferred_element_type=f32)

        def column(ct, _):
            at = pl.ds(pl.multiple_of(ct * 1024, 1024), 1024)
            gv_sum[spot, at] += jnp.dot(
                probs, grad_ref[0, :, at], preferred_element_type=f32
            )
            return 0

        lax.fori_loop(0, value_width // 1024, column, 0)
        return grad_query + lax.dot_general(
            grad_scores, keys[spot, :], tn, preferred_element_type=f32
        )

    grad_query = lax.fori_loop(0, reach, second, jnp.zeros((length, key_width), f32))
    gq_ref[0] = grad_query * scale

    @pl.when(step == pl.num_programs(0) - 1)
    def _():
        for slot in range(total):
            place = pl.ds(pl.multiple_of(table_ref[slot] * length, length), length)
            key_grad = (gk_sum[place, :] * scale).astype(bf16)
            value_grad = gv_sum[place, :].astype(bf16)
            if slot < 2:
                gk_own[slot] = key_grad
                gv_own[slot] = value_grad
            else:
                both_oth[slot - 2, :, :value_width] = value_grad
                both_oth[slot - 2, :, value_width:] = key_grad
        down = lax.broadcasted_iota(jnp.int32, (TILE, TILE), 0)
        across = lax.broadcasted_iota(jnp.int32, (TILE, TILE), 1)
        mirror = jnp.where(down + across == TILE - 1, 1.0, 0.0)
        for d in range(rel_out.shape[0]):
            flipped = jnp.dot(
                rel_ref[d + tiles - 1],
                mirror,
                precision=lax.Precision.HIGHEST,
                preferred_element_type=f32,
            )
            wide = jnp.concatenate([flipped, jnp.zeros((TILE, TILE), f32)], axis=1)
            turned = pltpu.roll(wide, 0, 1, stride=1, stride_axis=0)
            rel_out[d] = jnp.sum(turned, axis=0, keepdims=True)


def attend_back(table, q, grads, lse, bias, k_own, k_oth, v_own, v_oth, after=()):
    slots, length, key_width = q.shape
    value_width = v_own.shape[2]
    total = slots + k_oth.shape[0]
    rel_shape = (total * length // TILE, 1, 2 * TILE)
    both_shape = (k_oth.shape[0], length, key_width + value_width)
    anywhere = pl.BlockSpec(memory_space=pl.ANY)

    def all_of(shape):
        return pl.BlockSpec(
            shape, lambda k, t: (0,) * len(shape), pipeline_mode=pl.Buffered(1)
        )

    return pl.pallas_call(
        ignoring(functools.partial(attend_back_body, total=total), 9, len(after)),
        grid_spec=pltpu.PrefetchScalarGridSpec(
            num_scalar_prefetch=1,
            grid=(slots,),
            in_specs=[
                pl.BlockSpec((1, length, key_width), lambda k, t: (k, 0, 0)),
                pl.BlockSpec((1, length, value_width), lambda k, t: (k, 0, 0)),
                pl.BlockSpec((1, 1, length), lambda k, t: (k, 0, 0)),
                all_of(bias.shape),
                anywhere,
                anywhere,
                anywhere,
                anywhere,
            ]
            + [anywhere] * len(after),
            out_specs=[
                pl.BlockSpec((1, length, key_width), lambda k, t: (k, 0, 0)),
                all_of(k_own.shape),
                all_of(v_own.shape),
                all_of(both_shape),
                all_of(rel_shape),
            ],
            scratch_shapes=[
                pltpu.VMEM((total * length, key_width), bf16),
                pltpu.VMEM((total * length, value_width), bf16),
                pltpu.VMEM((total * length, key_width), f32),
                pltpu.VMEM((total * length, value_width), f32),
                pltpu.VMEM((total, length, length), f32),
                pltpu.VMEM((total, length, length), f32),
                pltpu.VMEM(bias.shape, f32),
                pltpu.SemaphoreType.DMA((total,)),
                pltpu.SemaphoreType.DMA((total,)),
            ],
        ),
        out_shape=[
            jax.ShapeDtypeStruct((slots, length, key_width), f32),
            jax.ShapeDtypeStruct(k_own.shape, bf16),
            jax.ShapeDtypeStruct(v_own.shape, bf16),
            jax.ShapeDtypeStruct(both_shape, bf16),
            jax.ShapeDtypeStruct(rel_shape, f32),
        ],
        compiler_params=params(("arbitrary",)),
        name="attend_back",
        cost_estimate=LONG,
    )(table, q, grads, lse, bias, k_own, k_oth, v_own, v_oth, *after)


def bias_body(flag_ref, back_row, front_row, back_ref, front_ref, *, spare):
    tile = pl.program_id(0) - spare
    full = flag_ref[0] == 1

    @pl.when(tile < 0)
    def _():
        back_ref[...] = jnp.full_like(back_ref, MASKED)
        front_ref[...] = jnp.full_like(front_ref, MASKED)

    @pl.when(tile >= 0)
    def _():
        down = lax.broadcasted_iota(jnp.int32, (TILE, TILE), 0)
        across = lax.broadcasted_iota(jnp.int32, (TILE, TILE), 1)
        near = jnp.where(down // STRETCH == across // STRETCH, 1, 0)
        for row, out, ordered in (
            (back_row, back_ref, jnp.where(down <= across, 1, 0)),
            (front_row, front_ref, jnp.where(across <= down, 1, 0)),
        ):
            wide = jnp.broadcast_to(row[0], (TILE, 2 * TILE))
            turned = pltpu.roll(wide, 0, 1, stride=1, stride_axis=0)[:, :TILE]
            allowed = jnp.where(
                tile == 0, jnp.where(full, ordered, ordered * near), jnp.where(full, 1, 0)
            )
            out[0] = jnp.where(allowed == 1, turned, MASKED)


def bias_tiles(relative_bias, spare, full):
    length = relative_bias.shape[0] // 2
    count = length // TILE
    windows = jnp.stack(
        [
            lax.slice_in_dim(relative_bias, length - d * TILE - TILE, length - d * TILE + TILE)
            for d in range(count)
        ]
    )
    front = jnp.concatenate([windows[:, TILE:], windows[:, :TILE]], axis=1)
    back = jnp.concatenate([windows[:, TILE:TILE + 1], windows[:, ::-1][:, TILE:], windows[:, ::-1][:, : TILE - 1]], axis=1)
    row = pl.BlockSpec((1, 1, 2 * TILE), lambda d, t: (jnp.maximum(d - spare, 0), 0, 0))
    out = pl.BlockSpec((1, TILE, TILE), lambda d, t: (d, 0, 0))
    shape = jax.ShapeDtypeStruct((spare + count, TILE, TILE), f32)
    return pl.pallas_call(
        functools.partial(bias_body, spare=spare),
        grid_spec=pltpu.PrefetchScalarGridSpec(
            num_scalar_prefetch=1,
            grid=(spare + count,),
            in_specs=[row, row],
            out_specs=[out, out],
        ),
        out_shape=[shape, shape],
        compiler_params=params(("arbitrary",)),
        name="bias",
    )(full.astype(jnp.int32)[None], back[:, None], front[:, None])


def bias_grad(sums, length):
    count = sums.shape[0]
    shifted = jnp.concatenate([jnp.zeros((count, 1), f32), sums[:, :-1]], axis=1)
    none = jnp.zeros((1, TILE), f32)
    blocks = jnp.concatenate([none, shifted[:, :TILE]]) + jnp.concatenate(
        [shifted[:, TILE:], none]
    )
    return jnp.concatenate(
        [blocks[::-1].reshape(-1), jnp.zeros((2 * length - (count + 1) * TILE,), f32)]
    )


def candidate_body(
    gated_ref, proj_ref, pre_ref, update_ref, x_ref, gain_ref, cand_ref, first_ref, low_ref
):
    cand_in = pre_ref[...].astype(f32) + jnp.dot(
        gated_ref[...], proj_ref[...], preferred_element_type=f32
    )
    cand_ref[...] = cand_in
    x = x_ref[...].astype(f32)
    update = jax.nn.sigmoid(update_ref[...].astype(f32))
    first = x + update * (cand_in * jax.nn.sigmoid(cand_in) - x)
    first_ref[...] = first
    unit, _ = unit_rows_of(first)
    low_ref[...] = (unit * gain_ref[...]).astype(bf16)


def candidate(gated, proj, base, x, gain):
    tokens, width = x.shape
    value_width = gated.shape[1]
    rows = min(256, tokens)
    wide = value_width // width

    def block(columns, at=0):
        return pl.BlockSpec((rows, columns), lambda i: (i, at))

    return pl.pallas_call(
        candidate_body,
        grid=(tokens // rows,),
        in_specs=[
            block(value_width),
            pl.BlockSpec(proj.shape, lambda i: (0, 0), pipeline_mode=pl.Buffered(1)),
            block(width, wide + 1),
            block(width, wide),
            block(width),
            pl.BlockSpec((1, width), lambda i: (0, 0)),
        ],
        out_specs=[block(width)] * 3,
        out_shape=[
            jax.ShapeDtypeStruct((tokens, width), f32),
            jax.ShapeDtypeStruct((tokens, width), f32),
            jax.ShapeDtypeStruct((tokens, width), bf16),
        ],
        compiler_params=params(("arbitrary",)),
        name="candidate",
        cost_estimate=BRIEF,
    )(gated, proj, base, base, x, gain)


def gate_body(
    back_ref,
    cot_a,
    cot_b,
    x_ref,
    cand_ref,
    update_ref,
    reset_ref,
    attended_ref,
    gain_ref,
    proj_ref,
    input_ref,
    main_ref,
    grad_att_ref,
    gain_grad_ref,
):
    width = x_ref.shape[1]
    value_width = proj_ref.shape[0]

    @pl.when(pl.program_id(0) == 0)
    def _():
        gain_grad_ref[...] = jnp.zeros_like(gain_grad_ref)

    x = x_ref[...].astype(f32)
    cand_in = cand_ref[...]
    gate = jax.nn.sigmoid(cand_in)
    candidate = cand_in * gate
    update = jax.nn.sigmoid(update_ref[...].astype(f32))
    change = candidate - x
    unit, inv = unit_rows_of(x + update * change)
    grad_feed = back_ref[...]
    gain_grad_ref[...] += jnp.sum(grad_feed * unit, axis=0, keepdims=True)
    early = pl.program_id(0) < pl.num_programs(0) // 2
    cot = jnp.where(early, cot_a[...].astype(f32), cot_b[...].astype(f32))
    grad_first = cot + norm_back_rows(
        grad_feed, gain_ref[...], unit, inv
    )
    kept = grad_first * (1.0 - update)
    input_ref[...] = kept
    main_ref[:, value_width : value_width + width] = (kept * change * update).astype(bf16)
    grad_cand = (grad_first * update * (gate + candidate * (1.0 - gate))).astype(bf16)
    main_ref[:, value_width + width :] = grad_cand
    for c in range(value_width // 512):
        at = slice(c * 512, (c + 1) * 512)
        grad_gated = mm_nt(grad_cand, proj_ref[at, :])
        reset = reset_ref[:, at].astype(f32)
        open_gate = jax.nn.sigmoid(reset)
        passed = reset * open_gate
        grad_att_ref[:, at] = (grad_gated * passed).astype(bf16)
        main_ref[:, at] = (
            grad_gated
            * attended_ref[:, at].astype(f32)
            * (open_gate + passed * (1.0 - open_gate))
        ).astype(bf16)


def gate(back, cots, x, cand_in, base, attended, gain, proj, after=()):
    tokens, width = x.shape
    value_width = proj.shape[0]
    rows = min(256, tokens // 2)
    half = tokens // rows // 2
    wide = value_width // width

    def block(columns, at=0):
        return pl.BlockSpec((rows, columns), lambda i: (i, at))

    return pl.pallas_call(
        ignoring(gate_body, 10, len(after)),
        grid=(tokens // rows,),
        in_specs=[
            block(width),
            pl.BlockSpec((rows, width), lambda i: (jnp.minimum(i, half - 1), 0)),
            pl.BlockSpec((rows, width), lambda i: (jnp.maximum(i - half, 0), 0)),
            block(width),
            block(width),
            block(width, wide),
            block(value_width),
            block(value_width),
            pl.BlockSpec((1, width), lambda i: (0, 0)),
            pl.BlockSpec(proj.shape, lambda i: (0, 0), pipeline_mode=pl.Buffered(1)),
        ]
        + [pl.BlockSpec(memory_space=pl.ANY)] * len(after),
        out_specs=[
            block(width),
            block(value_width + 2 * width),
            block(value_width),
            pl.BlockSpec((1, width), lambda i: (0, 0)),
        ],
        out_shape=[
            jax.ShapeDtypeStruct((tokens, width), f32),
            jax.ShapeDtypeStruct((tokens, value_width + 2 * width), bf16),
            jax.ShapeDtypeStruct((tokens, value_width), bf16),
            jax.ShapeDtypeStruct((1, width), f32),
        ],
        compiler_params=params(("arbitrary",)),
        name="gate",
        cost_estimate=LONG,
    )(back, *cots, x, cand_in, base, base, attended, gain, proj, *after)


def ordered_transpose(ids_ref, source, plain, ordered):
    plain[...] = source[...].T
    count = ids_ref.shape[0]
    rows = plain.shape[0] // count

    def place(p, _):
        ordered[pl.ds(pl.multiple_of(p * rows, rows), rows), :] = plain[
            pl.ds(pl.multiple_of(ids_ref[p] * rows, rows), rows), :
        ]
        return 0

    lax.fori_loop(0, count, place, 0)


def placed_transpose(places_ref, sources, plain, ordered):
    start = 0
    for source in sources:
        plain[:, start : start + source.shape[0]] = source[...].T
        start += source.shape[0]
    count = places_ref.shape[0]
    rows = plain.shape[0] // count

    def place(q, _):
        ordered[pl.ds(pl.multiple_of(places_ref[q] * rows, rows), rows), :] = plain[
            pl.ds(pl.multiple_of(q * rows, rows), rows), :
        ]
        return 0

    lax.fori_loop(0, count, place, 0)


def feed_body(
    ids_ref,
    places_ref,
    low_ref,
    cot_a,
    cot_b,
    first_ref,
    in_ref,
    out_ref,
    result_a,
    result_b,
    back_ref,
    out_send,
    out_keep,
    in_send,
    in_keep,
    total,
    cot_turned,
    low_turned,
    plain,
):
    step = pl.program_id(0)
    half = pl.num_programs(0) // 2
    tokens = low_ref.shape[0]
    middle = tokens // 2
    nt = (((1,), (1,)), ((), ()))

    @pl.when(step == 0)
    def _():
        placed_transpose(places_ref, (cot_a, cot_b), plain, cot_turned)
        ordered_transpose(ids_ref, low_ref, plain, low_turned)
        total[...] = first_ref[...]
        back_ref[...] = jnp.zeros_like(back_ref)

    acts, grads = [], []
    for r, cot_ref in enumerate((cot_a, cot_b)):
        at = slice(r * middle, (r + 1) * middle)
        hidden = jnp.dot(low_ref[at, :], in_ref[...], preferred_element_type=f32)
        grad_act = lax.dot_general(
            cot_ref[...], out_ref[...], nt, preferred_element_type=f32
        )
        gate = jax.nn.sigmoid(hidden)
        act = hidden * gate
        grad = (grad_act * (gate + act * (1.0 - gate))).astype(bf16)
        act = act.astype(bf16)
        total[at, :] += jnp.dot(act, out_ref[...], preferred_element_type=f32)
        back_ref[at, :] += lax.dot_general(
            grad, in_ref[...], nt, preferred_element_type=f32
        )
        acts.append(act)
        grads.append(grad)
    out_grad = jnp.dot(
        cot_turned[...], jnp.concatenate(acts), preferred_element_type=f32
    ).astype(bf16)
    in_grad = jnp.dot(
        low_turned[...], jnp.concatenate(grads), preferred_element_type=f32
    ).astype(bf16)
    split = in_grad.shape[0] // 2
    in_send[...] = in_grad[:split].reshape(in_send.shape)
    in_keep[...] = in_grad[split:].reshape(in_keep.shape)

    @pl.when(step < half)
    def _():
        out_send[0] = out_grad

    @pl.when(step >= half)
    def _():
        out_keep[0] = out_grad

    @pl.when(step == pl.num_programs(0) - 1)
    def _():
        result_a[...] = total[:middle, :].astype(bf16)
        result_b[...] = total[middle:, :].astype(bf16)


def feed(ids, places, low, cots, first_sum, feed_in, feed_out, seq, after=()):
    tokens, width = low.shape
    features = feed_in.shape[1]
    parts = ids.shape[0]
    half = parts // 2
    columns = features // parts
    rows = width // parts
    share = parts // seq
    anywhere = pl.BlockSpec(memory_space=pl.ANY)

    def all_of(shape):
        return pl.BlockSpec(
            shape, lambda i, t, u: (0,) * len(shape), pipeline_mode=pl.Buffered(1)
        )

    def at(i, t):
        return t[jnp.minimum(i, parts - 1)]

    split = pl.BlockSpec(
        (half, 1, 1, rows, columns),
        lambda i, t, u: (0, u[at(i, t) // share], at(i, t) % share, 0, 0),
    )
    return pl.pallas_call(
        ignoring(feed_body, 8, len(after)),
        grid_spec=pltpu.PrefetchScalarGridSpec(
            num_scalar_prefetch=2,
            grid=(parts,),
            in_specs=[
                all_of(low.shape),
                all_of(cots[0].shape),
                all_of(cots[1].shape),
                all_of(first_sum.shape),
                pl.BlockSpec((width, columns), lambda i, t, u: (0, at(i, t))),
                pl.BlockSpec((columns, width), lambda i, t, u: (at(i, t), 0)),
            ]
            + [anywhere] * len(after),
            out_specs=[
                all_of(cots[0].shape),
                all_of(cots[1].shape),
                all_of(low.shape),
                pl.BlockSpec(
                    (1, width, columns), lambda i, t, u: (jnp.minimum(i, half - 1), 0, 0)
                ),
                pl.BlockSpec(
                    (1, width, columns), lambda i, t, u: (jnp.maximum(i - half, 0), 0, 0)
                ),
                split,
                split,
            ],
            scratch_shapes=[
                pltpu.VMEM((tokens, width), f32),
                pltpu.VMEM((width, tokens), bf16),
                pltpu.VMEM((width, tokens), bf16),
                pltpu.VMEM((width, tokens), bf16),
            ],
        ),
        out_shape=[
            jax.ShapeDtypeStruct(cots[0].shape, bf16),
            jax.ShapeDtypeStruct(cots[1].shape, bf16),
            jax.ShapeDtypeStruct((tokens, width), f32),
            jax.ShapeDtypeStruct((half, width, columns), bf16),
            jax.ShapeDtypeStruct((half, width, columns), bf16),
            jax.ShapeDtypeStruct((half, seq, share, rows, columns), bf16),
            jax.ShapeDtypeStruct((half, seq, share, rows, columns), bf16),
        ],
        compiler_params=params(("arbitrary",)),
        name="feed",
        cost_estimate=BRIEF,
    )(ids, places, low, *cots, first_sum, feed_in, feed_out, *after)


def product_body(left_ref, right_ref, out_ref):
    out_ref[...] = jnp.dot(
        left_ref[...], right_ref[...], preferred_element_type=f32
    ).astype(out_ref.dtype)


def product(left, right, tile=1024):
    tokens, depth = left.shape
    columns = right.shape[1]
    return pl.pallas_call(
        product_body,
        grid=(columns // tile,),
        in_specs=[
            pl.BlockSpec(left.shape, lambda i: (0, 0), pipeline_mode=pl.Buffered(1)),
            pl.BlockSpec((depth, tile), lambda i: (0, i)),
        ],
        out_specs=pl.BlockSpec((tokens, tile), lambda i: (0, i)),
        out_shape=jax.ShapeDtypeStruct((tokens, columns), bf16),
        compiler_params=params(("arbitrary",)),
        name="product",
        cost_estimate=BRIEF,
    )(left, right)


def smooth_back_body(
    main_ref, shared_ref, weight_ref, shared_weight_ref, smooth_ref, out_ref, total
):
    step = pl.program_id(0)

    @pl.when(step == 0)
    def _():
        total[...] = mm_nt(shared_ref[...], shared_weight_ref[...])

    total[...] += mm_nt(main_ref[...], weight_ref[...])

    @pl.when(step == pl.num_programs(0) - 1)
    def _():
        out_ref[...] = total[...] * silu_slope(smooth_ref[...])


def smooth_back(main, shared, weight, shared_weight, smoothed, after=(), riders=None):
    tokens, width = smoothed.shape
    tile = 1024

    def all_of(shape):
        return pl.BlockSpec(shape, lambda i: (0, 0), pipeline_mode=pl.Buffered(1))

    extra = riders or Riders([], 1)
    taken, given = len(extra.ins), len(extra.out_shapes)

    def body(*refs):
        first = 5 + taken + len(after)
        smooth_back_body(*refs[:5], refs[first], *refs[first + 1 + given :])
        extra.body(refs[5 : 5 + taken], refs[first + 1 : first + 1 + given])

    out = pl.pallas_call(
        body,
        grid=(main.shape[1] // tile,),
        in_specs=[
            pl.BlockSpec((tokens, tile), lambda i: (0, i)),
            all_of(shared.shape),
            pl.BlockSpec((width, tile), lambda i: (0, i)),
            all_of(shared_weight.shape),
            all_of(smoothed.shape),
        ]
        + extra.in_specs
        + [pl.BlockSpec(memory_space=pl.ANY)] * len(after),
        out_specs=[all_of(smoothed.shape)] + extra.out_specs,
        out_shape=[jax.ShapeDtypeStruct(smoothed.shape, f32)] + extra.out_shapes,
        scratch_shapes=[pltpu.VMEM(smoothed.shape, f32)],
        compiler_params=params(("arbitrary",)),
        name="smooth_back",
        cost_estimate=LONG,
    )(main, shared, weight, shared_weight, smoothed, *extra.ins, *after)
    return (out[0], riders.result(out[1:])) if riders else out[0]


def by_columns_body(ids_ref, places_ref, left_ref, right_ref, send, keep, plain, turned):
    step = pl.program_id(0)
    half = pl.num_programs(0) // 2

    @pl.when(step == 0)
    def _():
        placed_transpose(places_ref, (left_ref,), plain, turned)

    grad = jnp.dot(turned[...], right_ref[...], preferred_element_type=f32).astype(bf16)

    @pl.when(step < half)
    def _():
        send[0] = grad

    @pl.when(step >= half)
    def _():
        keep[0] = grad


def by_columns(ids, places, left, right, after=(), rows=None, at=0):
    tokens = left.shape[0]
    rows = rows or left.shape[1]
    parts = ids.shape[0]
    half = parts // 2
    columns = right.shape[1] // parts
    shape = jax.ShapeDtypeStruct((half, rows, columns), bf16)
    if columns % 128:
        left = left[:, at * rows : (at + 1) * rows]
        grad = mm_tn(left, right).astype(bf16).reshape(rows, parts, columns)
        grad = jnp.take(grad, ids, axis=1).transpose(1, 0, 2)
        grad = grad.reshape(parts, places.shape[0], -1, columns)
        grad = jnp.take(grad, jnp.argsort(places), axis=1).reshape(parts, rows, columns)
        return grad[:half], grad[half:]
    return pl.pallas_call(
        ignoring(by_columns_body, 4, len(after)),
        grid_spec=pltpu.PrefetchScalarGridSpec(
            num_scalar_prefetch=2,
            grid=(parts,),
            in_specs=[
                pl.BlockSpec(
                    (tokens, rows), lambda i, t, u: (0, at), pipeline_mode=pl.Buffered(1)
                ),
                pl.BlockSpec((tokens, columns), lambda i, t, u: (0, t[jnp.minimum(i, parts - 1)])),
            ]
            + [pl.BlockSpec(memory_space=pl.ANY)] * len(after),
            out_specs=[
                pl.BlockSpec(
                    (1, rows, columns), lambda i, t, u: (jnp.minimum(i, half - 1), 0, 0)
                ),
                pl.BlockSpec(
                    (1, rows, columns), lambda i, t, u: (jnp.maximum(i - half, 0), 0, 0)
                ),
            ],
            scratch_shapes=[
                pltpu.VMEM((rows, tokens), bf16),
                pltpu.VMEM((rows, tokens), bf16),
            ],
        ),
        out_shape=[shape, shape],
        compiler_params=params(("arbitrary",)),
        name="by_columns",
        cost_estimate=BRIEF,
    )(ids, places, left, right, *after)


def by_rows_body(ids_ref, places_ref, left_ref, right_ref, send, keep, plain, turned):
    @pl.when(pl.program_id(0) == 0)
    def _():
        ordered_transpose(ids_ref, left_ref, plain, turned)

    grad = jnp.dot(turned[...], right_ref[...], preferred_element_type=f32).astype(bf16)
    middle = grad.shape[0] // 2
    send[...] = grad[:middle].reshape(send.shape)
    keep[...] = grad[middle:].reshape(keep.shape)


def by_rows(ids, places, left, right, seq=1, after=(), cost=BRIEF, riders=None):
    tokens, rows = left.shape
    parts = ids.shape[0]
    half = parts // 2
    if places is None:
        seq, places = 1, jnp.zeros((1,), jnp.int32)
    columns = right.shape[1] // seq
    tile = min(512, columns)
    share = columns // tile
    shape = jax.ShapeDtypeStruct((half, seq, rows // parts, columns), bf16)
    split = pl.BlockSpec(
        (half, 1, rows // parts, tile), lambda i, t, u: (0, u[jnp.minimum(i // share, seq - 1)], 0, i % share)
    )
    extra = riders or Riders([], 1)
    taken, given = len(extra.ins), len(extra.out_shapes)

    def body(*refs):
        first = 4 + taken + len(after)
        by_rows_body(*refs[:4], *refs[first : first + 2], *refs[first + 2 + given :])
        extra.body(refs[4 : 4 + taken], refs[first + 2 : first + 2 + given])

    out = pl.pallas_call(
        body,
        grid_spec=pltpu.PrefetchScalarGridSpec(
            num_scalar_prefetch=2,
            grid=(seq * share,),
            in_specs=[
                pl.BlockSpec(
                    left.shape, lambda i, t, u: (0, 0), pipeline_mode=pl.Buffered(1)
                ),
                pl.BlockSpec((tokens, tile), lambda i, t, u: (0, i)),
            ]
            + extra.in_specs
            + [pl.BlockSpec(memory_space=pl.ANY)] * len(after),
            out_specs=[split, split] + extra.out_specs,
            scratch_shapes=[
                pltpu.VMEM((rows, tokens), bf16),
                pltpu.VMEM((rows, tokens), bf16),
            ],
        ),
        out_shape=[shape, shape] + extra.out_shapes,
        compiler_params=params(("arbitrary",)),
        name="by_rows",
        cost_estimate=cost,
    )(ids, places, left, right, *extra.ins, *after)
    return (out[:2], riders.result(out[2:])) if riders else out


def value_back_body(
    ids_ref,
    places_ref,
    left_ref,
    own_ref,
    other_ref,
    slope_ref,
    proj_ref,
    total_ref,
    send,
    keep,
    plain,
    turned,
):
    @pl.when(pl.program_id(0) == 0)
    def _():
        total_ref[...] = jnp.zeros_like(total_ref)
        ordered_transpose(ids_ref, left_ref, plain, turned)

    grad = own_ref[...].astype(f32)
    for k in range(other_ref.shape[0]):
        grad = grad + other_ref[k].astype(f32)
    grad = (grad * slope_ref[...].astype(f32)).astype(bf16)
    total_ref[...] += mm_nt(grad, proj_ref[...])
    weights = jnp.dot(turned[...], grad, preferred_element_type=f32).astype(bf16)
    middle = weights.shape[0] // 2
    send[...] = weights[:middle].reshape(send.shape)
    keep[...] = weights[middle:].reshape(keep.shape)


def value_back(ids, places, left, own, others, slope, proj, seq, after=()):
    tokens, rows = left.shape
    parts = ids.shape[0]
    half = parts // 2
    columns = proj.shape[1] // seq
    tile = min(512, columns)
    share = columns // tile
    shape = jax.ShapeDtypeStruct((half, seq, rows // parts, columns), bf16)
    split = pl.BlockSpec(
        (half, 1, rows // parts, tile),
        lambda i, t, u: (0, u[jnp.minimum(i // share, seq - 1)], 0, i % share),
    )
    stripe = pl.BlockSpec((tokens, tile), lambda i, t, u: (0, i))
    fixed = pl.BlockSpec(
        (tokens, rows), lambda i, t, u: (0, 0), pipeline_mode=pl.Buffered(1)
    )
    return pl.pallas_call(
        ignoring(value_back_body, 7, len(after)),
        grid_spec=pltpu.PrefetchScalarGridSpec(
            num_scalar_prefetch=2,
            grid=(seq * share,),
            in_specs=[
                fixed,
                stripe,
                pl.BlockSpec((others.shape[0], tokens, tile), lambda i, t, u: (0, 0, i)),
                stripe,
                pl.BlockSpec((rows, tile), lambda i, t, u: (0, i)),
            ]
            + [pl.BlockSpec(memory_space=pl.ANY)] * len(after),
            out_specs=[fixed, split, split],
            scratch_shapes=[
                pltpu.VMEM((rows, tokens), bf16),
                pltpu.VMEM((rows, tokens), bf16),
            ],
        ),
        out_shape=[jax.ShapeDtypeStruct((tokens, rows), f32), shape, shape],
        compiler_params=params(("arbitrary",)),
        name="value_back",
        cost_estimate=LONG,
    )(ids, places, left, own, others, slope, proj, *after)


class Riders:
    def __init__(self, groups, steps):
        self.shapes, self.ins, self.whole = [], [], []
        self.in_specs, self.out_specs, self.out_shapes = [], [], []
        for pairs, single, kind in groups:
            halves = 1 if single else 2
            g, n, rows, columns = pairs[0][0].shape
            each = n * rows // halves // steps
            self.shapes.append((len(pairs), halves))
            for pair in pairs:
                for v in pair:
                    self.ins.append(v.reshape(g, halves, n * rows // halves, columns))
                    self.in_specs.append(
                        pl.BlockSpec((g, halves, each, columns), lambda i, *_: (0, 0, i, 0))
                    )
            for _ in range(halves):
                self.out_specs.append(
                    pl.BlockSpec((len(pairs) * g, each, columns), lambda i, *_: (0, i, 0))
                )
                self.out_shapes.append(
                    jax.ShapeDtypeStruct((len(pairs) * g, n * rows // halves, columns), kind)
                )
            self.whole.append((halves, (len(pairs) * g, n // halves, rows, columns)))

    @staticmethod
    def fit(groups, steps):
        for pairs, single, _ in groups:
            _, n, rows, _ = pairs[0][0].shape
            while (n * rows // (1 if single else 2)) % (16 * steps) and steps > 1:
                steps //= 2
        return steps

    def body(self, ins, outs):
        ins, outs = list(ins), list(outs)
        for pairs, halves in self.shapes:
            into = [outs.pop(0) for _ in range(halves)]
            start = 0
            for _ in range(pairs):
                kept, arrived = ins.pop(0), ins.pop(0)
                stop = start + kept.shape[0]
                for part, out in enumerate(into):
                    out[start:stop] = (
                        kept[:, part].astype(f32) + arrived[:, part].astype(f32)
                    ).astype(out.dtype)
                start = stop

    def result(self, sums):
        sums = list(sums)
        return [
            tuple(sums.pop(0).reshape(shape) for _ in range(halves))
            for halves, shape in self.whole
        ]


def stage_sums(groups, after=(), steps=4, cost=BRIEF):
    steps = Riders.fit(groups, steps)
    riders = Riders(groups, steps)
    count = len(riders.ins)

    def body(*refs):
        riders.body(refs[:count], refs[count + len(after) :])

    sums = pl.pallas_call(
        body,
        grid=(steps,),
        in_specs=riders.in_specs + [pl.BlockSpec(memory_space=pl.ANY)] * len(after),
        out_specs=riders.out_specs,
        out_shape=riders.out_shapes,
        compiler_params=params(("arbitrary",)),
        name="stage_sums",
        cost_estimate=cost,
    )(*riders.ins, *after)
    return riders.result(sums)


class Layout:
    def __init__(self, mesh):
        self.dp = mesh.shape["dp"]
        self.seq = mesh.shape["seq"]
        self.members = self.seq // 2
        self.chips = self.seq // 4

    def pairs(self, move):
        return [
            (d * self.seq + z, e * self.seq + w)
            for d in range(self.dp)
            for z in range(self.seq)
            for e, w in [move(d, z)]
        ]

    def send(self, value, move):
        return lax.ppermute(value, AXES, self.pairs(move))

    def place(self, sequence, member):
        return member % 2 ^ (1 - sequence % 2), sequence * self.chips + member // 2

    def member(self, core, z):
        sequence = z // self.chips
        return (z % self.chips) * 2 + (core ^ (1 - sequence % 2))

    def home_to_work(self, round_index):
        def move(d, z):
            part = (1 if z >= self.seq // 2 else 0) ^ round_index
            core, at = self.place(2 * (d % 2) + part, min(z, self.seq - 1 - z))
            return d - d % 2 + core, at

        return move

    def spread(self, value):
        late = lax.axis_index("seq") >= self.seq // 2
        out = []
        for round_index in range(2):
            sent = lax.dynamic_index_in_dim(
                value, jnp.where(late, 1 - round_index, round_index), 0, False
            )
            out.append(self.send(sent, self.home_to_work(round_index)))
        return out

    def homeward(self, value, round_index):
        pairs = [(b, a) for a, b in self.pairs(self.home_to_work(round_index))]
        return lax.ppermute(value, AXES, pairs)

    def gathered(self, back):
        late = lax.axis_index("seq") >= self.seq // 2
        return jnp.stack([jnp.where(late, back[1], back[0]), jnp.where(late, back[0], back[1])])

    def collect(self, values):
        return self.gathered([self.homeward(v, r) for r, v in enumerate(values)])

    def rotate(self, value, by):
        def move(d, z):
            member = (self.member(d % 2, z) + by) % self.members
            core, at = self.place(z // self.chips, member)
            return d - d % 2 + core, at

        return self.send(value, move)

    def gather(self, value):
        return jnp.concatenate([self.rotate(value, by) for by in range(1, self.members)], axis=0)

    def returns(self, others):
        slots = others.shape[0] // (self.members - 1)
        return jnp.stack(
            [
                self.rotate(others[(by - 1) * slots : by * slots], self.members - by).reshape(
                    -1, others.shape[-1]
                )
                for by in range(1, self.members)
            ]
        )

    def orders(self):
        dp, z = lax.axis_index("dp"), lax.axis_index("seq")
        bits = self.dp.bit_length() - 1
        ids = []
        for core in range(2):
            orders = [[0, *range(1, bits)], [0, *reversed(range(1, bits))]]
            flips = []
            for p in range(self.dp):
                order = orders[core if p >= self.dp // 2 else 1 - core]
                flips.append(
                    sum(
                        (0 if p >> (bits - 1 - i) & 1 else 1) << bit
                        for i, bit in enumerate(order)
                    )
                )
            ids.append(dp ^ jnp.array(flips, jnp.int32))
        ids = jnp.where(dp % 2 == 0, ids[0], ids[1])
        bits = self.seq.bit_length() - 1
        flips = [
            sum((0 if p >> (bits - 1 - i) & 1 else 1) << i for i in range(bits))
            for p in range(self.seq)
        ]
        blocks = z ^ jnp.array(flips, jnp.int32)
        return ids, jnp.argsort(blocks).astype(jnp.int32), blocks

    def partner(self, stage):
        bits = self.dp.bit_length() - 1
        if stage == 0:
            return lambda d, z: (d ^ 1, z)
        if stage < bits:
            return lambda d, z: (d ^ (1 << stage if d % 2 == 0 else 1 << (bits - stage)), z)
        return lambda d, z: (d, z ^ (1 << (stage - bits)))

    def turn(self, sums, after, cost=BRIEF, carrier=None, steps=None):
        sums = [s for s in sums if s.arrived]
        if not sums:
            return carrier(None, after) if carrier else after
        dp_stages = self.dp.bit_length() - 1
        last = dp_stages + self.seq.bit_length() - 1
        groups = []
        for s in sums:
            pairs = list(zip(s.kept, s.arrived))
            single = s.stage + 1 == last
            if s.stage + 1 == dp_stages:
                single = not s.over_seq
                if s.over_seq:
                    pairs = [
                        tuple(
                            v.reshape(v.shape[0], self.seq, -1, v.shape[-1]) for v in pair
                        )
                        for pair in pairs
                    ]
            groups.append((pairs, single, f32 if s.stage + 1 == last else bf16))
        if carrier:
            if Riders.fit(groups, steps) == steps:
                own, out = carrier(Riders(groups, steps), after)
            else:
                out = stage_sums(groups, after, cost=cost)
                own = carrier(None, [part for held in out for part in held])
        else:
            out = stage_sums(groups, after, cost=cost)
        for s, held, (_, single, _) in zip(sums, out, groups):
            s.stage += 1
            s.arrived = ()
            if single:
                s.total = held[0]
            else:
                s.send([held[0]], [held[1]])
        if carrier:
            return own
        return [part for held in out for part in held]

    def over_seq(self, held):
        bits = self.seq.bit_length() - 1
        for bit in range(bits - 1):
            held = held + self.send(held.astype(bf16), lambda d, z: (d, z ^ (1 << bit))).astype(f32)
        return held, self.send(held.astype(bf16), lambda d, z: (d, z ^ (1 << (bits - 1))))


    def over_dp(self, held):
        bits = self.dp.bit_length() - 1
        for bit in range(bits - 1):
            held = held + self.send(held, lambda d, z: (d ^ (1 << bit), z))
        return held, self.send(held, lambda d, z: (d ^ (1 << (bits - 1)), z))


def later_body(left, right, out):
    out[...] = left[...] + right[...]


def later_sum(left, right, after):
    inside = pl.BlockSpec(memory_space=pltpu.VMEM)
    return pl.pallas_call(
        ignoring(later_body, 2, len(after)),
        in_specs=[inside] * 2 + [pl.BlockSpec(memory_space=pl.ANY)] * len(after),
        out_specs=inside,
        out_shape=jax.ShapeDtypeStruct(left.shape, left.dtype),
        name="later_sum",
        cost_estimate=BRIEF,
    )(left, right, *after)


def pack_body(qx_a, qx_b, qs_a, qs_b, rest_ref, out):
    rows = qx_a.shape[0]
    out[:rows] = qx_a[...] + qx_b[...]
    out[rows : 2 * rows] = qs_a[...] + qs_b[...]
    out[2 * rows :] = rest_ref[...]


def pack(first, second, rest, after=()):
    ins = [v.reshape(-1, 128) for v in (first[0], second[0], first[1], second[1])] + [rest]
    rows = 2 * ins[0].shape[0] + rest.shape[0]
    inside = pl.BlockSpec(memory_space=pltpu.VMEM)
    return pl.pallas_call(
        ignoring(pack_body, 5, len(after)),
        in_specs=[inside] * 5 + [pl.BlockSpec(memory_space=pl.ANY)] * len(after),
        out_specs=inside,
        out_shape=jax.ShapeDtypeStruct((rows, 128), f32),
        name="pack",
        cost_estimate=BRIEF,
    )(*ins, *after)


def finish_body(
    mine, other, alpha, damp, beta, eta, alpha_out, damp_out, beta_out, eta_out, rest, rows
):
    rows[...] = mine[...] + other[...].astype(f32)
    states = alpha.shape[0]
    groups = alpha.shape[1] // 128
    for c in range(groups):
        at = slice(c * 128, (c + 1) * 128)
        x_sum = rows[pl.ds(c, states, stride=groups), :]
        s_sum = rows[pl.ds(states * groups + c, states, stride=groups), :]
        rate = alpha[:, at] * beta[:, at]
        input_total = eta[:, at] * x_sum
        decay_total = eta[:, at] * rate * s_sum
        alpha_out[:, at] = beta[:, at] * input_total - damp[:, at] * decay_total
        damp_out[:, at] = -alpha[:, at] * decay_total
        beta_out[:, at] = alpha[:, at] * input_total
        eta_out[:, at] = rate * x_sum
    rest[...] = rows[2 * states * groups :]


def finish(mine, other, alpha, damp, beta, eta):
    inside = pl.BlockSpec(memory_space=pltpu.VMEM)
    rows = mine.shape[0]
    shape = jax.ShapeDtypeStruct(alpha.shape, f32)
    left = rows - 2 * alpha.size // 128
    return pl.pallas_call(
        finish_body,
        in_specs=[inside] * 6,
        out_specs=[inside] * 5,
        out_shape=[shape] * 4 + [jax.ShapeDtypeStruct((left, 128), f32)],
        scratch_shapes=[pltpu.VMEM((rows, 128), f32)],
        name="finish",
        cost_estimate=BRIEF,
    )(mine, other, alpha, damp, beta, eta)


class Sum:
    def __init__(self, layout, *pairs, over_seq=True):
        self.layout, self.over_seq, self.stage = layout, over_seq, 0
        self.total = None
        pairs = [[v.reshape(1, v.shape[0], -1, v.shape[-1]) for v in pair] for pair in pairs]
        self.send([p[0] for p in pairs], [p[1] for p in pairs])

    def send(self, sent, kept):
        self.kept = kept
        self.arrived = [self.layout.send(v, self.layout.partner(self.stage)) for v in sent]

    def begin_seq(self, block):
        self.total = None
        middle = self.layout.seq // 2
        self.send([block[None, :middle]], [block[None, middle:]])


def mm(a, b):
    return jnp.dot(a, b, preferred_element_type=f32)


def mm_nt(a, b):
    return lax.dot_general(a, b, (((1,), (1,)), ((), ())), preferred_element_type=f32)


def mm_tn(a, b):
    return lax.dot_general(a, b, (((0,), (0,)), ((), ())), preferred_element_type=f32)


def layer(
    layout,
    inputs,
    cotangent,
    full_attention,
    mix_gain,
    smooth_alpha,
    smooth_damp,
    smooth_beta,
    smooth_eta,
    smooth_omega,
    value_proj,
    mix_proj,
    score_affine,
    relative_bias,
    out_proj,
    feed_gain,
    feed_in,
    feed_out,
):
    slots, chunk_rows, width = inputs.shape
    key_width = score_affine.shape[1]
    value_width = value_proj.shape[1]
    tokens = slots * chunk_rows
    total = layout.seq
    seq_length = relative_bias.shape[0] // 2
    block = min(128, chunk_rows)
    core = lax.axis_index("dp") % 2
    z = lax.axis_index("seq")

    sequence = z // layout.chips
    member = layout.member(core, z)
    swap = sequence % 2
    chunks = []
    for by in range(layout.members):
        source = (member - by) % layout.members
        low, high = source, total - 1 - source
        chunks += [jnp.where(swap == 0, low, high), jnp.where(swap == 0, high, low)]
    chunks = jnp.stack(chunks).astype(jnp.int32)
    slot_of = jnp.sum(
        jnp.where(chunks[None, :] == jnp.arange(total)[:, None], jnp.arange(total)[None, :], 0),
        axis=1,
    ).astype(jnp.int32)
    flags = full_attention.astype(f32)
    flags_other = layout.send(flags, lambda d, z: (d ^ 1, z))
    flags = jnp.where(
        core == 0, jnp.concatenate([flags, flags_other]), jnp.concatenate([flags_other, flags])
    )
    full = lax.dynamic_index_in_dim(flags, sequence, 0, False) == 1.0
    table = jnp.concatenate([chunks, slot_of, full.astype(jnp.int32)[None]])
    ids, places, blocks = layout.orders()

    arriving = layout.spread(inputs)
    bias_back, bias_front = bias_tiles(relative_bias, chunk_rows // TILE - 1, full)

    states = smooth_alpha.shape[0]
    lanes = (states, width // 128, 128)
    decay = 1.0 - smooth_alpha * smooth_damp
    rate = smooth_alpha * smooth_beta
    span = (decay**chunk_rows).reshape(lanes)
    coef = (smooth_eta * rate).reshape(lanes)
    decay_slab = decay.reshape(lanes)
    gain_row = mix_gain[None]
    omega_row = smooth_omega[None]
    mix_shared, mix_main = mix_proj[:, :key_width], mix_proj[:, key_width:]

    held, after = (), (bias_back, bias_front, mix_main, mix_shared, span, coef)
    for slot in range(slots):
        held = front(
            arriving[slot], slot, slots, held, gain_row, decay_slab, value_proj, after=after
        )
        after = ()
    normed_low, x, value_low, value_slope, ends = held
    ends_all = jnp.concatenate([ends, layout.gather(ends)])
    cotangent, ends_all = lax.optimization_barrier((cotangent, ends_all))
    cots = layout.spread(cotangent)
    normed_low = normed_low.reshape(tokens, width)
    value_slope = value_slope.reshape(tokens, value_width)
    value_others = layout.gather(value_low)
    smoothed, mixed, check, shared_pre, query_low, key_low = front_scan(
        table,
        x,
        gain_row,
        decay_slab,
        coef,
        span,
        omega_row,
        ends_all,
        mix_shared,
        score_affine,
        block,
    )
    smoothed = smoothed.reshape(tokens, width)
    mixed = mixed.reshape(tokens, width)
    shared_pre = shared_pre.reshape(tokens, key_width)
    key_others = layout.gather(key_low)
    base = product(mixed, mix_main)
    attended, gated, lse = attend(
        table,
        query_low,
        bias_front,
        base.reshape(slots, chunk_rows, -1),
        key_low,
        key_others,
        value_low,
        value_others,
    )
    attended = attended.reshape(tokens, value_width)
    gated = gated.reshape(tokens, value_width)

    flat_low = x.reshape(tokens, width)
    cand_in, first_sum, feed_low = candidate(gated, out_proj, base, flat_low, feed_gain[None])

    result_a, result_b, grad_feed, out_send, out_keep, in_send, in_keep = feed(
        ids, places, feed_low, cots, first_sum, feed_in, feed_out, layout.seq
    )
    home = [layout.homeward(result_a, 0), layout.homeward(result_b, 1)]
    block_out = layout.gathered(home)
    feed_sum = Sum(layout, (out_send, out_keep), (in_send, in_keep))

    grad_input, grad_main, grad_att, feed_gain_grad = gate(
        grad_feed, cots, flat_low, cand_in, base, attended, feed_gain[None], out_proj
    )
    after = layout.turn((feed_sum,), (grad_att,))
    mix_parts = by_rows(ids, None, mixed, grad_main, after=after, cost=LONG)
    proj_parts = by_columns(
        ids,
        places,
        grad_main,
        gated,
        rows=width,
        at=grad_main.shape[1] // width - 1,
        after=mix_parts,
    )
    after = (*proj_parts, *home)
    mix_sum = Sum(layout, mix_parts, over_seq=False)
    proj_sum = Sum(layout, proj_parts)
    grad_query, gk_own, gv_own, both_oth, rel_sums = attend_back(
        table,
        query_low,
        grad_att.reshape(slots, chunk_rows, value_width),
        lse.reshape(slots, 1, chunk_rows),
        bias_back,
        key_low,
        key_others,
        value_low,
        value_others,
        after=after,
    )
    both_back = layout.returns(both_oth)
    after = layout.turn((feed_sum, proj_sum), (grad_query,), cost=LONG)
    grad_normed, value_send, value_keep = value_back(
        ids,
        places,
        normed_low,
        gv_own.reshape(tokens, value_width),
        both_back,
        value_slope,
        value_proj,
        layout.seq,
        after=after,
    )
    grad_key = jnp.sum(both_back[:, :, value_width:].astype(f32), axis=0) + gk_own.reshape(
        tokens, key_width
    ).astype(f32)
    grad_query = grad_query.reshape(tokens, key_width)
    grad_shared = (
        (grad_query * score_affine[0] + grad_key * score_affine[2]) * silu_slope(shared_pre)
    ).astype(bf16)
    shared_parts = by_rows(ids, None, mixed, grad_shared, after=(grad_normed,))
    shared_sum = Sum(layout, shared_parts, over_seq=False)
    value_sum = Sum(layout, (value_send, value_keep))
    after = layout.turn((mix_sum,), shared_parts)
    grad_smooth = smooth_back(
        grad_main, grad_shared, mix_main, mix_shared, smoothed, after=after
    )
    grad_smooth = grad_smooth.reshape(slots, chunk_rows, width)
    after = layout.turn((feed_sum, value_sum, proj_sum, shared_sum), (grad_smooth,))
    back = back_ends(grad_smooth, decay_slab, after=after)
    back_all = jnp.concatenate([back, layout.gather(back)])
    after = layout.turn((feed_sum, mix_sum, value_sum, shared_sum), (back,))

    def scan_back(slot, after):
        return back_scan(
            table,
            slot,
            x,
            grad_smooth,
            grad_normed.reshape(slots, chunk_rows, width),
            grad_input.reshape(slots, chunk_rows, width),
            check,
            gain_row,
            decay_slab,
            coef,
            span,
            omega_row,
            back_all,
            after=after,
        )

    first = scan_back(0, after)
    after = layout.turn(
        (feed_sum, mix_sum, value_sum, proj_sum, shared_sum), (first[0],)
    )
    home_first = layout.homeward(first[0], 0)
    while mix_sum.total is None or shared_sum.total is None:
        after = layout.turn((mix_sum, shared_sum), after)
    rows = jnp.concatenate([shared_sum.total[0, 0], mix_sum.total[0, 0]], axis=1)
    rows = rows.reshape(rows.shape[0], layout.seq, -1).transpose(1, 0, 2)
    mix_sum.begin_seq(rows[blocks])
    second = scan_back(1, (*after, *mix_sum.kept))
    affine_grad = jnp.stack(
        [
            jnp.sum(grad_query * shared_pre * jax.nn.sigmoid(shared_pre), axis=0),
            jnp.sum(grad_query, axis=0),
            jnp.sum(grad_key * shared_pre * jax.nn.sigmoid(shared_pre), axis=0),
            jnp.sum(grad_key, axis=0),
        ]
    )
    relative_grad = bias_grad(rel_sums[:, 0], seq_length)
    small = [
        first[3] + second[3],
        first[4] + second[4],
        feed_gain_grad,
        affine_grad,
        relative_grad,
    ]
    small = [v.reshape(-1, 128) for v in small]
    rest = jnp.concatenate(small)
    rest = jnp.pad(rest, ((0, -rest.shape[0] % 16), (0, 0)))
    home_second = layout.homeward(second[0], 1)
    sums = (mix_sum, proj_sum, value_sum, feed_sum)
    turned = layout.turn(sums, (second[0], home_first), cost=LONG)
    totals = layout.over_dp(pack(first[1:3], second[1:3], rest, after=turned))
    after = layout.turn(sums, (*turned, home_second))
    totals = layout.over_seq(later_sum(*totals, after=after))
    while any(v.total is None for v in sums):
        after = layout.turn(sums, after)
    grad_in = layout.gathered([home_first, home_second]).astype(f32)
    feed_out_grad, feed_in_grad = feed_sum.total[0, 0].T, feed_sum.total[1, 0]
    rows = width // layout.dp
    feed_in_grad = feed_in_grad.reshape(-1, rows, feed_in_grad.shape[-1])
    feed_in_grad = feed_in_grad.transpose(1, 0, 2).reshape(rows, -1)
    out_grad, value_grad = proj_sum.total[0, 0].T, value_sum.total[0, 0]
    mix_grad = mix_sum.total[0, 0]
    alpha_grad, damp_grad, beta_grad, eta_grad, totals = finish(
        *totals, smooth_alpha, smooth_damp, smooth_beta, smooth_eta
    )
    parts, start = [], 0
    for item in small:
        parts.append(totals[start : start + item.shape[0]].reshape(-1))
        start += item.shape[0]
    return (
        block_out,
        grad_in,
        parts[0],
        alpha_grad,
        damp_grad,
        beta_grad,
        eta_grad,
        parts[1],
        value_grad,
        mix_grad,
        parts[3].reshape(4, key_width),
        parts[4],
        out_grad,
        parts[2],
        feed_in_grad,
        feed_out_grad,
    )


def solution(mesh):
    tokens = P("dp", "seq", None)
    split = P("dp", "seq")
    return jax.shard_map(
        functools.partial(layer, Layout(mesh)),
        mesh=mesh,
        in_specs=(tokens, tokens, P("dp")) + (P(),) * 14,
        out_specs=(tokens, tokens)
        + (P(),) * 6
        + (split, split, P(), P(), split, P(), split, split),
        check_vma=False,
    )
```

```python
import functools

import jax
import jax.numpy as jnp
from jax import lax
from jax.experimental import pallas as pl
from jax.experimental.pallas import tpu as pltpu
from jax.sharding import PartitionSpec as P

STRETCH = 128
EPSILON = 1e-05
TILE = 256
MASKED = -1e30
VMEM_LIMIT = 60 * 1024 * 1024
AXES = ("dp", "seq")
BRIEF = pl.CostEstimate(flops=1, bytes_accessed=1, transcendentals=0)
LONG = pl.CostEstimate(flops=10**11, bytes_accessed=1, transcendentals=0)

f32 = jnp.float32
bf16 = jnp.bfloat16


def unit_rows_of(values):
    centred = values - jnp.mean(values, axis=-1, keepdims=True)
    inv_std = lax.rsqrt(jnp.mean(centred * centred, axis=-1, keepdims=True) + EPSILON)
    return centred * inv_std, inv_std


def norm_back_rows(grad_out, gain_vec, unit_rows, inv_std):
    scaled = grad_out * gain_vec
    return inv_std * (
        scaled
        - jnp.mean(scaled, axis=-1, keepdims=True)
        - unit_rows * jnp.mean(scaled * unit_rows, axis=-1, keepdims=True)
    )


def silu_slope(pre_act):
    sigmoid_val = jax.nn.sigmoid(pre_act)
    return sigmoid_val * (1.0 + pre_act * (1.0 - sigmoid_val))


def params(semantics, limit=VMEM_LIMIT):
    return pltpu.CompilerParams(dimension_semantics=semantics, vmem_limit_bytes=limit)


def ignoring(body, first, count):
    def called(*refs):
        return body(*refs[:first], *refs[first + count :])

    return called


def to_slab(slab, rows):
    count, groups = rows.shape[0], rows.shape[1] // 128
    for c in range(groups):
        slab[pl.ds(c, count, stride=groups), :] = rows[:, c * 128 : (c + 1) * 128]


def from_slab(slab, count, groups):
    return jnp.concatenate(
        [slab[pl.ds(c, count, stride=groups), :] for c in range(groups)], axis=1
    )


def slab_row(slab, t, groups):
    return slab[pl.ds(pl.multiple_of(t * groups, groups), groups), :]


def front_body(
    x_ref,
    gain_ref,
    decay_ref,
    proj_ref,
    begin_ref,
    low_ref,
    copy_ref,
    value_ref,
    slope_ref,
    end_ref,
    slab,
    *,
    fresh,
):
    states, groups, _ = decay_ref.shape
    count = x_ref.shape[0]

    @pl.when(pl.program_id(0) == 0)
    def _():
        end_ref[...] = jnp.zeros_like(end_ref) if fresh else begin_ref[...]

    copy_ref[0] = x_ref[...]
    unit, _ = unit_rows_of(x_ref[...].astype(f32))
    normed = unit * gain_ref[...]
    low_ref[0] = normed.astype(bf16)
    to_slab(slab, normed)
    decay = [decay_ref[n] for n in range(states)]

    def step(t, state):
        row = slab_row(slab, t, groups)
        return tuple(d * s + row for d, s in zip(decay, state))

    state = lax.fori_loop(
        0, count, step, tuple(end_ref[0, n] for n in range(states)), unroll=8
    )
    for n in range(states):
        end_ref[0, n] = state[n]
    for c in range(proj_ref.shape[1] // 512):
        at = slice(c * 512, (c + 1) * 512)
        pre = jnp.dot(low_ref[0], proj_ref[:, at], preferred_element_type=f32)
        gate = jax.nn.sigmoid(pre)
        value = pre * gate
        value_ref[0, :, at] = value.astype(bf16)
        slope_ref[0, :, at] = (gate + value * (1.0 - gate)).astype(bf16)


def front(x, slot, row, whole, earlier, gain, decay, proj, after=()):
    rows, width = x.shape
    slots, length = whole
    value_width = proj.shape[1]
    states, groups, lanes = decay.shape
    block = min(256, rows)
    first = row // block
    begin = earlier[-1] if row else jnp.zeros((slots, *decay.shape), f32)
    anywhere = pl.BlockSpec(memory_space=pl.ANY)

    def tokens(columns):
        return pl.BlockSpec((1, block, columns), lambda b: (slot, first + b, 0))

    return pl.pallas_call(
        ignoring(functools.partial(front_body, fresh=row == 0), 5, len(earlier) + len(after)),
        grid=(rows // block,),
        in_specs=[
            pl.BlockSpec((block, width), lambda b: (b, 0)),
            pl.BlockSpec((1, width), lambda b: (0, 0)),
            pl.BlockSpec((states, groups, lanes), lambda b: (0, 0, 0)),
            pl.BlockSpec(proj.shape, lambda b: (0, 0), pipeline_mode=pl.Buffered(1)),
            pl.BlockSpec((1, states, groups, lanes), lambda b: (slot, 0, 0, 0)),
        ]
        + [anywhere] * (len(earlier) + len(after)),
        out_specs=[
            tokens(width),
            tokens(width),
            tokens(value_width),
            tokens(value_width),
            pl.BlockSpec((1, states, groups, lanes), lambda b: (slot, 0, 0, 0)),
        ],
        out_shape=[
            jax.ShapeDtypeStruct((slots, length, width), bf16),
            jax.ShapeDtypeStruct((slots, length, width), bf16),
            jax.ShapeDtypeStruct((slots, length, value_width), bf16),
            jax.ShapeDtypeStruct((slots, length, value_width), bf16),
            jax.ShapeDtypeStruct((slots, states, groups, lanes), f32),
        ],
        scratch_shapes=[pltpu.VMEM((block * groups, lanes), f32)],
        input_output_aliases={5 + k: k for k in range(len(earlier))},
        compiler_params=params(("arbitrary",)),
        name="front",
        cost_estimate=BRIEF,
    )(x, gain, decay, proj, begin, *earlier, *after)


def front_scan_body(
    table_ref,
    x_ref,
    gain_ref,
    decay_ref,
    coef_ref,
    span_ref,
    omega_ref,
    ends_own,
    ends_oth,
    proj_ref,
    affine_ref,
    smooth_ref,
    mixed_ref,
    check_ref,
    shared_ref,
    query_ref,
    key_ref,
    slab,
    out_slab,
    carry,
    ends_ref,
):
    states, groups, _ = decay_ref.shape
    count = x_ref.shape[1]
    slot = pl.program_id(0)
    slots = ends_own.shape[0]
    total = slots + ends_oth.shape[0]

    @pl.when(pl.program_id(1) == 0)
    def _():
        carry[...] = jnp.zeros_like(carry)
        ends_ref[:slots] = ends_own[...]
        ends_ref[slots:] = ends_oth[...]

        def link(i, _):
            carry[...] = span_ref[...] * carry[...] + ends_ref[table_ref[total + i]]
            return 0

        lax.fori_loop(0, table_ref[slot], link, 0)

    unit, _ = unit_rows_of(x_ref[0].astype(f32))
    normed = unit * gain_ref[...]
    to_slab(slab, normed)
    decay = [decay_ref[n] for n in range(states)]
    coef = [coef_ref[n] for n in range(states)]
    state = tuple(carry[n] for n in range(states))
    for n in range(states):
        check_ref[0, 0, n] = state[n]

    def step(t, state):
        row = slab_row(slab, t, groups)
        state = tuple(d * s + row for d, s in zip(decay, state))
        parts = [c * s for c, s in zip(coef, state)]
        while len(parts) > 1:
            parts = [a + b for a, b in zip(parts[::2], parts[1::2])]
        out_slab[pl.ds(pl.multiple_of(t * groups, groups), groups), :] = parts[0]
        return state

    state = lax.fori_loop(0, count, step, state, unroll=8)
    for n in range(states):
        carry[n] = state[n]
    smoothed = from_slab(out_slab, count, groups) + omega_ref[...] * normed
    smooth_ref[0] = smoothed
    mixed = (smoothed * jax.nn.sigmoid(smoothed)).astype(bf16)
    mixed_ref[0] = mixed
    shared_pre = jnp.dot(mixed, proj_ref[...], preferred_element_type=f32)
    shared = shared_pre * jax.nn.sigmoid(shared_pre)
    shared_ref[0] = shared_pre
    query_ref[0] = (shared * affine_ref[0:1] + affine_ref[1:2]).astype(bf16)
    key_ref[0] = (shared * affine_ref[2:3] + affine_ref[3:4]).astype(bf16)


def front_scan(table, x, gain, decay, coef, span, omega, ends, others, proj, affine, block):
    slots, length, width = x.shape
    states, groups, lanes = decay.shape
    whole3 = pl.BlockSpec((states, groups, lanes), lambda k, b, t: (0, 0, 0))
    row = pl.BlockSpec((1, width), lambda k, b, t: (0, 0))
    tokens = pl.BlockSpec((1, block, width), lambda k, b, t: (k, b, 0))
    narrow = pl.BlockSpec((1, block, proj.shape[1]), lambda k, b, t: (k, b, 0))
    return pl.pallas_call(
        front_scan_body,
        grid_spec=pltpu.PrefetchScalarGridSpec(
            num_scalar_prefetch=1,
            grid=(slots, length // block),
            in_specs=[
                tokens,
                row,
                whole3,
                whole3,
                whole3,
                row,
                pl.BlockSpec(ends.shape, lambda k, b, t: (0, 0, 0, 0)),
                pl.BlockSpec(others.shape, lambda k, b, t: (0, 0, 0, 0)),
                pl.BlockSpec(proj.shape, lambda k, b, t: (0, 0)),
                pl.BlockSpec(affine.shape, lambda k, b, t: (0, 0)),
            ],
            out_specs=[
                tokens,
                tokens,
                pl.BlockSpec((1, 1, states, groups, lanes), lambda k, b, t: (k, b, 0, 0, 0)),
                narrow,
                narrow,
                narrow,
            ],
            scratch_shapes=[
                pltpu.VMEM((block * groups, lanes), f32),
                pltpu.VMEM((block * groups, lanes), f32),
                pltpu.VMEM((states, groups, lanes), f32),
                pltpu.VMEM((ends.shape[0] + others.shape[0], states, groups, lanes), f32),
            ],
        ),
        out_shape=[
            jax.ShapeDtypeStruct((slots, length, width), f32),
            jax.ShapeDtypeStruct((slots, length, width), bf16),
            jax.ShapeDtypeStruct((slots, length // block, states, groups, lanes), f32),
            jax.ShapeDtypeStruct((slots, length, proj.shape[1]), f32),
            jax.ShapeDtypeStruct((slots, length, proj.shape[1]), bf16),
            jax.ShapeDtypeStruct((slots, length, proj.shape[1]), bf16),
        ],
        compiler_params=params(("arbitrary", "arbitrary")),
        name="front_scan",
        cost_estimate=LONG,
    )(table, x, gain, decay, coef, span, omega, ends, others, proj, affine)


def back_ends_body(gs_ref, decay_ref, end_ref, slab):
    states, groups, _ = decay_ref.shape
    slots, count, _ = gs_ref.shape

    @pl.when(pl.program_id(0) == 0)
    def _():
        end_ref[...] = jnp.zeros_like(end_ref)

    for k in range(slots):
        to_slab(slab.at[k], gs_ref[k])
    decay = [decay_ref[n] for n in range(states)]

    def step(t, state):
        rows = [slab_row(slab.at[k], count - 1 - t, groups) for k in range(slots)]
        return [tuple(d * s + row for d, s in zip(decay, held)) for row, held in zip(rows, state)]

    state = lax.fori_loop(
        0,
        count,
        step,
        [tuple(end_ref[k, n] for n in range(states)) for k in range(slots)],
        unroll=8,
    )
    for k in range(slots):
        for n in range(states):
            end_ref[k, n] = state[k][n]


def back_ends(gs, decay, block=128, after=()):
    slots, length, width = gs.shape
    states, groups, lanes = decay.shape
    block = min(block, length)
    blocks = length // block
    return pl.pallas_call(
        ignoring(back_ends_body, 2, len(after)),
        grid=(blocks,),
        in_specs=[
            pl.BlockSpec((slots, block, width), lambda b: (0, blocks - 1 - b, 0)),
            pl.BlockSpec((states, groups, lanes), lambda b: (0, 0, 0)),
        ]
        + [pl.BlockSpec(memory_space=pl.ANY)] * len(after),
        out_specs=pl.BlockSpec((slots, states, groups, lanes), lambda b: (0, 0, 0, 0)),
        out_shape=jax.ShapeDtypeStruct((slots, states, groups, lanes), f32),
        scratch_shapes=[pltpu.VMEM((slots, block * groups, lanes), f32)],
        compiler_params=params(("arbitrary",)),
        name="back_ends",
        cost_estimate=BRIEF,
    )(gs, decay, *after)


def back_scan_body(
    table_ref,
    slot_ref,
    x_ref,
    gs_ref,
    gv_ref,
    gi_ref,
    check_ref,
    gain_ref,
    decay_ref,
    coef_ref,
    span_ref,
    omega_ref,
    ends_own,
    ends_oth,
    grad_ref,
    qx_ref,
    qs_ref,
    gain_grad_ref,
    omega_grad_ref,
    slab,
    gs_slab,
    out_slab,
    history,
    carry,
    ends_ref,
):
    states, groups, _ = decay_ref.shape
    count = x_ref.shape[1]
    slot = slot_ref[0]
    slots = ends_own.shape[0]
    total = slots + ends_oth.shape[0]

    @pl.when(pl.program_id(0) == 0)
    def _():
        qx_ref[...] = jnp.zeros_like(qx_ref)
        qs_ref[...] = jnp.zeros_like(qs_ref)
        gain_grad_ref[...] = jnp.zeros_like(gain_grad_ref)
        omega_grad_ref[...] = jnp.zeros_like(omega_grad_ref)

    @pl.when(pl.program_id(0) == 0)
    def _():
        carry[...] = jnp.zeros_like(carry)
        ends_ref[:slots] = ends_own[...]
        ends_ref[slots:] = ends_oth[...]

        def link(i, _):
            carry[...] = (
                span_ref[...] * carry[...] + ends_ref[table_ref[total + total - 1 - i]]
            )
            return 0

        lax.fori_loop(0, total - 1 - table_ref[slot], link, 0)

    unit, inv = unit_rows_of(x_ref[0].astype(f32))
    normed = unit * gain_ref[...]
    gs = gs_ref[0]
    to_slab(slab, normed)
    to_slab(gs_slab, gs)
    decay = [decay_ref[n] for n in range(states)]

    def recompute(t, state):
        for n in range(states):
            history[t, n] = state[n]
        row = slab_row(slab, t, groups)
        return tuple(d * s + row for d, s in zip(decay, state))

    lax.fori_loop(
        0, count, recompute, tuple(check_ref[0, 0, n] for n in range(states)), unroll=4
    )

    half = states // 2
    for part in range(2):
        chosen = range(part * half, (part + 1) * half)
        decay = [decay_ref[n] for n in chosen]
        coef = [coef_ref[n] for n in chosen]

        def step(i, held):
            q, qx, qs = held
            t = count - 1 - i
            row = slab_row(slab, t, groups)
            g = slab_row(gs_slab, t, groups)
            q = tuple(d * a + g for d, a in zip(decay, q))
            parts = [c * a for c, a in zip(coef, q)]
            while len(parts) > 1:
                parts = [a + b for a, b in zip(parts[::2], parts[1::2])]
            spot = pl.ds(pl.multiple_of(t * groups, groups), groups)
            if part == 0:
                out_slab[spot, :] = parts[0]
            else:
                out_slab[spot, :] = out_slab[spot, :] + parts[0]
            qx = tuple(a + b * row for a, b in zip(qx, q))
            qs = tuple(a + b * history[t, n] for a, b, n in zip(qs, q, chosen))
            return q, qx, qs

        q, qx, qs = lax.fori_loop(
            0,
            count,
            step,
            (
                tuple(carry[n] for n in chosen),
                tuple(qx_ref[n] for n in chosen),
                tuple(qs_ref[n] for n in chosen),
            ),
            unroll=4,
        )
        for i, n in enumerate(chosen):
            carry[n] = q[i]
            qx_ref[n] = qx[i]
            qs_ref[n] = qs[i]

    grad_normed = (
        gv_ref[0] + from_slab(out_slab, count, groups) + omega_ref[...] * gs
    )
    gain_grad_ref[...] += jnp.sum(grad_normed * unit, axis=0, keepdims=True)
    omega_grad_ref[...] += jnp.sum(gs * normed, axis=0, keepdims=True)
    grad_ref[...] = (
        gi_ref[0] + norm_back_rows(grad_normed, gain_ref[...], unit, inv)
    ).astype(bf16)


def back_scan(table, slot, x, gs, gv, gi, check, gain, decay, coef, span, omega, ends, others, after=()):
    _, length, width = x.shape
    states, groups, lanes = decay.shape
    blocks = check.shape[1]
    block = length // blocks
    whole3 = pl.BlockSpec((states, groups, lanes), lambda b, t, u: (0, 0, 0))
    row = pl.BlockSpec((1, width), lambda b, t, u: (0, 0))
    tokens = pl.BlockSpec((1, block, width), lambda b, t, u: (slot, blocks - 1 - b, 0))
    return pl.pallas_call(
        ignoring(back_scan_body, 14, len(after)),
        grid_spec=pltpu.PrefetchScalarGridSpec(
            num_scalar_prefetch=2,
            grid=(blocks,),
            in_specs=[
                tokens,
                tokens,
                tokens,
                tokens,
                pl.BlockSpec(
                    (1, 1, states, groups, lanes),
                    lambda b, t, u: (slot, blocks - 1 - b, 0, 0, 0),
                ),
                row,
                whole3,
                whole3,
                whole3,
                row,
                pl.BlockSpec(ends.shape, lambda b, t, u: (0, 0, 0, 0)),
                pl.BlockSpec(others.shape, lambda b, t, u: (0, 0, 0, 0)),
            ]
            + [pl.BlockSpec(memory_space=pl.ANY)] * len(after),
            out_specs=[
                pl.BlockSpec((block, width), lambda b, t, u: (blocks - 1 - b, 0)),
                whole3,
                whole3,
                row,
                row,
            ],
            scratch_shapes=[
                pltpu.VMEM((block * groups, lanes), f32),
                pltpu.VMEM((block * groups, lanes), f32),
                pltpu.VMEM((block * groups, lanes), f32),
                pltpu.VMEM((block, states, groups, lanes), f32),
                pltpu.VMEM((states, groups, lanes), f32),
                pltpu.VMEM((ends.shape[0] + others.shape[0], states, groups, lanes), f32),
            ],
        ),
        out_shape=[
            jax.ShapeDtypeStruct((length, width), bf16),
            jax.ShapeDtypeStruct((states, groups, lanes), f32),
            jax.ShapeDtypeStruct((states, groups, lanes), f32),
            jax.ShapeDtypeStruct((1, width), f32),
            jax.ShapeDtypeStruct((1, width), f32),
        ],
        compiler_params=params(("arbitrary",)),
        name="back_scan",
        cost_estimate=LONG,
    )(table, jnp.full((1,), slot, jnp.int32), x, gs, gv, gi, check, gain, decay, coef, span, omega, ends, others, *after)


def chunk_copies(table_ref, own, others, kept, total, length, sem):
    copies = []
    for slot in range(total):
        place = pl.ds(pl.multiple_of(table_ref[slot] * length, length), length)
        source = own.at[slot] if slot < 2 else others.at[slot - 2]
        copies.append(pltpu.make_async_copy(source, kept.at[place, :], sem.at[slot]))
    return copies


def attend_body(
    table_ref,
    q_ref,
    bias_ref,
    reset_ref,
    k_own,
    k_oth,
    v_own,
    v_oth,
    out_ref,
    gated_ref,
    lse_ref,
    keys,
    values,
    scores,
    probs,
    key_sem,
    value_sem,
    *,
    total,
):
    length, key_width = q_ref.shape[1:]
    value_width = values.shape[1]
    tiles = length // TILE
    scale = float(key_width) ** (-0.5)

    key_copies = chunk_copies(table_ref, k_own, k_oth, keys, total, length, key_sem)
    value_copies = chunk_copies(table_ref, v_own, v_oth, values, total, length, value_sem)

    @pl.when(pl.program_id(0) == 0)
    def _():
        for copy in key_copies + value_copies:
            copy.start()
        for copy in key_copies:
            copy.wait()

    chunk = table_ref[pl.program_id(0)]
    reach = jnp.where(table_ref[2 * total] == 1, chunk + 1, 1)
    base = (chunk + 1 - reach) * length
    queries = q_ref[0]

    def first(kt, peak):
        spot = pl.ds(pl.multiple_of(base + kt * TILE, TILE), TILE)
        tile = (
            lax.dot_general(
                queries, keys[spot, :], (((1,), (1,)), ((), ())), preferred_element_type=f32
            )
            * scale
        )
        for r in range(tiles):
            rows = slice(r * TILE, (r + 1) * TILE)
            gap = (reach - 1) * tiles + r - kt + tiles - 1
            scores[kt, rows, :] = tile[rows] + bias_ref[gap]
        return jnp.maximum(peak, jnp.max(scores[kt], axis=1, keepdims=True))

    peak = lax.fori_loop(
        0, reach * tiles, first, jnp.full((length, 1), 2 * MASKED, f32)
    )

    def second(kt, sums):
        terms = jnp.exp(scores[kt] - peak)
        probs[:, pl.ds(pl.multiple_of(kt * TILE, TILE), TILE)] = terms.astype(bf16)
        return sums + jnp.sum(terms, axis=1, keepdims=True)

    sums = lax.fori_loop(0, reach * tiles, second, jnp.zeros((length, 1), f32))
    lse_ref[0] = jnp.broadcast_to(peak + jnp.log(sums), (length, 128)).T[:1]
    inverse = 1.0 / sums

    @pl.when(pl.program_id(0) == 0)
    def _():
        for copy in value_copies:
            copy.wait()

    for count in range(1, total + 1):

        @pl.when(reach == count)
        def _(count=count):
            width = count * length
            span = pl.ds(pl.multiple_of(base, length), width)

            def column(ct, _):
                at = pl.ds(pl.multiple_of(ct * 1024, 1024), 1024)
                rows = (
                    jnp.dot(probs[:, :width], values[span, at], preferred_element_type=f32)
                    * inverse
                )
                out_ref[0, :, at] = rows.astype(bf16)
                gate = reset_ref[0, :, at].astype(f32)
                gated_ref[0, :, at] = (gate * jax.nn.sigmoid(gate) * rows).astype(bf16)
                return 0

            lax.fori_loop(0, value_width // 1024, column, 0)


def attend(table, q, bias, reset, k_own, k_oth, v_own, v_oth):
    slots, length, key_width = q.shape
    value_width = v_own.shape[2]
    total = slots + k_oth.shape[0]
    anywhere = pl.BlockSpec(memory_space=pl.ANY)
    tokens = pl.BlockSpec((1, length, value_width), lambda k, t: (k, 0, 0))
    return pl.pallas_call(
        functools.partial(attend_body, total=total),
        grid_spec=pltpu.PrefetchScalarGridSpec(
            num_scalar_prefetch=1,
            grid=(slots,),
            in_specs=[
                pl.BlockSpec((1, length, key_width), lambda k, t: (k, 0, 0)),
                pl.BlockSpec(bias.shape, lambda k, t: (0, 0, 0)),
                tokens,
                anywhere,
                anywhere,
                anywhere,
                anywhere,
            ],
            out_specs=[
                tokens,
                tokens,
                pl.BlockSpec((1, 1, length), lambda k, t: (k, 0, 0)),
            ],
            scratch_shapes=[
                pltpu.VMEM((total * length, key_width), bf16),
                pltpu.VMEM((total * length, value_width), bf16),
                pltpu.VMEM((total * length // TILE, length, TILE), f32),
                pltpu.VMEM((length, total * length), bf16),
                pltpu.SemaphoreType.DMA((total,)),
                pltpu.SemaphoreType.DMA((total,)),
            ],
        ),
        out_shape=[
            jax.ShapeDtypeStruct((slots, length, value_width), bf16),
            jax.ShapeDtypeStruct((slots, length, value_width), bf16),
            jax.ShapeDtypeStruct((slots, 1, length), f32),
        ],
        compiler_params=params(("arbitrary",)),
        name="attend",
        cost_estimate=BRIEF,
    )(table, q, bias, reset, k_own, k_oth, v_own, v_oth)


def attend_back_body(
    table_ref,
    q_ref,
    grad_ref,
    lse_ref,
    bias_ref,
    k_own,
    k_oth,
    v_own,
    v_oth,
    gq_ref,
    gk_own,
    gv_own,
    both_oth,
    rel_out,
    keys,
    values,
    gk_sum,
    gv_sum,
    probs_kept,
    grads_kept,
    rel_ref,
    key_sem,
    value_sem,
    *,
    total,
):
    length, key_width = q_ref.shape[1:]
    value_width = values.shape[1]
    tiles = length // TILE
    scale = float(key_width) ** (-0.5)
    step = pl.program_id(0)
    nt = (((1,), (1,)), ((), ()))
    tn = (((0,), (0,)), ((), ()))

    copies = chunk_copies(
        table_ref, k_own, k_oth, keys, total, length, key_sem
    ) + chunk_copies(table_ref, v_own, v_oth, values, total, length, value_sem)

    @pl.when(step == 0)
    def _():
        for copy in copies:
            copy.start()
        gk_sum[...] = jnp.zeros_like(gk_sum)
        gv_sum[...] = jnp.zeros_like(gv_sum)
        rel_ref[...] = jnp.zeros_like(rel_ref)
        for copy in copies:
            copy.wait()

    chunk = table_ref[step]
    reach = jnp.where(table_ref[2 * total] == 1, chunk + 1, 1)
    base = (chunk + 1 - reach) * length
    queries = q_ref[0]
    log_total = lse_ref[0]

    def gap_of(kc, a, r):
        return (reach - 1 - kc) * tiles + r - a + tiles - 1

    def first(kc, delta):
        spot = pl.ds(pl.multiple_of(base + kc * length, length), length)
        grads_kept[kc] = lax.dot_general(
            values[spot, :], grad_ref[0], nt, preferred_element_type=f32
        )
        tile = (
            lax.dot_general(keys[spot, :], queries, nt, preferred_element_type=f32) * scale
        )
        for a in range(tiles):
            for r in range(tiles):
                rows = slice(a * TILE, (a + 1) * TILE)
                cols = slice(r * TILE, (r + 1) * TILE)
                probs_kept[kc, rows, cols] = jnp.exp(
                    tile[rows, cols] + bias_ref[gap_of(kc, a, r)] - log_total[:, cols]
                )
        return delta + jnp.sum(probs_kept[kc] * grads_kept[kc], axis=0, keepdims=True)

    delta = lax.fori_loop(0, reach, first, jnp.zeros((1, length), f32))

    def second(kc, grad_query):
        spot = pl.ds(pl.multiple_of(base + kc * length, length), length)
        probs = probs_kept[kc]
        grad_scores = (probs * (grads_kept[kc] - delta)).astype(bf16)
        probs = probs.astype(bf16)
        for a in range(tiles):
            for r in range(tiles):
                rel_ref[gap_of(kc, a, r)] += grad_scores[
                    a * TILE : (a + 1) * TILE, r * TILE : (r + 1) * TILE
                ].astype(f32)
        gk_sum[spot, :] += jnp.dot(grad_scores, queries, preferred_element_type=f32)

        def column(ct, _):
            at = pl.ds(pl.multiple_of(ct * 1024, 1024), 1024)
            gv_sum[spot, at] += jnp.dot(
                probs, grad_ref[0, :, at], preferred_element_type=f32
            )
            return 0

        lax.fori_loop(0, value_width // 1024, column, 0)
        return grad_query + lax.dot_general(
            grad_scores, keys[spot, :], tn, preferred_element_type=f32
        )

    grad_query = lax.fori_loop(0, reach, second, jnp.zeros((length, key_width), f32))
    gq_ref[0] = grad_query * scale

    @pl.when(step == pl.num_programs(0) - 1)
    def _():
        for slot in range(total):
            place = pl.ds(pl.multiple_of(table_ref[slot] * length, length), length)
            key_grad = (gk_sum[place, :] * scale).astype(bf16)
            value_grad = gv_sum[place, :].astype(bf16)
            if slot < 2:
                gk_own[slot] = key_grad
                gv_own[slot] = value_grad
            else:
                both_oth[slot - 2, :, :value_width] = value_grad
                both_oth[slot - 2, :, value_width:] = key_grad
        down = lax.broadcasted_iota(jnp.int32, (TILE, TILE), 0)
        across = lax.broadcasted_iota(jnp.int32, (TILE, TILE), 1)
        mirror = jnp.where(down + across == TILE - 1, 1.0, 0.0)
        for d in range(rel_out.shape[0]):
            flipped = jnp.dot(
                rel_ref[d + tiles - 1],
                mirror,
                precision=lax.Precision.HIGHEST,
                preferred_element_type=f32,
            )
            wide = jnp.concatenate([flipped, jnp.zeros((TILE, TILE), f32)], axis=1)
            turned = pltpu.roll(wide, 0, 1, stride=1, stride_axis=0)
            rel_out[d] = jnp.sum(turned, axis=0, keepdims=True)


def attend_back(table, q, grads, lse, bias, k_own, k_oth, v_own, v_oth, after=()):
    slots, length, key_width = q.shape
    value_width = v_own.shape[2]
    total = slots + k_oth.shape[0]
    rel_shape = (total * length // TILE, 1, 2 * TILE)
    both_shape = (k_oth.shape[0], length, key_width + value_width)
    anywhere = pl.BlockSpec(memory_space=pl.ANY)

    def all_of(shape):
        return pl.BlockSpec(
            shape, lambda k, t: (0,) * len(shape), pipeline_mode=pl.Buffered(1)
        )

    return pl.pallas_call(
        ignoring(functools.partial(attend_back_body, total=total), 9, len(after)),
        grid_spec=pltpu.PrefetchScalarGridSpec(
            num_scalar_prefetch=1,
            grid=(slots,),
            in_specs=[
                pl.BlockSpec((1, length, key_width), lambda k, t: (k, 0, 0)),
                pl.BlockSpec((1, length, value_width), lambda k, t: (k, 0, 0)),
                pl.BlockSpec((1, 1, length), lambda k, t: (k, 0, 0)),
                all_of(bias.shape),
                anywhere,
                anywhere,
                anywhere,
                anywhere,
            ]
            + [anywhere] * len(after),
            out_specs=[
                pl.BlockSpec((1, length, key_width), lambda k, t: (k, 0, 0)),
                all_of(k_own.shape),
                all_of(v_own.shape),
                all_of(both_shape),
                all_of(rel_shape),
            ],
            scratch_shapes=[
                pltpu.VMEM((total * length, key_width), bf16),
                pltpu.VMEM((total * length, value_width), bf16),
                pltpu.VMEM((total * length, key_width), f32),
                pltpu.VMEM((total * length, value_width), f32),
                pltpu.VMEM((total, length, length), f32),
                pltpu.VMEM((total, length, length), f32),
                pltpu.VMEM(bias.shape, f32),
                pltpu.SemaphoreType.DMA((total,)),
                pltpu.SemaphoreType.DMA((total,)),
            ],
        ),
        out_shape=[
            jax.ShapeDtypeStruct((slots, length, key_width), f32),
            jax.ShapeDtypeStruct(k_own.shape, bf16),
            jax.ShapeDtypeStruct(v_own.shape, bf16),
            jax.ShapeDtypeStruct(both_shape, bf16),
            jax.ShapeDtypeStruct(rel_shape, f32),
        ],
        compiler_params=params(("arbitrary",)),
        name="attend_back",
        cost_estimate=LONG,
    )(table, q, grads, lse, bias, k_own, k_oth, v_own, v_oth, *after)


def bias_body(flag_ref, back_row, front_row, back_ref, front_ref, *, spare):
    tile = pl.program_id(0) - spare
    full = flag_ref[0] == 1

    @pl.when(tile < 0)
    def _():
        back_ref[...] = jnp.full_like(back_ref, MASKED)
        front_ref[...] = jnp.full_like(front_ref, MASKED)

    @pl.when(tile >= 0)
    def _():
        down = lax.broadcasted_iota(jnp.int32, (TILE, TILE), 0)
        across = lax.broadcasted_iota(jnp.int32, (TILE, TILE), 1)
        near = jnp.where(down // STRETCH == across // STRETCH, 1, 0)
        for row, out, ordered in (
            (back_row, back_ref, jnp.where(down <= across, 1, 0)),
            (front_row, front_ref, jnp.where(across <= down, 1, 0)),
        ):
            wide = jnp.broadcast_to(row[0], (TILE, 2 * TILE))
            turned = pltpu.roll(wide, 0, 1, stride=1, stride_axis=0)[:, :TILE]
            allowed = jnp.where(
                tile == 0, jnp.where(full, ordered, ordered * near), jnp.where(full, 1, 0)
            )
            out[0] = jnp.where(allowed == 1, turned, MASKED)


def bias_tiles(relative_bias, spare, full):
    length = relative_bias.shape[0] // 2
    count = length // TILE
    windows = jnp.stack(
        [
            lax.slice_in_dim(relative_bias, length - d * TILE - TILE, length - d * TILE + TILE)
            for d in range(count)
        ]
    )
    front = jnp.concatenate([windows[:, TILE:], windows[:, :TILE]], axis=1)
    back = jnp.concatenate([windows[:, TILE:TILE + 1], windows[:, ::-1][:, TILE:], windows[:, ::-1][:, : TILE - 1]], axis=1)
    row = pl.BlockSpec((1, 1, 2 * TILE), lambda d, t: (jnp.maximum(d - spare, 0), 0, 0))
    out = pl.BlockSpec((1, TILE, TILE), lambda d, t: (d, 0, 0))
    shape = jax.ShapeDtypeStruct((spare + count, TILE, TILE), f32)
    return pl.pallas_call(
        functools.partial(bias_body, spare=spare),
        grid_spec=pltpu.PrefetchScalarGridSpec(
            num_scalar_prefetch=1,
            grid=(spare + count,),
            in_specs=[row, row],
            out_specs=[out, out],
        ),
        out_shape=[shape, shape],
        compiler_params=params(("arbitrary",)),
        name="bias",
    )(full.astype(jnp.int32)[None], back[:, None], front[:, None])


def bias_grad(sums, length):
    count = sums.shape[0]
    shifted = jnp.concatenate([jnp.zeros((count, 1), f32), sums[:, :-1]], axis=1)
    none = jnp.zeros((1, TILE), f32)
    blocks = jnp.concatenate([none, shifted[:, :TILE]]) + jnp.concatenate(
        [shifted[:, TILE:], none]
    )
    return jnp.concatenate(
        [blocks[::-1].reshape(-1), jnp.zeros((2 * length - (count + 1) * TILE,), f32)]
    )


def candidate_body(
    gated_ref, proj_ref, pre_ref, update_ref, x_ref, gain_ref, cand_ref, first_ref, low_ref
):
    cand_in = pre_ref[...].astype(f32) + jnp.dot(
        gated_ref[...], proj_ref[...], preferred_element_type=f32
    )
    cand_ref[...] = cand_in
    x = x_ref[...].astype(f32)
    update = jax.nn.sigmoid(update_ref[...].astype(f32))
    first = x + update * (cand_in * jax.nn.sigmoid(cand_in) - x)
    first_ref[...] = first
    unit, _ = unit_rows_of(first)
    low_ref[...] = (unit * gain_ref[...]).astype(bf16)


def candidate(gated, proj, base, x, gain):
    tokens, width = x.shape
    value_width = gated.shape[1]
    rows = min(256, tokens)
    wide = value_width // width

    def block(columns, at=0):
        return pl.BlockSpec((rows, columns), lambda i: (i, at))

    return pl.pallas_call(
        candidate_body,
        grid=(tokens // rows,),
        in_specs=[
            block(value_width),
            pl.BlockSpec(proj.shape, lambda i: (0, 0), pipeline_mode=pl.Buffered(1)),
            block(width, wide + 1),
            block(width, wide),
            block(width),
            pl.BlockSpec((1, width), lambda i: (0, 0)),
        ],
        out_specs=[block(width)] * 3,
        out_shape=[
            jax.ShapeDtypeStruct((tokens, width), f32),
            jax.ShapeDtypeStruct((tokens, width), f32),
            jax.ShapeDtypeStruct((tokens, width), bf16),
        ],
        compiler_params=params(("arbitrary",)),
        name="candidate",
        cost_estimate=BRIEF,
    )(gated, proj, base, base, x, gain)


def gate_body(
    back_ref,
    cot_a,
    cot_b,
    x_ref,
    cand_ref,
    update_ref,
    reset_ref,
    attended_ref,
    gain_ref,
    proj_ref,
    input_ref,
    main_ref,
    grad_att_ref,
    gain_grad_ref,
):
    width = x_ref.shape[1]
    value_width = proj_ref.shape[0]

    @pl.when(pl.program_id(0) == 0)
    def _():
        gain_grad_ref[...] = jnp.zeros_like(gain_grad_ref)

    x = x_ref[...].astype(f32)
    cand_in = cand_ref[...]
    gate = jax.nn.sigmoid(cand_in)
    candidate = cand_in * gate
    update = jax.nn.sigmoid(update_ref[...].astype(f32))
    change = candidate - x
    unit, inv = unit_rows_of(x + update * change)
    grad_feed = back_ref[...]
    gain_grad_ref[...] += jnp.sum(grad_feed * unit, axis=0, keepdims=True)
    early = pl.program_id(0) < pl.num_programs(0) // 2
    cot = jnp.where(early, cot_a[...].astype(f32), cot_b[...].astype(f32))
    grad_first = cot + norm_back_rows(
        grad_feed, gain_ref[...], unit, inv
    )
    kept = grad_first * (1.0 - update)
    input_ref[...] = kept
    main_ref[:, value_width : value_width + width] = (kept * change * update).astype(bf16)
    grad_cand = (grad_first * update * (gate + candidate * (1.0 - gate))).astype(bf16)
    main_ref[:, value_width + width :] = grad_cand
    for c in range(value_width // 512):
        at = slice(c * 512, (c + 1) * 512)
        grad_gated = mm_nt(grad_cand, proj_ref[at, :])
        reset = reset_ref[:, at].astype(f32)
        open_gate = jax.nn.sigmoid(reset)
        passed = reset * open_gate
        grad_att_ref[:, at] = (grad_gated * passed).astype(bf16)
        main_ref[:, at] = (
            grad_gated
            * attended_ref[:, at].astype(f32)
            * (open_gate + passed * (1.0 - open_gate))
        ).astype(bf16)


def gate(back, cots, x, cand_in, base, attended, gain, proj, after=()):
    tokens, width = x.shape
    value_width = proj.shape[0]
    rows = min(256, tokens // 2)
    half = tokens // rows // 2
    wide = value_width // width

    def block(columns, at=0):
        return pl.BlockSpec((rows, columns), lambda i: (i, at))

    return pl.pallas_call(
        ignoring(gate_body, 10, len(after)),
        grid=(tokens // rows,),
        in_specs=[
            block(width),
            pl.BlockSpec((rows, width), lambda i: (jnp.minimum(i, half - 1), 0)),
            pl.BlockSpec((rows, width), lambda i: (jnp.maximum(i - half, 0), 0)),
            block(width),
            block(width),
            block(width, wide),
            block(value_width),
            block(value_width),
            pl.BlockSpec((1, width), lambda i: (0, 0)),
            pl.BlockSpec(proj.shape, lambda i: (0, 0), pipeline_mode=pl.Buffered(1)),
        ]
        + [pl.BlockSpec(memory_space=pl.ANY)] * len(after),
        out_specs=[
            block(width),
            block(value_width + 2 * width),
            block(value_width),
            pl.BlockSpec((1, width), lambda i: (0, 0)),
        ],
        out_shape=[
            jax.ShapeDtypeStruct((tokens, width), f32),
            jax.ShapeDtypeStruct((tokens, value_width + 2 * width), bf16),
            jax.ShapeDtypeStruct((tokens, value_width), bf16),
            jax.ShapeDtypeStruct((1, width), f32),
        ],
        compiler_params=params(("arbitrary",)),
        name="gate",
        cost_estimate=LONG,
    )(back, *cots, x, cand_in, base, base, attended, gain, proj, *after)


def ordered_transpose(ids_ref, source, plain, ordered):
    plain[...] = source[...].T
    count = ids_ref.shape[0]
    rows = plain.shape[0] // count

    def place(p, _):
        ordered[pl.ds(pl.multiple_of(p * rows, rows), rows), :] = plain[
            pl.ds(pl.multiple_of(ids_ref[p] * rows, rows), rows), :
        ]
        return 0

    lax.fori_loop(0, count, place, 0)


def placed_transpose(places_ref, sources, plain, ordered):
    start = 0
    for source in sources:
        plain[:, start : start + source.shape[0]] = source[...].T
        start += source.shape[0]
    count = places_ref.shape[0]
    rows = plain.shape[0] // count

    def place(q, _):
        ordered[pl.ds(pl.multiple_of(places_ref[q] * rows, rows), rows), :] = plain[
            pl.ds(pl.multiple_of(q * rows, rows), rows), :
        ]
        return 0

    lax.fori_loop(0, count, place, 0)


def feed_body(
    ids_ref,
    places_ref,
    low_ref,
    cot_a,
    cot_b,
    first_ref,
    in_ref,
    out_ref,
    result_a,
    result_b,
    back_ref,
    out_send,
    out_keep,
    in_send,
    in_keep,
    total,
    cot_turned,
    low_turned,
    plain,
):
    step = pl.program_id(0)
    half = pl.num_programs(0) // 2
    tokens = low_ref.shape[0]
    middle = tokens // 2
    nt = (((1,), (1,)), ((), ()))

    @pl.when(step == 0)
    def _():
        placed_transpose(places_ref, (cot_a, cot_b), plain, cot_turned)
        ordered_transpose(ids_ref, low_ref, plain, low_turned)
        total[...] = first_ref[...]
        back_ref[...] = jnp.zeros_like(back_ref)

    acts, grads = [], []
    for r, cot_ref in enumerate((cot_a, cot_b)):
        at = slice(r * middle, (r + 1) * middle)
        hidden = jnp.dot(low_ref[at, :], in_ref[...], preferred_element_type=f32)
        grad_act = lax.dot_general(
            cot_ref[...], out_ref[...], nt, preferred_element_type=f32
        )
        gate = jax.nn.sigmoid(hidden)
        act = hidden * gate
        grad = (grad_act * (gate + act * (1.0 - gate))).astype(bf16)
        act = act.astype(bf16)
        total[at, :] += jnp.dot(act, out_ref[...], preferred_element_type=f32)
        back_ref[at, :] += lax.dot_general(
            grad, in_ref[...], nt, preferred_element_type=f32
        )
        acts.append(act)
        grads.append(grad)
    out_grad = jnp.dot(
        cot_turned[...], jnp.concatenate(acts), preferred_element_type=f32
    ).astype(bf16)
    in_grad = jnp.dot(
        low_turned[...], jnp.concatenate(grads), preferred_element_type=f32
    ).astype(bf16)
    split = in_grad.shape[0] // 2
    in_send[...] = in_grad[:split].reshape(in_send.shape)
    in_keep[...] = in_grad[split:].reshape(in_keep.shape)

    @pl.when(step < half)
    def _():
        out_send[0] = out_grad

    @pl.when(step >= half)
    def _():
        out_keep[0] = out_grad

    @pl.when(step == pl.num_programs(0) - 1)
    def _():
        result_a[...] = total[:middle, :].astype(bf16)
        result_b[...] = total[middle:, :].astype(bf16)


def feed(ids, places, low, cots, first_sum, feed_in, feed_out, seq, after=()):
    tokens, width = low.shape
    features = feed_in.shape[1]
    parts = ids.shape[0]
    half = parts // 2
    columns = features // parts
    rows = width // parts
    share = parts // seq
    anywhere = pl.BlockSpec(memory_space=pl.ANY)

    def all_of(shape):
        return pl.BlockSpec(
            shape, lambda i, t, u: (0,) * len(shape), pipeline_mode=pl.Buffered(1)
        )

    def at(i, t):
        return t[jnp.minimum(i, parts - 1)]

    split = pl.BlockSpec(
        (half, 1, 1, rows, columns),
        lambda i, t, u: (0, u[at(i, t) // share], at(i, t) % share, 0, 0),
    )
    return pl.pallas_call(
        ignoring(feed_body, 8, len(after)),
        grid_spec=pltpu.PrefetchScalarGridSpec(
            num_scalar_prefetch=2,
            grid=(parts,),
            in_specs=[
                all_of(low.shape),
                all_of(cots[0].shape),
                all_of(cots[1].shape),
                all_of(first_sum.shape),
                pl.BlockSpec((width, columns), lambda i, t, u: (0, at(i, t))),
                pl.BlockSpec((columns, width), lambda i, t, u: (at(i, t), 0)),
            ]
            + [anywhere] * len(after),
            out_specs=[
                all_of(cots[0].shape),
                all_of(cots[1].shape),
                all_of(low.shape),
                pl.BlockSpec(
                    (1, width, columns), lambda i, t, u: (jnp.minimum(i, half - 1), 0, 0)
                ),
                pl.BlockSpec(
                    (1, width, columns), lambda i, t, u: (jnp.maximum(i - half, 0), 0, 0)
                ),
                split,
                split,
            ],
            scratch_shapes=[
                pltpu.VMEM((tokens, width), f32),
                pltpu.VMEM((width, tokens), bf16),
                pltpu.VMEM((width, tokens), bf16),
                pltpu.VMEM((width, tokens), bf16),
            ],
        ),
        out_shape=[
            jax.ShapeDtypeStruct(cots[0].shape, bf16),
            jax.ShapeDtypeStruct(cots[1].shape, bf16),
            jax.ShapeDtypeStruct((tokens, width), f32),
            jax.ShapeDtypeStruct((half, width, columns), bf16),
            jax.ShapeDtypeStruct((half, width, columns), bf16),
            jax.ShapeDtypeStruct((half, seq, share, rows, columns), bf16),
            jax.ShapeDtypeStruct((half, seq, share, rows, columns), bf16),
        ],
        compiler_params=params(("arbitrary",)),
        name="feed",
        cost_estimate=BRIEF,
    )(ids, places, low, *cots, first_sum, feed_in, feed_out, *after)


def product_body(left_ref, right_ref, out_ref):
    out_ref[...] = jnp.dot(
        left_ref[...], right_ref[...], preferred_element_type=f32
    ).astype(out_ref.dtype)


def product(left, right, tile=1024):
    tokens, depth = left.shape
    columns = right.shape[1]
    return pl.pallas_call(
        product_body,
        grid=(columns // tile,),
        in_specs=[
            pl.BlockSpec(left.shape, lambda i: (0, 0), pipeline_mode=pl.Buffered(1)),
            pl.BlockSpec((depth, tile), lambda i: (0, i)),
        ],
        out_specs=pl.BlockSpec((tokens, tile), lambda i: (0, i)),
        out_shape=jax.ShapeDtypeStruct((tokens, columns), bf16),
        compiler_params=params(("arbitrary",)),
        name="product",
        cost_estimate=BRIEF,
    )(left, right)


def smooth_back_body(
    main_ref, shared_ref, weight_ref, shared_weight_ref, smooth_ref, out_ref, total
):
    step = pl.program_id(0)

    @pl.when(step == 0)
    def _():
        total[...] = mm_nt(shared_ref[...], shared_weight_ref[...])

    total[...] += mm_nt(main_ref[...], weight_ref[...])

    @pl.when(step == pl.num_programs(0) - 1)
    def _():
        out_ref[...] = total[...] * silu_slope(smooth_ref[...])


def smooth_back(main, shared, weight, shared_weight, smoothed, after=(), riders=None):
    tokens, width = smoothed.shape
    tile = 1024

    def all_of(shape):
        return pl.BlockSpec(shape, lambda i: (0, 0), pipeline_mode=pl.Buffered(1))

    extra = riders or Riders([], 1)
    taken, given = len(extra.ins), len(extra.out_shapes)

    def body(*refs):
        first = 5 + taken + len(after)
        smooth_back_body(*refs[:5], refs[first], *refs[first + 1 + given :])
        extra.body(refs[5 : 5 + taken], refs[first + 1 : first + 1 + given])

    out = pl.pallas_call(
        body,
        grid=(main.shape[1] // tile,),
        in_specs=[
            pl.BlockSpec((tokens, tile), lambda i: (0, i)),
            all_of(shared.shape),
            pl.BlockSpec((width, tile), lambda i: (0, i)),
            all_of(shared_weight.shape),
            all_of(smoothed.shape),
        ]
        + extra.in_specs
        + [pl.BlockSpec(memory_space=pl.ANY)] * len(after),
        out_specs=[all_of(smoothed.shape)] + extra.out_specs,
        out_shape=[jax.ShapeDtypeStruct(smoothed.shape, f32)] + extra.out_shapes,
        scratch_shapes=[pltpu.VMEM(smoothed.shape, f32)],
        compiler_params=params(("arbitrary",)),
        name="smooth_back",
        cost_estimate=LONG,
    )(main, shared, weight, shared_weight, smoothed, *extra.ins, *after)
    return (out[0], riders.result(out[1:])) if riders else out[0]


def by_columns_body(ids_ref, places_ref, left_ref, right_ref, send, keep, plain, turned):
    step = pl.program_id(0)
    half = pl.num_programs(0) // 2

    @pl.when(step == 0)
    def _():
        placed_transpose(places_ref, (left_ref,), plain, turned)

    grad = jnp.dot(turned[...], right_ref[...], preferred_element_type=f32).astype(bf16)

    @pl.when(step < half)
    def _():
        send[0] = grad

    @pl.when(step >= half)
    def _():
        keep[0] = grad


def by_columns(ids, places, left, right, after=(), rows=None, at=0):
    tokens = left.shape[0]
    rows = rows or left.shape[1]
    parts = ids.shape[0]
    half = parts // 2
    columns = right.shape[1] // parts
    shape = jax.ShapeDtypeStruct((half, rows, columns), bf16)
    if columns % 128:
        left = left[:, at * rows : (at + 1) * rows]
        grad = mm_tn(left, right).astype(bf16).reshape(rows, parts, columns)
        grad = jnp.take(grad, ids, axis=1).transpose(1, 0, 2)
        grad = grad.reshape(parts, places.shape[0], -1, columns)
        grad = jnp.take(grad, jnp.argsort(places), axis=1).reshape(parts, rows, columns)
        return grad[:half], grad[half:]
    return pl.pallas_call(
        ignoring(by_columns_body, 4, len(after)),
        grid_spec=pltpu.PrefetchScalarGridSpec(
            num_scalar_prefetch=2,
            grid=(parts,),
            in_specs=[
                pl.BlockSpec(
                    (tokens, rows), lambda i, t, u: (0, at), pipeline_mode=pl.Buffered(1)
                ),
                pl.BlockSpec((tokens, columns), lambda i, t, u: (0, t[jnp.minimum(i, parts - 1)])),
            ]
            + [pl.BlockSpec(memory_space=pl.ANY)] * len(after),
            out_specs=[
                pl.BlockSpec(
                    (1, rows, columns), lambda i, t, u: (jnp.minimum(i, half - 1), 0, 0)
                ),
                pl.BlockSpec(
                    (1, rows, columns), lambda i, t, u: (jnp.maximum(i - half, 0), 0, 0)
                ),
            ],
            scratch_shapes=[
                pltpu.VMEM((rows, tokens), bf16),
                pltpu.VMEM((rows, tokens), bf16),
            ],
        ),
        out_shape=[shape, shape],
        compiler_params=params(("arbitrary",)),
        name="by_columns",
        cost_estimate=BRIEF,
    )(ids, places, left, right, *after)


def by_rows_body(ids_ref, places_ref, left_ref, right_ref, send, keep, plain, turned):
    @pl.when(pl.program_id(0) == 0)
    def _():
        ordered_transpose(ids_ref, left_ref, plain, turned)

    grad = jnp.dot(turned[...], right_ref[...], preferred_element_type=f32).astype(bf16)
    middle = grad.shape[0] // 2
    send[...] = grad[:middle].reshape(send.shape)
    keep[...] = grad[middle:].reshape(keep.shape)


def by_rows(ids, places, left, right, seq=1, after=(), cost=BRIEF, riders=None):
    tokens, rows = left.shape
    parts = ids.shape[0]
    half = parts // 2
    if places is None:
        seq, places = 1, jnp.zeros((1,), jnp.int32)
    columns = right.shape[1] // seq
    tile = min(512, columns)
    share = columns // tile
    shape = jax.ShapeDtypeStruct((half, seq, rows // parts, columns), bf16)
    split = pl.BlockSpec(
        (half, 1, rows // parts, tile), lambda i, t, u: (0, u[jnp.minimum(i // share, seq - 1)], 0, i % share)
    )
    extra = riders or Riders([], 1)
    taken, given = len(extra.ins), len(extra.out_shapes)

    def body(*refs):
        first = 4 + taken + len(after)
        by_rows_body(*refs[:4], *refs[first : first + 2], *refs[first + 2 + given :])
        extra.body(refs[4 : 4 + taken], refs[first + 2 : first + 2 + given])

    out = pl.pallas_call(
        body,
        grid_spec=pltpu.PrefetchScalarGridSpec(
            num_scalar_prefetch=2,
            grid=(seq * share,),
            in_specs=[
                pl.BlockSpec(
                    left.shape, lambda i, t, u: (0, 0), pipeline_mode=pl.Buffered(1)
                ),
                pl.BlockSpec((tokens, tile), lambda i, t, u: (0, i)),
            ]
            + extra.in_specs
            + [pl.BlockSpec(memory_space=pl.ANY)] * len(after),
            out_specs=[split, split] + extra.out_specs,
            scratch_shapes=[
                pltpu.VMEM((rows, tokens), bf16),
                pltpu.VMEM((rows, tokens), bf16),
            ],
        ),
        out_shape=[shape, shape] + extra.out_shapes,
        compiler_params=params(("arbitrary",)),
        name="by_rows",
        cost_estimate=cost,
    )(ids, places, left, right, *extra.ins, *after)
    return (out[:2], riders.result(out[2:])) if riders else out


def value_back_body(
    ids_ref,
    places_ref,
    left_ref,
    own_ref,
    other_ref,
    slope_ref,
    proj_ref,
    total_ref,
    send,
    keep,
    plain,
    turned,
):
    @pl.when(pl.program_id(0) == 0)
    def _():
        total_ref[...] = jnp.zeros_like(total_ref)
        ordered_transpose(ids_ref, left_ref, plain, turned)

    grad = own_ref[...].astype(f32)
    for k in range(other_ref.shape[0]):
        grad = grad + other_ref[k].astype(f32)
    grad = (grad * slope_ref[...].astype(f32)).astype(bf16)
    total_ref[...] += mm_nt(grad, proj_ref[...])
    weights = jnp.dot(turned[...], grad, preferred_element_type=f32).astype(bf16)
    middle = weights.shape[0] // 2
    send[...] = weights[:middle].reshape(send.shape)
    keep[...] = weights[middle:].reshape(keep.shape)


def value_back(ids, places, left, own, others, slope, proj, seq, after=()):
    tokens, rows = left.shape
    parts = ids.shape[0]
    half = parts // 2
    columns = proj.shape[1] // seq
    tile = min(512, columns)
    share = columns // tile
    shape = jax.ShapeDtypeStruct((half, seq, rows // parts, columns), bf16)
    split = pl.BlockSpec(
        (half, 1, rows // parts, tile),
        lambda i, t, u: (0, u[jnp.minimum(i // share, seq - 1)], 0, i % share),
    )
    stripe = pl.BlockSpec((tokens, tile), lambda i, t, u: (0, i))
    fixed = pl.BlockSpec(
        (tokens, rows), lambda i, t, u: (0, 0), pipeline_mode=pl.Buffered(1)
    )
    return pl.pallas_call(
        ignoring(value_back_body, 7, len(after)),
        grid_spec=pltpu.PrefetchScalarGridSpec(
            num_scalar_prefetch=2,
            grid=(seq * share,),
            in_specs=[
                fixed,
                stripe,
                pl.BlockSpec((others.shape[0], tokens, tile), lambda i, t, u: (0, 0, i)),
                stripe,
                pl.BlockSpec((rows, tile), lambda i, t, u: (0, i)),
            ]
            + [pl.BlockSpec(memory_space=pl.ANY)] * len(after),
            out_specs=[fixed, split, split],
            scratch_shapes=[
                pltpu.VMEM((rows, tokens), bf16),
                pltpu.VMEM((rows, tokens), bf16),
            ],
        ),
        out_shape=[jax.ShapeDtypeStruct((tokens, rows), f32), shape, shape],
        compiler_params=params(("arbitrary",)),
        name="value_back",
        cost_estimate=LONG,
    )(ids, places, left, own, others, slope, proj, *after)


class Riders:
    def __init__(self, groups, steps):
        self.shapes, self.ins, self.whole = [], [], []
        self.in_specs, self.out_specs, self.out_shapes = [], [], []
        for pairs, single, kind in groups:
            halves = 1 if single else 2
            g, n, rows, columns = pairs[0][0].shape
            each = n * rows // halves // steps
            self.shapes.append((len(pairs), halves))
            for pair in pairs:
                for v in pair:
                    self.ins.append(v.reshape(g, halves, n * rows // halves, columns))
                    self.in_specs.append(
                        pl.BlockSpec((g, halves, each, columns), lambda i, *_: (0, 0, i, 0))
                    )
            for _ in range(halves):
                self.out_specs.append(
                    pl.BlockSpec((len(pairs) * g, each, columns), lambda i, *_: (0, i, 0))
                )
                self.out_shapes.append(
                    jax.ShapeDtypeStruct((len(pairs) * g, n * rows // halves, columns), kind)
                )
            self.whole.append((halves, (len(pairs) * g, n // halves, rows, columns)))

    @staticmethod
    def fit(groups, steps):
        for pairs, single, _ in groups:
            _, n, rows, _ = pairs[0][0].shape
            while (n * rows // (1 if single else 2)) % (16 * steps) and steps > 1:
                steps //= 2
        return steps

    def body(self, ins, outs):
        ins, outs = list(ins), list(outs)
        for pairs, halves in self.shapes:
            into = [outs.pop(0) for _ in range(halves)]
            start = 0
            for _ in range(pairs):
                kept, arrived = ins.pop(0), ins.pop(0)
                stop = start + kept.shape[0]
                for part, out in enumerate(into):
                    out[start:stop] = (
                        kept[:, part].astype(f32) + arrived[:, part].astype(f32)
                    ).astype(out.dtype)
                start = stop

    def result(self, sums):
        sums = list(sums)
        return [
            tuple(sums.pop(0).reshape(shape) for _ in range(halves))
            for halves, shape in self.whole
        ]


def stage_sums(groups, after=(), steps=4, cost=BRIEF):
    steps = Riders.fit(groups, steps)
    riders = Riders(groups, steps)
    count = len(riders.ins)

    def body(*refs):
        riders.body(refs[:count], refs[count + len(after) :])

    sums = pl.pallas_call(
        body,
        grid=(steps,),
        in_specs=riders.in_specs + [pl.BlockSpec(memory_space=pl.ANY)] * len(after),
        out_specs=riders.out_specs,
        out_shape=riders.out_shapes,
        compiler_params=params(("arbitrary",)),
        name="stage_sums",
        cost_estimate=cost,
    )(*riders.ins, *after)
    return riders.result(sums)


class Layout:
    def __init__(self, mesh):
        self.dp = mesh.shape["dp"]
        self.seq = mesh.shape["seq"]
        self.members = self.seq // 2
        self.chips = self.seq // 4

    def pairs(self, move):
        return [
            (d * self.seq + z, e * self.seq + w)
            for d in range(self.dp)
            for z in range(self.seq)
            for e, w in [move(d, z)]
        ]

    def send(self, value, move):
        return lax.ppermute(value, AXES, self.pairs(move))

    def place(self, sequence, member):
        return member % 2 ^ (1 - sequence % 2), sequence * self.chips + member // 2

    def member(self, core, z):
        sequence = z // self.chips
        return (z % self.chips) * 2 + (core ^ (1 - sequence % 2))

    def home_to_work(self, round_index):
        def move(d, z):
            part = (1 if z >= self.seq // 2 else 0) ^ round_index
            core, at = self.place(2 * (d % 2) + part, min(z, self.seq - 1 - z))
            return d - d % 2 + core, at

        return move

    def outgoing(self, value):
        late = lax.axis_index("seq") >= self.seq // 2
        return [
            lax.dynamic_index_in_dim(value, jnp.where(late, 1 - r, r), 0, False)
            for r in range(2)
        ]

    def to_work(self, value, round_index):
        return self.send(value, self.home_to_work(round_index))

    def homeward(self, value, round_index):
        pairs = [(b, a) for a, b in self.pairs(self.home_to_work(round_index))]
        return lax.ppermute(value, AXES, pairs)

    def gathered(self, back):
        late = lax.axis_index("seq") >= self.seq // 2
        return jnp.stack([jnp.where(late, back[1], back[0]), jnp.where(late, back[0], back[1])])

    def collect(self, values):
        return self.gathered([self.homeward(v, r) for r, v in enumerate(values)])

    def rotate(self, value, by):
        def move(d, z):
            member = (self.member(d % 2, z) + by) % self.members
            core, at = self.place(z // self.chips, member)
            return d - d % 2 + core, at

        return self.send(value, move)

    def gather(self, value):
        return jnp.concatenate([self.rotate(value, by) for by in range(1, self.members)], axis=0)

    def returns(self, others):
        slots = others.shape[0] // (self.members - 1)
        return jnp.stack(
            [
                self.rotate(others[(by - 1) * slots : by * slots], self.members - by).reshape(
                    -1, others.shape[-1]
                )
                for by in range(1, self.members)
            ]
        )

    def orders(self):
        dp, z = lax.axis_index("dp"), lax.axis_index("seq")
        bits = self.dp.bit_length() - 1
        ids = []
        for core in range(2):
            orders = [[0, *range(1, bits)], [0, *reversed(range(1, bits))]]
            flips = []
            for p in range(self.dp):
                order = orders[core if p >= self.dp // 2 else 1 - core]
                flips.append(
                    sum(
                        (0 if p >> (bits - 1 - i) & 1 else 1) << bit
                        for i, bit in enumerate(order)
                    )
                )
            ids.append(dp ^ jnp.array(flips, jnp.int32))
        ids = jnp.where(dp % 2 == 0, ids[0], ids[1])
        bits = self.seq.bit_length() - 1
        flips = [
            sum((0 if p >> (bits - 1 - i) & 1 else 1) << i for i in range(bits))
            for p in range(self.seq)
        ]
        blocks = z ^ jnp.array(flips, jnp.int32)
        return ids, jnp.argsort(blocks).astype(jnp.int32), blocks

    def partner(self, stage):
        bits = self.dp.bit_length() - 1
        if stage == 0:
            return lambda d, z: (d ^ 1, z)
        if stage < bits:
            return lambda d, z: (d ^ (1 << stage if d % 2 == 0 else 1 << (bits - stage)), z)
        return lambda d, z: (d, z ^ (1 << (stage - bits)))

    def turn(self, sums, after, cost=BRIEF, carrier=None, steps=None):
        sums = [s for s in sums if s.arrived]
        if not sums:
            return carrier(None, after) if carrier else after
        dp_stages = self.dp.bit_length() - 1
        last = dp_stages + self.seq.bit_length() - 1
        groups = []
        for s in sums:
            pairs = list(zip(s.kept, s.arrived))
            single = s.stage + 1 == last
            if s.stage + 1 == dp_stages:
                single = not s.over_seq
                if s.over_seq:
                    pairs = [
                        tuple(
                            v.reshape(v.shape[0], self.seq, -1, v.shape[-1]) for v in pair
                        )
                        for pair in pairs
                    ]
            groups.append((pairs, single, f32 if s.stage + 1 == last else bf16))
        if carrier:
            if Riders.fit(groups, steps) == steps:
                own, out = carrier(Riders(groups, steps), after)
            else:
                out = stage_sums(groups, after, cost=cost)
                own = carrier(None, [part for held in out for part in held])
        else:
            out = stage_sums(groups, after, cost=cost)
        for s, held, (_, single, _) in zip(sums, out, groups):
            s.stage += 1
            s.arrived = ()
            if single:
                s.total = held[0]
            else:
                s.send([held[0]], [held[1]])
        if carrier:
            return own
        return [part for held in out for part in held]

    def over_seq(self, held):
        bits = self.seq.bit_length() - 1
        for bit in range(bits - 1):
            held = held + self.send(held.astype(bf16), lambda d, z: (d, z ^ (1 << bit))).astype(f32)
        return held, self.send(held.astype(bf16), lambda d, z: (d, z ^ (1 << (bits - 1))))


    def over_dp(self, held):
        bits = self.dp.bit_length() - 1
        for bit in range(bits - 1):
            held = held + self.send(held, lambda d, z: (d ^ (1 << bit), z))
        return held, self.send(held, lambda d, z: (d ^ (1 << (bits - 1)), z))


def later_body(left, right, out):
    out[...] = left[...] + right[...]


def later_sum(left, right, after):
    inside = pl.BlockSpec(memory_space=pltpu.VMEM)
    return pl.pallas_call(
        ignoring(later_body, 2, len(after)),
        in_specs=[inside] * 2 + [pl.BlockSpec(memory_space=pl.ANY)] * len(after),
        out_specs=inside,
        out_shape=jax.ShapeDtypeStruct(left.shape, left.dtype),
        name="later_sum",
        cost_estimate=BRIEF,
    )(left, right, *after)


def pack_body(qx_a, qx_b, qs_a, qs_b, rest_ref, out):
    rows = qx_a.shape[0]
    out[:rows] = qx_a[...] + qx_b[...]
    out[rows : 2 * rows] = qs_a[...] + qs_b[...]
    out[2 * rows :] = rest_ref[...]


def pack(first, second, rest, after=()):
    ins = [v.reshape(-1, 128) for v in (first[0], second[0], first[1], second[1])] + [rest]
    rows = 2 * ins[0].shape[0] + rest.shape[0]
    inside = pl.BlockSpec(memory_space=pltpu.VMEM)
    return pl.pallas_call(
        ignoring(pack_body, 5, len(after)),
        in_specs=[inside] * 5 + [pl.BlockSpec(memory_space=pl.ANY)] * len(after),
        out_specs=inside,
        out_shape=jax.ShapeDtypeStruct((rows, 128), f32),
        name="pack",
        cost_estimate=BRIEF,
    )(*ins, *after)


def finish_body(
    mine, other, alpha, damp, beta, eta, alpha_out, damp_out, beta_out, eta_out, *rest
):
    *rest, rows = rest
    rows[...] = mine[...] + other[...].astype(f32)
    states = alpha.shape[0]
    groups = alpha.shape[1] // 128
    for c in range(groups):
        at = slice(c * 128, (c + 1) * 128)
        x_sum = rows[pl.ds(c, states, stride=groups), :]
        s_sum = rows[pl.ds(states * groups + c, states, stride=groups), :]
        rate = alpha[:, at] * beta[:, at]
        input_total = eta[:, at] * x_sum
        decay_total = eta[:, at] * rate * s_sum
        alpha_out[:, at] = beta[:, at] * input_total - damp[:, at] * decay_total
        damp_out[:, at] = -alpha[:, at] * decay_total
        beta_out[:, at] = alpha[:, at] * input_total
        eta_out[:, at] = rate * x_sum
    start = 2 * states * groups
    for out in rest:
        out[...] = rows[start : start + out.shape[0]]
        start += out.shape[0]


def finish(mine, other, alpha, damp, beta, eta, counts):
    inside = pl.BlockSpec(memory_space=pltpu.VMEM)
    rows = mine.shape[0]
    shape = jax.ShapeDtypeStruct(alpha.shape, f32)
    return pl.pallas_call(
        finish_body,
        in_specs=[inside] * 6,
        out_specs=[inside] * (4 + len(counts)),
        out_shape=[shape] * 4 + [jax.ShapeDtypeStruct((n, 128), f32) for n in counts],
        scratch_shapes=[pltpu.VMEM((rows, 128), f32)],
        name="finish",
        cost_estimate=BRIEF,
    )(mine, other, alpha, damp, beta, eta)


class Sum:
    def __init__(self, layout, *pairs, over_seq=True):
        self.layout, self.over_seq, self.stage = layout, over_seq, 0
        self.total = None
        pairs = [[v.reshape(1, v.shape[0], -1, v.shape[-1]) for v in pair] for pair in pairs]
        self.send([p[0] for p in pairs], [p[1] for p in pairs])

    def send(self, sent, kept):
        self.kept = kept
        self.arrived = [self.layout.send(v, self.layout.partner(self.stage)) for v in sent]

    def begin_seq(self, block):
        self.total = None
        middle = self.layout.seq // 2
        self.send([block[None, :middle]], [block[None, middle:]])


def mm(a, b):
    return jnp.dot(a, b, preferred_element_type=f32)


def mm_nt(a, b):
    return lax.dot_general(a, b, (((1,), (1,)), ((), ())), preferred_element_type=f32)


def mm_tn(a, b):
    return lax.dot_general(a, b, (((0,), (0,)), ((), ())), preferred_element_type=f32)


def layer(
    layout,
    inputs,
    cotangent,
    full_attention,
    mix_gain,
    smooth_alpha,
    smooth_damp,
    smooth_beta,
    smooth_eta,
    smooth_omega,
    value_proj,
    mix_proj,
    score_affine,
    relative_bias,
    out_proj,
    feed_gain,
    feed_in,
    feed_out,
):
    slots, chunk_rows, width = inputs.shape
    key_width = score_affine.shape[1]
    value_width = value_proj.shape[1]
    tokens = slots * chunk_rows
    total = layout.seq
    seq_length = relative_bias.shape[0] // 2
    block = min(128, chunk_rows)
    core = lax.axis_index("dp") % 2
    z = lax.axis_index("seq")

    sequence = z // layout.chips
    member = layout.member(core, z)
    swap = sequence % 2
    chunks = []
    for by in range(layout.members):
        source = (member - by) % layout.members
        low, high = source, total - 1 - source
        chunks += [jnp.where(swap == 0, low, high), jnp.where(swap == 0, high, low)]
    chunks = jnp.stack(chunks).astype(jnp.int32)
    slot_of = jnp.sum(
        jnp.where(chunks[None, :] == jnp.arange(total)[:, None], jnp.arange(total)[None, :], 0),
        axis=1,
    ).astype(jnp.int32)
    flags = full_attention.astype(f32)
    flags_other = layout.send(flags, lambda d, z: (d ^ 1, z))
    flags = jnp.where(
        core == 0, jnp.concatenate([flags, flags_other]), jnp.concatenate([flags_other, flags])
    )
    full = lax.dynamic_index_in_dim(flags, sequence, 0, False) == 1.0
    table = jnp.concatenate([chunks, slot_of, full.astype(jnp.int32)[None]])
    ids, places, blocks = layout.orders()

    arriving = [
        (slot, at * (chunk_rows // count), layout.to_work(piece, slot))
        for slot, count in ((0, 1), (1, 1))
        for at, piece in enumerate(jnp.split(layout.outgoing(inputs)[slot], count))
    ]
    leaving = layout.outgoing(cotangent)
    bias_back, bias_front = bias_tiles(relative_bias, chunk_rows // TILE - 1, full)

    states = smooth_alpha.shape[0]
    lanes = (states, width // 128, 128)
    decay = 1.0 - smooth_alpha * smooth_damp
    rate = smooth_alpha * smooth_beta
    span = (decay**chunk_rows).reshape(lanes)
    coef = (smooth_eta * rate).reshape(lanes)
    decay_slab = decay.reshape(lanes)
    gain_row = mix_gain[None]
    omega_row = smooth_omega[None]
    mix_shared, mix_main = mix_proj[:, :key_width], mix_proj[:, key_width:]

    held, after = (), (bias_back, bias_front, mix_main, mix_shared, span, coef)
    ready = (table, ids, places, blocks, *leaving)
    for slot, row, piece in arriving:
        held = front(
            piece, slot, row, (slots, chunk_rows), held, gain_row, decay_slab, value_proj, after=after
        )
        after, ready = ready, ()
    normed_low, x, value_low, value_slope, ends = held
    ends_others = layout.gather(ends)
    leaving, ends_others = lax.optimization_barrier((leaving, ends_others))
    cots = [layout.to_work(v, r) for r, v in enumerate(leaving)]
    normed_low = normed_low.reshape(tokens, width)
    value_slope = value_slope.reshape(tokens, value_width)
    value_others = layout.gather(value_low)
    smoothed, mixed, check, shared_pre, query_low, key_low = front_scan(
        table,
        x,
        gain_row,
        decay_slab,
        coef,
        span,
        omega_row,
        ends,
        ends_others,
        mix_shared,
        score_affine,
        block,
    )
    smoothed = smoothed.reshape(tokens, width)
    mixed = mixed.reshape(tokens, width)
    shared_pre = shared_pre.reshape(tokens, key_width)
    key_others = layout.gather(key_low)
    base = product(mixed, mix_main)
    attended, gated, lse = attend(
        table,
        query_low,
        bias_front,
        base.reshape(slots, chunk_rows, -1),
        key_low,
        key_others,
        value_low,
        value_others,
    )
    attended = attended.reshape(tokens, value_width)
    gated = gated.reshape(tokens, value_width)

    flat_low = x.reshape(tokens, width)
    cand_in, first_sum, feed_low = candidate(gated, out_proj, base, flat_low, feed_gain[None])

    result_a, result_b, grad_feed, out_send, out_keep, in_send, in_keep = feed(
        ids, places, feed_low, cots, first_sum, feed_in, feed_out, layout.seq
    )
    home = [layout.homeward(result_a, 0), layout.homeward(result_b, 1)]
    block_out = layout.gathered(home)
    feed_sum = Sum(layout, (out_send, out_keep), (in_send, in_keep))

    grad_input, grad_main, grad_att, feed_gain_grad = gate(
        grad_feed, cots, flat_low, cand_in, base, attended, feed_gain[None], out_proj
    )
    after = layout.turn((feed_sum,), (grad_att,))
    mix_parts = by_rows(ids, None, mixed, grad_main, after=after, cost=LONG)
    proj_parts = by_columns(
        ids,
        places,
        grad_main,
        gated,
        rows=width,
        at=grad_main.shape[1] // width - 1,
        after=mix_parts,
    )
    after = (*proj_parts, *home)
    mix_sum = Sum(layout, mix_parts, over_seq=False)
    proj_sum = Sum(layout, proj_parts)
    grad_query, gk_own, gv_own, both_oth, rel_sums = attend_back(
        table,
        query_low,
        grad_att.reshape(slots, chunk_rows, value_width),
        lse,
        bias_back,
        key_low,
        key_others,
        value_low,
        value_others,
        after=after,
    )
    both_back = layout.returns(both_oth)
    after = layout.turn((feed_sum, proj_sum), (grad_query,), cost=LONG)
    grad_normed, value_send, value_keep = value_back(
        ids,
        places,
        normed_low,
        gv_own.reshape(tokens, value_width),
        both_back,
        value_slope,
        value_proj,
        layout.seq,
        after=after,
    )
    grad_key = jnp.sum(both_back[:, :, value_width:].astype(f32), axis=0) + gk_own.reshape(
        tokens, key_width
    ).astype(f32)
    grad_query = grad_query.reshape(tokens, key_width)
    grad_shared = (
        (grad_query * score_affine[0] + grad_key * score_affine[2]) * silu_slope(shared_pre)
    ).astype(bf16)
    shared_parts = by_rows(ids, None, mixed, grad_shared, after=(grad_normed,))
    shared_sum = Sum(layout, shared_parts, over_seq=False)
    value_sum = Sum(layout, (value_send, value_keep))
    after = layout.turn((mix_sum,), shared_parts)
    grad_smooth = smooth_back(
        grad_main, grad_shared, mix_main, mix_shared, smoothed, after=after
    )
    grad_smooth = grad_smooth.reshape(slots, chunk_rows, width)
    after = layout.turn((feed_sum, value_sum, proj_sum, shared_sum), (grad_smooth,))
    back = back_ends(grad_smooth, decay_slab, after=after)
    back_others = layout.gather(back)
    after = layout.turn((feed_sum, mix_sum, value_sum, shared_sum), (back,))

    def scan_back(slot, after):
        return back_scan(
            table,
            slot,
            x,
            grad_smooth,
            grad_normed.reshape(slots, chunk_rows, width),
            grad_input.reshape(slots, chunk_rows, width),
            check,
            gain_row,
            decay_slab,
            coef,
            span,
            omega_row,
            back,
            back_others,
            after=after,
        )

    first = scan_back(0, after)
    after = layout.turn(
        (feed_sum, mix_sum, value_sum, proj_sum, shared_sum), (first[0],)
    )
    home_first = layout.homeward(first[0], 0)
    while mix_sum.total is None or shared_sum.total is None:
        after = layout.turn((mix_sum, shared_sum), after)
    rows = jnp.concatenate([shared_sum.total[0, 0], mix_sum.total[0, 0]], axis=1)
    rows = rows.reshape(rows.shape[0], layout.seq, -1).transpose(1, 0, 2)
    mix_sum.begin_seq(rows[blocks])
    second = scan_back(1, (*after, *mix_sum.kept))
    affine_grad = jnp.stack(
        [
            jnp.sum(grad_query * shared_pre * jax.nn.sigmoid(shared_pre), axis=0),
            jnp.sum(grad_query, axis=0),
            jnp.sum(grad_key * shared_pre * jax.nn.sigmoid(shared_pre), axis=0),
            jnp.sum(grad_key, axis=0),
        ]
    )
    relative_grad = bias_grad(rel_sums[:, 0], seq_length)
    small = [
        first[3] + second[3],
        first[4] + second[4],
        feed_gain_grad,
        affine_grad,
        relative_grad,
    ]
    small = [v.reshape(-1, 128) for v in small]
    rest = jnp.concatenate(small)
    rest = jnp.pad(rest, ((0, -rest.shape[0] % 16), (0, 0)))
    home_second = layout.homeward(second[0], 1)
    sums = (mix_sum, proj_sum, value_sum, feed_sum)
    turned = layout.turn(sums, (second[0], home_first), cost=LONG)
    totals = layout.over_dp(pack(first[1:3], second[1:3], rest, after=turned))
    after = layout.turn(sums, (*turned, home_second))
    totals = layout.over_seq(later_sum(*totals, after=after))
    while any(v.total is None for v in sums):
        after = layout.turn(sums, after)
    grad_in = layout.gathered([home_first, home_second]).astype(f32)
    feed_out_grad, feed_in_grad = feed_sum.total[0, 0].T, feed_sum.total[1, 0]
    rows = width // layout.dp
    feed_in_grad = feed_in_grad.reshape(-1, rows, feed_in_grad.shape[-1])
    feed_in_grad = feed_in_grad.transpose(1, 0, 2).reshape(rows, -1)
    out_grad, value_grad = proj_sum.total[0, 0].T, value_sum.total[0, 0]
    mix_grad = mix_sum.total[0, 0]
    alpha_grad, damp_grad, beta_grad, eta_grad, *parts = finish(
        *totals, smooth_alpha, smooth_damp, smooth_beta, smooth_eta, [v.shape[0] for v in small]
    )
    parts = [v.reshape(-1) for v in parts]
    return (
        block_out,
        grad_in,
        parts[0],
        alpha_grad,
        damp_grad,
        beta_grad,
        eta_grad,
        parts[1],
        value_grad,
        mix_grad,
        parts[3].reshape(4, key_width),
        parts[4],
        out_grad,
        parts[2],
        feed_in_grad,
        feed_out_grad,
    )


def solution(mesh):
    tokens = P("dp", "seq", None)
    split = P("dp", "seq")
    return jax.shard_map(
        functools.partial(layer, Layout(mesh)),
        mesh=mesh,
        in_specs=(tokens, tokens, P("dp")) + (P(),) * 14,
        out_specs=(tokens, tokens)
        + (P(),) * 6
        + (split, split, P(), P(), split, P(), split, split),
        check_vma=False,
    )
```

```python
import functools

import jax
import jax.numpy as jnp
from jax import lax
from jax.experimental import pallas as pl
from jax.experimental.pallas import tpu as pltpu
from jax.sharding import PartitionSpec as P

STRETCH = 128
EPSILON = 1e-05
TILE = 256
MASKED = -1e30
VMEM_LIMIT = 60 * 1024 * 1024
AXES = ("dp", "seq")
BRIEF = pl.CostEstimate(flops=1, bytes_accessed=1, transcendentals=0)
LONG = pl.CostEstimate(flops=10**11, bytes_accessed=1, transcendentals=0)

f32 = jnp.float32
bf16 = jnp.bfloat16


def unit_rows_of(values):
    centred = values - jnp.mean(values, axis=-1, keepdims=True)
    inv_std = lax.rsqrt(jnp.mean(centred * centred, axis=-1, keepdims=True) + EPSILON)
    return centred * inv_std, inv_std


def norm_back_rows(grad_out, gain_vec, unit_rows, inv_std):
    scaled = grad_out * gain_vec
    return inv_std * (
        scaled
        - jnp.mean(scaled, axis=-1, keepdims=True)
        - unit_rows * jnp.mean(scaled * unit_rows, axis=-1, keepdims=True)
    )


def silu_slope(pre_act):
    sigmoid_val = jax.nn.sigmoid(pre_act)
    return sigmoid_val * (1.0 + pre_act * (1.0 - sigmoid_val))


def params(semantics, limit=VMEM_LIMIT):
    return pltpu.CompilerParams(dimension_semantics=semantics, vmem_limit_bytes=limit)


def ignoring(body, first, count):
    def called(*refs):
        return body(*refs[:first], *refs[first + count :])

    return called


def to_slab(slab, rows):
    count, groups = rows.shape[0], rows.shape[1] // 128
    for c in range(groups):
        slab[pl.ds(c, count, stride=groups), :] = rows[:, c * 128 : (c + 1) * 128]


def from_slab(slab, count, groups):
    return jnp.concatenate(
        [slab[pl.ds(c, count, stride=groups), :] for c in range(groups)], axis=1
    )


def slab_row(slab, t, groups):
    return slab[pl.ds(pl.multiple_of(t * groups, groups), groups), :]


def front_body(
    x_ref,
    gain_ref,
    decay_ref,
    proj_ref,
    begin_ref,
    low_ref,
    copy_ref,
    value_ref,
    slope_ref,
    end_ref,
    slab,
    *,
    fresh,
):
    states, groups, _ = decay_ref.shape
    count = x_ref.shape[0]

    @pl.when(pl.program_id(0) == 0)
    def _():
        end_ref[...] = jnp.zeros_like(end_ref) if fresh else begin_ref[...]

    copy_ref[0] = x_ref[...]
    unit, _ = unit_rows_of(x_ref[...].astype(f32))
    normed = unit * gain_ref[...]
    low_ref[0] = normed.astype(bf16)
    to_slab(slab, normed)
    decay = [decay_ref[n] for n in range(states)]

    def step(t, state):
        row = slab_row(slab, t, groups)
        return tuple(d * s + row for d, s in zip(decay, state))

    state = lax.fori_loop(
        0, count, step, tuple(end_ref[0, n] for n in range(states)), unroll=8
    )
    for n in range(states):
        end_ref[0, n] = state[n]
    for c in range(proj_ref.shape[1] // 512):
        at = slice(c * 512, (c + 1) * 512)
        pre = jnp.dot(low_ref[0], proj_ref[:, at], preferred_element_type=f32)
        gate = jax.nn.sigmoid(pre)
        value = pre * gate
        value_ref[0, :, at] = value.astype(bf16)
        slope_ref[0, :, at] = (gate + value * (1.0 - gate)).astype(bf16)


def front(x, slot, row, whole, earlier, gain, decay, proj, after=()):
    rows, width = x.shape
    slots, length = whole
    value_width = proj.shape[1]
    states, groups, lanes = decay.shape
    block = min(256, rows)
    first = row // block
    begin = earlier[-1] if row else jnp.zeros((slots, *decay.shape), f32)
    anywhere = pl.BlockSpec(memory_space=pl.ANY)

    def tokens(columns):
        return pl.BlockSpec((1, block, columns), lambda b: (slot, first + b, 0))

    return pl.pallas_call(
        ignoring(functools.partial(front_body, fresh=row == 0), 5, len(earlier) + len(after)),
        grid=(rows // block,),
        in_specs=[
            pl.BlockSpec((block, width), lambda b: (b, 0)),
            pl.BlockSpec((1, width), lambda b: (0, 0)),
            pl.BlockSpec((states, groups, lanes), lambda b: (0, 0, 0)),
            pl.BlockSpec(proj.shape, lambda b: (0, 0), pipeline_mode=pl.Buffered(1)),
            pl.BlockSpec((1, states, groups, lanes), lambda b: (slot, 0, 0, 0)),
        ]
        + [anywhere] * (len(earlier) + len(after)),
        out_specs=[
            tokens(width),
            tokens(width),
            tokens(value_width),
            tokens(value_width),
            pl.BlockSpec((1, states, groups, lanes), lambda b: (slot, 0, 0, 0)),
        ],
        out_shape=[
            jax.ShapeDtypeStruct((slots, length, width), bf16),
            jax.ShapeDtypeStruct((slots, length, width), bf16),
            jax.ShapeDtypeStruct((slots, length, value_width), bf16),
            jax.ShapeDtypeStruct((slots, length, value_width), bf16),
            jax.ShapeDtypeStruct((slots, states, groups, lanes), f32),
        ],
        scratch_shapes=[pltpu.VMEM((block * groups, lanes), f32)],
        input_output_aliases={5 + k: k for k in range(len(earlier))},
        compiler_params=params(("arbitrary",)),
        name="front",
        cost_estimate=BRIEF,
    )(x, gain, decay, proj, begin, *earlier, *after)


def front_scan_body(
    table_ref,
    x_ref,
    gain_ref,
    decay_ref,
    coef_ref,
    span_ref,
    omega_ref,
    ends_own,
    ends_oth,
    proj_ref,
    affine_ref,
    smooth_ref,
    mixed_ref,
    check_ref,
    shared_ref,
    query_ref,
    key_ref,
    slab,
    out_slab,
    carry,
    ends_ref,
):
    states, groups, _ = decay_ref.shape
    count = x_ref.shape[1]
    slot = pl.program_id(0)
    slots = ends_own.shape[0]
    total = slots + ends_oth.shape[0]

    @pl.when(pl.program_id(1) == 0)
    def _():
        carry[...] = jnp.zeros_like(carry)
        ends_ref[:slots] = ends_own[...]
        ends_ref[slots:] = ends_oth[...]

        def link(i, _):
            carry[...] = span_ref[...] * carry[...] + ends_ref[table_ref[total + i]]
            return 0

        lax.fori_loop(0, table_ref[slot], link, 0)

    unit, _ = unit_rows_of(x_ref[0].astype(f32))
    normed = unit * gain_ref[...]
    to_slab(slab, normed)
    decay = [decay_ref[n] for n in range(states)]
    coef = [coef_ref[n] for n in range(states)]
    state = tuple(carry[n] for n in range(states))
    for n in range(states):
        check_ref[0, 0, n] = state[n]

    def step(t, state):
        row = slab_row(slab, t, groups)
        state = tuple(d * s + row for d, s in zip(decay, state))
        parts = [c * s for c, s in zip(coef, state)]
        while len(parts) > 1:
            parts = [a + b for a, b in zip(parts[::2], parts[1::2])]
        out_slab[pl.ds(pl.multiple_of(t * groups, groups), groups), :] = parts[0]
        return state

    state = lax.fori_loop(0, count, step, state, unroll=8)
    for n in range(states):
        carry[n] = state[n]
    smoothed = from_slab(out_slab, count, groups) + omega_ref[...] * normed
    smooth_ref[0] = smoothed
    mixed = (smoothed * jax.nn.sigmoid(smoothed)).astype(bf16)
    mixed_ref[0] = mixed
    shared_pre = jnp.dot(mixed, proj_ref[...], preferred_element_type=f32)
    shared = shared_pre * jax.nn.sigmoid(shared_pre)
    shared_ref[0] = shared_pre
    query_ref[0] = (shared * affine_ref[0:1] + affine_ref[1:2]).astype(bf16)
    key_ref[0] = (shared * affine_ref[2:3] + affine_ref[3:4]).astype(bf16)


def front_scan(table, x, gain, decay, coef, span, omega, ends, others, proj, affine, block):
    slots, length, width = x.shape
    states, groups, lanes = decay.shape
    whole3 = pl.BlockSpec((states, groups, lanes), lambda k, b, t: (0, 0, 0))
    row = pl.BlockSpec((1, width), lambda k, b, t: (0, 0))
    tokens = pl.BlockSpec((1, block, width), lambda k, b, t: (k, b, 0))
    narrow = pl.BlockSpec((1, block, proj.shape[1]), lambda k, b, t: (k, b, 0))
    return pl.pallas_call(
        front_scan_body,
        grid_spec=pltpu.PrefetchScalarGridSpec(
            num_scalar_prefetch=1,
            grid=(slots, length // block),
            in_specs=[
                tokens,
                row,
                whole3,
                whole3,
                whole3,
                row,
                pl.BlockSpec(ends.shape, lambda k, b, t: (0, 0, 0, 0)),
                pl.BlockSpec(others.shape, lambda k, b, t: (0, 0, 0, 0)),
                pl.BlockSpec(proj.shape, lambda k, b, t: (0, 0)),
                pl.BlockSpec(affine.shape, lambda k, b, t: (0, 0)),
            ],
            out_specs=[
                tokens,
                tokens,
                pl.BlockSpec((1, 1, states, groups, lanes), lambda k, b, t: (k, b, 0, 0, 0)),
                narrow,
                narrow,
                narrow,
            ],
            scratch_shapes=[
                pltpu.VMEM((block * groups, lanes), f32),
                pltpu.VMEM((block * groups, lanes), f32),
                pltpu.VMEM((states, groups, lanes), f32),
                pltpu.VMEM((ends.shape[0] + others.shape[0], states, groups, lanes), f32),
            ],
        ),
        out_shape=[
            jax.ShapeDtypeStruct((slots, length, width), f32),
            jax.ShapeDtypeStruct((slots, length, width), bf16),
            jax.ShapeDtypeStruct((slots, length // block, states, groups, lanes), f32),
            jax.ShapeDtypeStruct((slots, length, proj.shape[1]), f32),
            jax.ShapeDtypeStruct((slots, length, proj.shape[1]), bf16),
            jax.ShapeDtypeStruct((slots, length, proj.shape[1]), bf16),
        ],
        compiler_params=params(("arbitrary", "arbitrary")),
        name="front_scan",
        cost_estimate=LONG,
    )(table, x, gain, decay, coef, span, omega, ends, others, proj, affine)


def back_ends_body(gs_ref, decay_ref, end_ref, slab):
    states, groups, _ = decay_ref.shape
    slots, count, _ = gs_ref.shape

    @pl.when(pl.program_id(0) == 0)
    def _():
        end_ref[...] = jnp.zeros_like(end_ref)

    for k in range(slots):
        to_slab(slab.at[k], gs_ref[k])
    decay = [decay_ref[n] for n in range(states)]

    def step(t, state):
        rows = [slab_row(slab.at[k], count - 1 - t, groups) for k in range(slots)]
        return [tuple(d * s + row for d, s in zip(decay, held)) for row, held in zip(rows, state)]

    state = lax.fori_loop(
        0,
        count,
        step,
        [tuple(end_ref[k, n] for n in range(states)) for k in range(slots)],
        unroll=8,
    )
    for k in range(slots):
        for n in range(states):
            end_ref[k, n] = state[k][n]


def back_ends(gs, decay, block=128, after=()):
    slots, length, width = gs.shape
    states, groups, lanes = decay.shape
    block = min(block, length)
    blocks = length // block
    return pl.pallas_call(
        ignoring(back_ends_body, 2, len(after)),
        grid=(blocks,),
        in_specs=[
            pl.BlockSpec((slots, block, width), lambda b: (0, blocks - 1 - b, 0)),
            pl.BlockSpec((states, groups, lanes), lambda b: (0, 0, 0)),
        ]
        + [pl.BlockSpec(memory_space=pl.ANY)] * len(after),
        out_specs=pl.BlockSpec((slots, states, groups, lanes), lambda b: (0, 0, 0, 0)),
        out_shape=jax.ShapeDtypeStruct((slots, states, groups, lanes), f32),
        scratch_shapes=[pltpu.VMEM((slots, block * groups, lanes), f32)],
        compiler_params=params(("arbitrary",)),
        name="back_ends",
        cost_estimate=BRIEF,
    )(gs, decay, *after)


def back_scan_body(
    table_ref,
    slot_ref,
    x_ref,
    gs_ref,
    gv_ref,
    gi_ref,
    check_ref,
    gain_ref,
    decay_ref,
    coef_ref,
    span_ref,
    omega_ref,
    ends_own,
    ends_oth,
    grad_ref,
    qx_ref,
    qs_ref,
    gain_grad_ref,
    omega_grad_ref,
    slab,
    gs_slab,
    out_slab,
    history,
    carry,
    ends_ref,
):
    states, groups, _ = decay_ref.shape
    count = x_ref.shape[1]
    slot = slot_ref[0]
    slots = ends_own.shape[0]
    total = slots + ends_oth.shape[0]

    @pl.when(pl.program_id(0) == 0)
    def _():
        qx_ref[...] = jnp.zeros_like(qx_ref)
        qs_ref[...] = jnp.zeros_like(qs_ref)
        gain_grad_ref[...] = jnp.zeros_like(gain_grad_ref)
        omega_grad_ref[...] = jnp.zeros_like(omega_grad_ref)

    @pl.when(pl.program_id(0) == 0)
    def _():
        carry[...] = jnp.zeros_like(carry)
        ends_ref[:slots] = ends_own[...]
        ends_ref[slots:] = ends_oth[...]

        def link(i, _):
            carry[...] = (
                span_ref[...] * carry[...] + ends_ref[table_ref[total + total - 1 - i]]
            )
            return 0

        lax.fori_loop(0, total - 1 - table_ref[slot], link, 0)

    unit, inv = unit_rows_of(x_ref[0].astype(f32))
    normed = unit * gain_ref[...]
    gs = gs_ref[0]
    to_slab(slab, normed)
    to_slab(gs_slab, gs)
    decay = [decay_ref[n] for n in range(states)]

    def recompute(t, state):
        for n in range(states):
            history[t, n] = state[n]
        row = slab_row(slab, t, groups)
        return tuple(d * s + row for d, s in zip(decay, state))

    lax.fori_loop(
        0, count, recompute, tuple(check_ref[0, 0, n] for n in range(states)), unroll=4
    )

    half = states // 2
    for part in range(2):
        chosen = range(part * half, (part + 1) * half)
        decay = [decay_ref[n] for n in chosen]
        coef = [coef_ref[n] for n in chosen]

        def step(i, held):
            q, qx, qs = held
            t = count - 1 - i
            row = slab_row(slab, t, groups)
            g = slab_row(gs_slab, t, groups)
            q = tuple(d * a + g for d, a in zip(decay, q))
            parts = [c * a for c, a in zip(coef, q)]
            while len(parts) > 1:
                parts = [a + b for a, b in zip(parts[::2], parts[1::2])]
            spot = pl.ds(pl.multiple_of(t * groups, groups), groups)
            if part == 0:
                out_slab[spot, :] = parts[0]
            else:
                out_slab[spot, :] = out_slab[spot, :] + parts[0]
            qx = tuple(a + b * row for a, b in zip(qx, q))
            qs = tuple(a + b * history[t, n] for a, b, n in zip(qs, q, chosen))
            return q, qx, qs

        q, qx, qs = lax.fori_loop(
            0,
            count,
            step,
            (
                tuple(carry[n] for n in chosen),
                tuple(qx_ref[n] for n in chosen),
                tuple(qs_ref[n] for n in chosen),
            ),
            unroll=4,
        )
        for i, n in enumerate(chosen):
            carry[n] = q[i]
            qx_ref[n] = qx[i]
            qs_ref[n] = qs[i]

    grad_normed = (
        gv_ref[0] + from_slab(out_slab, count, groups) + omega_ref[...] * gs
    )
    gain_grad_ref[...] += jnp.sum(grad_normed * unit, axis=0, keepdims=True)
    omega_grad_ref[...] += jnp.sum(gs * normed, axis=0, keepdims=True)
    grad_ref[...] = (
        gi_ref[0] + norm_back_rows(grad_normed, gain_ref[...], unit, inv)
    ).astype(bf16)


def back_scan(table, slot, x, gs, gv, gi, check, gain, decay, coef, span, omega, ends, others, after=()):
    _, length, width = x.shape
    states, groups, lanes = decay.shape
    blocks = check.shape[1]
    block = length // blocks
    whole3 = pl.BlockSpec((states, groups, lanes), lambda b, t, u: (0, 0, 0))
    row = pl.BlockSpec((1, width), lambda b, t, u: (0, 0))
    tokens = pl.BlockSpec((1, block, width), lambda b, t, u: (slot, blocks - 1 - b, 0))
    return pl.pallas_call(
        ignoring(back_scan_body, 14, len(after)),
        grid_spec=pltpu.PrefetchScalarGridSpec(
            num_scalar_prefetch=2,
            grid=(blocks,),
            in_specs=[
                tokens,
                tokens,
                tokens,
                tokens,
                pl.BlockSpec(
                    (1, 1, states, groups, lanes),
                    lambda b, t, u: (slot, blocks - 1 - b, 0, 0, 0),
                ),
                row,
                whole3,
                whole3,
                whole3,
                row,
                pl.BlockSpec(ends.shape, lambda b, t, u: (0, 0, 0, 0)),
                pl.BlockSpec(others.shape, lambda b, t, u: (0, 0, 0, 0)),
            ]
            + [pl.BlockSpec(memory_space=pl.ANY)] * len(after),
            out_specs=[
                pl.BlockSpec((block, width), lambda b, t, u: (blocks - 1 - b, 0)),
                whole3,
                whole3,
                row,
                row,
            ],
            scratch_shapes=[
                pltpu.VMEM((block * groups, lanes), f32),
                pltpu.VMEM((block * groups, lanes), f32),
                pltpu.VMEM((block * groups, lanes), f32),
                pltpu.VMEM((block, states, groups, lanes), f32),
                pltpu.VMEM((states, groups, lanes), f32),
                pltpu.VMEM((ends.shape[0] + others.shape[0], states, groups, lanes), f32),
            ],
        ),
        out_shape=[
            jax.ShapeDtypeStruct((length, width), bf16),
            jax.ShapeDtypeStruct((states, groups, lanes), f32),
            jax.ShapeDtypeStruct((states, groups, lanes), f32),
            jax.ShapeDtypeStruct((1, width), f32),
            jax.ShapeDtypeStruct((1, width), f32),
        ],
        compiler_params=params(("arbitrary",)),
        name="back_scan",
        cost_estimate=LONG,
    )(table, jnp.full((1,), slot, jnp.int32), x, gs, gv, gi, check, gain, decay, coef, span, omega, ends, others, *after)


def chunk_copies(table_ref, own, others, kept, total, length, sem):
    copies = []
    for slot in range(total):
        place = pl.ds(pl.multiple_of(table_ref[slot] * length, length), length)
        source = own.at[slot] if slot < 2 else others.at[slot - 2]
        copies.append(pltpu.make_async_copy(source, kept.at[place, :], sem.at[slot]))
    return copies


def attend_body(
    table_ref,
    q_ref,
    bias_ref,
    reset_ref,
    k_own,
    k_oth,
    v_own,
    v_oth,
    out_ref,
    gated_ref,
    lse_ref,
    keys,
    values,
    scores,
    probs,
    key_sem,
    value_sem,
    *,
    total,
):
    length, key_width = q_ref.shape[1:]
    value_width = values.shape[1]
    tiles = length // TILE
    scale = float(key_width) ** (-0.5)

    key_copies = chunk_copies(table_ref, k_own, k_oth, keys, total, length, key_sem)
    value_copies = chunk_copies(table_ref, v_own, v_oth, values, total, length, value_sem)

    @pl.when(pl.program_id(0) == 0)
    def _():
        for copy in key_copies + value_copies:
            copy.start()
        for copy in key_copies:
            copy.wait()

    chunk = table_ref[pl.program_id(0)]
    reach = jnp.where(table_ref[2 * total] == 1, chunk + 1, 1)
    base = (chunk + 1 - reach) * length
    queries = q_ref[0]

    def first(kc, peak):
        spot = pl.ds(pl.multiple_of(base + kc * length, length), length)
        tile = (
            lax.dot_general(
                queries, keys[spot, :], (((1,), (1,)), ((), ())), preferred_element_type=f32
            )
            * scale
        )
        for r in range(tiles):
            for a in range(tiles):
                rows = slice(r * TILE, (r + 1) * TILE)
                cols = slice(a * TILE, (a + 1) * TILE)
                gap = (reach - 1 - kc) * tiles + r - a + tiles - 1
                scores[kc, rows, cols] = tile[rows, cols] + bias_ref[gap]
        return jnp.maximum(peak, jnp.max(scores[kc], axis=1, keepdims=True))

    peak = lax.fori_loop(0, reach, first, jnp.full((length, 1), 2 * MASKED, f32))

    def second(kc, sums):
        terms = jnp.exp(scores[kc] - peak)
        probs[:, pl.ds(pl.multiple_of(kc * length, length), length)] = terms.astype(bf16)
        return sums + jnp.sum(terms, axis=1, keepdims=True)

    sums = lax.fori_loop(0, reach, second, jnp.zeros((length, 1), f32))
    lse_ref[0] = jnp.broadcast_to(peak + jnp.log(sums), (length, 128)).T[:1]
    inverse = 1.0 / sums

    @pl.when(pl.program_id(0) == 0)
    def _():
        for copy in value_copies:
            copy.wait()

    for count in range(1, total + 1):

        @pl.when(reach == count)
        def _(count=count):
            width = count * length
            span = pl.ds(pl.multiple_of(base, length), width)

            def column(ct, _):
                at = pl.ds(pl.multiple_of(ct * 1024, 1024), 1024)
                rows = (
                    jnp.dot(probs[:, :width], values[span, at], preferred_element_type=f32)
                    * inverse
                )
                out_ref[0, :, at] = rows.astype(bf16)
                gate = reset_ref[0, :, at].astype(f32)
                gated_ref[0, :, at] = (gate * jax.nn.sigmoid(gate) * rows).astype(bf16)
                return 0

            lax.fori_loop(0, value_width // 1024, column, 0)


def attend(table, q, bias, reset, k_own, k_oth, v_own, v_oth):
    slots, length, key_width = q.shape
    value_width = v_own.shape[2]
    total = slots + k_oth.shape[0]
    anywhere = pl.BlockSpec(memory_space=pl.ANY)
    tokens = pl.BlockSpec((1, length, value_width), lambda k, t: (k, 0, 0))
    return pl.pallas_call(
        functools.partial(attend_body, total=total),
        grid_spec=pltpu.PrefetchScalarGridSpec(
            num_scalar_prefetch=1,
            grid=(slots,),
            in_specs=[
                pl.BlockSpec((1, length, key_width), lambda k, t: (k, 0, 0)),
                pl.BlockSpec(bias.shape, lambda k, t: (0, 0, 0)),
                tokens,
                anywhere,
                anywhere,
                anywhere,
                anywhere,
            ],
            out_specs=[
                tokens,
                tokens,
                pl.BlockSpec((1, 1, length), lambda k, t: (k, 0, 0)),
            ],
            scratch_shapes=[
                pltpu.VMEM((total * length, key_width), bf16),
                pltpu.VMEM((total * length, value_width), bf16),
                pltpu.VMEM((total, length, length), f32),
                pltpu.VMEM((length, total * length), bf16),
                pltpu.SemaphoreType.DMA((total,)),
                pltpu.SemaphoreType.DMA((total,)),
            ],
        ),
        out_shape=[
            jax.ShapeDtypeStruct((slots, length, value_width), bf16),
            jax.ShapeDtypeStruct((slots, length, value_width), bf16),
            jax.ShapeDtypeStruct((slots, 1, length), f32),
        ],
        compiler_params=params(("arbitrary",)),
        name="attend",
        cost_estimate=BRIEF,
    )(table, q, bias, reset, k_own, k_oth, v_own, v_oth)


def attend_back_body(
    table_ref,
    q_ref,
    grad_ref,
    lse_ref,
    bias_ref,
    k_own,
    k_oth,
    v_own,
    v_oth,
    gq_ref,
    gk_own,
    gv_own,
    both_oth,
    rel_out,
    keys,
    values,
    gk_sum,
    gv_sum,
    probs_kept,
    grads_kept,
    rel_ref,
    key_sem,
    value_sem,
    *,
    total,
):
    length, key_width = q_ref.shape[1:]
    value_width = values.shape[1]
    tiles = length // TILE
    scale = float(key_width) ** (-0.5)
    step = pl.program_id(0)
    nt = (((1,), (1,)), ((), ()))
    tn = (((0,), (0,)), ((), ()))

    copies = chunk_copies(
        table_ref, k_own, k_oth, keys, total, length, key_sem
    ) + chunk_copies(table_ref, v_own, v_oth, values, total, length, value_sem)

    @pl.when(step == 0)
    def _():
        for copy in copies:
            copy.start()
        gk_sum[...] = jnp.zeros_like(gk_sum)
        gv_sum[...] = jnp.zeros_like(gv_sum)
        rel_ref[...] = jnp.zeros_like(rel_ref)
        for copy in copies:
            copy.wait()

    chunk = table_ref[step]
    reach = jnp.where(table_ref[2 * total] == 1, chunk + 1, 1)
    base = (chunk + 1 - reach) * length
    queries = q_ref[0]
    log_total = lse_ref[0]

    def gap_of(kc, a, r):
        return (reach - 1 - kc) * tiles + r - a + tiles - 1

    def first(kc, delta):
        spot = pl.ds(pl.multiple_of(base + kc * length, length), length)
        grads_kept[kc] = lax.dot_general(
            values[spot, :], grad_ref[0], nt, preferred_element_type=f32
        )
        tile = (
            lax.dot_general(keys[spot, :], queries, nt, preferred_element_type=f32) * scale
        )
        for a in range(tiles):
            for r in range(tiles):
                rows = slice(a * TILE, (a + 1) * TILE)
                cols = slice(r * TILE, (r + 1) * TILE)
                probs_kept[kc, rows, cols] = jnp.exp(
                    tile[rows, cols] + bias_ref[gap_of(kc, a, r)] - log_total[:, cols]
                )
        return delta + jnp.sum(probs_kept[kc] * grads_kept[kc], axis=0, keepdims=True)

    delta = lax.fori_loop(0, reach, first, jnp.zeros((1, length), f32))

    def second(kc, grad_query):
        spot = pl.ds(pl.multiple_of(base + kc * length, length), length)
        probs = probs_kept[kc]
        grad_scores = (probs * (grads_kept[kc] - delta)).astype(bf16)
        probs = probs.astype(bf16)
        for a in range(tiles):
            for r in range(tiles):
                rel_ref[gap_of(kc, a, r)] += grad_scores[
                    a * TILE : (a + 1) * TILE, r * TILE : (r + 1) * TILE
                ].astype(f32)
        gk_sum[spot, :] += jnp.dot(grad_scores, queries, preferred_element_type=f32)

        def column(ct, _):
            at = pl.ds(pl.multiple_of(ct * 1024, 1024), 1024)
            gv_sum[spot, at] += jnp.dot(
                probs, grad_ref[0, :, at], preferred_element_type=f32
            )
            return 0

        lax.fori_loop(0, value_width // 1024, column, 0)
        return grad_query + lax.dot_general(
            grad_scores, keys[spot, :], tn, preferred_element_type=f32
        )

    grad_query = lax.fori_loop(0, reach, second, jnp.zeros((length, key_width), f32))
    gq_ref[0] = grad_query * scale

    @pl.when(step == pl.num_programs(0) - 1)
    def _():
        for slot in range(total):
            place = pl.ds(pl.multiple_of(table_ref[slot] * length, length), length)
            key_grad = (gk_sum[place, :] * scale).astype(bf16)
            value_grad = gv_sum[place, :].astype(bf16)
            if slot < 2:
                gk_own[slot] = key_grad
                gv_own[slot] = value_grad
            else:
                both_oth[slot - 2, :, :value_width] = value_grad
                both_oth[slot - 2, :, value_width:] = key_grad
        down = lax.broadcasted_iota(jnp.int32, (TILE, TILE), 0)
        across = lax.broadcasted_iota(jnp.int32, (TILE, TILE), 1)
        mirror = jnp.where(down + across == TILE - 1, 1.0, 0.0)
        for d in range(rel_out.shape[0]):
            flipped = jnp.dot(
                rel_ref[d + tiles - 1],
                mirror,
                precision=lax.Precision.HIGHEST,
                preferred_element_type=f32,
            )
            wide = jnp.concatenate([flipped, jnp.zeros((TILE, TILE), f32)], axis=1)
            turned = pltpu.roll(wide, 0, 1, stride=1, stride_axis=0)
            rel_out[d] = jnp.sum(turned, axis=0, keepdims=True)


def attend_back(table, q, grads, lse, bias, k_own, k_oth, v_own, v_oth, after=()):
    slots, length, key_width = q.shape
    value_width = v_own.shape[2]
    total = slots + k_oth.shape[0]
    rel_shape = (total * length // TILE, 1, 2 * TILE)
    both_shape = (k_oth.shape[0], length, key_width + value_width)
    anywhere = pl.BlockSpec(memory_space=pl.ANY)

    def all_of(shape):
        return pl.BlockSpec(
            shape, lambda k, t: (0,) * len(shape), pipeline_mode=pl.Buffered(1)
        )

    return pl.pallas_call(
        ignoring(functools.partial(attend_back_body, total=total), 9, len(after)),
        grid_spec=pltpu.PrefetchScalarGridSpec(
            num_scalar_prefetch=1,
            grid=(slots,),
            in_specs=[
                pl.BlockSpec((1, length, key_width), lambda k, t: (k, 0, 0)),
                pl.BlockSpec((1, length, value_width), lambda k, t: (k, 0, 0)),
                pl.BlockSpec((1, 1, length), lambda k, t: (k, 0, 0)),
                all_of(bias.shape),
                anywhere,
                anywhere,
                anywhere,
                anywhere,
            ]
            + [anywhere] * len(after),
            out_specs=[
                pl.BlockSpec((1, length, key_width), lambda k, t: (k, 0, 0)),
                all_of(k_own.shape),
                all_of(v_own.shape),
                all_of(both_shape),
                all_of(rel_shape),
            ],
            scratch_shapes=[
                pltpu.VMEM((total * length, key_width), bf16),
                pltpu.VMEM((total * length, value_width), bf16),
                pltpu.VMEM((total * length, key_width), f32),
                pltpu.VMEM((total * length, value_width), f32),
                pltpu.VMEM((total, length, length), f32),
                pltpu.VMEM((total, length, length), f32),
                pltpu.VMEM(bias.shape, f32),
                pltpu.SemaphoreType.DMA((total,)),
                pltpu.SemaphoreType.DMA((total,)),
            ],
        ),
        out_shape=[
            jax.ShapeDtypeStruct((slots, length, key_width), f32),
            jax.ShapeDtypeStruct(k_own.shape, bf16),
            jax.ShapeDtypeStruct(v_own.shape, bf16),
            jax.ShapeDtypeStruct(both_shape, bf16),
            jax.ShapeDtypeStruct(rel_shape, f32),
        ],
        compiler_params=params(("arbitrary",)),
        name="attend_back",
        cost_estimate=LONG,
    )(table, q, grads, lse, bias, k_own, k_oth, v_own, v_oth, *after)


def bias_body(flag_ref, back_row, front_row, back_ref, front_ref, *, spare):
    tile = pl.program_id(0) - spare
    full = flag_ref[0] == 1

    @pl.when(tile < 0)
    def _():
        back_ref[...] = jnp.full_like(back_ref, MASKED)
        front_ref[...] = jnp.full_like(front_ref, MASKED)

    @pl.when(tile >= 0)
    def _():
        down = lax.broadcasted_iota(jnp.int32, (TILE, TILE), 0)
        across = lax.broadcasted_iota(jnp.int32, (TILE, TILE), 1)
        near = jnp.where(down // STRETCH == across // STRETCH, 1, 0)
        for row, out, ordered in (
            (back_row, back_ref, jnp.where(down <= across, 1, 0)),
            (front_row, front_ref, jnp.where(across <= down, 1, 0)),
        ):
            wide = jnp.broadcast_to(row[0], (TILE, 2 * TILE))
            turned = pltpu.roll(wide, 0, 1, stride=1, stride_axis=0)[:, :TILE]
            allowed = jnp.where(
                tile == 0, jnp.where(full, ordered, ordered * near), jnp.where(full, 1, 0)
            )
            out[0] = jnp.where(allowed == 1, turned, MASKED)


def bias_tiles(relative_bias, spare, full):
    length = relative_bias.shape[0] // 2
    count = length // TILE
    windows = jnp.stack(
        [
            lax.slice_in_dim(relative_bias, length - d * TILE - TILE, length - d * TILE + TILE)
            for d in range(count)
        ]
    )
    front = jnp.concatenate([windows[:, TILE:], windows[:, :TILE]], axis=1)
    back = jnp.concatenate([windows[:, TILE:TILE + 1], windows[:, ::-1][:, TILE:], windows[:, ::-1][:, : TILE - 1]], axis=1)
    row = pl.BlockSpec((1, 1, 2 * TILE), lambda d, t: (jnp.maximum(d - spare, 0), 0, 0))
    out = pl.BlockSpec((1, TILE, TILE), lambda d, t: (d, 0, 0))
    shape = jax.ShapeDtypeStruct((spare + count, TILE, TILE), f32)
    return pl.pallas_call(
        functools.partial(bias_body, spare=spare),
        grid_spec=pltpu.PrefetchScalarGridSpec(
            num_scalar_prefetch=1,
            grid=(spare + count,),
            in_specs=[row, row],
            out_specs=[out, out],
        ),
        out_shape=[shape, shape],
        compiler_params=params(("arbitrary",)),
        name="bias",
    )(full.astype(jnp.int32)[None], back[:, None], front[:, None])


def bias_grad(sums, length):
    count = sums.shape[0]
    shifted = jnp.concatenate([jnp.zeros((count, 1), f32), sums[:, :-1]], axis=1)
    none = jnp.zeros((1, TILE), f32)
    blocks = jnp.concatenate([none, shifted[:, :TILE]]) + jnp.concatenate(
        [shifted[:, TILE:], none]
    )
    return jnp.concatenate(
        [blocks[::-1].reshape(-1), jnp.zeros((2 * length - (count + 1) * TILE,), f32)]
    )


def candidate_body(
    gated_ref, proj_ref, pre_ref, update_ref, x_ref, gain_ref, cand_ref, first_ref, low_ref
):
    cand_in = pre_ref[...].astype(f32) + jnp.dot(
        gated_ref[...], proj_ref[...], preferred_element_type=f32
    )
    cand_ref[...] = cand_in
    x = x_ref[...].astype(f32)
    update = jax.nn.sigmoid(update_ref[...].astype(f32))
    first = x + update * (cand_in * jax.nn.sigmoid(cand_in) - x)
    first_ref[...] = first
    unit, _ = unit_rows_of(first)
    low_ref[...] = (unit * gain_ref[...]).astype(bf16)


def candidate(gated, proj, base, x, gain):
    tokens, width = x.shape
    value_width = gated.shape[1]
    rows = min(256, tokens)
    wide = value_width // width

    def block(columns, at=0):
        return pl.BlockSpec((rows, columns), lambda i: (i, at))

    return pl.pallas_call(
        candidate_body,
        grid=(tokens // rows,),
        in_specs=[
            block(value_width),
            pl.BlockSpec(proj.shape, lambda i: (0, 0), pipeline_mode=pl.Buffered(1)),
            block(width, wide + 1),
            block(width, wide),
            block(width),
            pl.BlockSpec((1, width), lambda i: (0, 0)),
        ],
        out_specs=[block(width)] * 3,
        out_shape=[
            jax.ShapeDtypeStruct((tokens, width), f32),
            jax.ShapeDtypeStruct((tokens, width), f32),
            jax.ShapeDtypeStruct((tokens, width), bf16),
        ],
        compiler_params=params(("arbitrary",)),
        name="candidate",
        cost_estimate=BRIEF,
    )(gated, proj, base, base, x, gain)


def gate_body(
    back_ref,
    cot_a,
    cot_b,
    x_ref,
    cand_ref,
    update_ref,
    reset_ref,
    attended_ref,
    gain_ref,
    proj_ref,
    input_ref,
    main_ref,
    grad_att_ref,
    gain_grad_ref,
):
    width = x_ref.shape[1]
    value_width = proj_ref.shape[0]

    @pl.when(pl.program_id(0) == 0)
    def _():
        gain_grad_ref[...] = jnp.zeros_like(gain_grad_ref)

    x = x_ref[...].astype(f32)
    cand_in = cand_ref[...]
    gate = jax.nn.sigmoid(cand_in)
    candidate = cand_in * gate
    update = jax.nn.sigmoid(update_ref[...].astype(f32))
    change = candidate - x
    unit, inv = unit_rows_of(x + update * change)
    grad_feed = back_ref[...]
    gain_grad_ref[...] += jnp.sum(grad_feed * unit, axis=0, keepdims=True)
    early = pl.program_id(0) < pl.num_programs(0) // 2
    cot = jnp.where(early, cot_a[...].astype(f32), cot_b[...].astype(f32))
    grad_first = cot + norm_back_rows(
        grad_feed, gain_ref[...], unit, inv
    )
    kept = grad_first * (1.0 - update)
    input_ref[...] = kept
    main_ref[:, value_width : value_width + width] = (kept * change * update).astype(bf16)
    grad_cand = (grad_first * update * (gate + candidate * (1.0 - gate))).astype(bf16)
    main_ref[:, value_width + width :] = grad_cand
    for c in range(value_width // 512):
        at = slice(c * 512, (c + 1) * 512)
        grad_gated = mm_nt(grad_cand, proj_ref[at, :])
        reset = reset_ref[:, at].astype(f32)
        open_gate = jax.nn.sigmoid(reset)
        passed = reset * open_gate
        grad_att_ref[:, at] = (grad_gated * passed).astype(bf16)
        main_ref[:, at] = (
            grad_gated
            * attended_ref[:, at].astype(f32)
            * (open_gate + passed * (1.0 - open_gate))
        ).astype(bf16)


def gate(back, cots, x, cand_in, base, attended, gain, proj, after=()):
    tokens, width = x.shape
    value_width = proj.shape[0]
    rows = min(256, tokens // 2)
    half = tokens // rows // 2
    wide = value_width // width

    def block(columns, at=0):
        return pl.BlockSpec((rows, columns), lambda i: (i, at))

    return pl.pallas_call(
        ignoring(gate_body, 10, len(after)),
        grid=(tokens // rows,),
        in_specs=[
            block(width),
            pl.BlockSpec((rows, width), lambda i: (jnp.minimum(i, half - 1), 0)),
            pl.BlockSpec((rows, width), lambda i: (jnp.maximum(i - half, 0), 0)),
            block(width),
            block(width),
            block(width, wide),
            block(value_width),
            block(value_width),
            pl.BlockSpec((1, width), lambda i: (0, 0)),
            pl.BlockSpec(proj.shape, lambda i: (0, 0), pipeline_mode=pl.Buffered(1)),
        ]
        + [pl.BlockSpec(memory_space=pl.ANY)] * len(after),
        out_specs=[
            block(width),
            block(value_width + 2 * width),
            block(value_width),
            pl.BlockSpec((1, width), lambda i: (0, 0)),
        ],
        out_shape=[
            jax.ShapeDtypeStruct((tokens, width), f32),
            jax.ShapeDtypeStruct((tokens, value_width + 2 * width), bf16),
            jax.ShapeDtypeStruct((tokens, value_width), bf16),
            jax.ShapeDtypeStruct((1, width), f32),
        ],
        compiler_params=params(("arbitrary",)),
        name="gate",
        cost_estimate=LONG,
    )(back, *cots, x, cand_in, base, base, attended, gain, proj, *after)


def ordered_transpose(ids_ref, source, plain, ordered):
    plain[...] = source[...].T
    count = ids_ref.shape[0]
    rows = plain.shape[0] // count

    def place(p, _):
        ordered[pl.ds(pl.multiple_of(p * rows, rows), rows), :] = plain[
            pl.ds(pl.multiple_of(ids_ref[p] * rows, rows), rows), :
        ]
        return 0

    lax.fori_loop(0, count, place, 0)


def placed_transpose(places_ref, sources, plain, ordered):
    start = 0
    for source in sources:
        plain[:, start : start + source.shape[0]] = source[...].T
        start += source.shape[0]
    count = places_ref.shape[0]
    rows = plain.shape[0] // count

    def place(q, _):
        ordered[pl.ds(pl.multiple_of(places_ref[q] * rows, rows), rows), :] = plain[
            pl.ds(pl.multiple_of(q * rows, rows), rows), :
        ]
        return 0

    lax.fori_loop(0, count, place, 0)


def feed_body(
    ids_ref,
    places_ref,
    low_ref,
    cot_a,
    cot_b,
    first_ref,
    in_ref,
    out_ref,
    result_a,
    result_b,
    back_ref,
    out_send,
    out_keep,
    in_send,
    in_keep,
    total,
    cot_turned,
    low_turned,
    plain,
):
    step = pl.program_id(0)
    half = pl.num_programs(0) // 2
    tokens = low_ref.shape[0]
    middle = tokens // 2
    nt = (((1,), (1,)), ((), ()))

    @pl.when(step == 0)
    def _():
        placed_transpose(places_ref, (cot_a, cot_b), plain, cot_turned)
        ordered_transpose(ids_ref, low_ref, plain, low_turned)
        total[...] = first_ref[...]
        back_ref[...] = jnp.zeros_like(back_ref)

    acts, grads = [], []
    for r, cot_ref in enumerate((cot_a, cot_b)):
        at = slice(r * middle, (r + 1) * middle)
        hidden = jnp.dot(low_ref[at, :], in_ref[...], preferred_element_type=f32)
        grad_act = lax.dot_general(
            cot_ref[...], out_ref[...], nt, preferred_element_type=f32
        )
        gate = jax.nn.sigmoid(hidden)
        act = hidden * gate
        grad = (grad_act * (gate + act * (1.0 - gate))).astype(bf16)
        act = act.astype(bf16)
        total[at, :] += jnp.dot(act, out_ref[...], preferred_element_type=f32)
        back_ref[at, :] += lax.dot_general(
            grad, in_ref[...], nt, preferred_element_type=f32
        )
        acts.append(act)
        grads.append(grad)
    out_grad = jnp.dot(
        cot_turned[...], jnp.concatenate(acts), preferred_element_type=f32
    ).astype(bf16)
    in_grad = jnp.dot(
        low_turned[...], jnp.concatenate(grads), preferred_element_type=f32
    ).astype(bf16)
    split = in_grad.shape[0] // 2
    in_send[...] = in_grad[:split].reshape(in_send.shape)
    in_keep[...] = in_grad[split:].reshape(in_keep.shape)

    @pl.when(step < half)
    def _():
        out_send[0] = out_grad

    @pl.when(step >= half)
    def _():
        out_keep[0] = out_grad

    @pl.when(step == pl.num_programs(0) - 1)
    def _():
        result_a[...] = total[:middle, :].astype(bf16)
        result_b[...] = total[middle:, :].astype(bf16)


def feed(ids, places, low, cots, first_sum, feed_in, feed_out, seq, after=()):
    tokens, width = low.shape
    features = feed_in.shape[1]
    parts = ids.shape[0]
    half = parts // 2
    columns = features // parts
    rows = width // parts
    share = parts // seq
    anywhere = pl.BlockSpec(memory_space=pl.ANY)

    def all_of(shape):
        return pl.BlockSpec(
            shape, lambda i, t, u: (0,) * len(shape), pipeline_mode=pl.Buffered(1)
        )

    def at(i, t):
        return t[jnp.minimum(i, parts - 1)]

    split = pl.BlockSpec(
        (half, 1, 1, rows, columns),
        lambda i, t, u: (0, u[at(i, t) // share], at(i, t) % share, 0, 0),
    )
    return pl.pallas_call(
        ignoring(feed_body, 8, len(after)),
        grid_spec=pltpu.PrefetchScalarGridSpec(
            num_scalar_prefetch=2,
            grid=(parts,),
            in_specs=[
                all_of(low.shape),
                all_of(cots[0].shape),
                all_of(cots[1].shape),
                all_of(first_sum.shape),
                pl.BlockSpec((width, columns), lambda i, t, u: (0, at(i, t))),
                pl.BlockSpec((columns, width), lambda i, t, u: (at(i, t), 0)),
            ]
            + [anywhere] * len(after),
            out_specs=[
                all_of(cots[0].shape),
                all_of(cots[1].shape),
                all_of(low.shape),
                pl.BlockSpec(
                    (1, width, columns), lambda i, t, u: (jnp.minimum(i, half - 1), 0, 0)
                ),
                pl.BlockSpec(
                    (1, width, columns), lambda i, t, u: (jnp.maximum(i - half, 0), 0, 0)
                ),
                split,
                split,
            ],
            scratch_shapes=[
                pltpu.VMEM((tokens, width), f32),
                pltpu.VMEM((width, tokens), bf16),
                pltpu.VMEM((width, tokens), bf16),
                pltpu.VMEM((width, tokens), bf16),
            ],
        ),
        out_shape=[
            jax.ShapeDtypeStruct(cots[0].shape, bf16),
            jax.ShapeDtypeStruct(cots[1].shape, bf16),
            jax.ShapeDtypeStruct((tokens, width), f32),
            jax.ShapeDtypeStruct((half, width, columns), bf16),
            jax.ShapeDtypeStruct((half, width, columns), bf16),
            jax.ShapeDtypeStruct((half, seq, share, rows, columns), bf16),
            jax.ShapeDtypeStruct((half, seq, share, rows, columns), bf16),
        ],
        compiler_params=params(("arbitrary",)),
        name="feed",
        cost_estimate=BRIEF,
    )(ids, places, low, *cots, first_sum, feed_in, feed_out, *after)


def product_body(left_ref, right_ref, out_ref):
    out_ref[...] = jnp.dot(
        left_ref[...], right_ref[...], preferred_element_type=f32
    ).astype(out_ref.dtype)


def product(left, right, tile=1024):
    tokens, depth = left.shape
    columns = right.shape[1]
    return pl.pallas_call(
        product_body,
        grid=(columns // tile,),
        in_specs=[
            pl.BlockSpec(left.shape, lambda i: (0, 0), pipeline_mode=pl.Buffered(1)),
            pl.BlockSpec((depth, tile), lambda i: (0, i)),
        ],
        out_specs=pl.BlockSpec((tokens, tile), lambda i: (0, i)),
        out_shape=jax.ShapeDtypeStruct((tokens, columns), bf16),
        compiler_params=params(("arbitrary",)),
        name="product",
        cost_estimate=BRIEF,
    )(left, right)


def smooth_back_body(
    main_ref, shared_ref, weight_ref, shared_weight_ref, smooth_ref, out_ref, total
):
    step = pl.program_id(0)

    @pl.when(step == 0)
    def _():
        total[...] = mm_nt(shared_ref[...], shared_weight_ref[...])

    total[...] += mm_nt(main_ref[...], weight_ref[...])

    @pl.when(step == pl.num_programs(0) - 1)
    def _():
        out_ref[...] = total[...] * silu_slope(smooth_ref[...])


def smooth_back(main, shared, weight, shared_weight, smoothed, after=()):
    tokens, width = smoothed.shape
    tile = 1024

    def all_of(shape):
        return pl.BlockSpec(shape, lambda i: (0, 0), pipeline_mode=pl.Buffered(1))

    return pl.pallas_call(
        ignoring(smooth_back_body, 5, len(after)),
        grid=(main.shape[1] // tile,),
        in_specs=[
            pl.BlockSpec((tokens, tile), lambda i: (0, i)),
            all_of(shared.shape),
            pl.BlockSpec((width, tile), lambda i: (0, i)),
            all_of(shared_weight.shape),
            all_of(smoothed.shape),
        ]
        + [pl.BlockSpec(memory_space=pl.ANY)] * len(after),
        out_specs=all_of(smoothed.shape),
        out_shape=jax.ShapeDtypeStruct(smoothed.shape, f32),
        scratch_shapes=[pltpu.VMEM(smoothed.shape, f32)],
        compiler_params=params(("arbitrary",)),
        name="smooth_back",
        cost_estimate=LONG,
    )(main, shared, weight, shared_weight, smoothed, *after)


def by_columns_body(ids_ref, places_ref, left_ref, right_ref, send, keep, plain, turned):
    step = pl.program_id(0)
    half = pl.num_programs(0) // 2

    @pl.when(step == 0)
    def _():
        placed_transpose(places_ref, (left_ref,), plain, turned)

    grad = jnp.dot(turned[...], right_ref[...], preferred_element_type=f32).astype(bf16)

    @pl.when(step < half)
    def _():
        send[0] = grad

    @pl.when(step >= half)
    def _():
        keep[0] = grad


def by_columns(ids, places, left, right, after=(), rows=None, at=0):
    tokens = left.shape[0]
    rows = rows or left.shape[1]
    parts = ids.shape[0]
    half = parts // 2
    columns = right.shape[1] // parts
    shape = jax.ShapeDtypeStruct((half, rows, columns), bf16)
    if columns % 128:
        left = left[:, at * rows : (at + 1) * rows]
        grad = mm_tn(left, right).astype(bf16).reshape(rows, parts, columns)
        grad = jnp.take(grad, ids, axis=1).transpose(1, 0, 2)
        grad = grad.reshape(parts, places.shape[0], -1, columns)
        grad = jnp.take(grad, jnp.argsort(places), axis=1).reshape(parts, rows, columns)
        return grad[:half], grad[half:]
    return pl.pallas_call(
        ignoring(by_columns_body, 4, len(after)),
        grid_spec=pltpu.PrefetchScalarGridSpec(
            num_scalar_prefetch=2,
            grid=(parts,),
            in_specs=[
                pl.BlockSpec(
                    (tokens, rows), lambda i, t, u: (0, at), pipeline_mode=pl.Buffered(1)
                ),
                pl.BlockSpec((tokens, columns), lambda i, t, u: (0, t[jnp.minimum(i, parts - 1)])),
            ]
            + [pl.BlockSpec(memory_space=pl.ANY)] * len(after),
            out_specs=[
                pl.BlockSpec(
                    (1, rows, columns), lambda i, t, u: (jnp.minimum(i, half - 1), 0, 0)
                ),
                pl.BlockSpec(
                    (1, rows, columns), lambda i, t, u: (jnp.maximum(i - half, 0), 0, 0)
                ),
            ],
            scratch_shapes=[
                pltpu.VMEM((rows, tokens), bf16),
                pltpu.VMEM((rows, tokens), bf16),
            ],
        ),
        out_shape=[shape, shape],
        compiler_params=params(("arbitrary",)),
        name="by_columns",
        cost_estimate=BRIEF,
    )(ids, places, left, right, *after)


def by_rows_body(ids_ref, places_ref, left_ref, right_ref, send, keep, plain, turned):
    @pl.when(pl.program_id(0) == 0)
    def _():
        ordered_transpose(ids_ref, left_ref, plain, turned)

    grad = jnp.dot(turned[...], right_ref[...], preferred_element_type=f32).astype(bf16)
    middle = grad.shape[0] // 2
    send[...] = grad[:middle].reshape(send.shape)
    keep[...] = grad[middle:].reshape(keep.shape)


def by_rows(ids, places, left, right, seq=1, after=(), cost=BRIEF):
    tokens, rows = left.shape
    parts = ids.shape[0]
    half = parts // 2
    if places is None:
        seq, places = 1, jnp.zeros((1,), jnp.int32)
    columns = right.shape[1] // seq
    tile = min(512, columns)
    share = columns // tile
    shape = jax.ShapeDtypeStruct((half, seq, rows // parts, columns), bf16)
    split = pl.BlockSpec(
        (half, 1, rows // parts, tile), lambda i, t, u: (0, u[jnp.minimum(i // share, seq - 1)], 0, i % share)
    )
    return pl.pallas_call(
        ignoring(by_rows_body, 4, len(after)),
        grid_spec=pltpu.PrefetchScalarGridSpec(
            num_scalar_prefetch=2,
            grid=(seq * share,),
            in_specs=[
                pl.BlockSpec(
                    left.shape, lambda i, t, u: (0, 0), pipeline_mode=pl.Buffered(1)
                ),
                pl.BlockSpec((tokens, tile), lambda i, t, u: (0, i)),
            ]
            + [pl.BlockSpec(memory_space=pl.ANY)] * len(after),
            out_specs=[split, split],
            scratch_shapes=[
                pltpu.VMEM((rows, tokens), bf16),
                pltpu.VMEM((rows, tokens), bf16),
            ],
        ),
        out_shape=[shape, shape],
        compiler_params=params(("arbitrary",)),
        name="by_rows",
        cost_estimate=cost,
    )(ids, places, left, right, *after)


def value_back_body(
    ids_ref,
    places_ref,
    left_ref,
    own_ref,
    other_ref,
    slope_ref,
    proj_ref,
    total_ref,
    send,
    keep,
    plain,
    turned,
):
    @pl.when(pl.program_id(0) == 0)
    def _():
        total_ref[...] = jnp.zeros_like(total_ref)
        ordered_transpose(ids_ref, left_ref, plain, turned)

    grad = own_ref[...].astype(f32)
    for k in range(other_ref.shape[0]):
        grad = grad + other_ref[k].astype(f32)
    grad = (grad * slope_ref[...].astype(f32)).astype(bf16)
    total_ref[...] += mm_nt(grad, proj_ref[...])
    weights = jnp.dot(turned[...], grad, preferred_element_type=f32).astype(bf16)
    middle = weights.shape[0] // 2
    send[...] = weights[:middle].reshape(send.shape)
    keep[...] = weights[middle:].reshape(keep.shape)


def value_back(ids, places, left, own, others, slope, proj, seq, after=()):
    tokens, rows = left.shape
    parts = ids.shape[0]
    half = parts // 2
    columns = proj.shape[1] // seq
    tile = min(512, columns)
    share = columns // tile
    shape = jax.ShapeDtypeStruct((half, seq, rows // parts, columns), bf16)
    split = pl.BlockSpec(
        (half, 1, rows // parts, tile),
        lambda i, t, u: (0, u[jnp.minimum(i // share, seq - 1)], 0, i % share),
    )
    stripe = pl.BlockSpec((tokens, tile), lambda i, t, u: (0, i))
    fixed = pl.BlockSpec(
        (tokens, rows), lambda i, t, u: (0, 0), pipeline_mode=pl.Buffered(1)
    )
    return pl.pallas_call(
        ignoring(value_back_body, 7, len(after)),
        grid_spec=pltpu.PrefetchScalarGridSpec(
            num_scalar_prefetch=2,
            grid=(seq * share,),
            in_specs=[
                fixed,
                stripe,
                pl.BlockSpec((others.shape[0], tokens, tile), lambda i, t, u: (0, 0, i)),
                stripe,
                pl.BlockSpec((rows, tile), lambda i, t, u: (0, i)),
            ]
            + [pl.BlockSpec(memory_space=pl.ANY)] * len(after),
            out_specs=[fixed, split, split],
            scratch_shapes=[
                pltpu.VMEM((rows, tokens), bf16),
                pltpu.VMEM((rows, tokens), bf16),
            ],
        ),
        out_shape=[jax.ShapeDtypeStruct((tokens, rows), f32), shape, shape],
        compiler_params=params(("arbitrary",)),
        name="value_back",
        cost_estimate=LONG,
    )(ids, places, left, own, others, slope, proj, *after)


def stage_body(*refs, jobs):
    ins, outs = list(refs), list(refs[sum(map(sum, jobs)) :])
    for counts, out in zip(jobs, outs):
        for g, count in enumerate(counts):
            total = ins.pop(0)[0].astype(f32)
            for _ in range(count - 1):
                total = total + ins.pop(0)[0].astype(f32)
            out[g] = total.astype(out.dtype)


def stage_sums(jobs, after=(), steps=4, cost=BRIEF):
    for _, rows, _ in jobs:
        while rows % (16 * steps) and steps > 1:
            steps //= 2
    ins, in_specs, out_specs, out_shapes, counts = [], [], [], [], []
    for terms, rows, kind in jobs:
        each = rows // steps
        columns = terms[0][0][0].shape[2]
        for array, entry, start in (term for group in terms for term in group):
            ins.append(array)
            in_specs.append(
                pl.BlockSpec(
                    (1, each, columns),
                    lambda i, entry=entry, first=start // each: (entry, first + i, 0),
                )
            )
        out_specs.append(pl.BlockSpec((len(terms), each, columns), lambda i: (0, i, 0)))
        out_shapes.append(jax.ShapeDtypeStruct((len(terms), rows, columns), kind))
        counts.append([len(group) for group in terms])
    return pl.pallas_call(
        ignoring(functools.partial(stage_body, jobs=counts), len(ins), len(after)),
        grid=(steps,),
        in_specs=in_specs + [pl.BlockSpec(memory_space=pl.ANY)] * len(after),
        out_specs=out_specs,
        out_shape=out_shapes,
        compiler_params=params(("arbitrary",)),
        name="stage_sums",
        cost_estimate=cost,
    )(*ins, *after)


class Layout:
    def __init__(self, mesh):
        self.dp = mesh.shape["dp"]
        self.seq = mesh.shape["seq"]
        self.members = self.seq // 2
        self.chips = self.seq // 4

    def pairs(self, move):
        return [
            (d * self.seq + z, e * self.seq + w)
            for d in range(self.dp)
            for z in range(self.seq)
            for e, w in [move(d, z)]
        ]

    def send(self, value, move):
        return lax.ppermute(value, AXES, self.pairs(move))

    def place(self, sequence, member):
        return member % 2 ^ (1 - sequence % 2), sequence * self.chips + member // 2

    def member(self, core, z):
        sequence = z // self.chips
        return (z % self.chips) * 2 + (core ^ (1 - sequence % 2))

    def home_to_work(self, round_index):
        def move(d, z):
            part = (1 if z >= self.seq // 2 else 0) ^ round_index
            core, at = self.place(2 * (d % 2) + part, min(z, self.seq - 1 - z))
            return d - d % 2 + core, at

        return move

    def outgoing(self, value):
        late = lax.axis_index("seq") >= self.seq // 2
        return [
            lax.dynamic_index_in_dim(value, jnp.where(late, 1 - r, r), 0, False)
            for r in range(2)
        ]

    def to_work(self, value, round_index):
        return self.send(value, self.home_to_work(round_index))

    def homeward(self, value, round_index):
        pairs = [(b, a) for a, b in self.pairs(self.home_to_work(round_index))]
        return lax.ppermute(value, AXES, pairs)

    def gathered(self, back):
        late = lax.axis_index("seq") >= self.seq // 2
        return jnp.stack([jnp.where(late, back[1], back[0]), jnp.where(late, back[0], back[1])])

    def collect(self, values):
        return self.gathered([self.homeward(v, r) for r, v in enumerate(values)])

    def rotate(self, value, by):
        def move(d, z):
            member = (self.member(d % 2, z) + by) % self.members
            core, at = self.place(z // self.chips, member)
            return d - d % 2 + core, at

        return self.send(value, move)

    def gather(self, value):
        return jnp.concatenate([self.rotate(value, by) for by in range(1, self.members)], axis=0)

    def returns(self, others):
        slots = others.shape[0] // (self.members - 1)
        return jnp.stack(
            [
                self.rotate(others[(by - 1) * slots : by * slots], self.members - by).reshape(
                    -1, others.shape[-1]
                )
                for by in range(1, self.members)
            ]
        )

    def orders(self):
        dp, z = lax.axis_index("dp"), lax.axis_index("seq")
        bits = self.dp.bit_length() - 1
        ids = []
        for core in range(2):
            orders = [[0, *range(1, bits)], [0, *reversed(range(1, bits))]]
            flips = []
            for p in range(self.dp):
                order = orders[core if p >= self.dp // 2 else 1 - core]
                flips.append(
                    sum(
                        (0 if p >> (bits - 1 - i) & 1 else 1) << bit
                        for i, bit in enumerate(order)
                    )
                )
            ids.append(dp ^ jnp.array(flips, jnp.int32))
        ids = jnp.where(dp % 2 == 0, ids[0], ids[1])
        bits = self.seq.bit_length() - 1
        flips = [
            sum((0 if p >> (bits - 1 - i) & 1 else 1) << i for i in range(bits))
            for p in range(self.seq)
        ]
        blocks = z ^ jnp.array(flips, jnp.int32)
        return ids, jnp.argsort(blocks).astype(jnp.int32), blocks

    def partner(self, stage):
        bits = self.dp.bit_length() - 1
        if stage == 0:
            return lambda d, z: (d ^ 1, z)
        if stage < bits:
            return lambda d, z: (d ^ (1 << stage if d % 2 == 0 else 1 << (bits - stage)), z)
        return lambda d, z: (d, z ^ (1 << (stage - bits)))

    def turn(self, sums, after, cost=BRIEF):
        sums = [s for s in sums if s.total is None]
        if not sums:
            return after
        jobs = []
        for s in sums:
            s.stage += 1
            ended = s.stage == s.stages
            rows = s.rows if ended else s.rows // 2
            jobs.append((s.terms, rows, f32 if ended and s.over_seq else bf16))
        out = stage_sums(jobs, after, cost=cost)
        for s, held, (_, rows, _) in zip(sums, out, jobs):
            if s.stage == s.stages:
                s.total = held
            else:
                s.terms = [[(a, e, start + rows) for a, e, start in group] for group in s.terms]
                s.rows = rows
                s.send(held)
        return list(out)

    def from_seq(self, held):
        return [
            self.send(held.astype(bf16), lambda d, z: (d, z ^ other))
            for other in range(1, self.seq)
        ]


    def over_dp(self, held):
        bits = self.dp.bit_length() - 1
        for bit in range(bits - 1):
            held = held + self.send(held, lambda d, z: (d ^ (1 << bit), z))
        return held, self.send(held, lambda d, z: (d ^ (1 << (bits - 1)), z))


def later_body(left, right, out):
    out[...] = left[...] + right[...]


def later_sum(left, right, after):
    inside = pl.BlockSpec(memory_space=pltpu.VMEM)
    return pl.pallas_call(
        ignoring(later_body, 2, len(after)),
        in_specs=[inside] * 2 + [pl.BlockSpec(memory_space=pl.ANY)] * len(after),
        out_specs=inside,
        out_shape=jax.ShapeDtypeStruct(left.shape, left.dtype),
        name="later_sum",
        cost_estimate=BRIEF,
    )(left, right, *after)


def pack_body(qx_a, qx_b, qs_a, qs_b, rest_ref, out):
    rows = qx_a.shape[0]
    out[:rows] = qx_a[...] + qx_b[...]
    out[rows : 2 * rows] = qs_a[...] + qs_b[...]
    out[2 * rows :] = rest_ref[...]


def pack(first, second, rest, after=()):
    ins = [v.reshape(-1, 128) for v in (first[0], second[0], first[1], second[1])] + [rest]
    rows = 2 * ins[0].shape[0] + rest.shape[0]
    inside = pl.BlockSpec(memory_space=pltpu.VMEM)
    return pl.pallas_call(
        ignoring(pack_body, 5, len(after)),
        in_specs=[inside] * 5 + [pl.BlockSpec(memory_space=pl.ANY)] * len(after),
        out_specs=inside,
        out_shape=jax.ShapeDtypeStruct((rows, 128), f32),
        name="pack",
        cost_estimate=BRIEF,
    )(*ins, *after)


def finish_body(*refs, terms):
    alpha, damp, beta, eta, alpha_out, damp_out, beta_out, eta_out, *rest = refs[terms:]
    *rest, rows = rest
    total = refs[0][...]
    for term in refs[1:terms]:
        total = total + term[...].astype(f32)
    rows[...] = total
    states = alpha.shape[0]
    groups = alpha.shape[1] // 128
    for c in range(groups):
        at = slice(c * 128, (c + 1) * 128)
        x_sum = rows[pl.ds(c, states, stride=groups), :]
        s_sum = rows[pl.ds(states * groups + c, states, stride=groups), :]
        rate = alpha[:, at] * beta[:, at]
        input_total = eta[:, at] * x_sum
        decay_total = eta[:, at] * rate * s_sum
        alpha_out[:, at] = beta[:, at] * input_total - damp[:, at] * decay_total
        damp_out[:, at] = -alpha[:, at] * decay_total
        beta_out[:, at] = alpha[:, at] * input_total
        eta_out[:, at] = rate * x_sum
    start = 2 * states * groups
    for out in rest:
        out[...] = rows[start : start + out.shape[0]]
        start += out.shape[0]


def finish(terms, alpha, damp, beta, eta, counts):
    inside = pl.BlockSpec(memory_space=pltpu.VMEM)
    rows = terms[0].shape[0]
    shape = jax.ShapeDtypeStruct(alpha.shape, f32)
    return pl.pallas_call(
        functools.partial(finish_body, terms=len(terms)),
        in_specs=[inside] * (len(terms) + 4),
        out_specs=[inside] * (4 + len(counts)),
        out_shape=[shape] * 4 + [jax.ShapeDtypeStruct((n, 128), f32) for n in counts],
        scratch_shapes=[pltpu.VMEM((rows, 128), f32)],
        name="finish",
        cost_estimate=BRIEF,
    )(*terms, alpha, damp, beta, eta)


class Sum:
    def __init__(self, layout, *pairs, over_seq=True):
        self.layout = layout
        self.stage = 0
        self.dp_stages = layout.dp.bit_length() - 1
        self.stages = self.dp_stages + (layout.seq.bit_length() - 1 if over_seq else 0)
        self.over_seq = over_seq
        self.total = None
        pairs = [[v.reshape(1, -1, v.shape[-1]) for v in pair] for pair in pairs]
        self.rows = pairs[0][1].shape[1]
        self.terms = [
            [(kept, 0, 0), (layout.send(sent, layout.partner(0)), 0, 0)] for sent, kept in pairs
        ]

    def send(self, held):
        arrived = self.layout.send(held, self.layout.partner(self.stage))
        for entry, group in enumerate(self.terms):
            group.append((arrived, entry, 0))

    def begin_seq(self, block):
        self.stage = self.dp_stages
        self.stages = self.stage + self.layout.seq.bit_length() - 1
        self.over_seq, self.total = True, None
        block = block.reshape(1, -1, block.shape[-1])
        self.rows = block.shape[1] // 2
        self.terms = [[(block, 0, self.rows)]]
        self.send(block[:, : self.rows])


def mm(a, b):
    return jnp.dot(a, b, preferred_element_type=f32)


def mm_nt(a, b):
    return lax.dot_general(a, b, (((1,), (1,)), ((), ())), preferred_element_type=f32)


def mm_tn(a, b):
    return lax.dot_general(a, b, (((0,), (0,)), ((), ())), preferred_element_type=f32)


def layer(
    layout,
    inputs,
    cotangent,
    full_attention,
    mix_gain,
    smooth_alpha,
    smooth_damp,
    smooth_beta,
    smooth_eta,
    smooth_omega,
    value_proj,
    mix_proj,
    score_affine,
    relative_bias,
    out_proj,
    feed_gain,
    feed_in,
    feed_out,
):
    slots, chunk_rows, width = inputs.shape
    key_width = score_affine.shape[1]
    value_width = value_proj.shape[1]
    tokens = slots * chunk_rows
    total = layout.seq
    seq_length = relative_bias.shape[0] // 2
    block = min(128, chunk_rows)
    core = lax.axis_index("dp") % 2
    z = lax.axis_index("seq")

    sequence = z // layout.chips
    member = layout.member(core, z)
    swap = sequence % 2
    chunks = []
    for by in range(layout.members):
        source = (member - by) % layout.members
        low, high = source, total - 1 - source
        chunks += [jnp.where(swap == 0, low, high), jnp.where(swap == 0, high, low)]
    chunks = jnp.stack(chunks).astype(jnp.int32)
    slot_of = jnp.sum(
        jnp.where(chunks[None, :] == jnp.arange(total)[:, None], jnp.arange(total)[None, :], 0),
        axis=1,
    ).astype(jnp.int32)
    flags = full_attention.astype(f32)
    flags_other = layout.send(flags, lambda d, z: (d ^ 1, z))
    flags = jnp.where(
        core == 0, jnp.concatenate([flags, flags_other]), jnp.concatenate([flags_other, flags])
    )
    full = lax.dynamic_index_in_dim(flags, sequence, 0, False) == 1.0
    table = jnp.concatenate([chunks, slot_of, full.astype(jnp.int32)[None]])
    ids, places, blocks = layout.orders()

    arriving = [
        (slot, at * (chunk_rows // count), layout.to_work(piece, slot))
        for slot, count in ((0, 1), (1, 1))
        for at, piece in enumerate(jnp.split(layout.outgoing(inputs)[slot], count))
    ]
    leaving = layout.outgoing(cotangent)
    bias_back, bias_front = bias_tiles(relative_bias, chunk_rows // TILE - 1, full)

    states = smooth_alpha.shape[0]
    lanes = (states, width // 128, 128)
    decay = 1.0 - smooth_alpha * smooth_damp
    rate = smooth_alpha * smooth_beta
    span = (decay**chunk_rows).reshape(lanes)
    coef = (smooth_eta * rate).reshape(lanes)
    decay_slab = decay.reshape(lanes)
    gain_row = mix_gain[None]
    omega_row = smooth_omega[None]
    mix_shared, mix_main = mix_proj[:, :key_width], mix_proj[:, key_width:]

    held, after = (), (bias_back, bias_front, mix_main, mix_shared, span, coef)
    ready = (table, ids, places, blocks, *leaving)
    for slot, row, piece in arriving:
        held = front(
            piece, slot, row, (slots, chunk_rows), held, gain_row, decay_slab, value_proj, after=after
        )
        after, ready = ready, ()
    normed_low, x, value_low, value_slope, ends = held
    ends_others = layout.gather(ends)
    leaving, ends_others = lax.optimization_barrier((leaving, ends_others))
    cots = [layout.to_work(v, r) for r, v in enumerate(leaving)]
    normed_low = normed_low.reshape(tokens, width)
    value_slope = value_slope.reshape(tokens, value_width)
    value_others = layout.gather(value_low)
    smoothed, mixed, check, shared_pre, query_low, key_low = front_scan(
        table,
        x,
        gain_row,
        decay_slab,
        coef,
        span,
        omega_row,
        ends,
        ends_others,
        mix_shared,
        score_affine,
        block,
    )
    smoothed = smoothed.reshape(tokens, width)
    mixed = mixed.reshape(tokens, width)
    shared_pre = shared_pre.reshape(tokens, key_width)
    key_others = layout.gather(key_low)
    base = product(mixed, mix_main)
    attended, gated, lse = attend(
        table,
        query_low,
        bias_front,
        base.reshape(slots, chunk_rows, -1),
        key_low,
        key_others,
        value_low,
        value_others,
    )
    attended = attended.reshape(tokens, value_width)
    gated = gated.reshape(tokens, value_width)

    flat_low = x.reshape(tokens, width)
    cand_in, first_sum, feed_low = candidate(gated, out_proj, base, flat_low, feed_gain[None])

    result_a, result_b, grad_feed, out_send, out_keep, in_send, in_keep = feed(
        ids, places, feed_low, cots, first_sum, feed_in, feed_out, layout.seq
    )
    home = [layout.homeward(result_a, 0), layout.homeward(result_b, 1)]
    block_out = layout.gathered(home)
    feed_sum = Sum(layout, (out_send, out_keep), (in_send, in_keep))

    grad_input, grad_main, grad_att, feed_gain_grad = gate(
        grad_feed, cots, flat_low, cand_in, base, attended, feed_gain[None], out_proj
    )
    after = layout.turn((feed_sum,), (grad_att,))
    mix_parts = by_rows(ids, None, mixed, grad_main, after=after, cost=LONG)
    proj_parts = by_columns(
        ids,
        places,
        grad_main,
        gated,
        rows=width,
        at=grad_main.shape[1] // width - 1,
        after=mix_parts,
    )
    after = (*proj_parts, *home)
    mix_sum = Sum(layout, mix_parts, over_seq=False)
    proj_sum = Sum(layout, proj_parts)
    grad_query, gk_own, gv_own, both_oth, rel_sums = attend_back(
        table,
        query_low,
        grad_att.reshape(slots, chunk_rows, value_width),
        lse,
        bias_back,
        key_low,
        key_others,
        value_low,
        value_others,
        after=after,
    )
    both_back = layout.returns(both_oth)
    after = layout.turn((feed_sum, proj_sum), (grad_query,), cost=LONG)
    grad_normed, value_send, value_keep = value_back(
        ids,
        places,
        normed_low,
        gv_own.reshape(tokens, value_width),
        both_back,
        value_slope,
        value_proj,
        layout.seq,
        after=after,
    )
    grad_key = jnp.sum(both_back[:, :, value_width:].astype(f32), axis=0) + gk_own.reshape(
        tokens, key_width
    ).astype(f32)
    grad_query = grad_query.reshape(tokens, key_width)
    grad_shared = (
        (grad_query * score_affine[0] + grad_key * score_affine[2]) * silu_slope(shared_pre)
    ).astype(bf16)
    shared_parts = by_rows(ids, None, mixed, grad_shared, after=(grad_normed,))
    shared_sum = Sum(layout, shared_parts, over_seq=False)
    value_sum = Sum(layout, (value_send, value_keep))
    after = layout.turn((mix_sum,), shared_parts)
    grad_smooth = smooth_back(
        grad_main, grad_shared, mix_main, mix_shared, smoothed, after=after
    )
    grad_smooth = grad_smooth.reshape(slots, chunk_rows, width)
    after = layout.turn((feed_sum, value_sum, proj_sum, shared_sum), (grad_smooth,))
    back = back_ends(grad_smooth, decay_slab, after=after)
    back_others = layout.gather(back)
    after = layout.turn((feed_sum, mix_sum, value_sum, shared_sum), (back,))

    def scan_back(slot, after):
        return back_scan(
            table,
            slot,
            x,
            grad_smooth,
            grad_normed.reshape(slots, chunk_rows, width),
            grad_input.reshape(slots, chunk_rows, width),
            check,
            gain_row,
            decay_slab,
            coef,
            span,
            omega_row,
            back,
            back_others,
            after=after,
        )

    first = scan_back(0, after)
    after = layout.turn(
        (feed_sum, mix_sum, value_sum, proj_sum, shared_sum), (first[0],)
    )
    home_first = layout.homeward(first[0], 0)
    while mix_sum.total is None or shared_sum.total is None:
        after = layout.turn((mix_sum, shared_sum), after)
    rows = jnp.concatenate([shared_sum.total[0], mix_sum.total[0]], axis=1)
    rows = rows.reshape(rows.shape[0], layout.seq, -1).transpose(1, 0, 2)
    mix_sum.begin_seq(rows[blocks])
    second = scan_back(1, (*after, mix_sum.terms[0][0][0]))
    affine_grad = jnp.stack(
        [
            jnp.sum(grad_query * shared_pre * jax.nn.sigmoid(shared_pre), axis=0),
            jnp.sum(grad_query, axis=0),
            jnp.sum(grad_key * shared_pre * jax.nn.sigmoid(shared_pre), axis=0),
            jnp.sum(grad_key, axis=0),
        ]
    )
    relative_grad = bias_grad(rel_sums[:, 0], seq_length)
    small = [
        first[3] + second[3],
        first[4] + second[4],
        feed_gain_grad,
        affine_grad,
        relative_grad,
    ]
    small = [v.reshape(-1, 128) for v in small]
    rest = jnp.concatenate(small)
    rest = jnp.pad(rest, ((0, -rest.shape[0] % 16), (0, 0)))
    home_second = layout.homeward(second[0], 1)
    sums = (mix_sum, proj_sum, value_sum, feed_sum)
    turned = layout.turn(sums, (second[0], home_first), cost=LONG)
    totals = layout.over_dp(pack(first[1:3], second[1:3], rest, after=turned))
    after = layout.turn(sums, (*turned, home_second))
    totals = later_sum(*totals, after=after)
    while any(v.total is None for v in sums):
        after = layout.turn(sums, after)
    grad_in = layout.gathered([home_first, home_second]).astype(f32)
    feed_out_grad, feed_in_grad = feed_sum.total[0].T, feed_sum.total[1]
    rows = width // layout.dp
    feed_in_grad = feed_in_grad.reshape(-1, rows, feed_in_grad.shape[-1])
    feed_in_grad = feed_in_grad.transpose(1, 0, 2).reshape(rows, -1)
    out_grad, value_grad = proj_sum.total[0].T, value_sum.total[0]
    mix_grad = mix_sum.total[0]
    alpha_grad, damp_grad, beta_grad, eta_grad, *parts = finish(
        [totals, *layout.from_seq(totals)],
        smooth_alpha,
        smooth_damp,
        smooth_beta,
        smooth_eta,
        [v.shape[0] for v in small],
    )
    parts = [v.reshape(-1) for v in parts]
    return (
        block_out,
        grad_in,
        parts[0],
        alpha_grad,
        damp_grad,
        beta_grad,
        eta_grad,
        parts[1],
        value_grad,
        mix_grad,
        parts[3].reshape(4, key_width),
        parts[4],
        out_grad,
        parts[2],
        feed_in_grad,
        feed_out_grad,
    )


def solution(mesh):
    tokens = P("dp", "seq", None)
    split = P("dp", "seq")
    return jax.shard_map(
        functools.partial(layer, Layout(mesh)),
        mesh=mesh,
        in_specs=(tokens, tokens, P("dp")) + (P(),) * 14,
        out_specs=(tokens, tokens)
        + (P(),) * 6
        + (split, split, P(), P(), split, P(), split, split),
        check_vma=False,
    )
```

```python
import functools

import jax
import jax.numpy as jnp
from jax import lax
from jax.experimental import pallas as pl
from jax.experimental.pallas import tpu as pltpu
from jax.sharding import PartitionSpec as P

STRETCH = 128
EPSILON = 1e-05
TILE = 256
MASKED = -1e30
VMEM_LIMIT = 60 * 1024 * 1024
AXES = ("dp", "seq")
BRIEF = pl.CostEstimate(flops=1, bytes_accessed=1, transcendentals=0)
LONG = pl.CostEstimate(flops=10**11, bytes_accessed=1, transcendentals=0)

f32 = jnp.float32
bf16 = jnp.bfloat16


def unit_rows_of(values):
    centred = values - jnp.mean(values, axis=-1, keepdims=True)
    inv_std = lax.rsqrt(jnp.mean(centred * centred, axis=-1, keepdims=True) + EPSILON)
    return centred * inv_std, inv_std


def norm_back_rows(grad_out, gain_vec, unit_rows, inv_std):
    scaled = grad_out * gain_vec
    return inv_std * (
        scaled
        - jnp.mean(scaled, axis=-1, keepdims=True)
        - unit_rows * jnp.mean(scaled * unit_rows, axis=-1, keepdims=True)
    )


def silu_slope(pre_act):
    sigmoid_val = jax.nn.sigmoid(pre_act)
    return sigmoid_val * (1.0 + pre_act * (1.0 - sigmoid_val))


def params(semantics, limit=VMEM_LIMIT):
    return pltpu.CompilerParams(dimension_semantics=semantics, vmem_limit_bytes=limit)


def ignoring(body, first, count):
    def called(*refs):
        return body(*refs[:first], *refs[first + count :])

    return called


def to_slab(slab, rows):
    count, groups = rows.shape[0], rows.shape[1] // 128
    for c in range(groups):
        slab[pl.ds(c, count, stride=groups), :] = rows[:, c * 128 : (c + 1) * 128]


def from_slab(slab, count, groups):
    return jnp.concatenate(
        [slab[pl.ds(c, count, stride=groups), :] for c in range(groups)], axis=1
    )


def slab_row(slab, t, groups):
    return slab[pl.ds(pl.multiple_of(t * groups, groups), groups), :]


def front_body(
    x_ref,
    gain_ref,
    decay_ref,
    proj_ref,
    begin_ref,
    low_ref,
    copy_ref,
    value_ref,
    slope_ref,
    end_ref,
    slab,
    *,
    fresh,
):
    states, groups, _ = decay_ref.shape
    count = x_ref.shape[0]

    @pl.when(pl.program_id(0) == 0)
    def _():
        end_ref[...] = jnp.zeros_like(end_ref) if fresh else begin_ref[...]

    copy_ref[0] = x_ref[...]
    unit, _ = unit_rows_of(x_ref[...].astype(f32))
    normed = unit * gain_ref[...]
    low_ref[0] = normed.astype(bf16)
    to_slab(slab, normed)
    decay = [decay_ref[n] for n in range(states)]

    def step(t, state):
        row = slab_row(slab, t, groups)
        return tuple(d * s + row for d, s in zip(decay, state))

    state = lax.fori_loop(
        0, count, step, tuple(end_ref[0, n] for n in range(states)), unroll=8
    )
    for n in range(states):
        end_ref[0, n] = state[n]
    for c in range(proj_ref.shape[1] // 512):
        at = slice(c * 512, (c + 1) * 512)
        pre = jnp.dot(low_ref[0], proj_ref[:, at], preferred_element_type=f32)
        gate = jax.nn.sigmoid(pre)
        value = pre * gate
        value_ref[0, :, at] = value.astype(bf16)
        slope_ref[0, :, at] = (gate + value * (1.0 - gate)).astype(bf16)


def front(x, slot, row, whole, earlier, gain, decay, proj, after=()):
    rows, width = x.shape
    slots, length = whole
    value_width = proj.shape[1]
    states, groups, lanes = decay.shape
    block = min(256, rows)
    first = row // block
    begin = earlier[-1] if row else jnp.zeros((slots, *decay.shape), f32)
    anywhere = pl.BlockSpec(memory_space=pl.ANY)

    def tokens(columns):
        return pl.BlockSpec((1, block, columns), lambda b: (slot, first + b, 0))

    return pl.pallas_call(
        ignoring(functools.partial(front_body, fresh=row == 0), 5, len(earlier) + len(after)),
        grid=(rows // block,),
        in_specs=[
            pl.BlockSpec((block, width), lambda b: (b, 0)),
            pl.BlockSpec((1, width), lambda b: (0, 0)),
            pl.BlockSpec((states, groups, lanes), lambda b: (0, 0, 0)),
            pl.BlockSpec(proj.shape, lambda b: (0, 0), pipeline_mode=pl.Buffered(1)),
            pl.BlockSpec((1, states, groups, lanes), lambda b: (slot, 0, 0, 0)),
        ]
        + [anywhere] * (len(earlier) + len(after)),
        out_specs=[
            tokens(width),
            tokens(width),
            tokens(value_width),
            tokens(value_width),
            pl.BlockSpec((1, states, groups, lanes), lambda b: (slot, 0, 0, 0)),
        ],
        out_shape=[
            jax.ShapeDtypeStruct((slots, length, width), bf16),
            jax.ShapeDtypeStruct((slots, length, width), bf16),
            jax.ShapeDtypeStruct((slots, length, value_width), bf16),
            jax.ShapeDtypeStruct((slots, length, value_width), bf16),
            jax.ShapeDtypeStruct((slots, states, groups, lanes), f32),
        ],
        scratch_shapes=[pltpu.VMEM((block * groups, lanes), f32)],
        input_output_aliases={5 + k: k for k in range(len(earlier))},
        compiler_params=params(("arbitrary",)),
        name="front",
        cost_estimate=BRIEF,
    )(x, gain, decay, proj, begin, *earlier, *after)


def front_scan_body(
    table_ref,
    x_ref,
    gain_ref,
    decay_ref,
    coef_ref,
    span_ref,
    omega_ref,
    ends_own,
    ends_oth,
    proj_ref,
    affine_ref,
    smooth_ref,
    mixed_ref,
    check_ref,
    shared_ref,
    query_ref,
    key_ref,
    slab,
    out_slab,
    carry,
    ends_ref,
):
    states, groups, _ = decay_ref.shape
    count = x_ref.shape[1]
    slot = pl.program_id(0)
    slots = ends_own.shape[0]
    total = slots + ends_oth.shape[0]

    @pl.when(pl.program_id(1) == 0)
    def _():
        carry[...] = jnp.zeros_like(carry)
        ends_ref[:slots] = ends_own[...]
        ends_ref[slots:] = ends_oth[...]

        def link(i, _):
            carry[...] = span_ref[...] * carry[...] + ends_ref[table_ref[total + i]]
            return 0

        lax.fori_loop(0, table_ref[slot], link, 0)

    unit, _ = unit_rows_of(x_ref[0].astype(f32))
    normed = unit * gain_ref[...]
    to_slab(slab, normed)
    decay = [decay_ref[n] for n in range(states)]
    coef = [coef_ref[n] for n in range(states)]
    state = tuple(carry[n] for n in range(states))
    for n in range(states):
        check_ref[0, 0, n] = state[n]

    def step(t, state):
        row = slab_row(slab, t, groups)
        state = tuple(d * s + row for d, s in zip(decay, state))
        parts = [c * s for c, s in zip(coef, state)]
        while len(parts) > 1:
            parts = [a + b for a, b in zip(parts[::2], parts[1::2])]
        out_slab[pl.ds(pl.multiple_of(t * groups, groups), groups), :] = parts[0]
        return state

    state = lax.fori_loop(0, count, step, state, unroll=8)
    for n in range(states):
        carry[n] = state[n]
    smoothed = from_slab(out_slab, count, groups) + omega_ref[...] * normed
    smooth_ref[0] = smoothed
    mixed = (smoothed * jax.nn.sigmoid(smoothed)).astype(bf16)
    mixed_ref[0] = mixed
    shared_pre = jnp.dot(mixed, proj_ref[...], preferred_element_type=f32)
    shared = shared_pre * jax.nn.sigmoid(shared_pre)
    shared_ref[0] = shared_pre
    query_ref[0] = (shared * affine_ref[0:1] + affine_ref[1:2]).astype(bf16)
    key_ref[0] = (shared * affine_ref[2:3] + affine_ref[3:4]).astype(bf16)


def front_scan(table, x, gain, decay, coef, span, omega, ends, others, proj, affine, block):
    slots, length, width = x.shape
    states, groups, lanes = decay.shape
    whole3 = pl.BlockSpec((states, groups, lanes), lambda k, b, t: (0, 0, 0))
    row = pl.BlockSpec((1, width), lambda k, b, t: (0, 0))
    tokens = pl.BlockSpec((1, block, width), lambda k, b, t: (k, b, 0))
    narrow = pl.BlockSpec((1, block, proj.shape[1]), lambda k, b, t: (k, b, 0))
    return pl.pallas_call(
        front_scan_body,
        grid_spec=pltpu.PrefetchScalarGridSpec(
            num_scalar_prefetch=1,
            grid=(slots, length // block),
            in_specs=[
                tokens,
                row,
                whole3,
                whole3,
                whole3,
                row,
                pl.BlockSpec(ends.shape, lambda k, b, t: (0, 0, 0, 0)),
                pl.BlockSpec(others.shape, lambda k, b, t: (0, 0, 0, 0)),
                pl.BlockSpec(proj.shape, lambda k, b, t: (0, 0)),
                pl.BlockSpec(affine.shape, lambda k, b, t: (0, 0)),
            ],
            out_specs=[
                tokens,
                tokens,
                pl.BlockSpec((1, 1, states, groups, lanes), lambda k, b, t: (k, b, 0, 0, 0)),
                narrow,
                narrow,
                narrow,
            ],
            scratch_shapes=[
                pltpu.VMEM((block * groups, lanes), f32),
                pltpu.VMEM((block * groups, lanes), f32),
                pltpu.VMEM((states, groups, lanes), f32),
                pltpu.VMEM((ends.shape[0] + others.shape[0], states, groups, lanes), f32),
            ],
        ),
        out_shape=[
            jax.ShapeDtypeStruct((slots, length, width), f32),
            jax.ShapeDtypeStruct((slots, length, width), bf16),
            jax.ShapeDtypeStruct((slots, length // block, states, groups, lanes), f32),
            jax.ShapeDtypeStruct((slots, length, proj.shape[1]), f32),
            jax.ShapeDtypeStruct((slots, length, proj.shape[1]), bf16),
            jax.ShapeDtypeStruct((slots, length, proj.shape[1]), bf16),
        ],
        compiler_params=params(("arbitrary", "arbitrary")),
        name="front_scan",
        cost_estimate=LONG,
    )(table, x, gain, decay, coef, span, omega, ends, others, proj, affine)


def back_ends_body(gs_ref, decay_ref, end_ref, slab):
    states, groups, _ = decay_ref.shape
    slots, count, _ = gs_ref.shape

    @pl.when(pl.program_id(0) == 0)
    def _():
        end_ref[...] = jnp.zeros_like(end_ref)

    for k in range(slots):
        to_slab(slab.at[k], gs_ref[k])
    decay = [decay_ref[n] for n in range(states)]

    def step(t, state):
        rows = [slab_row(slab.at[k], count - 1 - t, groups) for k in range(slots)]
        return [tuple(d * s + row for d, s in zip(decay, held)) for row, held in zip(rows, state)]

    state = lax.fori_loop(
        0,
        count,
        step,
        [tuple(end_ref[k, n] for n in range(states)) for k in range(slots)],
        unroll=8,
    )
    for k in range(slots):
        for n in range(states):
            end_ref[k, n] = state[k][n]


def back_ends(gs, decay, block=128, after=()):
    slots, length, width = gs.shape
    states, groups, lanes = decay.shape
    block = min(block, length)
    blocks = length // block
    return pl.pallas_call(
        ignoring(back_ends_body, 2, len(after)),
        grid=(blocks,),
        in_specs=[
            pl.BlockSpec((slots, block, width), lambda b: (0, blocks - 1 - b, 0)),
            pl.BlockSpec((states, groups, lanes), lambda b: (0, 0, 0)),
        ]
        + [pl.BlockSpec(memory_space=pl.ANY)] * len(after),
        out_specs=pl.BlockSpec((slots, states, groups, lanes), lambda b: (0, 0, 0, 0)),
        out_shape=jax.ShapeDtypeStruct((slots, states, groups, lanes), f32),
        scratch_shapes=[pltpu.VMEM((slots, block * groups, lanes), f32)],
        compiler_params=params(("arbitrary",)),
        name="back_ends",
        cost_estimate=BRIEF,
    )(gs, decay, *after)


def back_scan_body(
    table_ref,
    slot_ref,
    x_ref,
    gs_ref,
    gv_ref,
    gi_ref,
    check_ref,
    gain_ref,
    decay_ref,
    coef_ref,
    span_ref,
    omega_ref,
    ends_own,
    ends_oth,
    grad_ref,
    qx_ref,
    qs_ref,
    gain_grad_ref,
    omega_grad_ref,
    slab,
    gs_slab,
    out_slab,
    history,
    carry,
    ends_ref,
):
    states, groups, _ = decay_ref.shape
    count = x_ref.shape[1]
    slot = slot_ref[0]
    slots = ends_own.shape[0]
    total = slots + ends_oth.shape[0]

    @pl.when(pl.program_id(0) == 0)
    def _():
        qx_ref[...] = jnp.zeros_like(qx_ref)
        qs_ref[...] = jnp.zeros_like(qs_ref)
        gain_grad_ref[...] = jnp.zeros_like(gain_grad_ref)
        omega_grad_ref[...] = jnp.zeros_like(omega_grad_ref)

    @pl.when(pl.program_id(0) == 0)
    def _():
        carry[...] = jnp.zeros_like(carry)
        ends_ref[:slots] = ends_own[...]
        ends_ref[slots:] = ends_oth[...]

        def link(i, _):
            carry[...] = (
                span_ref[...] * carry[...] + ends_ref[table_ref[total + total - 1 - i]]
            )
            return 0

        lax.fori_loop(0, total - 1 - table_ref[slot], link, 0)

    unit, inv = unit_rows_of(x_ref[0].astype(f32))
    normed = unit * gain_ref[...]
    gs = gs_ref[0]
    to_slab(slab, normed)
    to_slab(gs_slab, gs)
    decay = [decay_ref[n] for n in range(states)]

    def recompute(t, state):
        for n in range(states):
            history[t, n] = state[n]
        row = slab_row(slab, t, groups)
        return tuple(d * s + row for d, s in zip(decay, state))

    lax.fori_loop(
        0, count, recompute, tuple(check_ref[0, 0, n] for n in range(states)), unroll=4
    )

    half = states // 2
    for part in range(2):
        chosen = range(part * half, (part + 1) * half)
        decay = [decay_ref[n] for n in chosen]
        coef = [coef_ref[n] for n in chosen]

        def step(i, held):
            q, qx, qs = held
            t = count - 1 - i
            row = slab_row(slab, t, groups)
            g = slab_row(gs_slab, t, groups)
            q = tuple(d * a + g for d, a in zip(decay, q))
            parts = [c * a for c, a in zip(coef, q)]
            while len(parts) > 1:
                parts = [a + b for a, b in zip(parts[::2], parts[1::2])]
            spot = pl.ds(pl.multiple_of(t * groups, groups), groups)
            if part == 0:
                out_slab[spot, :] = parts[0]
            else:
                out_slab[spot, :] = out_slab[spot, :] + parts[0]
            qx = tuple(a + b * row for a, b in zip(qx, q))
            qs = tuple(a + b * history[t, n] for a, b, n in zip(qs, q, chosen))
            return q, qx, qs

        q, qx, qs = lax.fori_loop(
            0,
            count,
            step,
            (
                tuple(carry[n] for n in chosen),
                tuple(qx_ref[n] for n in chosen),
                tuple(qs_ref[n] for n in chosen),
            ),
            unroll=4,
        )
        for i, n in enumerate(chosen):
            carry[n] = q[i]
            qx_ref[n] = qx[i]
            qs_ref[n] = qs[i]

    grad_normed = (
        gv_ref[0] + from_slab(out_slab, count, groups) + omega_ref[...] * gs
    )
    gain_grad_ref[...] += jnp.sum(grad_normed * unit, axis=0, keepdims=True)
    omega_grad_ref[...] += jnp.sum(gs * normed, axis=0, keepdims=True)
    grad_ref[...] = (
        gi_ref[0] + norm_back_rows(grad_normed, gain_ref[...], unit, inv)
    ).astype(bf16)


def back_scan(table, slot, x, gs, gv, gi, check, gain, decay, coef, span, omega, ends, others, after=()):
    _, length, width = x.shape
    states, groups, lanes = decay.shape
    blocks = check.shape[1]
    block = length // blocks
    whole3 = pl.BlockSpec((states, groups, lanes), lambda b, t, u: (0, 0, 0))
    row = pl.BlockSpec((1, width), lambda b, t, u: (0, 0))
    tokens = pl.BlockSpec((1, block, width), lambda b, t, u: (slot, blocks - 1 - b, 0))
    return pl.pallas_call(
        ignoring(back_scan_body, 14, len(after)),
        grid_spec=pltpu.PrefetchScalarGridSpec(
            num_scalar_prefetch=2,
            grid=(blocks,),
            in_specs=[
                tokens,
                tokens,
                tokens,
                tokens,
                pl.BlockSpec(
                    (1, 1, states, groups, lanes),
                    lambda b, t, u: (slot, blocks - 1 - b, 0, 0, 0),
                ),
                row,
                whole3,
                whole3,
                whole3,
                row,
                pl.BlockSpec(ends.shape, lambda b, t, u: (0, 0, 0, 0)),
                pl.BlockSpec(others.shape, lambda b, t, u: (0, 0, 0, 0)),
            ]
            + [pl.BlockSpec(memory_space=pl.ANY)] * len(after),
            out_specs=[
                pl.BlockSpec((block, width), lambda b, t, u: (blocks - 1 - b, 0)),
                whole3,
                whole3,
                row,
                row,
            ],
            scratch_shapes=[
                pltpu.VMEM((block * groups, lanes), f32),
                pltpu.VMEM((block * groups, lanes), f32),
                pltpu.VMEM((block * groups, lanes), f32),
                pltpu.VMEM((block, states, groups, lanes), f32),
                pltpu.VMEM((states, groups, lanes), f32),
                pltpu.VMEM((ends.shape[0] + others.shape[0], states, groups, lanes), f32),
            ],
        ),
        out_shape=[
            jax.ShapeDtypeStruct((length, width), bf16),
            jax.ShapeDtypeStruct((states, groups, lanes), f32),
            jax.ShapeDtypeStruct((states, groups, lanes), f32),
            jax.ShapeDtypeStruct((1, width), f32),
            jax.ShapeDtypeStruct((1, width), f32),
        ],
        compiler_params=params(("arbitrary",)),
        name="back_scan",
        cost_estimate=LONG,
    )(table, jnp.full((1,), slot, jnp.int32), x, gs, gv, gi, check, gain, decay, coef, span, omega, ends, others, *after)


def chunk_copies(table_ref, own, others, kept, total, length, sem):
    copies = []
    for slot in range(total):
        place = pl.ds(pl.multiple_of(table_ref[slot] * length, length), length)
        source = own.at[slot] if slot < 2 else others.at[slot - 2]
        copies.append(pltpu.make_async_copy(source, kept.at[place, :], sem.at[slot]))
    return copies


def attend_body(
    table_ref,
    q_ref,
    bias_ref,
    reset_ref,
    k_own,
    k_oth,
    v_own,
    v_oth,
    out_ref,
    gated_ref,
    lse_ref,
    keys,
    values,
    scores,
    probs,
    key_sem,
    value_sem,
    *,
    total,
):
    length, key_width = q_ref.shape[1:]
    value_width = values.shape[1]
    tiles = length // TILE
    scale = float(key_width) ** (-0.5)

    key_copies = chunk_copies(table_ref, k_own, k_oth, keys, total, length, key_sem)
    value_copies = chunk_copies(table_ref, v_own, v_oth, values, total, length, value_sem)

    @pl.when(pl.program_id(0) == 0)
    def _():
        for copy in key_copies + value_copies:
            copy.start()
        for copy in key_copies:
            copy.wait()

    chunk = table_ref[pl.program_id(0)]
    reach = jnp.where(table_ref[2 * total] == 1, chunk + 1, 1)
    base = (chunk + 1 - reach) * length
    queries = q_ref[0]

    def first(kc, peak):
        spot = pl.ds(pl.multiple_of(base + kc * length, length), length)
        tile = (
            lax.dot_general(
                queries, keys[spot, :], (((1,), (1,)), ((), ())), preferred_element_type=f32
            )
            * scale
        )
        for r in range(tiles):
            for a in range(tiles):
                rows = slice(r * TILE, (r + 1) * TILE)
                cols = slice(a * TILE, (a + 1) * TILE)
                gap = (reach - 1 - kc) * tiles + r - a + tiles - 1
                scores[kc, rows, cols] = tile[rows, cols] + bias_ref[gap]
        return jnp.maximum(peak, jnp.max(scores[kc], axis=1, keepdims=True))

    peak = lax.fori_loop(0, reach, first, jnp.full((length, 1), 2 * MASKED, f32))

    def second(kc, sums):
        terms = jnp.exp(scores[kc] - peak)
        probs[:, pl.ds(pl.multiple_of(kc * length, length), length)] = terms.astype(bf16)
        return sums + jnp.sum(terms, axis=1, keepdims=True)

    sums = lax.fori_loop(0, reach, second, jnp.zeros((length, 1), f32))
    lse_ref[0] = jnp.broadcast_to(peak + jnp.log(sums), (length, 128)).T[:1]
    inverse = 1.0 / sums

    @pl.when(pl.program_id(0) == 0)
    def _():
        for copy in value_copies:
            copy.wait()

    for count in range(1, total + 1):

        @pl.when(reach == count)
        def _(count=count):
            width = count * length
            span = pl.ds(pl.multiple_of(base, length), width)

            def column(ct, _):
                at = pl.ds(pl.multiple_of(ct * 1024, 1024), 1024)
                rows = (
                    jnp.dot(probs[:, :width], values[span, at], preferred_element_type=f32)
                    * inverse
                )
                out_ref[0, :, at] = rows.astype(bf16)
                gate = reset_ref[0, :, at].astype(f32)
                gated_ref[0, :, at] = (gate * jax.nn.sigmoid(gate) * rows).astype(bf16)
                return 0

            lax.fori_loop(0, value_width // 1024, column, 0)


def attend(table, q, bias, reset, k_own, k_oth, v_own, v_oth):
    slots, length, key_width = q.shape
    value_width = v_own.shape[2]
    total = slots + k_oth.shape[0]
    anywhere = pl.BlockSpec(memory_space=pl.ANY)
    tokens = pl.BlockSpec((1, length, value_width), lambda k, t: (k, 0, 0))
    return pl.pallas_call(
        functools.partial(attend_body, total=total),
        grid_spec=pltpu.PrefetchScalarGridSpec(
            num_scalar_prefetch=1,
            grid=(slots,),
            in_specs=[
                pl.BlockSpec((1, length, key_width), lambda k, t: (k, 0, 0)),
                pl.BlockSpec(bias.shape, lambda k, t: (0, 0, 0)),
                tokens,
                anywhere,
                anywhere,
                anywhere,
                anywhere,
            ],
            out_specs=[
                tokens,
                tokens,
                pl.BlockSpec((1, 1, length), lambda k, t: (k, 0, 0)),
            ],
            scratch_shapes=[
                pltpu.VMEM((total * length, key_width), bf16),
                pltpu.VMEM((total * length, value_width), bf16),
                pltpu.VMEM((total, length, length), f32),
                pltpu.VMEM((length, total * length), bf16),
                pltpu.SemaphoreType.DMA((total,)),
                pltpu.SemaphoreType.DMA((total,)),
            ],
        ),
        out_shape=[
            jax.ShapeDtypeStruct((slots, length, value_width), bf16),
            jax.ShapeDtypeStruct((slots, length, value_width), bf16),
            jax.ShapeDtypeStruct((slots, 1, length), f32),
        ],
        compiler_params=params(("arbitrary",)),
        name="attend",
        cost_estimate=BRIEF,
    )(table, q, bias, reset, k_own, k_oth, v_own, v_oth)


def attend_back_body(
    table_ref,
    q_ref,
    grad_ref,
    lse_ref,
    bias_ref,
    k_own,
    k_oth,
    v_own,
    v_oth,
    gq_ref,
    gk_own,
    gv_own,
    both_oth,
    rel_out,
    keys,
    values,
    gk_sum,
    gv_sum,
    probs_kept,
    grads_kept,
    rel_ref,
    key_sem,
    value_sem,
    *,
    total,
):
    length, key_width = q_ref.shape[1:]
    value_width = values.shape[1]
    tiles = length // TILE
    scale = float(key_width) ** (-0.5)
    step = pl.program_id(0)
    nt = (((1,), (1,)), ((), ()))
    tn = (((0,), (0,)), ((), ()))

    copies = chunk_copies(
        table_ref, k_own, k_oth, keys, total, length, key_sem
    ) + chunk_copies(table_ref, v_own, v_oth, values, total, length, value_sem)

    @pl.when(step == 0)
    def _():
        for copy in copies:
            copy.start()
        gk_sum[...] = jnp.zeros_like(gk_sum)
        gv_sum[...] = jnp.zeros_like(gv_sum)
        rel_ref[...] = jnp.zeros_like(rel_ref)
        for copy in copies:
            copy.wait()

    chunk = table_ref[step]
    reach = jnp.where(table_ref[2 * total] == 1, chunk + 1, 1)
    base = (chunk + 1 - reach) * length
    queries = q_ref[0]
    log_total = lse_ref[0]

    def gap_of(kc, a, r):
        return (reach - 1 - kc) * tiles + r - a + tiles - 1

    def first(kc, delta):
        spot = pl.ds(pl.multiple_of(base + kc * length, length), length)
        grads_kept[kc] = lax.dot_general(
            values[spot, :], grad_ref[0], nt, preferred_element_type=f32
        )
        tile = (
            lax.dot_general(keys[spot, :], queries, nt, preferred_element_type=f32) * scale
        )
        for a in range(tiles):
            for r in range(tiles):
                rows = slice(a * TILE, (a + 1) * TILE)
                cols = slice(r * TILE, (r + 1) * TILE)
                probs_kept[kc, rows, cols] = jnp.exp(
                    tile[rows, cols] + bias_ref[gap_of(kc, a, r)] - log_total[:, cols]
                )
        return delta + jnp.sum(probs_kept[kc] * grads_kept[kc], axis=0, keepdims=True)

    delta = lax.fori_loop(0, reach, first, jnp.zeros((1, length), f32))

    def second(kc, grad_query):
        spot = pl.ds(pl.multiple_of(base + kc * length, length), length)
        probs = probs_kept[kc]
        grad_scores = (probs * (grads_kept[kc] - delta)).astype(bf16)
        probs = probs.astype(bf16)
        for a in range(tiles):
            for r in range(tiles):
                rel_ref[gap_of(kc, a, r)] += grad_scores[
                    a * TILE : (a + 1) * TILE, r * TILE : (r + 1) * TILE
                ].astype(f32)
        gk_sum[spot, :] += jnp.dot(grad_scores, queries, preferred_element_type=f32)

        def column(ct, _):
            at = pl.ds(pl.multiple_of(ct * 1024, 1024), 1024)
            gv_sum[spot, at] += jnp.dot(
                probs, grad_ref[0, :, at], preferred_element_type=f32
            )
            return 0

        lax.fori_loop(0, value_width // 1024, column, 0)
        return grad_query + lax.dot_general(
            grad_scores, keys[spot, :], tn, preferred_element_type=f32
        )

    grad_query = lax.fori_loop(0, reach, second, jnp.zeros((length, key_width), f32))
    gq_ref[0] = grad_query * scale

    @pl.when(step == pl.num_programs(0) - 1)
    def _():
        for slot in range(total):
            place = pl.ds(pl.multiple_of(table_ref[slot] * length, length), length)
            key_grad = (gk_sum[place, :] * scale).astype(bf16)
            value_grad = gv_sum[place, :].astype(bf16)
            if slot < 2:
                gk_own[slot] = key_grad
                gv_own[slot] = value_grad
            else:
                both_oth[slot - 2, :, :value_width] = value_grad
                both_oth[slot - 2, :, value_width:] = key_grad
        down = lax.broadcasted_iota(jnp.int32, (TILE, TILE), 0)
        across = lax.broadcasted_iota(jnp.int32, (TILE, TILE), 1)
        mirror = jnp.where(down + across == TILE - 1, 1.0, 0.0)
        for d in range(rel_out.shape[0]):
            flipped = jnp.dot(
                rel_ref[d + tiles - 1],
                mirror,
                precision=lax.Precision.HIGHEST,
                preferred_element_type=f32,
            )
            wide = jnp.concatenate([flipped, jnp.zeros((TILE, TILE), f32)], axis=1)
            turned = pltpu.roll(wide, 0, 1, stride=1, stride_axis=0)
            rel_out[d] = jnp.sum(turned, axis=0, keepdims=True)


def attend_back(table, q, grads, lse, bias, k_own, k_oth, v_own, v_oth, after=()):
    slots, length, key_width = q.shape
    value_width = v_own.shape[2]
    total = slots + k_oth.shape[0]
    rel_shape = (total * length // TILE, 1, 2 * TILE)
    both_shape = (k_oth.shape[0], length, key_width + value_width)
    anywhere = pl.BlockSpec(memory_space=pl.ANY)

    def all_of(shape):
        return pl.BlockSpec(
            shape, lambda k, t: (0,) * len(shape), pipeline_mode=pl.Buffered(1)
        )

    return pl.pallas_call(
        ignoring(functools.partial(attend_back_body, total=total), 9, len(after)),
        grid_spec=pltpu.PrefetchScalarGridSpec(
            num_scalar_prefetch=1,
            grid=(slots,),
            in_specs=[
                pl.BlockSpec((1, length, key_width), lambda k, t: (k, 0, 0)),
                pl.BlockSpec((1, length, value_width), lambda k, t: (k, 0, 0)),
                pl.BlockSpec((1, 1, length), lambda k, t: (k, 0, 0)),
                all_of(bias.shape),
                anywhere,
                anywhere,
                anywhere,
                anywhere,
            ]
            + [anywhere] * len(after),
            out_specs=[
                pl.BlockSpec((1, length, key_width), lambda k, t: (k, 0, 0)),
                all_of(k_own.shape),
                all_of(v_own.shape),
                all_of(both_shape),
                all_of(rel_shape),
            ],
            scratch_shapes=[
                pltpu.VMEM((total * length, key_width), bf16),
                pltpu.VMEM((total * length, value_width), bf16),
                pltpu.VMEM((total * length, key_width), f32),
                pltpu.VMEM((total * length, value_width), f32),
                pltpu.VMEM((total, length, length), f32),
                pltpu.VMEM((total, length, length), f32),
                pltpu.VMEM(bias.shape, f32),
                pltpu.SemaphoreType.DMA((total,)),
                pltpu.SemaphoreType.DMA((total,)),
            ],
        ),
        out_shape=[
            jax.ShapeDtypeStruct((slots, length, key_width), f32),
            jax.ShapeDtypeStruct(k_own.shape, bf16),
            jax.ShapeDtypeStruct(v_own.shape, bf16),
            jax.ShapeDtypeStruct(both_shape, bf16),
            jax.ShapeDtypeStruct(rel_shape, f32),
        ],
        compiler_params=params(("arbitrary",)),
        name="attend_back",
        cost_estimate=LONG,
    )(table, q, grads, lse, bias, k_own, k_oth, v_own, v_oth, *after)


def bias_body(flag_ref, back_row, front_row, back_ref, front_ref, *, spare):
    tile = pl.program_id(0) - spare
    full = flag_ref[0] == 1

    @pl.when(tile < 0)
    def _():
        back_ref[...] = jnp.full_like(back_ref, MASKED)
        front_ref[...] = jnp.full_like(front_ref, MASKED)

    @pl.when(tile >= 0)
    def _():
        down = lax.broadcasted_iota(jnp.int32, (TILE, TILE), 0)
        across = lax.broadcasted_iota(jnp.int32, (TILE, TILE), 1)
        near = jnp.where(down // STRETCH == across // STRETCH, 1, 0)
        for row, out, ordered in (
            (back_row, back_ref, jnp.where(down <= across, 1, 0)),
            (front_row, front_ref, jnp.where(across <= down, 1, 0)),
        ):
            wide = jnp.broadcast_to(row[0], (TILE, 2 * TILE))
            turned = pltpu.roll(wide, 0, 1, stride=1, stride_axis=0)[:, :TILE]
            allowed = jnp.where(
                tile == 0, jnp.where(full, ordered, ordered * near), jnp.where(full, 1, 0)
            )
            out[0] = jnp.where(allowed == 1, turned, MASKED)


def bias_tiles(relative_bias, spare, full):
    length = relative_bias.shape[0] // 2
    count = length // TILE
    windows = jnp.stack(
        [
            lax.slice_in_dim(relative_bias, length - d * TILE - TILE, length - d * TILE + TILE)
            for d in range(count)
        ]
    )
    front = jnp.concatenate([windows[:, TILE:], windows[:, :TILE]], axis=1)
    back = jnp.concatenate([windows[:, TILE:TILE + 1], windows[:, ::-1][:, TILE:], windows[:, ::-1][:, : TILE - 1]], axis=1)
    row = pl.BlockSpec((1, 1, 2 * TILE), lambda d, t: (jnp.maximum(d - spare, 0), 0, 0))
    out = pl.BlockSpec((1, TILE, TILE), lambda d, t: (d, 0, 0))
    shape = jax.ShapeDtypeStruct((spare + count, TILE, TILE), f32)
    return pl.pallas_call(
        functools.partial(bias_body, spare=spare),
        grid_spec=pltpu.PrefetchScalarGridSpec(
            num_scalar_prefetch=1,
            grid=(spare + count,),
            in_specs=[row, row],
            out_specs=[out, out],
        ),
        out_shape=[shape, shape],
        compiler_params=params(("arbitrary",)),
        name="bias",
    )(full.astype(jnp.int32)[None], back[:, None], front[:, None])


def bias_grad(sums, length):
    count = sums.shape[0]
    shifted = jnp.concatenate([jnp.zeros((count, 1), f32), sums[:, :-1]], axis=1)
    none = jnp.zeros((1, TILE), f32)
    blocks = jnp.concatenate([none, shifted[:, :TILE]]) + jnp.concatenate(
        [shifted[:, TILE:], none]
    )
    return jnp.concatenate(
        [blocks[::-1].reshape(-1), jnp.zeros((2 * length - (count + 1) * TILE,), f32)]
    )


def candidate_body(
    gated_ref, proj_ref, pre_ref, update_ref, x_ref, gain_ref, cand_ref, first_ref, low_ref
):
    cand_in = pre_ref[...].astype(f32) + jnp.dot(
        gated_ref[...], proj_ref[...], preferred_element_type=f32
    )
    cand_ref[...] = cand_in
    x = x_ref[...].astype(f32)
    update = jax.nn.sigmoid(update_ref[...].astype(f32))
    first = x + update * (cand_in * jax.nn.sigmoid(cand_in) - x)
    first_ref[...] = first
    unit, _ = unit_rows_of(first)
    low_ref[...] = (unit * gain_ref[...]).astype(bf16)


def candidate(gated, proj, base, x, gain):
    tokens, width = x.shape
    value_width = gated.shape[1]
    rows = min(256, tokens)
    wide = value_width // width

    def block(columns, at=0):
        return pl.BlockSpec((rows, columns), lambda i: (i, at))

    return pl.pallas_call(
        candidate_body,
        grid=(tokens // rows,),
        in_specs=[
            block(value_width),
            pl.BlockSpec(proj.shape, lambda i: (0, 0), pipeline_mode=pl.Buffered(1)),
            block(width, wide + 1),
            block(width, wide),
            block(width),
            pl.BlockSpec((1, width), lambda i: (0, 0)),
        ],
        out_specs=[block(width)] * 3,
        out_shape=[
            jax.ShapeDtypeStruct((tokens, width), f32),
            jax.ShapeDtypeStruct((tokens, width), f32),
            jax.ShapeDtypeStruct((tokens, width), bf16),
        ],
        compiler_params=params(("arbitrary",)),
        name="candidate",
        cost_estimate=BRIEF,
    )(gated, proj, base, base, x, gain)


def gate_body(
    back_ref,
    cot_a,
    cot_b,
    x_ref,
    cand_ref,
    update_ref,
    reset_ref,
    attended_ref,
    gain_ref,
    proj_ref,
    input_ref,
    main_ref,
    grad_att_ref,
    gain_grad_ref,
):
    width = x_ref.shape[1]
    value_width = proj_ref.shape[0]

    @pl.when(pl.program_id(0) == 0)
    def _():
        gain_grad_ref[...] = jnp.zeros_like(gain_grad_ref)

    x = x_ref[...].astype(f32)
    cand_in = cand_ref[...]
    gate = jax.nn.sigmoid(cand_in)
    candidate = cand_in * gate
    update = jax.nn.sigmoid(update_ref[...].astype(f32))
    change = candidate - x
    unit, inv = unit_rows_of(x + update * change)
    grad_feed = back_ref[...]
    gain_grad_ref[...] += jnp.sum(grad_feed * unit, axis=0, keepdims=True)
    early = pl.program_id(0) < pl.num_programs(0) // 2
    cot = jnp.where(early, cot_a[...].astype(f32), cot_b[...].astype(f32))
    grad_first = cot + norm_back_rows(
        grad_feed, gain_ref[...], unit, inv
    )
    kept = grad_first * (1.0 - update)
    input_ref[...] = kept
    main_ref[:, value_width : value_width + width] = (kept * change * update).astype(bf16)
    grad_cand = (grad_first * update * (gate + candidate * (1.0 - gate))).astype(bf16)
    main_ref[:, value_width + width :] = grad_cand
    for c in range(value_width // 512):
        at = slice(c * 512, (c + 1) * 512)
        grad_gated = mm_nt(grad_cand, proj_ref[at, :])
        reset = reset_ref[:, at].astype(f32)
        open_gate = jax.nn.sigmoid(reset)
        passed = reset * open_gate
        grad_att_ref[:, at] = (grad_gated * passed).astype(bf16)
        main_ref[:, at] = (
            grad_gated
            * attended_ref[:, at].astype(f32)
            * (open_gate + passed * (1.0 - open_gate))
        ).astype(bf16)


def gate(back, cots, x, cand_in, base, attended, gain, proj, after=()):
    tokens, width = x.shape
    value_width = proj.shape[0]
    rows = min(256, tokens // 2)
    half = tokens // rows // 2
    wide = value_width // width

    def block(columns, at=0):
        return pl.BlockSpec((rows, columns), lambda i: (i, at))

    return pl.pallas_call(
        ignoring(gate_body, 10, len(after)),
        grid=(tokens // rows,),
        in_specs=[
            block(width),
            pl.BlockSpec((rows, width), lambda i: (jnp.minimum(i, half - 1), 0)),
            pl.BlockSpec((rows, width), lambda i: (jnp.maximum(i - half, 0), 0)),
            block(width),
            block(width),
            block(width, wide),
            block(value_width),
            block(value_width),
            pl.BlockSpec((1, width), lambda i: (0, 0)),
            pl.BlockSpec(proj.shape, lambda i: (0, 0), pipeline_mode=pl.Buffered(1)),
        ]
        + [pl.BlockSpec(memory_space=pl.ANY)] * len(after),
        out_specs=[
            block(width),
            block(value_width + 2 * width),
            block(value_width),
            pl.BlockSpec((1, width), lambda i: (0, 0)),
        ],
        out_shape=[
            jax.ShapeDtypeStruct((tokens, width), f32),
            jax.ShapeDtypeStruct((tokens, value_width + 2 * width), bf16),
            jax.ShapeDtypeStruct((tokens, value_width), bf16),
            jax.ShapeDtypeStruct((1, width), f32),
        ],
        compiler_params=params(("arbitrary",)),
        name="gate",
        cost_estimate=LONG,
    )(back, *cots, x, cand_in, base, base, attended, gain, proj, *after)


def ordered_transpose(ids_ref, source, plain, ordered):
    plain[...] = source[...].T
    count = ids_ref.shape[0]
    rows = plain.shape[0] // count

    def place(p, _):
        ordered[pl.ds(pl.multiple_of(p * rows, rows), rows), :] = plain[
            pl.ds(pl.multiple_of(ids_ref[p] * rows, rows), rows), :
        ]
        return 0

    lax.fori_loop(0, count, place, 0)


def placed_transpose(places_ref, sources, plain, ordered):
    start = 0
    for source in sources:
        plain[:, start : start + source.shape[0]] = source[...].T
        start += source.shape[0]
    count = places_ref.shape[0]
    rows = plain.shape[0] // count

    def place(q, _):
        ordered[pl.ds(pl.multiple_of(places_ref[q] * rows, rows), rows), :] = plain[
            pl.ds(pl.multiple_of(q * rows, rows), rows), :
        ]
        return 0

    lax.fori_loop(0, count, place, 0)


def feed_body(
    ids_ref,
    places_ref,
    low_ref,
    cot_a,
    cot_b,
    first_ref,
    in_ref,
    out_ref,
    result_a,
    result_b,
    back_ref,
    out_send,
    out_keep,
    in_send,
    in_keep,
    total,
    cot_turned,
    low_turned,
    plain,
):
    step = pl.program_id(0)
    half = pl.num_programs(0) // 2
    tokens = low_ref.shape[0]
    middle = tokens // 2
    nt = (((1,), (1,)), ((), ()))

    @pl.when(step == 0)
    def _():
        placed_transpose(places_ref, (cot_a, cot_b), plain, cot_turned)
        ordered_transpose(ids_ref, low_ref, plain, low_turned)
        total[...] = first_ref[...]
        back_ref[...] = jnp.zeros_like(back_ref)

    acts, grads = [], []
    for r, cot_ref in enumerate((cot_a, cot_b)):
        at = slice(r * middle, (r + 1) * middle)
        hidden = jnp.dot(low_ref[at, :], in_ref[...], preferred_element_type=f32)
        grad_act = lax.dot_general(
            cot_ref[...], out_ref[...], nt, preferred_element_type=f32
        )
        gate = jax.nn.sigmoid(hidden)
        act = hidden * gate
        grad = (grad_act * (gate + act * (1.0 - gate))).astype(bf16)
        act = act.astype(bf16)
        total[at, :] += jnp.dot(act, out_ref[...], preferred_element_type=f32)
        back_ref[at, :] += lax.dot_general(
            grad, in_ref[...], nt, preferred_element_type=f32
        )
        acts.append(act)
        grads.append(grad)
    out_grad = jnp.dot(
        cot_turned[...], jnp.concatenate(acts), preferred_element_type=f32
    ).astype(bf16)
    in_grad = jnp.dot(
        low_turned[...], jnp.concatenate(grads), preferred_element_type=f32
    ).astype(bf16)
    split = in_grad.shape[0] // 2
    in_send[...] = in_grad[:split].reshape(in_send.shape)
    in_keep[...] = in_grad[split:].reshape(in_keep.shape)

    @pl.when(step < half)
    def _():
        out_send[0] = out_grad

    @pl.when(step >= half)
    def _():
        out_keep[0] = out_grad

    @pl.when(step == pl.num_programs(0) - 1)
    def _():
        result_a[...] = total[:middle, :].astype(bf16)
        result_b[...] = total[middle:, :].astype(bf16)


def feed(ids, places, low, cots, first_sum, feed_in, feed_out, seq, after=()):
    tokens, width = low.shape
    features = feed_in.shape[1]
    parts = ids.shape[0]
    half = parts // 2
    columns = features // parts
    rows = width // parts
    share = parts // seq
    anywhere = pl.BlockSpec(memory_space=pl.ANY)

    def all_of(shape):
        return pl.BlockSpec(
            shape, lambda i, t, u: (0,) * len(shape), pipeline_mode=pl.Buffered(1)
        )

    def at(i, t):
        return t[jnp.minimum(i, parts - 1)]

    split = pl.BlockSpec(
        (half, 1, 1, rows, columns),
        lambda i, t, u: (0, u[at(i, t) // share], at(i, t) % share, 0, 0),
    )
    return pl.pallas_call(
        ignoring(feed_body, 8, len(after)),
        grid_spec=pltpu.PrefetchScalarGridSpec(
            num_scalar_prefetch=2,
            grid=(parts,),
            in_specs=[
                all_of(low.shape),
                all_of(cots[0].shape),
                all_of(cots[1].shape),
                all_of(first_sum.shape),
                pl.BlockSpec((width, columns), lambda i, t, u: (0, at(i, t))),
                pl.BlockSpec((columns, width), lambda i, t, u: (at(i, t), 0)),
            ]
            + [anywhere] * len(after),
            out_specs=[
                all_of(cots[0].shape),
                all_of(cots[1].shape),
                all_of(low.shape),
                pl.BlockSpec(
                    (1, width, columns), lambda i, t, u: (jnp.minimum(i, half - 1), 0, 0)
                ),
                pl.BlockSpec(
                    (1, width, columns), lambda i, t, u: (jnp.maximum(i - half, 0), 0, 0)
                ),
                split,
                split,
            ],
            scratch_shapes=[
                pltpu.VMEM((tokens, width), f32),
                pltpu.VMEM((width, tokens), bf16),
                pltpu.VMEM((width, tokens), bf16),
                pltpu.VMEM((width, tokens), bf16),
            ],
        ),
        out_shape=[
            jax.ShapeDtypeStruct(cots[0].shape, bf16),
            jax.ShapeDtypeStruct(cots[1].shape, bf16),
            jax.ShapeDtypeStruct((tokens, width), f32),
            jax.ShapeDtypeStruct((half, width, columns), bf16),
            jax.ShapeDtypeStruct((half, width, columns), bf16),
            jax.ShapeDtypeStruct((half, seq, share, rows, columns), bf16),
            jax.ShapeDtypeStruct((half, seq, share, rows, columns), bf16),
        ],
        compiler_params=params(("arbitrary",)),
        name="feed",
        cost_estimate=BRIEF,
    )(ids, places, low, *cots, first_sum, feed_in, feed_out, *after)


def product_body(left_ref, right_ref, out_ref):
    out_ref[...] = jnp.dot(
        left_ref[...], right_ref[...], preferred_element_type=f32
    ).astype(out_ref.dtype)


def product(left, right, tile=1024):
    tokens, depth = left.shape
    columns = right.shape[1]
    return pl.pallas_call(
        product_body,
        grid=(columns // tile,),
        in_specs=[
            pl.BlockSpec(left.shape, lambda i: (0, 0), pipeline_mode=pl.Buffered(1)),
            pl.BlockSpec((depth, tile), lambda i: (0, i)),
        ],
        out_specs=pl.BlockSpec((tokens, tile), lambda i: (0, i)),
        out_shape=jax.ShapeDtypeStruct((tokens, columns), bf16),
        compiler_params=params(("arbitrary",)),
        name="product",
        cost_estimate=BRIEF,
    )(left, right)


def smooth_back_body(
    main_ref, shared_ref, weight_ref, shared_weight_ref, smooth_ref, out_ref, total
):
    step = pl.program_id(0)

    @pl.when(step == 0)
    def _():
        total[...] = mm_nt(shared_ref[...], shared_weight_ref[...])

    total[...] += mm_nt(main_ref[...], weight_ref[...])

    @pl.when(step == pl.num_programs(0) - 1)
    def _():
        out_ref[...] = total[...] * silu_slope(smooth_ref[...])


def smooth_back(main, shared, weight, shared_weight, smoothed, after=()):
    tokens, width = smoothed.shape
    tile = 1024

    def all_of(shape):
        return pl.BlockSpec(shape, lambda i: (0, 0), pipeline_mode=pl.Buffered(1))

    return pl.pallas_call(
        ignoring(smooth_back_body, 5, len(after)),
        grid=(main.shape[1] // tile,),
        in_specs=[
            pl.BlockSpec((tokens, tile), lambda i: (0, i)),
            all_of(shared.shape),
            pl.BlockSpec((width, tile), lambda i: (0, i)),
            all_of(shared_weight.shape),
            all_of(smoothed.shape),
        ]
        + [pl.BlockSpec(memory_space=pl.ANY)] * len(after),
        out_specs=all_of(smoothed.shape),
        out_shape=jax.ShapeDtypeStruct(smoothed.shape, f32),
        scratch_shapes=[pltpu.VMEM(smoothed.shape, f32)],
        compiler_params=params(("arbitrary",)),
        name="smooth_back",
        cost_estimate=LONG,
    )(main, shared, weight, shared_weight, smoothed, *after)


def by_columns_body(ids_ref, places_ref, left_ref, right_ref, send, keep, plain, turned):
    step = pl.program_id(0)
    half = pl.num_programs(0) // 2

    @pl.when(step == 0)
    def _():
        placed_transpose(places_ref, (left_ref,), plain, turned)

    grad = jnp.dot(turned[...], right_ref[...], preferred_element_type=f32).astype(bf16)

    @pl.when(step < half)
    def _():
        send[0] = grad

    @pl.when(step >= half)
    def _():
        keep[0] = grad


def by_columns(ids, places, left, right, after=(), rows=None, at=0):
    tokens = left.shape[0]
    rows = rows or left.shape[1]
    parts = ids.shape[0]
    half = parts // 2
    columns = right.shape[1] // parts
    shape = jax.ShapeDtypeStruct((half, rows, columns), bf16)
    if columns % 128:
        left = left[:, at * rows : (at + 1) * rows]
        grad = mm_tn(left, right).astype(bf16).reshape(rows, parts, columns)
        grad = jnp.take(grad, ids, axis=1).transpose(1, 0, 2)
        grad = grad.reshape(parts, places.shape[0], -1, columns)
        grad = jnp.take(grad, jnp.argsort(places), axis=1).reshape(parts, rows, columns)
        return grad[:half], grad[half:]
    return pl.pallas_call(
        ignoring(by_columns_body, 4, len(after)),
        grid_spec=pltpu.PrefetchScalarGridSpec(
            num_scalar_prefetch=2,
            grid=(parts,),
            in_specs=[
                pl.BlockSpec(
                    (tokens, rows), lambda i, t, u: (0, at), pipeline_mode=pl.Buffered(1)
                ),
                pl.BlockSpec((tokens, columns), lambda i, t, u: (0, t[jnp.minimum(i, parts - 1)])),
            ]
            + [pl.BlockSpec(memory_space=pl.ANY)] * len(after),
            out_specs=[
                pl.BlockSpec(
                    (1, rows, columns), lambda i, t, u: (jnp.minimum(i, half - 1), 0, 0)
                ),
                pl.BlockSpec(
                    (1, rows, columns), lambda i, t, u: (jnp.maximum(i - half, 0), 0, 0)
                ),
            ],
            scratch_shapes=[
                pltpu.VMEM((rows, tokens), bf16),
                pltpu.VMEM((rows, tokens), bf16),
            ],
        ),
        out_shape=[shape, shape],
        compiler_params=params(("arbitrary",)),
        name="by_columns",
        cost_estimate=BRIEF,
    )(ids, places, left, right, *after)


def by_rows_body(ids_ref, places_ref, left_ref, right_ref, send, keep, plain, turned):
    @pl.when(pl.program_id(0) == 0)
    def _():
        ordered_transpose(ids_ref, left_ref, plain, turned)

    grad = jnp.dot(turned[...], right_ref[...], preferred_element_type=f32).astype(bf16)
    middle = grad.shape[0] // 2
    send[...] = grad[:middle].reshape(send.shape)
    keep[...] = grad[middle:].reshape(keep.shape)


def by_rows(ids, places, left, right, seq=1, after=(), cost=BRIEF):
    tokens, rows = left.shape
    parts = ids.shape[0]
    half = parts // 2
    if places is None:
        seq, places = 1, jnp.zeros((1,), jnp.int32)
    columns = right.shape[1] // seq
    tile = min(512, columns)
    share = columns // tile
    shape = jax.ShapeDtypeStruct((half, seq, rows // parts, columns), bf16)
    split = pl.BlockSpec(
        (half, 1, rows // parts, tile), lambda i, t, u: (0, u[jnp.minimum(i // share, seq - 1)], 0, i % share)
    )
    return pl.pallas_call(
        ignoring(by_rows_body, 4, len(after)),
        grid_spec=pltpu.PrefetchScalarGridSpec(
            num_scalar_prefetch=2,
            grid=(seq * share,),
            in_specs=[
                pl.BlockSpec(
                    left.shape, lambda i, t, u: (0, 0), pipeline_mode=pl.Buffered(1)
                ),
                pl.BlockSpec((tokens, tile), lambda i, t, u: (0, i)),
            ]
            + [pl.BlockSpec(memory_space=pl.ANY)] * len(after),
            out_specs=[split, split],
            scratch_shapes=[
                pltpu.VMEM((rows, tokens), bf16),
                pltpu.VMEM((rows, tokens), bf16),
            ],
        ),
        out_shape=[shape, shape],
        compiler_params=params(("arbitrary",)),
        name="by_rows",
        cost_estimate=cost,
    )(ids, places, left, right, *after)


def value_back_body(
    ids_ref,
    places_ref,
    left_ref,
    own_ref,
    other_ref,
    slope_ref,
    proj_ref,
    total_ref,
    send,
    keep,
    plain,
    turned,
):
    @pl.when(pl.program_id(0) == 0)
    def _():
        total_ref[...] = jnp.zeros_like(total_ref)
        ordered_transpose(ids_ref, left_ref, plain, turned)

    grad = own_ref[...].astype(f32)
    for k in range(other_ref.shape[0]):
        grad = grad + other_ref[k].astype(f32)
    grad = (grad * slope_ref[...].astype(f32)).astype(bf16)
    total_ref[...] += mm_nt(grad, proj_ref[...])
    weights = jnp.dot(turned[...], grad, preferred_element_type=f32).astype(bf16)
    middle = weights.shape[0] // 2
    send[...] = weights[:middle].reshape(send.shape)
    keep[...] = weights[middle:].reshape(keep.shape)


def value_back(ids, places, left, own, others, slope, proj, seq, after=()):
    tokens, rows = left.shape
    parts = ids.shape[0]
    half = parts // 2
    columns = proj.shape[1] // seq
    tile = min(512, columns)
    share = columns // tile
    shape = jax.ShapeDtypeStruct((half, seq, rows // parts, columns), bf16)
    split = pl.BlockSpec(
        (half, 1, rows // parts, tile),
        lambda i, t, u: (0, u[jnp.minimum(i // share, seq - 1)], 0, i % share),
    )
    stripe = pl.BlockSpec((tokens, tile), lambda i, t, u: (0, i))
    fixed = pl.BlockSpec(
        (tokens, rows), lambda i, t, u: (0, 0), pipeline_mode=pl.Buffered(1)
    )
    return pl.pallas_call(
        ignoring(value_back_body, 7, len(after)),
        grid_spec=pltpu.PrefetchScalarGridSpec(
            num_scalar_prefetch=2,
            grid=(seq * share,),
            in_specs=[
                fixed,
                stripe,
                pl.BlockSpec((others.shape[0], tokens, tile), lambda i, t, u: (0, 0, i)),
                stripe,
                pl.BlockSpec((rows, tile), lambda i, t, u: (0, i)),
            ]
            + [pl.BlockSpec(memory_space=pl.ANY)] * len(after),
            out_specs=[fixed, split, split],
            scratch_shapes=[
                pltpu.VMEM((rows, tokens), bf16),
                pltpu.VMEM((rows, tokens), bf16),
            ],
        ),
        out_shape=[jax.ShapeDtypeStruct((tokens, rows), f32), shape, shape],
        compiler_params=params(("arbitrary",)),
        name="value_back",
        cost_estimate=LONG,
    )(ids, places, left, own, others, slope, proj, *after)


def stage_body(*refs, jobs):
    ins, outs = list(refs), list(refs[sum(map(sum, jobs)) :])
    for counts, out in zip(jobs, outs):
        for g, count in enumerate(counts):
            total = ins.pop(0)[0].astype(f32)
            for _ in range(count - 1):
                total = total + ins.pop(0)[0].astype(f32)
            out[g] = total.astype(out.dtype)


def stage_sums(jobs, after=(), steps=2, cost=BRIEF):
    for _, rows, _ in jobs:
        while rows % (16 * steps) and steps > 1:
            steps //= 2
    ins, in_specs, out_specs, out_shapes, counts = [], [], [], [], []
    for terms, rows, kind in jobs:
        each = rows // steps
        columns = terms[0][0][0].shape[2]
        for array, entry, start in (term for group in terms for term in group):
            ins.append(array)
            in_specs.append(
                pl.BlockSpec(
                    (1, each, columns),
                    lambda i, entry=entry, first=start // each: (entry, first + i, 0),
                )
            )
        out_specs.append(pl.BlockSpec((len(terms), each, columns), lambda i: (0, i, 0)))
        out_shapes.append(jax.ShapeDtypeStruct((len(terms), rows, columns), kind))
        counts.append([len(group) for group in terms])
    return pl.pallas_call(
        ignoring(functools.partial(stage_body, jobs=counts), len(ins), len(after)),
        grid=(steps,),
        in_specs=in_specs + [pl.BlockSpec(memory_space=pl.ANY)] * len(after),
        out_specs=out_specs,
        out_shape=out_shapes,
        compiler_params=params(("arbitrary",)),
        name="stage_sums",
        cost_estimate=cost,
    )(*ins, *after)


class Layout:
    def __init__(self, mesh):
        self.dp = mesh.shape["dp"]
        self.seq = mesh.shape["seq"]
        self.members = self.seq // 2
        self.chips = self.seq // 4

    def pairs(self, move):
        return [
            (d * self.seq + z, e * self.seq + w)
            for d in range(self.dp)
            for z in range(self.seq)
            for e, w in [move(d, z)]
        ]

    def send(self, value, move):
        return lax.ppermute(value, AXES, self.pairs(move))

    def place(self, sequence, member):
        return member % 2 ^ (1 - sequence % 2), sequence * self.chips + member // 2

    def member(self, core, z):
        sequence = z // self.chips
        return (z % self.chips) * 2 + (core ^ (1 - sequence % 2))

    def home_to_work(self, round_index):
        def move(d, z):
            part = (1 if z >= self.seq // 2 else 0) ^ round_index
            core, at = self.place(2 * (d % 2) + part, min(z, self.seq - 1 - z))
            return d - d % 2 + core, at

        return move

    def outgoing(self, value):
        late = lax.axis_index("seq") >= self.seq // 2
        return [
            lax.dynamic_index_in_dim(value, jnp.where(late, 1 - r, r), 0, False)
            for r in range(2)
        ]

    def to_work(self, value, round_index):
        return self.send(value, self.home_to_work(round_index))

    def homeward(self, value, round_index):
        pairs = [(b, a) for a, b in self.pairs(self.home_to_work(round_index))]
        return lax.ppermute(value, AXES, pairs)

    def gathered(self, back):
        late = lax.axis_index("seq") >= self.seq // 2
        return jnp.stack([jnp.where(late, back[1], back[0]), jnp.where(late, back[0], back[1])])

    def collect(self, values):
        return self.gathered([self.homeward(v, r) for r, v in enumerate(values)])

    def rotate(self, value, by):
        def move(d, z):
            member = (self.member(d % 2, z) + by) % self.members
            core, at = self.place(z // self.chips, member)
            return d - d % 2 + core, at

        return self.send(value, move)

    def gather(self, value):
        return jnp.concatenate([self.rotate(value, by) for by in range(1, self.members)], axis=0)

    def returns(self, others):
        slots = others.shape[0] // (self.members - 1)
        return jnp.stack(
            [
                self.rotate(others[(by - 1) * slots : by * slots], self.members - by).reshape(
                    -1, others.shape[-1]
                )
                for by in range(1, self.members)
            ]
        )

    def orders(self):
        dp, z = lax.axis_index("dp"), lax.axis_index("seq")
        bits = self.dp.bit_length() - 1
        ids = []
        for core in range(2):
            orders = [[0, *range(1, bits)], [0, *reversed(range(1, bits))]]
            flips = []
            for p in range(self.dp):
                order = orders[core if p >= self.dp // 2 else 1 - core]
                flips.append(
                    sum(
                        (0 if p >> (bits - 1 - i) & 1 else 1) << bit
                        for i, bit in enumerate(order)
                    )
                )
            ids.append(dp ^ jnp.array(flips, jnp.int32))
        ids = jnp.where(dp % 2 == 0, ids[0], ids[1])
        bits = self.seq.bit_length() - 1
        flips = [
            sum((0 if p >> (bits - 1 - i) & 1 else 1) << i for i in range(bits))
            for p in range(self.seq)
        ]
        blocks = z ^ jnp.array(flips, jnp.int32)
        return ids, jnp.argsort(blocks).astype(jnp.int32), blocks

    def partner(self, stage):
        bits = self.dp.bit_length() - 1
        if stage == 0:
            return lambda d, z: (d ^ 1, z)
        if stage < bits:
            return lambda d, z: (d ^ (1 << stage if d % 2 == 0 else 1 << (bits - stage)), z)
        return lambda d, z: (d, z ^ (1 << (stage - bits)))

    def turn(self, sums, after, cost=BRIEF):
        sums = [s for s in sums if s.total is None]
        if not sums:
            return after
        jobs = []
        for s in sums:
            s.stage += 1
            ended = s.stage == s.stages
            rows = s.rows if ended else s.rows // 2
            jobs.append((s.terms, rows, f32 if ended and s.over_seq else bf16))
        out = stage_sums(jobs, after, cost=cost)
        for s, held, (_, rows, _) in zip(sums, out, jobs):
            if s.stage == s.stages:
                s.total = held
            else:
                s.terms = [[(a, e, start + rows) for a, e, start in group] for group in s.terms]
                s.rows = rows
                s.send(held)
        return list(out)

    def from_seq(self, held):
        return [
            self.send(held.astype(bf16), lambda d, z: (d, z ^ other))
            for other in range(1, self.seq)
        ]


    def over_dp(self, held):
        bits = self.dp.bit_length() - 1
        for bit in range(bits - 1):
            held = held + self.send(held, lambda d, z: (d ^ (1 << bit), z))
        return held, self.send(held, lambda d, z: (d ^ (1 << (bits - 1)), z))


def later_body(left, right, out):
    out[...] = left[...] + right[...]


def later_sum(left, right, after):
    inside = pl.BlockSpec(memory_space=pltpu.VMEM)
    return pl.pallas_call(
        ignoring(later_body, 2, len(after)),
        in_specs=[inside] * 2 + [pl.BlockSpec(memory_space=pl.ANY)] * len(after),
        out_specs=inside,
        out_shape=jax.ShapeDtypeStruct(left.shape, left.dtype),
        name="later_sum",
        cost_estimate=BRIEF,
    )(left, right, *after)


def pack_body(qx_a, qx_b, qs_a, qs_b, rest_ref, out):
    rows = qx_a.shape[0]
    out[:rows] = qx_a[...] + qx_b[...]
    out[rows : 2 * rows] = qs_a[...] + qs_b[...]
    out[2 * rows :] = rest_ref[...]


def pack(first, second, rest, after=()):
    ins = [v.reshape(-1, 128) for v in (first[0], second[0], first[1], second[1])] + [rest]
    rows = 2 * ins[0].shape[0] + rest.shape[0]
    inside = pl.BlockSpec(memory_space=pltpu.VMEM)
    return pl.pallas_call(
        ignoring(pack_body, 5, len(after)),
        in_specs=[inside] * 5 + [pl.BlockSpec(memory_space=pl.ANY)] * len(after),
        out_specs=inside,
        out_shape=jax.ShapeDtypeStruct((rows, 128), f32),
        name="pack",
        cost_estimate=BRIEF,
    )(*ins, *after)


def finish_body(*refs, terms):
    alpha, damp, beta, eta, alpha_out, damp_out, beta_out, eta_out, *rest = refs[terms:]
    *rest, rows = rest
    total = refs[0][...]
    for term in refs[1:terms]:
        total = total + term[...].astype(f32)
    rows[...] = total
    states = alpha.shape[0]
    groups = alpha.shape[1] // 128
    for c in range(groups):
        at = slice(c * 128, (c + 1) * 128)
        x_sum = rows[pl.ds(c, states, stride=groups), :]
        s_sum = rows[pl.ds(states * groups + c, states, stride=groups), :]
        rate = alpha[:, at] * beta[:, at]
        input_total = eta[:, at] * x_sum
        decay_total = eta[:, at] * rate * s_sum
        alpha_out[:, at] = beta[:, at] * input_total - damp[:, at] * decay_total
        damp_out[:, at] = -alpha[:, at] * decay_total
        beta_out[:, at] = alpha[:, at] * input_total
        eta_out[:, at] = rate * x_sum
    start = 2 * states * groups
    for out in rest:
        out[...] = rows[start : start + out.shape[0]]
        start += out.shape[0]


def finish(terms, alpha, damp, beta, eta, counts):
    inside = pl.BlockSpec(memory_space=pltpu.VMEM)
    rows = terms[0].shape[0]
    shape = jax.ShapeDtypeStruct(alpha.shape, f32)
    return pl.pallas_call(
        functools.partial(finish_body, terms=len(terms)),
        in_specs=[inside] * (len(terms) + 4),
        out_specs=[inside] * (4 + len(counts)),
        out_shape=[shape] * 4 + [jax.ShapeDtypeStruct((n, 128), f32) for n in counts],
        scratch_shapes=[pltpu.VMEM((rows, 128), f32)],
        name="finish",
        cost_estimate=BRIEF,
    )(*terms, alpha, damp, beta, eta)


class Sum:
    def __init__(self, layout, *pairs, over_seq=True):
        self.layout = layout
        self.stage = 0
        self.dp_stages = layout.dp.bit_length() - 1
        self.stages = self.dp_stages + (layout.seq.bit_length() - 1 if over_seq else 0)
        self.over_seq = over_seq
        self.total = None
        pairs = [[v.reshape(1, -1, v.shape[-1]) for v in pair] for pair in pairs]
        self.rows = pairs[0][1].shape[1]
        self.terms = [
            [(kept, 0, 0), (layout.send(sent, layout.partner(0)), 0, 0)] for sent, kept in pairs
        ]

    def send(self, held):
        arrived = self.layout.send(held, self.layout.partner(self.stage))
        for entry, group in enumerate(self.terms):
            group.append((arrived, entry, 0))

    def begin_seq(self, block):
        self.stage = self.dp_stages
        self.stages = self.stage + self.layout.seq.bit_length() - 1
        self.over_seq, self.total = True, None
        block = block.reshape(1, -1, block.shape[-1])
        self.rows = block.shape[1] // 2
        self.terms = [[(block, 0, self.rows)]]
        self.send(block[:, : self.rows])


def mm(a, b):
    return jnp.dot(a, b, preferred_element_type=f32)


def mm_nt(a, b):
    return lax.dot_general(a, b, (((1,), (1,)), ((), ())), preferred_element_type=f32)


def mm_tn(a, b):
    return lax.dot_general(a, b, (((0,), (0,)), ((), ())), preferred_element_type=f32)


def layer(
    layout,
    inputs,
    cotangent,
    full_attention,
    mix_gain,
    smooth_alpha,
    smooth_damp,
    smooth_beta,
    smooth_eta,
    smooth_omega,
    value_proj,
    mix_proj,
    score_affine,
    relative_bias,
    out_proj,
    feed_gain,
    feed_in,
    feed_out,
):
    slots, chunk_rows, width = inputs.shape
    key_width = score_affine.shape[1]
    value_width = value_proj.shape[1]
    tokens = slots * chunk_rows
    total = layout.seq
    seq_length = relative_bias.shape[0] // 2
    block = min(128, chunk_rows)
    core = lax.axis_index("dp") % 2
    z = lax.axis_index("seq")

    sequence = z // layout.chips
    member = layout.member(core, z)
    swap = sequence % 2
    chunks = []
    for by in range(layout.members):
        source = (member - by) % layout.members
        low, high = source, total - 1 - source
        chunks += [jnp.where(swap == 0, low, high), jnp.where(swap == 0, high, low)]
    chunks = jnp.stack(chunks).astype(jnp.int32)
    slot_of = jnp.sum(
        jnp.where(chunks[None, :] == jnp.arange(total)[:, None], jnp.arange(total)[None, :], 0),
        axis=1,
    ).astype(jnp.int32)
    flags = full_attention.astype(f32)
    flags_other = layout.send(flags, lambda d, z: (d ^ 1, z))
    flags = jnp.where(
        core == 0, jnp.concatenate([flags, flags_other]), jnp.concatenate([flags_other, flags])
    )
    full = lax.dynamic_index_in_dim(flags, sequence, 0, False) == 1.0
    table = jnp.concatenate([chunks, slot_of, full.astype(jnp.int32)[None]])
    ids, places, blocks = layout.orders()

    arriving = [
        (slot, at * (chunk_rows // count), layout.to_work(piece, slot))
        for slot, count in ((0, 1), (1, 1))
        for at, piece in enumerate(jnp.split(layout.outgoing(inputs)[slot], count))
    ]
    leaving = layout.outgoing(cotangent)
    bias_back, bias_front = bias_tiles(relative_bias, chunk_rows // TILE - 1, full)

    states = smooth_alpha.shape[0]
    lanes = (states, width // 128, 128)
    decay = 1.0 - smooth_alpha * smooth_damp
    rate = smooth_alpha * smooth_beta
    span = (decay**chunk_rows).reshape(lanes)
    coef = (smooth_eta * rate).reshape(lanes)
    decay_slab = decay.reshape(lanes)
    gain_row = mix_gain[None]
    omega_row = smooth_omega[None]
    mix_shared, mix_main = mix_proj[:, :key_width], mix_proj[:, key_width:]

    held, after = (), (bias_back, bias_front, mix_main, mix_shared, span, coef)
    ready = (table, ids, places, blocks, *leaving)
    for slot, row, piece in arriving:
        held = front(
            piece, slot, row, (slots, chunk_rows), held, gain_row, decay_slab, value_proj, after=after
        )
        after, ready = ready, ()
    normed_low, x, value_low, value_slope, ends = held
    ends_others = layout.gather(ends)
    leaving, ends_others = lax.optimization_barrier((leaving, ends_others))
    cots = [layout.to_work(v, r) for r, v in enumerate(leaving)]
    normed_low = normed_low.reshape(tokens, width)
    value_slope = value_slope.reshape(tokens, value_width)
    value_others = layout.gather(value_low)
    smoothed, mixed, check, shared_pre, query_low, key_low = front_scan(
        table,
        x,
        gain_row,
        decay_slab,
        coef,
        span,
        omega_row,
        ends,
        ends_others,
        mix_shared,
        score_affine,
        block,
    )
    smoothed = smoothed.reshape(tokens, width)
    mixed = mixed.reshape(tokens, width)
    shared_pre = shared_pre.reshape(tokens, key_width)
    key_others = layout.gather(key_low)
    base = product(mixed, mix_main)
    attended, gated, lse = attend(
        table,
        query_low,
        bias_front,
        base.reshape(slots, chunk_rows, -1),
        key_low,
        key_others,
        value_low,
        value_others,
    )
    attended = attended.reshape(tokens, value_width)
    gated = gated.reshape(tokens, value_width)

    flat_low = x.reshape(tokens, width)
    cand_in, first_sum, feed_low = candidate(gated, out_proj, base, flat_low, feed_gain[None])

    result_a, result_b, grad_feed, out_send, out_keep, in_send, in_keep = feed(
        ids, places, feed_low, cots, first_sum, feed_in, feed_out, layout.seq
    )
    home = [layout.homeward(result_a, 0), layout.homeward(result_b, 1)]
    block_out = layout.gathered(home)
    feed_sum = Sum(layout, (out_send, out_keep), (in_send, in_keep))

    grad_input, grad_main, grad_att, feed_gain_grad = gate(
        grad_feed, cots, flat_low, cand_in, base, attended, feed_gain[None], out_proj
    )
    after = layout.turn((feed_sum,), (grad_att,))
    mix_parts = by_rows(ids, None, mixed, grad_main, after=after, cost=LONG)
    proj_parts = by_columns(
        ids,
        places,
        grad_main,
        gated,
        rows=width,
        at=grad_main.shape[1] // width - 1,
        after=mix_parts,
    )
    after = (*proj_parts, *home)
    mix_sum = Sum(layout, mix_parts, over_seq=False)
    proj_sum = Sum(layout, proj_parts)
    grad_query, gk_own, gv_own, both_oth, rel_sums = attend_back(
        table,
        query_low,
        grad_att.reshape(slots, chunk_rows, value_width),
        lse,
        bias_back,
        key_low,
        key_others,
        value_low,
        value_others,
        after=after,
    )
    both_back = layout.returns(both_oth)
    after = layout.turn((feed_sum, proj_sum), (grad_query,), cost=LONG)
    grad_normed, value_send, value_keep = value_back(
        ids,
        places,
        normed_low,
        gv_own.reshape(tokens, value_width),
        both_back,
        value_slope,
        value_proj,
        layout.seq,
        after=after,
    )
    grad_key = jnp.sum(both_back[:, :, value_width:].astype(f32), axis=0) + gk_own.reshape(
        tokens, key_width
    ).astype(f32)
    grad_query = grad_query.reshape(tokens, key_width)
    grad_shared = (
        (grad_query * score_affine[0] + grad_key * score_affine[2]) * silu_slope(shared_pre)
    ).astype(bf16)
    shared_parts = by_rows(ids, None, mixed, grad_shared, after=(grad_normed,))
    shared_sum = Sum(layout, shared_parts, over_seq=False)
    value_sum = Sum(layout, (value_send, value_keep))
    after = layout.turn((mix_sum,), shared_parts)
    grad_smooth = smooth_back(
        grad_main, grad_shared, mix_main, mix_shared, smoothed, after=after
    )
    grad_smooth = grad_smooth.reshape(slots, chunk_rows, width)
    after = layout.turn((feed_sum, value_sum, proj_sum, shared_sum), (grad_smooth,))
    back = back_ends(grad_smooth, decay_slab, after=after)
    back_others = layout.gather(back)
    after = layout.turn((feed_sum, mix_sum, value_sum, shared_sum), (back,))

    def scan_back(slot, after):
        return back_scan(
            table,
            slot,
            x,
            grad_smooth,
            grad_normed.reshape(slots, chunk_rows, width),
            grad_input.reshape(slots, chunk_rows, width),
            check,
            gain_row,
            decay_slab,
            coef,
            span,
            omega_row,
            back,
            back_others,
            after=after,
        )

    first = scan_back(0, after)
    after = layout.turn(
        (feed_sum, mix_sum, value_sum, proj_sum, shared_sum), (first[0],)
    )
    home_first = layout.homeward(first[0], 0)
    while mix_sum.total is None or shared_sum.total is None:
        after = layout.turn((mix_sum, shared_sum), after)
    rows = jnp.concatenate([shared_sum.total[0], mix_sum.total[0]], axis=1)
    rows = rows.reshape(rows.shape[0], layout.seq, -1).transpose(1, 0, 2)
    mix_sum.begin_seq(rows[blocks])
    second = scan_back(1, (*after, mix_sum.terms[0][0][0]))
    affine_grad = jnp.stack(
        [
            jnp.sum(grad_query * shared_pre * jax.nn.sigmoid(shared_pre), axis=0),
            jnp.sum(grad_query, axis=0),
            jnp.sum(grad_key * shared_pre * jax.nn.sigmoid(shared_pre), axis=0),
            jnp.sum(grad_key, axis=0),
        ]
    )
    relative_grad = bias_grad(rel_sums[:, 0], seq_length)
    small = [
        first[3] + second[3],
        first[4] + second[4],
        feed_gain_grad,
        affine_grad,
        relative_grad,
    ]
    small = [v.reshape(-1, 128) for v in small]
    rest = jnp.concatenate(small)
    rest = jnp.pad(rest, ((0, -rest.shape[0] % 16), (0, 0)))
    home_second = layout.homeward(second[0], 1)
    sums = (mix_sum, proj_sum, value_sum, feed_sum)
    turned = layout.turn(sums, (second[0], home_first), cost=LONG)
    totals = layout.over_dp(pack(first[1:3], second[1:3], rest, after=turned))
    after = layout.turn(sums, (*turned, home_second))
    totals = later_sum(*totals, after=after)
    while any(v.total is None for v in sums):
        after = layout.turn(sums, after)
    grad_in = layout.gathered([home_first, home_second]).astype(f32)
    feed_out_grad, feed_in_grad = feed_sum.total[0].T, feed_sum.total[1]
    rows = width // layout.dp
    feed_in_grad = feed_in_grad.reshape(-1, rows, feed_in_grad.shape[-1])
    feed_in_grad = feed_in_grad.transpose(1, 0, 2).reshape(rows, -1)
    out_grad, value_grad = proj_sum.total[0].T, value_sum.total[0]
    mix_grad = mix_sum.total[0]
    alpha_grad, damp_grad, beta_grad, eta_grad, *parts = finish(
        [totals, *layout.from_seq(totals)],
        smooth_alpha,
        smooth_damp,
        smooth_beta,
        smooth_eta,
        [v.shape[0] for v in small],
    )
    parts = [v.reshape(-1) for v in parts]
    return (
        block_out,
        grad_in,
        parts[0],
        alpha_grad,
        damp_grad,
        beta_grad,
        eta_grad,
        parts[1],
        value_grad,
        mix_grad,
        parts[3].reshape(4, key_width),
        parts[4],
        out_grad,
        parts[2],
        feed_in_grad,
        feed_out_grad,
    )


def solution(mesh):
    tokens = P("dp", "seq", None)
    split = P("dp", "seq")
    return jax.shard_map(
        functools.partial(layer, Layout(mesh)),
        mesh=mesh,
        in_specs=(tokens, tokens, P("dp")) + (P(),) * 14,
        out_specs=(tokens, tokens)
        + (P(),) * 6
        + (split, split, P(), P(), split, P(), split, split),
        check_vma=False,
    )
```

```python
import functools

import jax
import jax.numpy as jnp
from jax import lax
from jax.experimental import pallas as pl
from jax.experimental.pallas import tpu as pltpu
from jax.sharding import PartitionSpec as P

STRETCH = 128
EPSILON = 1e-05
TILE = 256
MASKED = -1e30
VMEM_LIMIT = 60 * 1024 * 1024
AXES = ("dp", "seq")
BRIEF = pl.CostEstimate(flops=1, bytes_accessed=1, transcendentals=0)
LONG = pl.CostEstimate(flops=10**11, bytes_accessed=1, transcendentals=0)

f32 = jnp.float32
bf16 = jnp.bfloat16


def unit_rows_of(values):
    centred = values - jnp.mean(values, axis=-1, keepdims=True)
    inv_std = lax.rsqrt(jnp.mean(centred * centred, axis=-1, keepdims=True) + EPSILON)
    return centred * inv_std, inv_std


def norm_back_rows(grad_out, gain_vec, unit_rows, inv_std):
    scaled = grad_out * gain_vec
    return inv_std * (
        scaled
        - jnp.mean(scaled, axis=-1, keepdims=True)
        - unit_rows * jnp.mean(scaled * unit_rows, axis=-1, keepdims=True)
    )


def silu_slope(pre_act):
    sigmoid_val = jax.nn.sigmoid(pre_act)
    return sigmoid_val * (1.0 + pre_act * (1.0 - sigmoid_val))


def params(semantics, limit=VMEM_LIMIT):
    return pltpu.CompilerParams(dimension_semantics=semantics, vmem_limit_bytes=limit)


def ignoring(body, first, count):
    def called(*refs):
        return body(*refs[:first], *refs[first + count :])

    return called


def to_slab(slab, rows):
    count, groups = rows.shape[0], rows.shape[1] // 128
    for c in range(groups):
        slab[pl.ds(c, count, stride=groups), :] = rows[:, c * 128 : (c + 1) * 128]


def from_slab(slab, count, groups):
    return jnp.concatenate(
        [slab[pl.ds(c, count, stride=groups), :] for c in range(groups)], axis=1
    )


def slab_row(slab, t, groups):
    return slab[pl.ds(pl.multiple_of(t * groups, groups), groups), :]


def front_body(
    x_ref,
    gain_ref,
    decay_ref,
    proj_ref,
    begin_ref,
    low_ref,
    copy_ref,
    value_ref,
    slope_ref,
    end_ref,
    slab,
    *,
    fresh,
):
    states, groups, _ = decay_ref.shape
    count = x_ref.shape[0]

    @pl.when(pl.program_id(0) == 0)
    def _():
        end_ref[...] = jnp.zeros_like(end_ref) if fresh else begin_ref[...]

    copy_ref[0] = x_ref[...]
    unit, _ = unit_rows_of(x_ref[...].astype(f32))
    normed = unit * gain_ref[...]
    low_ref[0] = normed.astype(bf16)
    to_slab(slab, normed)
    decay = [decay_ref[n] for n in range(states)]

    def step(t, state):
        row = slab_row(slab, t, groups)
        return tuple(d * s + row for d, s in zip(decay, state))

    state = lax.fori_loop(
        0, count, step, tuple(end_ref[0, n] for n in range(states)), unroll=8
    )
    for n in range(states):
        end_ref[0, n] = state[n]
    for c in range(proj_ref.shape[1] // 512):
        at = slice(c * 512, (c + 1) * 512)
        pre = jnp.dot(low_ref[0], proj_ref[:, at], preferred_element_type=f32)
        gate = jax.nn.sigmoid(pre)
        value = pre * gate
        value_ref[0, :, at] = value.astype(bf16)
        slope_ref[0, :, at] = (gate + value * (1.0 - gate)).astype(bf16)


def front(x, slot, row, whole, earlier, gain, decay, proj, after=()):
    rows, width = x.shape
    slots, length = whole
    value_width = proj.shape[1]
    states, groups, lanes = decay.shape
    block = min(256, rows)
    first = row // block
    begin = earlier[-1] if row else jnp.zeros((slots, *decay.shape), f32)
    anywhere = pl.BlockSpec(memory_space=pl.ANY)

    def tokens(columns):
        return pl.BlockSpec((1, block, columns), lambda b: (slot, first + b, 0))

    return pl.pallas_call(
        ignoring(functools.partial(front_body, fresh=row == 0), 5, len(earlier) + len(after)),
        grid=(rows // block,),
        in_specs=[
            pl.BlockSpec((block, width), lambda b: (b, 0)),
            pl.BlockSpec((1, width), lambda b: (0, 0)),
            pl.BlockSpec((states, groups, lanes), lambda b: (0, 0, 0)),
            pl.BlockSpec(proj.shape, lambda b: (0, 0), pipeline_mode=pl.Buffered(1)),
            pl.BlockSpec((1, states, groups, lanes), lambda b: (slot, 0, 0, 0)),
        ]
        + [anywhere] * (len(earlier) + len(after)),
        out_specs=[
            tokens(width),
            tokens(width),
            tokens(value_width),
            tokens(value_width),
            pl.BlockSpec((1, states, groups, lanes), lambda b: (slot, 0, 0, 0)),
        ],
        out_shape=[
            jax.ShapeDtypeStruct((slots, length, width), bf16),
            jax.ShapeDtypeStruct((slots, length, width), bf16),
            jax.ShapeDtypeStruct((slots, length, value_width), bf16),
            jax.ShapeDtypeStruct((slots, length, value_width), bf16),
            jax.ShapeDtypeStruct((slots, states, groups, lanes), f32),
        ],
        scratch_shapes=[pltpu.VMEM((block * groups, lanes), f32)],
        input_output_aliases={5 + k: k for k in range(len(earlier))},
        compiler_params=params(("arbitrary",)),
        name="front",
        cost_estimate=BRIEF,
    )(x, gain, decay, proj, begin, *earlier, *after)


def front_scan_body(
    table_ref,
    x_ref,
    gain_ref,
    decay_ref,
    coef_ref,
    span_ref,
    omega_ref,
    ends_own,
    ends_oth,
    proj_ref,
    affine_ref,
    smooth_ref,
    mixed_ref,
    check_ref,
    shared_ref,
    query_ref,
    key_ref,
    slab,
    out_slab,
    carry,
    ends_ref,
):
    states, groups, _ = decay_ref.shape
    count = x_ref.shape[1]
    slot = pl.program_id(0)
    slots = ends_own.shape[0]
    total = slots + ends_oth.shape[0]

    @pl.when(pl.program_id(1) == 0)
    def _():
        carry[...] = jnp.zeros_like(carry)
        ends_ref[:slots] = ends_own[...]
        ends_ref[slots:] = ends_oth[...]

        def link(i, _):
            carry[...] = span_ref[...] * carry[...] + ends_ref[table_ref[total + i]]
            return 0

        lax.fori_loop(0, table_ref[slot], link, 0)

    unit, _ = unit_rows_of(x_ref[0].astype(f32))
    normed = unit * gain_ref[...]
    to_slab(slab, normed)
    decay = [decay_ref[n] for n in range(states)]
    coef = [coef_ref[n] for n in range(states)]
    state = tuple(carry[n] for n in range(states))
    for n in range(states):
        check_ref[0, 0, n] = state[n]

    def step(t, state):
        row = slab_row(slab, t, groups)
        state = tuple(d * s + row for d, s in zip(decay, state))
        parts = [c * s for c, s in zip(coef, state)]
        while len(parts) > 1:
            parts = [a + b for a, b in zip(parts[::2], parts[1::2])]
        out_slab[pl.ds(pl.multiple_of(t * groups, groups), groups), :] = parts[0]
        return state

    state = lax.fori_loop(0, count, step, state, unroll=8)
    for n in range(states):
        carry[n] = state[n]
    smoothed = from_slab(out_slab, count, groups) + omega_ref[...] * normed
    smooth_ref[0] = smoothed
    mixed = (smoothed * jax.nn.sigmoid(smoothed)).astype(bf16)
    mixed_ref[0] = mixed
    shared_pre = jnp.dot(mixed, proj_ref[...], preferred_element_type=f32)
    shared = shared_pre * jax.nn.sigmoid(shared_pre)
    shared_ref[0] = shared_pre
    query_ref[0] = (shared * affine_ref[0:1] + affine_ref[1:2]).astype(bf16)
    key_ref[0] = (shared * affine_ref[2:3] + affine_ref[3:4]).astype(bf16)


def front_scan(table, x, gain, decay, coef, span, omega, ends, others, proj, affine, block):
    slots, length, width = x.shape
    states, groups, lanes = decay.shape
    whole3 = pl.BlockSpec((states, groups, lanes), lambda k, b, t: (0, 0, 0))
    row = pl.BlockSpec((1, width), lambda k, b, t: (0, 0))
    tokens = pl.BlockSpec((1, block, width), lambda k, b, t: (k, b, 0))
    narrow = pl.BlockSpec((1, block, proj.shape[1]), lambda k, b, t: (k, b, 0))
    return pl.pallas_call(
        front_scan_body,
        grid_spec=pltpu.PrefetchScalarGridSpec(
            num_scalar_prefetch=1,
            grid=(slots, length // block),
            in_specs=[
                tokens,
                row,
                whole3,
                whole3,
                whole3,
                row,
                pl.BlockSpec(ends.shape, lambda k, b, t: (0, 0, 0, 0)),
                pl.BlockSpec(others.shape, lambda k, b, t: (0, 0, 0, 0)),
                pl.BlockSpec(proj.shape, lambda k, b, t: (0, 0)),
                pl.BlockSpec(affine.shape, lambda k, b, t: (0, 0)),
            ],
            out_specs=[
                tokens,
                tokens,
                pl.BlockSpec((1, 1, states, groups, lanes), lambda k, b, t: (k, b, 0, 0, 0)),
                narrow,
                narrow,
                narrow,
            ],
            scratch_shapes=[
                pltpu.VMEM((block * groups, lanes), f32),
                pltpu.VMEM((block * groups, lanes), f32),
                pltpu.VMEM((states, groups, lanes), f32),
                pltpu.VMEM((ends.shape[0] + others.shape[0], states, groups, lanes), f32),
            ],
        ),
        out_shape=[
            jax.ShapeDtypeStruct((slots, length, width), f32),
            jax.ShapeDtypeStruct((slots, length, width), bf16),
            jax.ShapeDtypeStruct((slots, length // block, states, groups, lanes), f32),
            jax.ShapeDtypeStruct((slots, length, proj.shape[1]), f32),
            jax.ShapeDtypeStruct((slots, length, proj.shape[1]), bf16),
            jax.ShapeDtypeStruct((slots, length, proj.shape[1]), bf16),
        ],
        compiler_params=params(("arbitrary", "arbitrary")),
        name="front_scan",
        cost_estimate=LONG,
    )(table, x, gain, decay, coef, span, omega, ends, others, proj, affine)


def back_ends_body(gs_ref, decay_ref, end_ref, slab):
    states, groups, _ = decay_ref.shape
    slots, count, _ = gs_ref.shape

    @pl.when(pl.program_id(0) == 0)
    def _():
        end_ref[...] = jnp.zeros_like(end_ref)

    for k in range(slots):
        to_slab(slab.at[k], gs_ref[k])
    decay = [decay_ref[n] for n in range(states)]

    def step(t, state):
        rows = [slab_row(slab.at[k], count - 1 - t, groups) for k in range(slots)]
        return [tuple(d * s + row for d, s in zip(decay, held)) for row, held in zip(rows, state)]

    state = lax.fori_loop(
        0,
        count,
        step,
        [tuple(end_ref[k, n] for n in range(states)) for k in range(slots)],
        unroll=8,
    )
    for k in range(slots):
        for n in range(states):
            end_ref[k, n] = state[k][n]


def back_ends(gs, decay, block=128, after=()):
    slots, length, width = gs.shape
    states, groups, lanes = decay.shape
    block = min(block, length)
    blocks = length // block
    return pl.pallas_call(
        ignoring(back_ends_body, 2, len(after)),
        grid=(blocks,),
        in_specs=[
            pl.BlockSpec((slots, block, width), lambda b: (0, blocks - 1 - b, 0)),
            pl.BlockSpec((states, groups, lanes), lambda b: (0, 0, 0)),
        ]
        + [pl.BlockSpec(memory_space=pl.ANY)] * len(after),
        out_specs=pl.BlockSpec((slots, states, groups, lanes), lambda b: (0, 0, 0, 0)),
        out_shape=jax.ShapeDtypeStruct((slots, states, groups, lanes), f32),
        scratch_shapes=[pltpu.VMEM((slots, block * groups, lanes), f32)],
        compiler_params=params(("arbitrary",)),
        name="back_ends",
        cost_estimate=BRIEF,
    )(gs, decay, *after)


def back_scan_body(
    table_ref,
    slot_ref,
    x_ref,
    gs_ref,
    gv_ref,
    gi_ref,
    check_ref,
    gain_ref,
    decay_ref,
    coef_ref,
    span_ref,
    omega_ref,
    ends_own,
    ends_oth,
    grad_ref,
    qx_ref,
    qs_ref,
    gain_grad_ref,
    omega_grad_ref,
    slab,
    gs_slab,
    out_slab,
    history,
    carry,
    ends_ref,
):
    states, groups, _ = decay_ref.shape
    count = x_ref.shape[1]
    slot = slot_ref[0]
    slots = ends_own.shape[0]
    total = slots + ends_oth.shape[0]

    @pl.when(pl.program_id(0) == 0)
    def _():
        qx_ref[...] = jnp.zeros_like(qx_ref)
        qs_ref[...] = jnp.zeros_like(qs_ref)
        gain_grad_ref[...] = jnp.zeros_like(gain_grad_ref)
        omega_grad_ref[...] = jnp.zeros_like(omega_grad_ref)

    @pl.when(pl.program_id(0) == 0)
    def _():
        carry[...] = jnp.zeros_like(carry)
        ends_ref[:slots] = ends_own[...]
        ends_ref[slots:] = ends_oth[...]

        def link(i, _):
            carry[...] = (
                span_ref[...] * carry[...] + ends_ref[table_ref[total + total - 1 - i]]
            )
            return 0

        lax.fori_loop(0, total - 1 - table_ref[slot], link, 0)

    unit, inv = unit_rows_of(x_ref[0].astype(f32))
    normed = unit * gain_ref[...]
    gs = gs_ref[0]
    to_slab(slab, normed)
    to_slab(gs_slab, gs)
    decay = [decay_ref[n] for n in range(states)]

    def recompute(t, state):
        for n in range(states):
            history[t, n] = state[n]
        row = slab_row(slab, t, groups)
        return tuple(d * s + row for d, s in zip(decay, state))

    lax.fori_loop(
        0, count, recompute, tuple(check_ref[0, 0, n] for n in range(states)), unroll=4
    )

    half = states // 2
    for part in range(2):
        chosen = range(part * half, (part + 1) * half)
        decay = [decay_ref[n] for n in chosen]
        coef = [coef_ref[n] for n in chosen]

        def step(i, held):
            q, qx, qs = held
            t = count - 1 - i
            row = slab_row(slab, t, groups)
            g = slab_row(gs_slab, t, groups)
            q = tuple(d * a + g for d, a in zip(decay, q))
            parts = [c * a for c, a in zip(coef, q)]
            while len(parts) > 1:
                parts = [a + b for a, b in zip(parts[::2], parts[1::2])]
            spot = pl.ds(pl.multiple_of(t * groups, groups), groups)
            if part == 0:
                out_slab[spot, :] = parts[0]
            else:
                out_slab[spot, :] = out_slab[spot, :] + parts[0]
            qx = tuple(a + b * row for a, b in zip(qx, q))
            qs = tuple(a + b * history[t, n] for a, b, n in zip(qs, q, chosen))
            return q, qx, qs

        q, qx, qs = lax.fori_loop(
            0,
            count,
            step,
            (
                tuple(carry[n] for n in chosen),
                tuple(qx_ref[n] for n in chosen),
                tuple(qs_ref[n] for n in chosen),
            ),
            unroll=4,
        )
        for i, n in enumerate(chosen):
            carry[n] = q[i]
            qx_ref[n] = qx[i]
            qs_ref[n] = qs[i]

    grad_normed = (
        gv_ref[0] + from_slab(out_slab, count, groups) + omega_ref[...] * gs
    )
    gain_grad_ref[...] += jnp.sum(grad_normed * unit, axis=0, keepdims=True)
    omega_grad_ref[...] += jnp.sum(gs * normed, axis=0, keepdims=True)
    grad_ref[...] = (
        gi_ref[0] + norm_back_rows(grad_normed, gain_ref[...], unit, inv)
    ).astype(bf16)


def back_scan(table, slot, x, gs, gv, gi, check, gain, decay, coef, span, omega, ends, others, after=()):
    _, length, width = x.shape
    states, groups, lanes = decay.shape
    blocks = check.shape[1]
    block = length // blocks
    whole3 = pl.BlockSpec((states, groups, lanes), lambda b, t, u: (0, 0, 0))
    row = pl.BlockSpec((1, width), lambda b, t, u: (0, 0))
    tokens = pl.BlockSpec((1, block, width), lambda b, t, u: (slot, blocks - 1 - b, 0))
    return pl.pallas_call(
        ignoring(back_scan_body, 14, len(after)),
        grid_spec=pltpu.PrefetchScalarGridSpec(
            num_scalar_prefetch=2,
            grid=(blocks,),
            in_specs=[
                tokens,
                tokens,
                tokens,
                tokens,
                pl.BlockSpec(
                    (1, 1, states, groups, lanes),
                    lambda b, t, u: (slot, blocks - 1 - b, 0, 0, 0),
                ),
                row,
                whole3,
                whole3,
                whole3,
                row,
                pl.BlockSpec(ends.shape, lambda b, t, u: (0, 0, 0, 0)),
                pl.BlockSpec(others.shape, lambda b, t, u: (0, 0, 0, 0)),
            ]
            + [pl.BlockSpec(memory_space=pl.ANY)] * len(after),
            out_specs=[
                pl.BlockSpec((block, width), lambda b, t, u: (blocks - 1 - b, 0)),
                whole3,
                whole3,
                row,
                row,
            ],
            scratch_shapes=[
                pltpu.VMEM((block * groups, lanes), f32),
                pltpu.VMEM((block * groups, lanes), f32),
                pltpu.VMEM((block * groups, lanes), f32),
                pltpu.VMEM((block, states, groups, lanes), f32),
                pltpu.VMEM((states, groups, lanes), f32),
                pltpu.VMEM((ends.shape[0] + others.shape[0], states, groups, lanes), f32),
            ],
        ),
        out_shape=[
            jax.ShapeDtypeStruct((length, width), bf16),
            jax.ShapeDtypeStruct((states, groups, lanes), f32),
            jax.ShapeDtypeStruct((states, groups, lanes), f32),
            jax.ShapeDtypeStruct((1, width), f32),
            jax.ShapeDtypeStruct((1, width), f32),
        ],
        compiler_params=params(("arbitrary",)),
        name="back_scan",
        cost_estimate=LONG,
    )(table, jnp.full((1,), slot, jnp.int32), x, gs, gv, gi, check, gain, decay, coef, span, omega, ends, others, *after)


def chunk_copies(table_ref, own, others, kept, total, length, sem):
    copies = []
    for slot in range(total):
        place = pl.ds(pl.multiple_of(table_ref[slot] * length, length), length)
        source = own.at[slot] if slot < 2 else others.at[slot - 2]
        copies.append(pltpu.make_async_copy(source, kept.at[place, :], sem.at[slot]))
    return copies


def attend_body(
    table_ref,
    q_ref,
    bias_ref,
    reset_ref,
    k_own,
    k_oth,
    v_own,
    v_oth,
    out_ref,
    gated_ref,
    lse_ref,
    keys,
    values,
    scores,
    probs,
    key_sem,
    value_sem,
    *,
    total,
):
    length, key_width = q_ref.shape[1:]
    value_width = values.shape[1]
    tiles = length // TILE
    scale = float(key_width) ** (-0.5)

    key_copies = chunk_copies(table_ref, k_own, k_oth, keys, total, length, key_sem)
    value_copies = chunk_copies(table_ref, v_own, v_oth, values, total, length, value_sem)

    @pl.when(pl.program_id(0) == 0)
    def _():
        for copy in key_copies + value_copies:
            copy.start()
        for copy in key_copies:
            copy.wait()

    chunk = table_ref[pl.program_id(0)]
    reach = jnp.where(table_ref[2 * total] == 1, chunk + 1, 1)
    base = (chunk + 1 - reach) * length
    queries = q_ref[0]

    def first(kc, peak):
        spot = pl.ds(pl.multiple_of(base + kc * length, length), length)
        tile = (
            lax.dot_general(
                queries, keys[spot, :], (((1,), (1,)), ((), ())), preferred_element_type=f32
            )
            * scale
        )
        for r in range(tiles):
            for a in range(tiles):
                rows = slice(r * TILE, (r + 1) * TILE)
                cols = slice(a * TILE, (a + 1) * TILE)
                gap = (reach - 1 - kc) * tiles + r - a + tiles - 1
                scores[kc, rows, cols] = tile[rows, cols] + bias_ref[gap]
        return jnp.maximum(peak, jnp.max(scores[kc], axis=1, keepdims=True))

    peak = lax.fori_loop(0, reach, first, jnp.full((length, 1), 2 * MASKED, f32))

    def second(kc, sums):
        terms = jnp.exp(scores[kc] - peak)
        probs[:, pl.ds(pl.multiple_of(kc * length, length), length)] = terms.astype(bf16)
        return sums + jnp.sum(terms, axis=1, keepdims=True)

    sums = lax.fori_loop(0, reach, second, jnp.zeros((length, 1), f32))
    lse_ref[0] = jnp.broadcast_to(peak + jnp.log(sums), (length, 128)).T[:1]
    inverse = 1.0 / sums

    @pl.when(pl.program_id(0) == 0)
    def _():
        for copy in value_copies:
            copy.wait()

    for count in range(1, total + 1):

        @pl.when(reach == count)
        def _(count=count):
            width = count * length
            span = pl.ds(pl.multiple_of(base, length), width)

            def column(ct, _):
                at = pl.ds(pl.multiple_of(ct * 1024, 1024), 1024)
                rows = (
                    jnp.dot(probs[:, :width], values[span, at], preferred_element_type=f32)
                    * inverse
                )
                out_ref[0, :, at] = rows.astype(bf16)
                gate = reset_ref[0, :, at].astype(f32)
                gated_ref[0, :, at] = (gate * jax.nn.sigmoid(gate) * rows).astype(bf16)
                return 0

            lax.fori_loop(0, value_width // 1024, column, 0)


def attend(table, q, bias, reset, k_own, k_oth, v_own, v_oth):
    slots, length, key_width = q.shape
    value_width = v_own.shape[2]
    total = slots + k_oth.shape[0]
    anywhere = pl.BlockSpec(memory_space=pl.ANY)
    tokens = pl.BlockSpec((1, length, value_width), lambda k, t: (k, 0, 0))
    return pl.pallas_call(
        functools.partial(attend_body, total=total),
        grid_spec=pltpu.PrefetchScalarGridSpec(
            num_scalar_prefetch=1,
            grid=(slots,),
            in_specs=[
                pl.BlockSpec((1, length, key_width), lambda k, t: (k, 0, 0)),
                pl.BlockSpec(bias.shape, lambda k, t: (0, 0, 0)),
                tokens,
                anywhere,
                anywhere,
                anywhere,
                anywhere,
            ],
            out_specs=[
                tokens,
                tokens,
                pl.BlockSpec((1, 1, length), lambda k, t: (k, 0, 0)),
            ],
            scratch_shapes=[
                pltpu.VMEM((total * length, key_width), bf16),
                pltpu.VMEM((total * length, value_width), bf16),
                pltpu.VMEM((total, length, length), f32),
                pltpu.VMEM((length, total * length), bf16),
                pltpu.SemaphoreType.DMA((total,)),
                pltpu.SemaphoreType.DMA((total,)),
            ],
        ),
        out_shape=[
            jax.ShapeDtypeStruct((slots, length, value_width), bf16),
            jax.ShapeDtypeStruct((slots, length, value_width), bf16),
            jax.ShapeDtypeStruct((slots, 1, length), f32),
        ],
        compiler_params=params(("arbitrary",)),
        name="attend",
        cost_estimate=BRIEF,
    )(table, q, bias, reset, k_own, k_oth, v_own, v_oth)


def attend_back_body(
    table_ref,
    q_ref,
    grad_ref,
    lse_ref,
    bias_ref,
    k_own,
    k_oth,
    v_own,
    v_oth,
    gq_ref,
    gk_own,
    gv_own,
    both_oth,
    rel_out,
    keys,
    values,
    gk_sum,
    gv_sum,
    probs_kept,
    grads_kept,
    rel_ref,
    key_sem,
    value_sem,
    *,
    total,
):
    length, key_width = q_ref.shape[1:]
    value_width = values.shape[1]
    tiles = length // TILE
    scale = float(key_width) ** (-0.5)
    step = pl.program_id(0)
    nt = (((1,), (1,)), ((), ()))
    tn = (((0,), (0,)), ((), ()))

    copies = chunk_copies(
        table_ref, k_own, k_oth, keys, total, length, key_sem
    ) + chunk_copies(table_ref, v_own, v_oth, values, total, length, value_sem)

    @pl.when(step == 0)
    def _():
        for copy in copies:
            copy.start()
        gk_sum[...] = jnp.zeros_like(gk_sum)
        gv_sum[...] = jnp.zeros_like(gv_sum)
        rel_ref[...] = jnp.zeros_like(rel_ref)
        for copy in copies:
            copy.wait()

    chunk = table_ref[step]
    reach = jnp.where(table_ref[2 * total] == 1, chunk + 1, 1)
    base = (chunk + 1 - reach) * length
    queries = q_ref[0]
    log_total = lse_ref[0]

    def gap_of(kc, a, r):
        return (reach - 1 - kc) * tiles + r - a + tiles - 1

    def first(kc, delta):
        spot = pl.ds(pl.multiple_of(base + kc * length, length), length)
        grads_kept[kc] = lax.dot_general(
            values[spot, :], grad_ref[0], nt, preferred_element_type=f32
        )
        tile = (
            lax.dot_general(keys[spot, :], queries, nt, preferred_element_type=f32) * scale
        )
        for a in range(tiles):
            for r in range(tiles):
                rows = slice(a * TILE, (a + 1) * TILE)
                cols = slice(r * TILE, (r + 1) * TILE)
                probs_kept[kc, rows, cols] = jnp.exp(
                    tile[rows, cols] + bias_ref[gap_of(kc, a, r)] - log_total[:, cols]
                )
        return delta + jnp.sum(probs_kept[kc] * grads_kept[kc], axis=0, keepdims=True)

    delta = lax.fori_loop(0, reach, first, jnp.zeros((1, length), f32))

    def second(kc, grad_query):
        spot = pl.ds(pl.multiple_of(base + kc * length, length), length)
        probs = probs_kept[kc]
        grad_scores = (probs * (grads_kept[kc] - delta)).astype(bf16)
        probs = probs.astype(bf16)
        for a in range(tiles):
            for r in range(tiles):
                rel_ref[gap_of(kc, a, r)] += grad_scores[
                    a * TILE : (a + 1) * TILE, r * TILE : (r + 1) * TILE
                ].astype(f32)
        gk_sum[spot, :] += jnp.dot(grad_scores, queries, preferred_element_type=f32)

        def column(ct, _):
            at = pl.ds(pl.multiple_of(ct * 1024, 1024), 1024)
            gv_sum[spot, at] += jnp.dot(
                probs, grad_ref[0, :, at], preferred_element_type=f32
            )
            return 0

        lax.fori_loop(0, value_width // 1024, column, 0)
        return grad_query + lax.dot_general(
            grad_scores, keys[spot, :], tn, preferred_element_type=f32
        )

    grad_query = lax.fori_loop(0, reach, second, jnp.zeros((length, key_width), f32))
    gq_ref[0] = grad_query * scale

    @pl.when(step == pl.num_programs(0) - 1)
    def _():
        for slot in range(total):
            place = pl.ds(pl.multiple_of(table_ref[slot] * length, length), length)
            key_grad = (gk_sum[place, :] * scale).astype(bf16)
            value_grad = gv_sum[place, :].astype(bf16)
            if slot < 2:
                gk_own[slot] = key_grad
                gv_own[slot] = value_grad
            else:
                both_oth[slot - 2, :, :value_width] = value_grad
                both_oth[slot - 2, :, value_width:] = key_grad
        down = lax.broadcasted_iota(jnp.int32, (TILE, TILE), 0)
        across = lax.broadcasted_iota(jnp.int32, (TILE, TILE), 1)
        mirror = jnp.where(down + across == TILE - 1, 1.0, 0.0)
        for d in range(rel_out.shape[0]):
            flipped = jnp.dot(
                rel_ref[d + tiles - 1],
                mirror,
                precision=lax.Precision.HIGHEST,
                preferred_element_type=f32,
            )
            wide = jnp.concatenate([flipped, jnp.zeros((TILE, TILE), f32)], axis=1)
            turned = pltpu.roll(wide, 0, 1, stride=1, stride_axis=0)
            rel_out[d] = jnp.sum(turned, axis=0, keepdims=True)


def attend_back(table, q, grads, lse, bias, k_own, k_oth, v_own, v_oth, after=()):
    slots, length, key_width = q.shape
    value_width = v_own.shape[2]
    total = slots + k_oth.shape[0]
    rel_shape = (total * length // TILE, 1, 2 * TILE)
    both_shape = (k_oth.shape[0], length, key_width + value_width)
    anywhere = pl.BlockSpec(memory_space=pl.ANY)

    def all_of(shape):
        return pl.BlockSpec(
            shape, lambda k, t: (0,) * len(shape), pipeline_mode=pl.Buffered(1)
        )

    return pl.pallas_call(
        ignoring(functools.partial(attend_back_body, total=total), 9, len(after)),
        grid_spec=pltpu.PrefetchScalarGridSpec(
            num_scalar_prefetch=1,
            grid=(slots,),
            in_specs=[
                pl.BlockSpec((1, length, key_width), lambda k, t: (k, 0, 0)),
                pl.BlockSpec((1, length, value_width), lambda k, t: (k, 0, 0)),
                pl.BlockSpec((1, 1, length), lambda k, t: (k, 0, 0)),
                all_of(bias.shape),
                anywhere,
                anywhere,
                anywhere,
                anywhere,
            ]
            + [anywhere] * len(after),
            out_specs=[
                pl.BlockSpec((1, length, key_width), lambda k, t: (k, 0, 0)),
                all_of(k_own.shape),
                all_of(v_own.shape),
                all_of(both_shape),
                all_of(rel_shape),
            ],
            scratch_shapes=[
                pltpu.VMEM((total * length, key_width), bf16),
                pltpu.VMEM((total * length, value_width), bf16),
                pltpu.VMEM((total * length, key_width), f32),
                pltpu.VMEM((total * length, value_width), f32),
                pltpu.VMEM((total, length, length), f32),
                pltpu.VMEM((total, length, length), f32),
                pltpu.VMEM(bias.shape, f32),
                pltpu.SemaphoreType.DMA((total,)),
                pltpu.SemaphoreType.DMA((total,)),
            ],
        ),
        out_shape=[
            jax.ShapeDtypeStruct((slots, length, key_width), f32),
            jax.ShapeDtypeStruct(k_own.shape, bf16),
            jax.ShapeDtypeStruct(v_own.shape, bf16),
            jax.ShapeDtypeStruct(both_shape, bf16),
            jax.ShapeDtypeStruct(rel_shape, f32),
        ],
        compiler_params=params(("arbitrary",)),
        name="attend_back",
        cost_estimate=LONG,
    )(table, q, grads, lse, bias, k_own, k_oth, v_own, v_oth, *after)


def bias_body(flag_ref, back_row, front_row, back_ref, front_ref, *, spare):
    tile = pl.program_id(0) - spare
    full = flag_ref[0] == 1

    @pl.when(tile < 0)
    def _():
        back_ref[...] = jnp.full_like(back_ref, MASKED)
        front_ref[...] = jnp.full_like(front_ref, MASKED)

    @pl.when(tile >= 0)
    def _():
        down = lax.broadcasted_iota(jnp.int32, (TILE, TILE), 0)
        across = lax.broadcasted_iota(jnp.int32, (TILE, TILE), 1)
        near = jnp.where(down // STRETCH == across // STRETCH, 1, 0)
        for row, out, ordered in (
            (back_row, back_ref, jnp.where(down <= across, 1, 0)),
            (front_row, front_ref, jnp.where(across <= down, 1, 0)),
        ):
            wide = jnp.broadcast_to(row[0], (TILE, 2 * TILE))
            turned = pltpu.roll(wide, 0, 1, stride=1, stride_axis=0)[:, :TILE]
            allowed = jnp.where(
                tile == 0, jnp.where(full, ordered, ordered * near), jnp.where(full, 1, 0)
            )
            out[0] = jnp.where(allowed == 1, turned, MASKED)


def bias_tiles(relative_bias, spare, full):
    length = relative_bias.shape[0] // 2
    count = length // TILE
    windows = jnp.stack(
        [
            lax.slice_in_dim(relative_bias, length - d * TILE - TILE, length - d * TILE + TILE)
            for d in range(count)
        ]
    )
    front = jnp.concatenate([windows[:, TILE:], windows[:, :TILE]], axis=1)
    back = jnp.concatenate([windows[:, TILE:TILE + 1], windows[:, ::-1][:, TILE:], windows[:, ::-1][:, : TILE - 1]], axis=1)
    row = pl.BlockSpec((1, 1, 2 * TILE), lambda d, t: (jnp.maximum(d - spare, 0), 0, 0))
    out = pl.BlockSpec((1, TILE, TILE), lambda d, t: (d, 0, 0))
    shape = jax.ShapeDtypeStruct((spare + count, TILE, TILE), f32)
    return pl.pallas_call(
        functools.partial(bias_body, spare=spare),
        grid_spec=pltpu.PrefetchScalarGridSpec(
            num_scalar_prefetch=1,
            grid=(spare + count,),
            in_specs=[row, row],
            out_specs=[out, out],
        ),
        out_shape=[shape, shape],
        compiler_params=params(("arbitrary",)),
        name="bias",
    )(full.astype(jnp.int32)[None], back[:, None], front[:, None])


def bias_grad(sums, length):
    count = sums.shape[0]
    shifted = jnp.concatenate([jnp.zeros((count, 1), f32), sums[:, :-1]], axis=1)
    none = jnp.zeros((1, TILE), f32)
    blocks = jnp.concatenate([none, shifted[:, :TILE]]) + jnp.concatenate(
        [shifted[:, TILE:], none]
    )
    return jnp.concatenate(
        [blocks[::-1].reshape(-1), jnp.zeros((2 * length - (count + 1) * TILE,), f32)]
    )


def candidate_body(
    gated_ref, proj_ref, pre_ref, update_ref, x_ref, gain_ref, cand_ref, first_ref, low_ref
):
    cand_in = pre_ref[...].astype(f32) + jnp.dot(
        gated_ref[...], proj_ref[...], preferred_element_type=f32
    )
    cand_ref[...] = cand_in
    x = x_ref[...].astype(f32)
    update = jax.nn.sigmoid(update_ref[...].astype(f32))
    first = x + update * (cand_in * jax.nn.sigmoid(cand_in) - x)
    first_ref[...] = first
    unit, _ = unit_rows_of(first)
    low_ref[...] = (unit * gain_ref[...]).astype(bf16)


def candidate(gated, proj, base, x, gain):
    tokens, width = x.shape
    value_width = gated.shape[1]
    rows = min(256, tokens)
    wide = value_width // width

    def block(columns, at=0):
        return pl.BlockSpec((rows, columns), lambda i: (i, at))

    return pl.pallas_call(
        candidate_body,
        grid=(tokens // rows,),
        in_specs=[
            block(value_width),
            pl.BlockSpec(proj.shape, lambda i: (0, 0), pipeline_mode=pl.Buffered(1)),
            block(width, wide + 1),
            block(width, wide),
            block(width),
            pl.BlockSpec((1, width), lambda i: (0, 0)),
        ],
        out_specs=[block(width)] * 3,
        out_shape=[
            jax.ShapeDtypeStruct((tokens, width), f32),
            jax.ShapeDtypeStruct((tokens, width), f32),
            jax.ShapeDtypeStruct((tokens, width), bf16),
        ],
        compiler_params=params(("arbitrary",)),
        name="candidate",
        cost_estimate=BRIEF,
    )(gated, proj, base, base, x, gain)


def gate_body(
    back_ref,
    cot_a,
    cot_b,
    x_ref,
    cand_ref,
    update_ref,
    reset_ref,
    attended_ref,
    gain_ref,
    proj_ref,
    input_ref,
    main_ref,
    grad_att_ref,
    gain_grad_ref,
):
    width = x_ref.shape[1]
    value_width = proj_ref.shape[0]

    @pl.when(pl.program_id(0) == 0)
    def _():
        gain_grad_ref[...] = jnp.zeros_like(gain_grad_ref)

    x = x_ref[...].astype(f32)
    cand_in = cand_ref[...]
    gate = jax.nn.sigmoid(cand_in)
    candidate = cand_in * gate
    update = jax.nn.sigmoid(update_ref[...].astype(f32))
    change = candidate - x
    unit, inv = unit_rows_of(x + update * change)
    grad_feed = back_ref[...]
    gain_grad_ref[...] += jnp.sum(grad_feed * unit, axis=0, keepdims=True)
    early = pl.program_id(0) < pl.num_programs(0) // 2
    cot = jnp.where(early, cot_a[...].astype(f32), cot_b[...].astype(f32))
    grad_first = cot + norm_back_rows(
        grad_feed, gain_ref[...], unit, inv
    )
    kept = grad_first * (1.0 - update)
    input_ref[...] = kept
    main_ref[:, value_width : value_width + width] = (kept * change * update).astype(bf16)
    grad_cand = (grad_first * update * (gate + candidate * (1.0 - gate))).astype(bf16)
    main_ref[:, value_width + width :] = grad_cand
    for c in range(value_width // 512):
        at = slice(c * 512, (c + 1) * 512)
        grad_gated = mm_nt(grad_cand, proj_ref[at, :])
        reset = reset_ref[:, at].astype(f32)
        open_gate = jax.nn.sigmoid(reset)
        passed = reset * open_gate
        grad_att_ref[:, at] = (grad_gated * passed).astype(bf16)
        main_ref[:, at] = (
            grad_gated
            * attended_ref[:, at].astype(f32)
            * (open_gate + passed * (1.0 - open_gate))
        ).astype(bf16)


def gate(back, cots, x, cand_in, base, attended, gain, proj, after=()):
    tokens, width = x.shape
    value_width = proj.shape[0]
    rows = min(256, tokens // 2)
    half = tokens // rows // 2
    wide = value_width // width

    def block(columns, at=0):
        return pl.BlockSpec((rows, columns), lambda i: (i, at))

    return pl.pallas_call(
        ignoring(gate_body, 10, len(after)),
        grid=(tokens // rows,),
        in_specs=[
            block(width),
            pl.BlockSpec((rows, width), lambda i: (jnp.minimum(i, half - 1), 0)),
            pl.BlockSpec((rows, width), lambda i: (jnp.maximum(i - half, 0), 0)),
            block(width),
            block(width),
            block(width, wide),
            block(value_width),
            block(value_width),
            pl.BlockSpec((1, width), lambda i: (0, 0)),
            pl.BlockSpec(proj.shape, lambda i: (0, 0), pipeline_mode=pl.Buffered(1)),
        ]
        + [pl.BlockSpec(memory_space=pl.ANY)] * len(after),
        out_specs=[
            block(width),
            block(value_width + 2 * width),
            block(value_width),
            pl.BlockSpec((1, width), lambda i: (0, 0)),
        ],
        out_shape=[
            jax.ShapeDtypeStruct((tokens, width), f32),
            jax.ShapeDtypeStruct((tokens, value_width + 2 * width), bf16),
            jax.ShapeDtypeStruct((tokens, value_width), bf16),
            jax.ShapeDtypeStruct((1, width), f32),
        ],
        compiler_params=params(("arbitrary",)),
        name="gate",
        cost_estimate=LONG,
    )(back, *cots, x, cand_in, base, base, attended, gain, proj, *after)


def ordered_transpose(ids_ref, source, plain, ordered):
    plain[...] = source[...].T
    count = ids_ref.shape[0]
    rows = plain.shape[0] // count

    def place(p, _):
        ordered[pl.ds(pl.multiple_of(p * rows, rows), rows), :] = plain[
            pl.ds(pl.multiple_of(ids_ref[p] * rows, rows), rows), :
        ]
        return 0

    lax.fori_loop(0, count, place, 0)


def placed_transpose(places_ref, sources, plain, ordered):
    rows = ordered.shape[0] // places_ref.shape[0]
    for q in range(places_ref.shape[0]):
        place = pl.ds(pl.multiple_of(places_ref[q] * rows, rows), rows)
        start = 0
        for source in sources:
            stop = start + source.shape[0]
            ordered[place, start:stop] = source[:, q * rows : (q + 1) * rows].T
            start = stop


def feed_body(
    ids_ref,
    places_ref,
    low_ref,
    cot_a,
    cot_b,
    first_ref,
    in_ref,
    out_ref,
    result_a,
    result_b,
    back_ref,
    out_send,
    out_keep,
    in_send,
    in_keep,
    total,
    cot_turned,
    low_turned,
    plain,
):
    step = pl.program_id(0)
    half = pl.num_programs(0) // 2
    tokens = low_ref.shape[0]
    middle = tokens // 2
    nt = (((1,), (1,)), ((), ()))

    @pl.when(step == 0)
    def _():
        placed_transpose(places_ref, (cot_a, cot_b), plain, cot_turned)
        ordered_transpose(ids_ref, low_ref, plain, low_turned)
        total[...] = first_ref[...]
        back_ref[...] = jnp.zeros_like(back_ref)

    acts, grads = [], []
    for r, cot_ref in enumerate((cot_a, cot_b)):
        at = slice(r * middle, (r + 1) * middle)
        hidden = jnp.dot(low_ref[at, :], in_ref[...], preferred_element_type=f32)
        grad_act = lax.dot_general(
            cot_ref[...], out_ref[...], nt, preferred_element_type=f32
        )
        gate = jax.nn.sigmoid(hidden)
        act = hidden * gate
        grad = (grad_act * (gate + act * (1.0 - gate))).astype(bf16)
        act = act.astype(bf16)
        total[at, :] += jnp.dot(act, out_ref[...], preferred_element_type=f32)
        back_ref[at, :] += lax.dot_general(
            grad, in_ref[...], nt, preferred_element_type=f32
        )
        acts.append(act)
        grads.append(grad)
    out_grad = jnp.dot(
        cot_turned[...], jnp.concatenate(acts), preferred_element_type=f32
    ).astype(bf16)
    in_grad = jnp.dot(
        low_turned[...], jnp.concatenate(grads), preferred_element_type=f32
    ).astype(bf16)
    split = in_grad.shape[0] // 2
    in_send[...] = in_grad[:split].reshape(in_send.shape)
    in_keep[...] = in_grad[split:].reshape(in_keep.shape)

    @pl.when(step < half)
    def _():
        out_send[0] = out_grad

    @pl.when(step >= half)
    def _():
        out_keep[0] = out_grad

    @pl.when(step == pl.num_programs(0) - 1)
    def _():
        result_a[...] = total[:middle, :].astype(bf16)
        result_b[...] = total[middle:, :].astype(bf16)


def feed(ids, places, low, cots, first_sum, feed_in, feed_out, seq, after=()):
    tokens, width = low.shape
    features = feed_in.shape[1]
    parts = ids.shape[0]
    half = parts // 2
    columns = features // parts
    rows = width // parts
    share = parts // seq
    anywhere = pl.BlockSpec(memory_space=pl.ANY)

    def all_of(shape):
        return pl.BlockSpec(
            shape, lambda i, t, u: (0,) * len(shape), pipeline_mode=pl.Buffered(1)
        )

    def at(i, t):
        return t[jnp.minimum(i, parts - 1)]

    split = pl.BlockSpec(
        (half, 1, 1, rows, columns),
        lambda i, t, u: (0, u[at(i, t) // share], at(i, t) % share, 0, 0),
    )
    return pl.pallas_call(
        ignoring(feed_body, 8, len(after)),
        grid_spec=pltpu.PrefetchScalarGridSpec(
            num_scalar_prefetch=2,
            grid=(parts,),
            in_specs=[
                all_of(low.shape),
                all_of(cots[0].shape),
                all_of(cots[1].shape),
                all_of(first_sum.shape),
                pl.BlockSpec((width, columns), lambda i, t, u: (0, at(i, t))),
                pl.BlockSpec((columns, width), lambda i, t, u: (at(i, t), 0)),
            ]
            + [anywhere] * len(after),
            out_specs=[
                all_of(cots[0].shape),
                all_of(cots[1].shape),
                all_of(low.shape),
                pl.BlockSpec(
                    (1, width, columns), lambda i, t, u: (jnp.minimum(i, half - 1), 0, 0)
                ),
                pl.BlockSpec(
                    (1, width, columns), lambda i, t, u: (jnp.maximum(i - half, 0), 0, 0)
                ),
                split,
                split,
            ],
            scratch_shapes=[
                pltpu.VMEM((tokens, width), f32),
                pltpu.VMEM((width, tokens), bf16),
                pltpu.VMEM((width, tokens), bf16),
                pltpu.VMEM((width, tokens), bf16),
            ],
        ),
        out_shape=[
            jax.ShapeDtypeStruct(cots[0].shape, bf16),
            jax.ShapeDtypeStruct(cots[1].shape, bf16),
            jax.ShapeDtypeStruct((tokens, width), f32),
            jax.ShapeDtypeStruct((half, width, columns), bf16),
            jax.ShapeDtypeStruct((half, width, columns), bf16),
            jax.ShapeDtypeStruct((half, seq, share, rows, columns), bf16),
            jax.ShapeDtypeStruct((half, seq, share, rows, columns), bf16),
        ],
        compiler_params=params(("arbitrary",)),
        name="feed",
        cost_estimate=BRIEF,
    )(ids, places, low, *cots, first_sum, feed_in, feed_out, *after)


def product_body(left_ref, right_ref, out_ref):
    out_ref[...] = jnp.dot(
        left_ref[...], right_ref[...], preferred_element_type=f32
    ).astype(out_ref.dtype)


def product(left, right, tile=1024):
    tokens, depth = left.shape
    columns = right.shape[1]
    return pl.pallas_call(
        product_body,
        grid=(columns // tile,),
        in_specs=[
            pl.BlockSpec(left.shape, lambda i: (0, 0), pipeline_mode=pl.Buffered(1)),
            pl.BlockSpec((depth, tile), lambda i: (0, i)),
        ],
        out_specs=pl.BlockSpec((tokens, tile), lambda i: (0, i)),
        out_shape=jax.ShapeDtypeStruct((tokens, columns), bf16),
        compiler_params=params(("arbitrary",)),
        name="product",
        cost_estimate=BRIEF,
    )(left, right)


def smooth_back_body(
    main_ref, shared_ref, weight_ref, shared_weight_ref, smooth_ref, out_ref, total
):
    step = pl.program_id(0)

    @pl.when(step == 0)
    def _():
        total[...] = mm_nt(shared_ref[...], shared_weight_ref[...])

    total[...] += mm_nt(main_ref[...], weight_ref[...])

    @pl.when(step == pl.num_programs(0) - 1)
    def _():
        out_ref[...] = total[...] * silu_slope(smooth_ref[...])


def smooth_back(main, shared, weight, shared_weight, smoothed, after=()):
    tokens, width = smoothed.shape
    tile = 1024

    def all_of(shape):
        return pl.BlockSpec(shape, lambda i: (0, 0), pipeline_mode=pl.Buffered(1))

    return pl.pallas_call(
        ignoring(smooth_back_body, 5, len(after)),
        grid=(main.shape[1] // tile,),
        in_specs=[
            pl.BlockSpec((tokens, tile), lambda i: (0, i)),
            all_of(shared.shape),
            pl.BlockSpec((width, tile), lambda i: (0, i)),
            all_of(shared_weight.shape),
            all_of(smoothed.shape),
        ]
        + [pl.BlockSpec(memory_space=pl.ANY)] * len(after),
        out_specs=all_of(smoothed.shape),
        out_shape=jax.ShapeDtypeStruct(smoothed.shape, f32),
        scratch_shapes=[pltpu.VMEM(smoothed.shape, f32)],
        compiler_params=params(("arbitrary",)),
        name="smooth_back",
        cost_estimate=LONG,
    )(main, shared, weight, shared_weight, smoothed, *after)


def by_columns_body(ids_ref, places_ref, left_ref, right_ref, send, keep, plain, turned):
    step = pl.program_id(0)
    half = pl.num_programs(0) // 2

    @pl.when(step == 0)
    def _():
        placed_transpose(places_ref, (left_ref,), plain, turned)

    grad = jnp.dot(turned[...], right_ref[...], preferred_element_type=f32).astype(bf16)

    @pl.when(step < half)
    def _():
        send[0] = grad

    @pl.when(step >= half)
    def _():
        keep[0] = grad


def by_columns(ids, places, left, right, after=(), rows=None, at=0):
    tokens = left.shape[0]
    rows = rows or left.shape[1]
    parts = ids.shape[0]
    half = parts // 2
    columns = right.shape[1] // parts
    shape = jax.ShapeDtypeStruct((half, rows, columns), bf16)
    if columns % 128:
        left = left[:, at * rows : (at + 1) * rows]
        grad = mm_tn(left, right).astype(bf16).reshape(rows, parts, columns)
        grad = jnp.take(grad, ids, axis=1).transpose(1, 0, 2)
        grad = grad.reshape(parts, places.shape[0], -1, columns)
        grad = jnp.take(grad, jnp.argsort(places), axis=1).reshape(parts, rows, columns)
        return grad[:half], grad[half:]
    return pl.pallas_call(
        ignoring(by_columns_body, 4, len(after)),
        grid_spec=pltpu.PrefetchScalarGridSpec(
            num_scalar_prefetch=2,
            grid=(parts,),
            in_specs=[
                pl.BlockSpec(
                    (tokens, rows), lambda i, t, u: (0, at), pipeline_mode=pl.Buffered(1)
                ),
                pl.BlockSpec((tokens, columns), lambda i, t, u: (0, t[jnp.minimum(i, parts - 1)])),
            ]
            + [pl.BlockSpec(memory_space=pl.ANY)] * len(after),
            out_specs=[
                pl.BlockSpec(
                    (1, rows, columns), lambda i, t, u: (jnp.minimum(i, half - 1), 0, 0)
                ),
                pl.BlockSpec(
                    (1, rows, columns), lambda i, t, u: (jnp.maximum(i - half, 0), 0, 0)
                ),
            ],
            scratch_shapes=[
                pltpu.VMEM((rows, tokens), bf16),
                pltpu.VMEM((rows, tokens), bf16),
            ],
        ),
        out_shape=[shape, shape],
        compiler_params=params(("arbitrary",)),
        name="by_columns",
        cost_estimate=BRIEF,
    )(ids, places, left, right, *after)


def by_rows_body(ids_ref, places_ref, left_ref, right_ref, send, keep, plain, turned):
    @pl.when(pl.program_id(0) == 0)
    def _():
        ordered_transpose(ids_ref, left_ref, plain, turned)

    grad = jnp.dot(turned[...], right_ref[...], preferred_element_type=f32).astype(bf16)
    middle = grad.shape[0] // 2
    send[...] = grad[:middle].reshape(send.shape)
    keep[...] = grad[middle:].reshape(keep.shape)


def by_rows(ids, places, left, right, seq=1, after=(), cost=BRIEF):
    tokens, rows = left.shape
    parts = ids.shape[0]
    half = parts // 2
    if places is None:
        seq, places = 1, jnp.zeros((1,), jnp.int32)
    columns = right.shape[1] // seq
    tile = min(512, columns)
    share = columns // tile
    shape = jax.ShapeDtypeStruct((half, seq, rows // parts, columns), bf16)
    split = pl.BlockSpec(
        (half, 1, rows // parts, tile), lambda i, t, u: (0, u[jnp.minimum(i // share, seq - 1)], 0, i % share)
    )
    return pl.pallas_call(
        ignoring(by_rows_body, 4, len(after)),
        grid_spec=pltpu.PrefetchScalarGridSpec(
            num_scalar_prefetch=2,
            grid=(seq * share,),
            in_specs=[
                pl.BlockSpec(
                    left.shape, lambda i, t, u: (0, 0), pipeline_mode=pl.Buffered(1)
                ),
                pl.BlockSpec((tokens, tile), lambda i, t, u: (0, i)),
            ]
            + [pl.BlockSpec(memory_space=pl.ANY)] * len(after),
            out_specs=[split, split],
            scratch_shapes=[
                pltpu.VMEM((rows, tokens), bf16),
                pltpu.VMEM((rows, tokens), bf16),
            ],
        ),
        out_shape=[shape, shape],
        compiler_params=params(("arbitrary",)),
        name="by_rows",
        cost_estimate=cost,
    )(ids, places, left, right, *after)


def value_back_body(
    ids_ref,
    places_ref,
    left_ref,
    own_ref,
    other_ref,
    slope_ref,
    proj_ref,
    total_ref,
    send,
    keep,
    plain,
    turned,
):
    @pl.when(pl.program_id(0) == 0)
    def _():
        total_ref[...] = jnp.zeros_like(total_ref)
        ordered_transpose(ids_ref, left_ref, plain, turned)

    grad = own_ref[...].astype(f32)
    for k in range(other_ref.shape[0]):
        grad = grad + other_ref[k].astype(f32)
    grad = (grad * slope_ref[...].astype(f32)).astype(bf16)
    total_ref[...] += mm_nt(grad, proj_ref[...])
    weights = jnp.dot(turned[...], grad, preferred_element_type=f32).astype(bf16)
    middle = weights.shape[0] // 2
    send[...] = weights[:middle].reshape(send.shape)
    keep[...] = weights[middle:].reshape(keep.shape)


def value_back(ids, places, left, own, others, slope, proj, seq, after=()):
    tokens, rows = left.shape
    parts = ids.shape[0]
    half = parts // 2
    columns = proj.shape[1] // seq
    tile = min(512, columns)
    share = columns // tile
    shape = jax.ShapeDtypeStruct((half, seq, rows // parts, columns), bf16)
    split = pl.BlockSpec(
        (half, 1, rows // parts, tile),
        lambda i, t, u: (0, u[jnp.minimum(i // share, seq - 1)], 0, i % share),
    )
    stripe = pl.BlockSpec((tokens, tile), lambda i, t, u: (0, i))
    fixed = pl.BlockSpec(
        (tokens, rows), lambda i, t, u: (0, 0), pipeline_mode=pl.Buffered(1)
    )
    return pl.pallas_call(
        ignoring(value_back_body, 7, len(after)),
        grid_spec=pltpu.PrefetchScalarGridSpec(
            num_scalar_prefetch=2,
            grid=(seq * share,),
            in_specs=[
                fixed,
                stripe,
                pl.BlockSpec((others.shape[0], tokens, tile), lambda i, t, u: (0, 0, i)),
                stripe,
                pl.BlockSpec((rows, tile), lambda i, t, u: (0, i)),
            ]
            + [pl.BlockSpec(memory_space=pl.ANY)] * len(after),
            out_specs=[fixed, split, split],
            scratch_shapes=[
                pltpu.VMEM((rows, tokens), bf16),
                pltpu.VMEM((rows, tokens), bf16),
            ],
        ),
        out_shape=[jax.ShapeDtypeStruct((tokens, rows), f32), shape, shape],
        compiler_params=params(("arbitrary",)),
        name="value_back",
        cost_estimate=LONG,
    )(ids, places, left, own, others, slope, proj, *after)


def stage_body(*refs, jobs):
    ins, outs = list(refs), list(refs[sum(map(sum, jobs)) :])
    for counts, out in zip(jobs, outs):
        for g, count in enumerate(counts):
            total = ins.pop(0)[0].astype(f32)
            for _ in range(count - 1):
                total = total + ins.pop(0)[0].astype(f32)
            out[g] = total.astype(out.dtype)


def stage_sums(jobs, after=(), steps=2, cost=BRIEF):
    for _, rows, _ in jobs:
        while rows % (16 * steps) and steps > 1:
            steps //= 2
    ins, in_specs, out_specs, out_shapes, counts = [], [], [], [], []
    for terms, rows, kind in jobs:
        each = rows // steps
        columns = terms[0][0][0].shape[2]
        for array, entry, start in (term for group in terms for term in group):
            ins.append(array)
            in_specs.append(
                pl.BlockSpec(
                    (1, each, columns),
                    lambda i, entry=entry, first=start // each: (entry, first + i, 0),
                )
            )
        out_specs.append(pl.BlockSpec((len(terms), each, columns), lambda i: (0, i, 0)))
        out_shapes.append(jax.ShapeDtypeStruct((len(terms), rows, columns), kind))
        counts.append([len(group) for group in terms])
    return pl.pallas_call(
        ignoring(functools.partial(stage_body, jobs=counts), len(ins), len(after)),
        grid=(steps,),
        in_specs=in_specs + [pl.BlockSpec(memory_space=pl.ANY)] * len(after),
        out_specs=out_specs,
        out_shape=out_shapes,
        compiler_params=params(("arbitrary",)),
        name="stage_sums",
        cost_estimate=cost,
    )(*ins, *after)


class Layout:
    def __init__(self, mesh):
        self.dp = mesh.shape["dp"]
        self.seq = mesh.shape["seq"]
        self.members = self.seq // 2
        self.chips = self.seq // 4

    def pairs(self, move):
        return [
            (d * self.seq + z, e * self.seq + w)
            for d in range(self.dp)
            for z in range(self.seq)
            for e, w in [move(d, z)]
        ]

    def send(self, value, move):
        return lax.ppermute(value, AXES, self.pairs(move))

    def place(self, sequence, member):
        return member % 2 ^ (1 - sequence % 2), sequence * self.chips + member // 2

    def member(self, core, z):
        sequence = z // self.chips
        return (z % self.chips) * 2 + (core ^ (1 - sequence % 2))

    def home_to_work(self, round_index):
        def move(d, z):
            part = (1 if z >= self.seq // 2 else 0) ^ round_index
            core, at = self.place(2 * (d % 2) + part, min(z, self.seq - 1 - z))
            return d - d % 2 + core, at

        return move

    def outgoing(self, value):
        late = lax.axis_index("seq") >= self.seq // 2
        return [
            lax.dynamic_index_in_dim(value, jnp.where(late, 1 - r, r), 0, False)
            for r in range(2)
        ]

    def to_work(self, value, round_index):
        return self.send(value, self.home_to_work(round_index))

    def homeward(self, value, round_index):
        pairs = [(b, a) for a, b in self.pairs(self.home_to_work(round_index))]
        return lax.ppermute(value, AXES, pairs)

    def gathered(self, back):
        late = lax.axis_index("seq") >= self.seq // 2
        return jnp.stack([jnp.where(late, back[1], back[0]), jnp.where(late, back[0], back[1])])

    def collect(self, values):
        return self.gathered([self.homeward(v, r) for r, v in enumerate(values)])

    def rotate(self, value, by):
        def move(d, z):
            member = (self.member(d % 2, z) + by) % self.members
            core, at = self.place(z // self.chips, member)
            return d - d % 2 + core, at

        return self.send(value, move)

    def gather(self, value):
        return jnp.concatenate([self.rotate(value, by) for by in range(1, self.members)], axis=0)

    def returns(self, others):
        slots = others.shape[0] // (self.members - 1)
        return jnp.stack(
            [
                self.rotate(others[(by - 1) * slots : by * slots], self.members - by).reshape(
                    -1, others.shape[-1]
                )
                for by in range(1, self.members)
            ]
        )

    def orders(self):
        dp, z = lax.axis_index("dp"), lax.axis_index("seq")
        bits = self.dp.bit_length() - 1
        ids = []
        for core in range(2):
            orders = [[0, *range(1, bits)], [0, *reversed(range(1, bits))]]
            flips = []
            for p in range(self.dp):
                order = orders[core if p >= self.dp // 2 else 1 - core]
                flips.append(
                    sum(
                        (0 if p >> (bits - 1 - i) & 1 else 1) << bit
                        for i, bit in enumerate(order)
                    )
                )
            ids.append(dp ^ jnp.array(flips, jnp.int32))
        ids = jnp.where(dp % 2 == 0, ids[0], ids[1])
        bits = self.seq.bit_length() - 1
        flips = [
            sum((0 if p >> (bits - 1 - i) & 1 else 1) << i for i in range(bits))
            for p in range(self.seq)
        ]
        blocks = z ^ jnp.array(flips, jnp.int32)
        return ids, jnp.argsort(blocks).astype(jnp.int32), blocks

    def partner(self, stage):
        bits = self.dp.bit_length() - 1
        if stage == 0:
            return lambda d, z: (d ^ 1, z)
        if stage < bits:
            return lambda d, z: (d ^ (1 << stage if d % 2 == 0 else 1 << (bits - stage)), z)
        return lambda d, z: (d, z ^ (1 << (stage - bits)))

    def turn(self, sums, after, cost=BRIEF):
        sums = [s for s in sums if s.total is None]
        if not sums:
            return after
        jobs = []
        for s in sums:
            s.stage += 1
            ended = s.stage == s.stages
            rows = s.rows if ended else s.rows // 2
            jobs.append((s.terms, rows, f32 if ended and s.over_seq else bf16))
        out = stage_sums(jobs, after, cost=cost)
        for s, held, (_, rows, _) in zip(sums, out, jobs):
            if s.stage == s.stages:
                s.total = held
            else:
                s.terms = [[(a, e, start + rows) for a, e, start in group] for group in s.terms]
                s.rows = rows
                s.send(held)
        return list(out)

    def from_seq(self, held):
        return [
            self.send(held.astype(bf16), lambda d, z: (d, z ^ other))
            for other in range(1, self.seq)
        ]


    def over_dp(self, held):
        bits = self.dp.bit_length() - 1
        for bit in range(bits - 1):
            held = held + self.send(held, lambda d, z: (d ^ (1 << bit), z))
        return held, self.send(held, lambda d, z: (d ^ (1 << (bits - 1)), z))


def later_body(left, right, out):
    out[...] = left[...] + right[...]


def later_sum(left, right, after):
    inside = pl.BlockSpec(memory_space=pltpu.VMEM)
    return pl.pallas_call(
        ignoring(later_body, 2, len(after)),
        in_specs=[inside] * 2 + [pl.BlockSpec(memory_space=pl.ANY)] * len(after),
        out_specs=inside,
        out_shape=jax.ShapeDtypeStruct(left.shape, left.dtype),
        name="later_sum",
        cost_estimate=BRIEF,
    )(left, right, *after)


def pack_body(qx_a, qx_b, qs_a, qs_b, rest_ref, out):
    rows = qx_a.shape[0]
    out[:rows] = qx_a[...] + qx_b[...]
    out[rows : 2 * rows] = qs_a[...] + qs_b[...]
    out[2 * rows :] = rest_ref[...]


def pack(first, second, rest, after=()):
    ins = [v.reshape(-1, 128) for v in (first[0], second[0], first[1], second[1])] + [rest]
    rows = 2 * ins[0].shape[0] + rest.shape[0]
    inside = pl.BlockSpec(memory_space=pltpu.VMEM)
    return pl.pallas_call(
        ignoring(pack_body, 5, len(after)),
        in_specs=[inside] * 5 + [pl.BlockSpec(memory_space=pl.ANY)] * len(after),
        out_specs=inside,
        out_shape=jax.ShapeDtypeStruct((rows, 128), f32),
        name="pack",
        cost_estimate=BRIEF,
    )(*ins, *after)


def finish_body(*refs, terms):
    alpha, damp, beta, eta, alpha_out, damp_out, beta_out, eta_out, *rest = refs[terms:]
    *rest, rows = rest
    total = refs[0][...]
    for term in refs[1:terms]:
        total = total + term[...].astype(f32)
    rows[...] = total
    states = alpha.shape[0]
    groups = alpha.shape[1] // 128
    for c in range(groups):
        at = slice(c * 128, (c + 1) * 128)
        x_sum = rows[pl.ds(c, states, stride=groups), :]
        s_sum = rows[pl.ds(states * groups + c, states, stride=groups), :]
        rate = alpha[:, at] * beta[:, at]
        input_total = eta[:, at] * x_sum
        decay_total = eta[:, at] * rate * s_sum
        alpha_out[:, at] = beta[:, at] * input_total - damp[:, at] * decay_total
        damp_out[:, at] = -alpha[:, at] * decay_total
        beta_out[:, at] = alpha[:, at] * input_total
        eta_out[:, at] = rate * x_sum
    start = 2 * states * groups
    for out in rest:
        out[...] = rows[start : start + out.shape[0]]
        start += out.shape[0]


def finish(terms, alpha, damp, beta, eta, counts):
    inside = pl.BlockSpec(memory_space=pltpu.VMEM)
    rows = terms[0].shape[0]
    shape = jax.ShapeDtypeStruct(alpha.shape, f32)
    return pl.pallas_call(
        functools.partial(finish_body, terms=len(terms)),
        in_specs=[inside] * (len(terms) + 4),
        out_specs=[inside] * (4 + len(counts)),
        out_shape=[shape] * 4 + [jax.ShapeDtypeStruct((n, 128), f32) for n in counts],
        scratch_shapes=[pltpu.VMEM((rows, 128), f32)],
        name="finish",
        cost_estimate=BRIEF,
    )(*terms, alpha, damp, beta, eta)


class Sum:
    def __init__(self, layout, *pairs, over_seq=True):
        self.layout = layout
        self.stage = 0
        self.dp_stages = layout.dp.bit_length() - 1
        self.stages = self.dp_stages + (layout.seq.bit_length() - 1 if over_seq else 0)
        self.over_seq = over_seq
        self.total = None
        pairs = [[v.reshape(1, -1, v.shape[-1]) for v in pair] for pair in pairs]
        self.rows = pairs[0][1].shape[1]
        self.terms = [
            [(kept, 0, 0), (layout.send(sent, layout.partner(0)), 0, 0)] for sent, kept in pairs
        ]

    def send(self, held):
        arrived = self.layout.send(held, self.layout.partner(self.stage))
        for entry, group in enumerate(self.terms):
            group.append((arrived, entry, 0))

    def begin_seq(self, block):
        self.stage = self.dp_stages
        self.stages = self.stage + self.layout.seq.bit_length() - 1
        self.over_seq, self.total = True, None
        block = block.reshape(1, -1, block.shape[-1])
        self.rows = block.shape[1] // 2
        self.terms = [[(block, 0, self.rows)]]
        self.send(block[:, : self.rows])


def mm(a, b):
    return jnp.dot(a, b, preferred_element_type=f32)


def mm_nt(a, b):
    return lax.dot_general(a, b, (((1,), (1,)), ((), ())), preferred_element_type=f32)


def mm_tn(a, b):
    return lax.dot_general(a, b, (((0,), (0,)), ((), ())), preferred_element_type=f32)


def layer(
    layout,
    inputs,
    cotangent,
    full_attention,
    mix_gain,
    smooth_alpha,
    smooth_damp,
    smooth_beta,
    smooth_eta,
    smooth_omega,
    value_proj,
    mix_proj,
    score_affine,
    relative_bias,
    out_proj,
    feed_gain,
    feed_in,
    feed_out,
):
    slots, chunk_rows, width = inputs.shape
    key_width = score_affine.shape[1]
    value_width = value_proj.shape[1]
    tokens = slots * chunk_rows
    total = layout.seq
    seq_length = relative_bias.shape[0] // 2
    block = min(128, chunk_rows)
    core = lax.axis_index("dp") % 2
    z = lax.axis_index("seq")

    sequence = z // layout.chips
    member = layout.member(core, z)
    swap = sequence % 2
    chunks = []
    for by in range(layout.members):
        source = (member - by) % layout.members
        low, high = source, total - 1 - source
        chunks += [jnp.where(swap == 0, low, high), jnp.where(swap == 0, high, low)]
    chunks = jnp.stack(chunks).astype(jnp.int32)
    slot_of = jnp.sum(
        jnp.where(chunks[None, :] == jnp.arange(total)[:, None], jnp.arange(total)[None, :], 0),
        axis=1,
    ).astype(jnp.int32)
    flags = full_attention.astype(f32)
    flags_other = layout.send(flags, lambda d, z: (d ^ 1, z))
    flags = jnp.where(
        core == 0, jnp.concatenate([flags, flags_other]), jnp.concatenate([flags_other, flags])
    )
    full = lax.dynamic_index_in_dim(flags, sequence, 0, False) == 1.0
    table = jnp.concatenate([chunks, slot_of, full.astype(jnp.int32)[None]])
    ids, places, blocks = layout.orders()

    arriving = [
        (slot, at * (chunk_rows // count), layout.to_work(piece, slot))
        for slot, count in ((0, 1), (1, 1))
        for at, piece in enumerate(jnp.split(layout.outgoing(inputs)[slot], count))
    ]
    leaving = layout.outgoing(cotangent)
    bias_back, bias_front = bias_tiles(relative_bias, chunk_rows // TILE - 1, full)

    states = smooth_alpha.shape[0]
    lanes = (states, width // 128, 128)
    decay = 1.0 - smooth_alpha * smooth_damp
    rate = smooth_alpha * smooth_beta
    span = (decay**chunk_rows).reshape(lanes)
    coef = (smooth_eta * rate).reshape(lanes)
    decay_slab = decay.reshape(lanes)
    gain_row = mix_gain[None]
    omega_row = smooth_omega[None]
    mix_shared, mix_main = mix_proj[:, :key_width], mix_proj[:, key_width:]

    held, after = (), (bias_back, bias_front, mix_main, mix_shared, span, coef)
    ready = (table, ids, places, blocks, *leaving)
    for slot, row, piece in arriving:
        held = front(
            piece, slot, row, (slots, chunk_rows), held, gain_row, decay_slab, value_proj, after=after
        )
        after, ready = ready, ()
    normed_low, x, value_low, value_slope, ends = held
    ends_others = layout.gather(ends)
    leaving, ends_others = lax.optimization_barrier((leaving, ends_others))
    cots = [layout.to_work(v, r) for r, v in enumerate(leaving)]
    normed_low = normed_low.reshape(tokens, width)
    value_slope = value_slope.reshape(tokens, value_width)
    value_others = layout.gather(value_low)
    smoothed, mixed, check, shared_pre, query_low, key_low = front_scan(
        table,
        x,
        gain_row,
        decay_slab,
        coef,
        span,
        omega_row,
        ends,
        ends_others,
        mix_shared,
        score_affine,
        block,
    )
    smoothed = smoothed.reshape(tokens, width)
    mixed = mixed.reshape(tokens, width)
    shared_pre = shared_pre.reshape(tokens, key_width)
    key_others = layout.gather(key_low)
    base = product(mixed, mix_main)
    attended, gated, lse = attend(
        table,
        query_low,
        bias_front,
        base.reshape(slots, chunk_rows, -1),
        key_low,
        key_others,
        value_low,
        value_others,
    )
    attended = attended.reshape(tokens, value_width)
    gated = gated.reshape(tokens, value_width)

    flat_low = x.reshape(tokens, width)
    cand_in, first_sum, feed_low = candidate(gated, out_proj, base, flat_low, feed_gain[None])

    result_a, result_b, grad_feed, out_send, out_keep, in_send, in_keep = feed(
        ids, places, feed_low, cots, first_sum, feed_in, feed_out, layout.seq
    )
    home = [layout.homeward(result_a, 0), layout.homeward(result_b, 1)]
    block_out = layout.gathered(home)
    feed_sum = Sum(layout, (out_send, out_keep), (in_send, in_keep))

    grad_input, grad_main, grad_att, feed_gain_grad = gate(
        grad_feed, cots, flat_low, cand_in, base, attended, feed_gain[None], out_proj
    )
    after = layout.turn((feed_sum,), (grad_att,))
    mix_parts = by_rows(ids, None, mixed, grad_main, after=after, cost=LONG)
    proj_parts = by_columns(
        ids,
        places,
        grad_main,
        gated,
        rows=width,
        at=grad_main.shape[1] // width - 1,
        after=mix_parts,
    )
    after = (*proj_parts, *home)
    mix_sum = Sum(layout, mix_parts, over_seq=False)
    proj_sum = Sum(layout, proj_parts)
    grad_query, gk_own, gv_own, both_oth, rel_sums = attend_back(
        table,
        query_low,
        grad_att.reshape(slots, chunk_rows, value_width),
        lse,
        bias_back,
        key_low,
        key_others,
        value_low,
        value_others,
        after=after,
    )
    both_back = layout.returns(both_oth)
    after = layout.turn((feed_sum, proj_sum), (grad_query,), cost=LONG)
    grad_normed, value_send, value_keep = value_back(
        ids,
        places,
        normed_low,
        gv_own.reshape(tokens, value_width),
        both_back,
        value_slope,
        value_proj,
        layout.seq,
        after=after,
    )
    grad_key = jnp.sum(both_back[:, :, value_width:].astype(f32), axis=0) + gk_own.reshape(
        tokens, key_width
    ).astype(f32)
    grad_query = grad_query.reshape(tokens, key_width)
    grad_shared = (
        (grad_query * score_affine[0] + grad_key * score_affine[2]) * silu_slope(shared_pre)
    ).astype(bf16)
    shared_parts = by_rows(ids, None, mixed, grad_shared, after=(grad_normed,))
    shared_sum = Sum(layout, shared_parts, over_seq=False)
    value_sum = Sum(layout, (value_send, value_keep))
    after = layout.turn((mix_sum,), shared_parts)
    grad_smooth = smooth_back(
        grad_main, grad_shared, mix_main, mix_shared, smoothed, after=after
    )
    grad_smooth = grad_smooth.reshape(slots, chunk_rows, width)
    after = layout.turn((feed_sum, value_sum, proj_sum, shared_sum), (grad_smooth,))
    back = back_ends(grad_smooth, decay_slab, after=after)
    back_others = layout.gather(back)
    after = layout.turn((feed_sum, mix_sum, value_sum, shared_sum), (back,))

    def scan_back(slot, after):
        return back_scan(
            table,
            slot,
            x,
            grad_smooth,
            grad_normed.reshape(slots, chunk_rows, width),
            grad_input.reshape(slots, chunk_rows, width),
            check,
            gain_row,
            decay_slab,
            coef,
            span,
            omega_row,
            back,
            back_others,
            after=after,
        )

    first = scan_back(0, after)
    after = layout.turn(
        (feed_sum, mix_sum, value_sum, proj_sum, shared_sum), (first[0],)
    )
    home_first = layout.homeward(first[0], 0)
    while mix_sum.total is None or shared_sum.total is None:
        after = layout.turn((mix_sum, shared_sum), after)
    rows = jnp.concatenate([shared_sum.total[0], mix_sum.total[0]], axis=1)
    rows = rows.reshape(rows.shape[0], layout.seq, -1).transpose(1, 0, 2)
    mix_sum.begin_seq(rows[blocks])
    second = scan_back(1, (*after, mix_sum.terms[0][0][0]))
    affine_grad = jnp.stack(
        [
            jnp.sum(grad_query * shared_pre * jax.nn.sigmoid(shared_pre), axis=0),
            jnp.sum(grad_query, axis=0),
            jnp.sum(grad_key * shared_pre * jax.nn.sigmoid(shared_pre), axis=0),
            jnp.sum(grad_key, axis=0),
        ]
    )
    relative_grad = bias_grad(rel_sums[:, 0], seq_length)
    small = [
        first[3] + second[3],
        first[4] + second[4],
        feed_gain_grad,
        affine_grad,
        relative_grad,
    ]
    small = [v.reshape(-1, 128) for v in small]
    rest = jnp.concatenate(small)
    rest = jnp.pad(rest, ((0, -rest.shape[0] % 16), (0, 0)))
    home_second = layout.homeward(second[0], 1)
    sums = (mix_sum, proj_sum, value_sum, feed_sum)
    turned = layout.turn(sums, (second[0], home_first), cost=LONG)
    totals = layout.over_dp(pack(first[1:3], second[1:3], rest, after=turned))
    after = layout.turn(sums, (*turned, home_second))
    totals = later_sum(*totals, after=after)
    while any(v.total is None for v in sums):
        after = layout.turn(sums, after)
    grad_in = layout.gathered([home_first, home_second]).astype(f32)
    feed_out_grad, feed_in_grad = feed_sum.total[0].T, feed_sum.total[1]
    rows = width // layout.dp
    feed_in_grad = feed_in_grad.reshape(-1, rows, feed_in_grad.shape[-1])
    feed_in_grad = feed_in_grad.transpose(1, 0, 2).reshape(rows, -1)
    out_grad, value_grad = proj_sum.total[0].T, value_sum.total[0]
    mix_grad = mix_sum.total[0]
    alpha_grad, damp_grad, beta_grad, eta_grad, *parts = finish(
        [totals, *layout.from_seq(totals)],
        smooth_alpha,
        smooth_damp,
        smooth_beta,
        smooth_eta,
        [v.shape[0] for v in small],
    )
    parts = [v.reshape(-1) for v in parts]
    return (
        block_out,
        grad_in,
        parts[0],
        alpha_grad,
        damp_grad,
        beta_grad,
        eta_grad,
        parts[1],
        value_grad,
        mix_grad,
        parts[3].reshape(4, key_width),
        parts[4],
        out_grad,
        parts[2],
        feed_in_grad,
        feed_out_grad,
    )


def solution(mesh):
    tokens = P("dp", "seq", None)
    split = P("dp", "seq")
    return jax.shard_map(
        functools.partial(layer, Layout(mesh)),
        mesh=mesh,
        in_specs=(tokens, tokens, P("dp")) + (P(),) * 14,
        out_specs=(tokens, tokens)
        + (P(),) * 6
        + (split, split, P(), P(), split, P(), split, split),
        check_vma=False,
    )
```
